32 devices in a mesh: seq: 8 (over z, x), feat: 4 (over y, core).
Axes of the slice: x: 2, y: 2, z: 4, core: 2. Of those that a mesh axis runs over, the one named last changes fastest.
Arguments:
- tokens: bfloat16 [16, 512, 768], P('feat', 'seq'), may hold values from -6 to 6
- cotangent: bfloat16 [16, 512, 768], P('feat', 'seq'), may hold values from -6 to 6
- doc_starts: int32 [16, 4], P('feat'), may hold values from 1 to 31, as said below
- mixer_gain: float32 [768], replicated, may hold values from 0.5 to 1.5
- query_weight: bfloat16 [768, 768], replicated, may hold values from -0.21875 to 0.21875
- key_weight: bfloat16 [768, 768], replicated, may hold values from -0.21875 to 0.21875
- value_weight: bfloat16 [768, 768], replicated, may hold values from -0.21875 to 0.21875
- out_weight: bfloat16 [768, 768], replicated, may hold values from -0.21875 to 0.21875
- rate_weight: bfloat16 [768, 12], replicated, may hold values from -0.4375 to 0.4375
- rate_bias: float32 [12], replicated, may hold values from -3 to 3
- first_init: float32 [12, 64, 256], replicated, may hold values from -0.75 to 0.75
- first_bias_init: float32 [12, 256], replicated, may hold values from -3 to 3
- second_init: float32 [12, 64, 256], replicated, may hold values from -0.375 to 0.375
- second_bias_init: float32 [12, 64], replicated, may hold values from -3 to 3
- inner_gain: float32 [12, 64], replicated, may hold values from 0.25 to 1.75
- inner_bias: float32 [12, 64], replicated, may hold values from -3 to 3
- feed_gain: float32 [768], replicated, may hold values from 0.5 to 1.5
- gate_weight: bfloat16 [768, 2048], P(None, 'feat'), may hold values from -0.21875 to 0.21875
- up_weight: bfloat16 [768, 2048], P(None, 'feat'), may hold values from -0.21875 to 0.21875
- down_weight: bfloat16 [768, 2048], P(None, 'feat'), may hold values from -0.25 to 0.25
Outputs:
- block_out: bfloat16 [16, 512, 768], P('feat', 'seq')
- input_grad: float32 [16, 512, 768], P('feat', 'seq')
- grad_mixer_gain: float32 [768], replicated
- grad_query_weight: float32 [768, 768], replicated
- grad_key_weight: float32 [768, 768], replicated
- grad_value_weight: float32 [768, 768], replicated
- grad_out_weight: float32 [768, 768], replicated
- grad_rate_weight: float32 [768, 12], replicated
- grad_rate_bias: float32 [12], replicated
- grad_first_init: float32 [12, 64, 256], replicated
- grad_first_bias_init: float32 [12, 256], replicated
- grad_second_init: float32 [12, 64, 256], replicated
- grad_second_bias_init: float32 [12, 64], replicated
- grad_inner_gain: float32 [12, 64], replicated
- grad_inner_bias: float32 [12, 64], replicated
- grad_feed_gain: float32 [768], replicated
- grad_gate_weight: float32 [768, 2048], P(None, 'feat')
- grad_up_weight: float32 [768, 2048], P(None, 'feat')
- grad_down_weight: float32 [768, 2048], P(None, 'feat')
- rate_stats: float32 [2], replicated
The draws below stay inside these ranges and needn't reach their ends.
Inputs may be any that keep to these rules, and one draw needn't show every extreme that they name: `doc_starts`: Mini-batch indices (16 tokens each) at which a document starts; index 0 always starts one. In each aligned block of 4 rows, one row, drawn, has all its starts inside its first 64 tokens.
All inputs are finite; a program needn't handle non-finite values.
Results may differ from the reference program's by a relative error of at most 0.013.
Values may be sent and summed in bfloat16 or wider, within the bound.
A program may use at most 192 MiB of HBM per device.

```python
from functools import partial
import jax
import jax.numpy as jnp
from jax import lax

D = 768
HEADS = 12
HEAD_DIM = 64
INNER = 256
FF = 2048
MB = 16
SPAN = 64
ROWS_DEV = 4
DOCS = 4
LEN = 512
ROWS = 16
MB_ROW = 32


def draw_doc_starts(key, part):
    key = jax.random.fold_in(key, 11)
    spread_key, early_key, pick_key = jax.random.split(key, 3)
    spread = jax.random.randint(spread_key, (ROWS, DOCS), 1, MB_ROW)
    early = jax.random.randint(early_key, (ROWS, DOCS), 1, SPAN // MB)
    chosen_row = jax.random.randint(pick_key, (), 0, ROWS_DEV)
    chosen = jnp.arange(ROWS) % ROWS_DEV == chosen_row
    return jnp.where(chosen[:, None], early, spread).astype(jnp.int32)


def block_levels(key, dims, pieces, least, top_value):
    loudness = 1.0
    for position, parts in pieces:
        heights = jax.random.uniform(jax.random.fold_in(jax.random.fold_in(key, 6), position), (parts,), jnp.float32, least / len(pieces), top_value / len(pieces))
        loudness = loudness * jnp.repeat(jnp.exp(heights), dims[position] // parts).reshape((-1,) + (1,) * (len(dims) - 1 - position))
    return loudness


def bell_draw(stream_key, extent, scale, limit, cuts=(), held_as=jnp.bfloat16):
    values = scale * jax.random.normal(stream_key, extent, jnp.float32)
    if cuts:
        values = values * block_levels(stream_key, extent, cuts, -0.22, 0.18)
    return jnp.clip(values, -limit, limit).astype(held_as)


def setup_inputs(seed: int = 0) -> dict:
    key_of = jax.random.split(jax.random.key(seed), 21)
    return {
        "tokens": bell_draw(key_of[0], (ROWS, LEN, D), 1.0, 6.0, ((0, 4), (1, 8))),
        "cotangent": bell_draw(key_of[1], (ROWS, LEN, D), 1.0, 6.0, ((0, 4), (1, 8))),
        "doc_starts": draw_doc_starts(jax.random.fold_in(key_of[20], 71), 0),
        "mixer_gain": jnp.clip(1.0 + 0.1 * jax.random.normal(key_of[3], (D,), jnp.float32), 0.5, 1.5),
        "query_weight": bell_draw(key_of[4], (D, D), D ** -0.5, 0.21875),
        "key_weight": bell_draw(key_of[5], (D, D), D ** -0.5, 0.21875),
        "value_weight": bell_draw(key_of[6], (D, D), D ** -0.5, 0.21875),
        "out_weight": bell_draw(key_of[7], (D, D), D ** -0.5, 0.21875),
        "rate_weight": bell_draw(key_of[8], (D, HEADS), (D // 4) ** -0.5, 0.4375),
        "rate_bias": bell_draw(key_of[9], (HEADS,), 1.0, 3.0, (), jnp.float32),
        "first_init": bell_draw(key_of[10], (HEADS, HEAD_DIM, INNER), HEAD_DIM ** -0.5, 0.75, (), jnp.float32),
        "first_bias_init": bell_draw(key_of[11], (HEADS, INNER), 0.5, 3.0, (), jnp.float32),
        "second_init": bell_draw(key_of[12], (HEADS, HEAD_DIM, INNER), INNER ** -0.5, 0.375, (), jnp.float32),
        "second_bias_init": bell_draw(key_of[13], (HEADS, HEAD_DIM), 0.5, 3.0, (), jnp.float32),
        "inner_gain": jnp.clip(1.0 + 0.15 * jax.random.normal(key_of[14], (HEADS, HEAD_DIM), jnp.float32), 0.25, 1.75),
        "inner_bias": bell_draw(key_of[15], (HEADS, HEAD_DIM), 0.5, 3.0, (), jnp.float32),
        "feed_gain": jnp.clip(1.0 + 0.1 * jax.random.normal(key_of[16], (D,), jnp.float32), 0.5, 1.5),
        "gate_weight": bell_draw(key_of[17], (D, FF), D ** -0.5, 0.21875, ((1, 4),)),
        "up_weight": bell_draw(key_of[18], (D, FF), D ** -0.5, 0.21875, ((1, 4),)),
        "down_weight": bell_draw(key_of[19], (D, FF), (FF // 4) ** -0.5, 0.25, ((1, 4),)),
    }


@jax.custom_vjp
def low(v):
    return lax.optimization_barrier(v.astype(jnp.bfloat16)).astype(jnp.float32)

@jax.custom_vjp
def low_back(v):
    return v

def low_keep(v):
    return (low(v), None)

def low_pass(kept, grad):
    return (grad,)

def back_keep(v):
    return (v, None)

def back_low(kept, grad):
    return (low(grad),)
low.defvjp(low_keep, low_pass)
low_back.defvjp(back_keep, back_low)
epsilon = 1e-05
highest = lax.Precision.HIGHEST

def matmul(left, right):
    return jnp.dot(left, right, precision=highest, preferred_element_type=jnp.float32)

def layer_norm(vector, gain):
    centered = vector - lax.optimization_barrier(jnp.mean(vector, -1, keepdims=True))
    variance = lax.optimization_barrier(jnp.mean(centered * centered, -1, keepdims=True))
    return centered * lax.rsqrt(variance + epsilon) * gain

def standardize(vector):
    centered = vector - lax.optimization_barrier(jnp.mean(vector, -1, keepdims=True))
    variance = lax.optimization_barrier(jnp.mean(centered * centered, -1, keepdims=True))
    inv_scale = lax.rsqrt(variance + epsilon)
    return (centered * inv_scale, inv_scale)

def gelu_exact(vector):
    return 0.5 * vector * (1.0 + lax.erf(vector * 0.7071067811865476))

def gelu_slope(vector):
    return 0.5 * (1.0 + lax.erf(vector * 0.7071067811865476)) + vector * jnp.exp(-0.5 * vector * vector) * 0.3989422804014327

def inner_step(params, carried, inputs):
    first_init, first_bias_init, second_init, second_bias_init, inner_gain, inner_bias = params
    first_layer, first_bias, second_layer, second_bias = carried
    queries, keys_in, values_in, step_rates, restart = inputs
    first_layer = jnp.where(restart, first_init, first_layer)
    first_bias = jnp.where(restart, first_bias_init, first_bias)
    second_layer = jnp.where(restart, second_init, second_layer)
    second_bias = jnp.where(restart, second_bias_init, second_bias)
    query_heads = jnp.swapaxes(queries, 0, 1)
    key_heads = jnp.swapaxes(keys_in, 0, 1)
    value_heads = jnp.swapaxes(values_in, 0, 1)
    rate_heads = jnp.swapaxes(step_rates, 0, 1)
    hidden_pre = jnp.einsum('hbd,hdi->hbi', key_heads, first_layer, precision=highest) + first_bias[:, None, :]
    hidden_act = gelu_exact(hidden_pre)
    rebuilt = jnp.einsum('hbi,hdi->hbd', hidden_act, second_layer, precision=highest) + second_bias[:, None, :]
    normed_unit, inv_scale = standardize(rebuilt)
    mismatch = normed_unit * inner_gain[:, None, :] + inner_bias[:, None, :] - (value_heads - key_heads)
    scaled = mismatch * inner_gain[:, None, :]
    grad_rebuilt = inv_scale * (scaled - lax.optimization_barrier(jnp.mean(scaled, -1, keepdims=True)) - normed_unit * lax.optimization_barrier(jnp.mean(scaled * normed_unit, -1, keepdims=True)))
    grad_hidden = jnp.einsum('hbd,hdi->hbi', grad_rebuilt, second_layer, precision=highest) * gelu_slope(hidden_pre)
    batch_len = queries.shape[0]
    positions = jnp.arange(batch_len, dtype=jnp.int32)
    causal = (positions[:, None] >= positions[None, :]).astype(jnp.float32)
    weights = causal[None, :, :] * rate_heads[:, None, :]
    first_scores = weights * jnp.einsum('htd,hsd->hts', query_heads, key_heads, precision=highest) + weights
    query_pre = jnp.einsum('htd,hdi->hti', query_heads, first_layer, precision=highest) + first_bias[:, None, :] - jnp.einsum('hts,hsi->hti', first_scores, grad_hidden, precision=highest)
    query_act = gelu_exact(query_pre)
    second_scores = weights * jnp.einsum('hti,hsi->hts', query_act, hidden_act, precision=highest) + weights
    query_rebuilt = jnp.einsum('hti,hdi->htd', query_act, second_layer, precision=highest) + second_bias[:, None, :] - jnp.einsum('hts,hsd->htd', second_scores, grad_rebuilt, precision=highest)
    query_unit, query_scale = standardize(query_rebuilt)
    output = query_heads + query_unit * inner_gain[:, None, :] + inner_bias[:, None, :]
    weighted_hidden = grad_hidden * rate_heads[:, :, None]
    weighted_rebuilt = grad_rebuilt * rate_heads[:, :, None]
    first_layer = first_layer - jnp.einsum('hbd,hbi->hdi', key_heads, weighted_hidden, precision=highest)
    first_bias = first_bias - lax.optimization_barrier(jnp.sum(weighted_hidden, 1))
    second_layer = second_layer - jnp.einsum('hbd,hbi->hdi', weighted_rebuilt, hidden_act, precision=highest)
    second_bias = second_bias - lax.optimization_barrier(jnp.sum(weighted_rebuilt, 1))
    return ((first_layer, first_bias, second_layer, second_bias), jnp.swapaxes(output, 0, 1))

def ttt_row(params, item):
    queries, keys_in, values_in, step_rates, restarts = item
    blocks = queries.shape[0] // MB
    inputs = (queries.reshape(blocks, MB, HEADS, HEAD_DIM), keys_in.reshape(blocks, MB, HEADS, HEAD_DIM), values_in.reshape(blocks, MB, HEADS, HEAD_DIM), step_rates.reshape(blocks, MB, HEADS), restarts)
    start_state = (jnp.zeros_like(params[0]), jnp.zeros_like(params[1]), jnp.zeros_like(params[2]), jnp.zeros_like(params[3]))
    final_state, outputs = lax.scan(jax.checkpoint(partial(inner_step, params)), start_state, inputs)
    return outputs.reshape(blocks * MB, HEADS, HEAD_DIM)

def block_forward(restarts, tokens, mixer_gain, query_weight, key_weight, value_weight, out_weight, rate_weight, rate_bias, first_init, first_bias_init, second_init, second_bias_init, inner_gain, inner_bias, feed_gain, gate_weight, up_weight, down_weight):
    flat_in = tokens.reshape(ROWS * LEN, D)
    act_one = low(layer_norm(flat_in, mixer_gain))
    queries = low_back(matmul(act_one, query_weight))
    keys_all = low_back(matmul(act_one, key_weight))
    values_all = low_back(matmul(act_one, value_weight))
    logits = low_back(matmul(act_one, rate_weight) + rate_bias)
    step_rates = jax.nn.sigmoid(logits) / HEAD_DIM
    params = (first_init, first_bias_init, second_init, second_bias_init, inner_gain, inner_bias)
    items = (queries.reshape(ROWS, LEN, HEADS, HEAD_DIM), keys_all.reshape(ROWS, LEN, HEADS, HEAD_DIM), values_all.reshape(ROWS, LEN, HEADS, HEAD_DIM), step_rates.reshape(ROWS, LEN, HEADS), restarts)
    mixed = lax.map(jax.checkpoint(partial(ttt_row, params)), items)
    branch = low_back(matmul(low(mixed.reshape(ROWS * LEN, D)), out_weight))
    hidden_in = flat_in + branch
    act_two = low(layer_norm(hidden_in, feed_gain))
    gate_pre = low_back(matmul(act_two, gate_weight))
    up_value = low_back(matmul(act_two, up_weight))
    hidden_act = low(jax.nn.silu(gate_pre) * up_value)
    feed_out = low_back(jnp.einsum('nf,df->nd', hidden_act, down_weight, precision=highest))
    return (hidden_in + feed_out, logits)

def reference(tokens, cotangent, doc_starts, mixer_gain, query_weight, key_weight, value_weight, out_weight, rate_weight, rate_bias, first_init, first_bias_init, second_init, second_bias_init, inner_gain, inner_bias, feed_gain, gate_weight, up_weight, down_weight):
    block_ids = jnp.arange(MB_ROW, dtype=jnp.int32)
    restarts = (block_ids[None, :] == 0) | jnp.any(doc_starts[:, :, None] == block_ids[None, None, :], axis=1)
    floats = tuple((item.astype(jnp.float32) for item in (tokens, mixer_gain, query_weight, key_weight, value_weight, out_weight, rate_weight, rate_bias, first_init, first_bias_init, second_init, second_bias_init, inner_gain, inner_bias, feed_gain, gate_weight, up_weight, down_weight)))
    result, pull, rate_logits = jax.vjp(partial(block_forward, restarts), *floats, has_aux=True)
    grads = pull(cotangent.astype(jnp.float32).reshape(ROWS * LEN, D))
    stats = jnp.stack([jnp.mean(rate_logits), jnp.max(rate_logits)])
    return (result.reshape(ROWS, LEN, D).astype(jnp.bfloat16), grads[0], grads[1], grads[2], grads[3], grads[4], grads[5], grads[6], grads[7], grads[8], grads[9], grads[10], grads[11], grads[12], grads[13], grads[14], grads[15], grads[16], grads[17], stats)
```

```python
from functools import partial

import jax
import jax.numpy as jnp
from jax import lax
from jax.experimental import pallas as pl
from jax.experimental.pallas import tpu as pltpu
from jax.sharding import PartitionSpec as P

MB = 16
epsilon = 1e-05
f32, bf16 = jnp.float32, jnp.bfloat16


def dot(a, b):
    return lax.dot_general(a, b, (((1,), (0,)), ((), ())), preferred_element_type=f32)


def dot_nt(a, b):
    return lax.dot_general(a, b, (((1,), (1,)), ((), ())), preferred_element_type=f32)


def dot_tn(a, b):
    return lax.dot_general(a, b, (((0,), (0,)), ((), ())), preferred_element_type=f32)


def low(v):
    return v.astype(bf16)


def gelu_parts(z):
    a = jnp.abs(z)
    d = 1.0 + 0.23164189 * a
    t = pl.reciprocal(d, approx=True)
    t = t * (2.0 - d * t)
    ex = jnp.exp(-0.5 * (z * z))
    poly = t * (
        0.127414796 + t * (-0.142248368 + t * (0.7107068705 + t * (-0.7265760135 + t * 0.5307027145)))
    )
    h = poly * ex
    cdf = jnp.where(z >= 0, 1.0 - h, h)
    pdf = 0.3989422804014327 * ex
    return z * cdf, cdf + z * pdf, pdf


def lane_sum(v):
    return jnp.sum(v, -1, keepdims=True)


def masks(head_dim):
    pair = 2 * head_dim
    rows, cols = 2 * MB, pair
    r = lax.broadcasted_iota(jnp.int32, (rows, cols), 0)
    c = lax.broadcasted_iota(jnp.int32, (rows, cols), 1)
    own = ((r < MB) == (c < head_dim)).astype(f32)
    r = lax.broadcasted_iota(jnp.int32, (rows, rows), 0)
    c = lax.broadcasted_iota(jnp.int32, (rows, rows), 1)
    same = (r < MB) == (c < MB)
    causal = (same & (c <= r)).astype(f32)
    return own, causal, same.astype(bf16)


def spread(v, own):
    return jnp.concatenate([v, v], 0) * own


def fold(v):
    return v[:MB] + v[MB:]


def twice(v):
    return jnp.concatenate([v, v], 1)


def forward_kernel(pairs, head_dim, restart_ref, q_ref, k_ref, v_ref, e_ref, w1i_ref, b1i_ref, w2i_ref, b2i_ref, gain_ref, bias_ref,
                   big_ref, mid_ref, small_ref, n1_ref, pq_ref, uq_ref, n2_ref, out_ref,
                   w1, b1, w2, b2, s_q1, s_x2, s_e2, s_w2, s_b2, s_q):
    j = pl.program_id(0)
    pair = 2 * head_dim
    inv = 1.0 / head_dim
    own, causal, ones = masks(head_dim)

    @pl.when(restart_ref[j] > 0)
    def _():
        w1[...] = w1i_ref[...]
        b1[...] = b1i_ref[...]
        w2[...] = w2i_ref[...]
        b2[...] = b2i_ref[...]

    before = [(s_q1[p], s_x2[p], s_e2[p], s_w2[p], s_b2[p], s_q[p]) for p in range(pairs)]
    for p in range(pairs):
        cols = slice(p * pair, (p + 1) * pair)
        gain, bias = gain_ref[:, cols], bias_ref[:, cols]
        qc, kc, vc = q_ref[:, cols], k_ref[:, cols], v_ref[:, cols]
        kb, qb = low(spread(kc, own)), low(spread(qc, own))
        w1c, w2c = w1[p], w2[p]
        w1b, w2b = low(w1c), low(w2c)
        b1c, b2c = b1[p], b2[p]
        kq = dot(jnp.concatenate([kb, qb], 0), w1b)
        z1 = kq[: 2 * MB] + b1c
        x2, l1, pdf = gelu_parts(z1)
        x2b = low(x2)
        c = dot_nt(x2b, w2b) * own + b2c
        s = lax.rsqrt(lane_sum(c * c) * inv + epsilon)
        u = c * s
        r = u * (gain * gain) + spread((bias - (vc - kc)) * gain, own)
        mr, m2 = lane_sum(r) * inv, lane_sum(r * u) * inv
        g2 = s * (r - mr * own - u * m2)
        e = e_ref[0, p]
        h = dot(low(g2), w2b)
        g1 = h * l1
        e1b, e2b = low(twice(e) * g1), low(e * g2)
        n1 = causal * (dot_nt(qb, kb) + 1.0)
        q1 = kq[2 * MB :] + b1c - dot(low(n1), e1b)
        w1[p] = w1c - dot_tn(kb, e1b)
        b1[p] = b1c - dot(ones, e1b)
        w2[p] = w2c - dot_tn(e2b, x2b)
        b2[p] = b2c - dot(ones, e2b)
        big_ref[0, p, 0:pair] = w1b
        big_ref[0, p, pair : 2 * pair] = w2b
        big_ref[0, p, 2 * pair : 2 * pair + 2 * MB] = x2b
        big_ref[0, p, 2 * pair + 2 * MB : 2 * pair + 4 * MB] = e1b
        mid_ref[0, p, 0 : 2 * MB] = low(g1)
        mid_ref[0, p, 2 * MB : 4 * MB] = low(l1)
        mid_ref[0, p, 4 * MB : 6 * MB] = low(h * pdf * (2.0 - z1 * z1))
        small_ref[0, p, 0 : 2 * MB] = u
        small_ref[0, p, 2 * MB : 4 * MB] = jnp.broadcast_to(s, u.shape)
        small_ref[0, p, 4 * MB : 6 * MB] = r
        small_ref[0, p, 6 * MB : 8 * MB] = jnp.broadcast_to(m2, u.shape)
        small_ref[0, p, 8 * MB : 10 * MB] = g2
        n1_ref[0, p] = low(n1)
        q1p, x2p, e2p, w2p, b2p, qp = before[p]
        s_q1[p], s_x2[p], s_e2[p], s_w2[p], s_b2[p], s_q[p] = q1, x2b, e2b, w2b, b2c, qc
        p2, lq, _ = gelu_parts(q1p)
        p2b = low(p2)
        n2 = causal * (dot_nt(p2b, x2p) + 1.0)
        q2 = dot_nt(p2b, w2p) * own - dot(low(n2), e2p) + b2p
        sq = lax.rsqrt(lane_sum(q2 * q2) * inv + epsilon)
        uq = q2 * sq
        out_ref[:, cols] = qp + fold(uq) * gain + bias
        pq_ref[0, p, 0 : 2 * MB] = p2b
        pq_ref[0, p, 2 * MB : 4 * MB] = low(lq)
        uq_ref[0, p, 0 : 2 * MB] = uq
        uq_ref[0, p, 2 * MB : 4 * MB] = jnp.broadcast_to(sq, uq.shape)
        n2_ref[0, p] = low(n2)


def forward_inner(restarts, q, k, v, e, w1i, b1i, w2i, b2i, gain, bias):
    blocks, pairs, _, pair = e.shape
    head_dim = pair // 2
    inner = w1i.shape[-1]
    steps = blocks + 1
    last = blocks - 1
    tok = pl.BlockSpec((MB, pairs * pair), lambda j, r: (jnp.minimum(j, last), 0))
    whole = lambda a: pl.BlockSpec(a.shape, lambda j, r: (0,) * a.ndim)

    def per_step(rows, width, dtype):
        return (
            jax.ShapeDtypeStruct((steps, pairs, rows, width), dtype),
            pl.BlockSpec((1, pairs, rows, width), lambda j, r: (j, 0, 0, 0)),
        )

    outs = [
        per_step(2 * pair + 4 * MB, inner, bf16),
        per_step(6 * MB, inner, bf16),
        per_step(10 * MB, pair, f32),
        per_step(2 * MB, 2 * MB, bf16),
        per_step(4 * MB, inner, bf16),
        per_step(4 * MB, pair, f32),
        per_step(2 * MB, 2 * MB, bf16),
        (
            jax.ShapeDtypeStruct((steps * MB, pairs * pair), f32),
            pl.BlockSpec((MB, pairs * pair), lambda j, r: (j, 0)),
        ),
    ]
    return pl.pallas_call(
        partial(forward_kernel, pairs, head_dim),
        grid_spec=pltpu.PrefetchScalarGridSpec(
            num_scalar_prefetch=1,
            grid=(steps,),
            in_specs=[tok, tok, tok, pl.BlockSpec((1, pairs, 2 * MB, pair), lambda j, r: (jnp.minimum(j, last), 0, 0, 0))]
            + [whole(a) for a in (w1i, b1i, w2i, b2i, gain, bias)],
            out_specs=[o[1] for o in outs],
            scratch_shapes=[
                pltpu.VMEM((pairs, pair, inner), f32),
                pltpu.VMEM((pairs, 2 * MB, inner), f32),
                pltpu.VMEM((pairs, pair, inner), f32),
                pltpu.VMEM((pairs, 2 * MB, pair), f32),
                pltpu.VMEM((pairs, 2 * MB, inner), f32),
                pltpu.VMEM((pairs, 2 * MB, inner), bf16),
                pltpu.VMEM((pairs, 2 * MB, pair), bf16),
                pltpu.VMEM((pairs, pair, inner), bf16),
                pltpu.VMEM((pairs, 2 * MB, pair), f32),
                pltpu.VMEM((pairs, MB, pair), f32),
            ],
        ),
        out_shape=[o[0] for o in outs],
        compiler_params=pltpu.CompilerParams(vmem_limit_bytes=48 * 1024 * 1024),
        name="inner_forward",
    )(restarts, q, k, v, e, w1i, b1i, w2i, b2i, gain, bias)


def backward_kernel(pairs, head_dim, restart_ref,
                    qq_ref, kq_ref, doq_ref, eq_ref, bigq_ref, g2q_ref, n1_ref, pqq_ref, uqq_ref, n2_ref,
                    q_ref, k_ref, v_ref, do_ref, e_ref, big_ref, mid_ref, small_ref, pq_ref, uq_ref, gain_ref, bias_ref,
                    dq_ref, dk_ref, dv_ref, de_ref, gw1, gb1, gw2, gb2, ggain, gbias,
                    w1, b1, w2, b2, s_e1, s_e2, s_k, s_x2, s_q1, s_q2, s_q):
    j = pl.program_id(0)
    steps = pl.num_programs(0)
    pair = 2 * head_dim
    inv = 1.0 / head_dim
    own, causal, ones = masks(head_dim)

    @pl.when(j <= 1)
    def _():
        for ref in (w1, b1, w2, b2, gw1, gb1, gw2, gb2, ggain, gbias):
            ref[...] = jnp.zeros_like(ref)

    before = [(s_e1[p], s_e2[p], s_k[p], s_x2[p], s_q1[p], s_q2[p], s_q[p]) for p in range(pairs)]
    for p in range(pairs):
        cols = slice(p * pair, (p + 1) * pair)
        gain, bias = gain_ref[:, cols], bias_ref[:, cols]
        qb, kb, do = low(spread(qq_ref[:, cols], own)), low(spread(kq_ref[:, cols], own)), doq_ref[:, cols]
        w1b, w2b = bigq_ref[0, p, 0:pair], bigq_ref[0, p, pair : 2 * pair]
        x2b, e1b = bigq_ref[0, p, 2 * pair : 2 * pair + 2 * MB], bigq_ref[0, p, 2 * pair + 2 * MB : 2 * pair + 4 * MB]
        e2b = low(eq_ref[0, p] * g2q_ref[0, p])
        n1b, n2b = n1_ref[0, p], n2_ref[0, p]
        p2b, lq = pqq_ref[0, p, 0 : 2 * MB], pqq_ref[0, p, 2 * MB : 4 * MB].astype(f32)
        uq, sq = uqq_ref[0, p, 0 : 2 * MB], uqq_ref[0, p, 2 * MB : 4 * MB]
        w = spread(do * gain, own)
        new_q2 = low(sq * (w - (lane_sum(w) * inv) * own - uq * (lane_sum(w * uq) * inv)))
        dpx = low(-causal * dot_nt(new_q2, e2b))
        new_q1 = low((dot(new_q2, w2b) + dot(dpx, x2b)) * lq)
        dqk = low(-causal * dot_nt(new_q1, e1b))
        new_e1 = dot_tn(n1b, new_q1)
        new_e2 = dot_tn(n2b, new_q2)
        new_k = dot_tn(dqk, qb)
        new_x2 = dot_tn(dpx, p2b)
        new_q = do + fold((dot_nt(new_q1, w1b) + dot(dqk, kb)) * own)
        e1q, e2q, dkq, x2q, dq1, dq2, dqc = before[p]
        s_e1[p], s_e2[p], s_k[p], s_x2[p], s_q1[p], s_q2[p], s_q[p] = (
            new_e1, new_e2, new_k, new_x2, new_q1, new_q2, new_q,
        )
        qc, kc, vc, do = q_ref[:, cols], k_ref[:, cols], v_ref[:, cols], do_ref[:, cols]
        qb, kb = low(spread(qc, own)), low(spread(kc, own))
        w1b, w2b = big_ref[0, p, 0:pair], big_ref[0, p, pair : 2 * pair]
        x2b, e1b = big_ref[0, p, 2 * pair : 2 * pair + 2 * MB], big_ref[0, p, 2 * pair + 2 * MB : 2 * pair + 4 * MB]
        g1, l1, hg = (mid_ref[0, p, i * 2 * MB : (i + 1) * 2 * MB].astype(f32) for i in range(3))
        u, s, r, m2, g2 = (small_ref[0, p, i * 2 * MB : (i + 1) * 2 * MB] for i in range(5))
        p2b, uq = pq_ref[0, p, 0 : 2 * MB], uq_ref[0, p, 0 : 2 * MB]
        e = e_ref[0, p]
        e2b = low(e * g2)
        dw1, dw2, db1, db2 = w1[p], w2[p], b1[p], b2[p]
        dw1b, dw2b = low(dw1), low(dw2)
        de1 = -(e1q + dot(kb, dw1b) + db1)
        de2 = -(e2q + dot_nt(x2b, dw2b) * own + db2)
        dk = dkq - dot_nt(e1b, dw1b) * own
        dx2 = x2q - dot(e2b, dw2b)
        de_ref[0, p] = jnp.broadcast_to(lane_sum(g1 * de1) + lane_sum(g2 * de2), u.shape)
        dg1 = twice(e) * de1
        dh = low(dg1 * l1)
        dg2 = e * de2 + dot_nt(dh, w2b) * own
        ma, mg = lane_sum(dg2 * u) * inv, lane_sum(dg2) * inv
        dr = s * (dg2 - mg * own - u * ma)
        gg = gain * gain
        du = dr * gg - s * (dg2 * m2 + r * ma)
        md, mu = lane_sum(du) * inv, lane_sum(du * u + dg2 * g2) * inv
        dz2 = low(s * (du - md * own - u * mu))
        dx2 = dx2 + dot(dz2, w2b)
        dz1 = low(dg1 * hg + dx2 * l1)
        dk = dk + dot_nt(dz1, w1b) * own
        drg = fold(dr) * gain
        dq_ref[:, cols] = low(dqc)
        dk_ref[:, cols] = low(fold(dk) + drg)
        dv_ref[:, cols] = low(-drg)
        ggain[:, cols] += fold(do_spread_times(do, uq)) + fold(dr * u) * (2.0 * gain) + fold(dr) * (bias - (vc - kc))
        gbias[:, cols] += do + drg
        ndw1 = dw1 + dot_tn(jnp.concatenate([qb, kb], 0), jnp.concatenate([dq1, dz1], 0))
        ndw2 = dw2 + dot_tn(jnp.concatenate([dq2, low(g2), dz2], 0), jnp.concatenate([p2b, dh, x2b], 0))
        ndb1 = db1 + dot(ones, dq1) + dot(ones, dz1)
        ndb2 = db2 + dot(ones, dq2) + dot(ones, dz2)
        w1[p], w2[p], b1[p], b2[p] = ndw1, ndw2, ndb1, ndb2

    @pl.when(restart_ref[jnp.minimum(steps - 1 - j, steps - 2)] > 0)
    def _():
        gw1[...] += w1[...]
        gb1[...] += b1[...]
        gw2[...] += w2[...]
        gb2[...] += b2[...]
        for ref in (w1, b1, w2, b2):
            ref[...] = jnp.zeros_like(ref)


def do_spread_times(do, uq):
    return jnp.concatenate([do, do], 0) * uq


def backward_inner(restarts, q, k, v, do, e, saved, gain, bias):
    big, mid, small, n1, pq, uq, n2 = saved
    blocks, pairs, _, pair = e.shape
    head_dim = pair // 2
    inner = big.shape[-1]
    steps = blocks + 1
    now = lambda j: jnp.minimum(blocks - j, blocks - 1)
    ahead = lambda j: jnp.maximum(blocks - 1 - j, 0)
    tok = lambda at: pl.BlockSpec((MB, pairs * pair), lambda j, r: (at(j), 0))

    def block(a, at, rows=None, part=0):
        shape = (1, pairs, rows or a.shape[2], a.shape[3])
        return pl.BlockSpec(shape, lambda j, r: (at(j), 0, part, 0))

    whole = lambda a: pl.BlockSpec(a.shape, lambda j, r: (0,) * a.ndim)
    later = lambda j: ahead(j) + 1
    at_now = lambda j: now(j) + 1
    operands = [
        (q, tok(ahead)), (k, tok(ahead)), (do, tok(ahead)), (e, block(e, ahead)), (big, block(big, ahead)),
        (small, block(small, ahead, 2 * MB, 4)), (n1, block(n1, ahead)), (pq, block(pq, later)), (uq, block(uq, later)),
        (n2, block(n2, later)),
        (q, tok(now)), (k, tok(now)), (v, tok(now)), (do, tok(now)), (e, block(e, now)), (big, block(big, now)),
        (mid, block(mid, now)), (small, block(small, now)), (pq, block(pq, at_now, 2 * MB)), (uq, block(uq, at_now, 2 * MB)),
        (gain, whole(gain)), (bias, whole(bias)),
    ]
    width = pairs * pair
    tok_out = (jax.ShapeDtypeStruct((steps * MB, width), bf16), pl.BlockSpec((MB, width), lambda j, r: (blocks - j, 0)))
    state = [((pairs, pair, inner), f32), ((pairs, 2 * MB, inner), f32), ((pairs, pair, inner), f32), ((pairs, 2 * MB, pair), f32)]
    keep = lambda shape: (jax.ShapeDtypeStruct(shape, f32), pl.BlockSpec(shape, lambda j, r: (0,) * len(shape)))
    outs = [tok_out] * 3 + [
        (jax.ShapeDtypeStruct((steps, pairs, 2 * MB, pair), f32), pl.BlockSpec((1, pairs, 2 * MB, pair), lambda j, r: (blocks - j, 0, 0, 0)))
    ] + [keep(shape) for shape, _ in state] + [keep((MB, width))] * 2
    return pl.pallas_call(
        partial(backward_kernel, pairs, head_dim),
        grid_spec=pltpu.PrefetchScalarGridSpec(
            num_scalar_prefetch=1,
            grid=(steps,),
            in_specs=[o[1] for o in operands],
            out_specs=[o[1] for o in outs],
            scratch_shapes=[pltpu.VMEM(shape, kind) for shape, kind in state] + [
                pltpu.VMEM((pairs, 2 * MB, inner), f32),
                pltpu.VMEM((pairs, 2 * MB, pair), f32),
                pltpu.VMEM((pairs, 2 * MB, pair), f32),
                pltpu.VMEM((pairs, 2 * MB, inner), f32),
                pltpu.VMEM((pairs, 2 * MB, inner), bf16),
                pltpu.VMEM((pairs, 2 * MB, pair), bf16),
                pltpu.VMEM((pairs, MB, pair), f32),
            ],
        ),
        out_shape=[o[0] for o in outs],
        compiler_params=pltpu.CompilerParams(vmem_limit_bytes=48 * 1024 * 1024),
        name="inner_backward",
    )(restarts, *[o[0] for o in operands])


def normalize(vector, gain):
    centered = vector - jnp.mean(vector, -1, keepdims=True)
    variance = jnp.mean(centered * centered, -1, keepdims=True)
    inv_scale = lax.rsqrt(variance + epsilon)
    normed_unit = centered * inv_scale
    return (normed_unit * gain, normed_unit, inv_scale)


def norm_back(grad_out, gain, normed_unit, inv_scale):
    scaled = grad_out * gain
    return inv_scale * (
        scaled
        - jnp.mean(scaled, -1, keepdims=True)
        - normed_unit * jnp.mean(scaled * normed_unit, -1, keepdims=True)
    )


SEQ = ("row", "group")


def per_device(
    tokens,
    cotangent,
    doc_starts,
    mixer_gain,
    query_weight,
    key_weight,
    value_weight,
    out_weight,
    rate_weight,
    rate_bias,
    first_init,
    first_bias_init,
    second_init,
    second_bias_init,
    inner_gain,
    inner_bias,
    feed_gain,
    gate_weight,
    up_weight,
    down_weight,
):
    rows, span, width = tokens.shape
    heads, head_dim, inner = first_init.shape
    groups = lax.axis_size("group")
    feats = lax.axis_size("feat")
    row, group = lax.axis_index("row"), lax.axis_index("group")
    count = rows * span
    length = span * rows * groups
    blocks = length // MB
    pairs = -(-heads // (2 * groups))
    mine = 2 * pairs
    pair = 2 * head_dim
    cols = mine * head_dim
    spare = mine * groups - heads

    def own_heads(array, axis, per_head=1):
        if spare:
            pad = [(0, 0)] * array.ndim
            pad[axis] = (0, spare * per_head)
            array = jnp.pad(array, pad)
        return lax.dynamic_slice_in_dim(array, group * mine * per_head, mine * per_head, axis)

    def to_rows(array):
        got = lax.all_to_all(jnp.repeat(array, groups, 0), SEQ, 0, 0, tiled=True)
        return got.reshape(length, array.shape[-1])

    def from_rows(array):
        parts = array.reshape(rows * groups, span, array.shape[-1])
        got = lax.all_to_all(parts, SEQ, 0, 0, tiled=True)
        return got.reshape(rows, groups, span, array.shape[-1])

    row_in = to_rows(tokens).astype(f32)
    act_row = low(normalize(row_in, mixer_gain)[0])
    w_q, w_k, w_v = (own_heads(w, 1, head_dim) for w in (query_weight, key_weight, value_weight))
    w_o = own_heads(out_weight, 0, head_dim)
    w_r = own_heads(rate_weight, 1)
    queries, keys, values = (dot(act_row, w) for w in (w_q, w_k, w_v))
    logits = dot(act_row, w_r) + own_heads(rate_bias, 0)
    sigma = jax.nn.sigmoid(logits)
    rates = sigma / head_dim
    e = jnp.broadcast_to(
        rates.reshape(blocks, MB, pairs, 2).transpose(0, 2, 3, 1).reshape(blocks, pairs, 2 * MB, 1),
        (blocks, pairs, 2 * MB, pair),
    )
    block_ids = jnp.arange(blocks, dtype=jnp.int32)
    starts = lax.dynamic_index_in_dim(doc_starts, row, 0, False)
    restarts = ((block_ids == 0) | jnp.any(starts[:, None] == block_ids[None], 0)).astype(jnp.int32)
    pack = lambda a: own_heads(a, 0).reshape(pairs, pair, inner)
    start_first = pack(first_init)
    start_second = pack(second_init - jnp.mean(second_init, 1, keepdims=True))
    start_first_bias = jnp.repeat(own_heads(first_bias_init, 0).reshape(pairs, 2, 1, inner), MB, 2).reshape(
        pairs, 2 * MB, inner
    )
    centered = own_heads(second_bias_init - jnp.mean(second_bias_init, 1, keepdims=True), 0)
    start_second_bias = (
        jnp.eye(2, dtype=f32)[None, :, None, :, None] * centered.reshape(pairs, 1, 1, 2, head_dim)
    ) * jnp.ones((1, 1, MB, 1, 1), f32)
    start_second_bias = start_second_bias.reshape(pairs, 2 * MB, pair)
    gain, bias = own_heads(inner_gain, 0).reshape(1, cols), own_heads(inner_bias, 0).reshape(1, cols)
    *saved, mixed = forward_inner(
        jnp.concatenate([restarts, jnp.zeros((1,), jnp.int32)]),
        queries, keys, values, e, start_first, start_first_bias, start_second, start_second_bias, gain, bias,
    )
    mixed_row = low(mixed[MB:])
    mixed_low = from_rows(mixed_row).transpose(0, 2, 1, 3).reshape(count, groups * cols)[:, :width]

    flat_in = tokens.astype(f32).reshape(count, width)
    hidden_in = flat_in + dot(mixed_low, out_weight)
    normed_two, unit_two, scale_two = normalize(hidden_in, feed_gain)
    act_two = low(normed_two)
    grad_low = cotangent.reshape(count, width)
    group_grad = lax.all_gather(grad_low, "feat", axis=0, tiled=True)
    grad_act = dot(group_grad, down_weight)
    group_rows = lax.all_gather(act_two, "feat", axis=0, tiled=True)
    gate_pre, up_value = dot(group_rows, gate_weight), dot(group_rows, up_weight)
    gate_sig = jax.nn.sigmoid(gate_pre)
    silu = gate_pre * gate_sig
    hidden_act = low(silu * up_value)
    grad_gate = low(grad_act * up_value * gate_sig * (1.0 + gate_pre * (1.0 - gate_sig)))
    grad_up = low(grad_act * silu)
    grad_act_two = lax.psum_scatter(
        low(dot_nt(grad_gate, gate_weight) + dot_nt(grad_up, up_weight)), "feat", scatter_dimension=0, tiled=True
    ).astype(f32)
    feed_out = lax.psum_scatter(
        low(dot_nt(hidden_act, down_weight)), "feat", scatter_dimension=0, tiled=True
    ).astype(f32)
    block_out = low(hidden_in + feed_out).reshape(rows, span, width)
    feed_grads = lax.psum(
        (low(dot_tn(group_rows, grad_gate)), low(dot_tn(group_rows, grad_up)), low(dot_tn(group_grad, hidden_act))), SEQ
    )
    grad_feed_gain = jnp.sum(grad_act_two * unit_two, 0)
    grad_hidden = grad_low.astype(f32) + norm_back(grad_act_two, feed_gain, unit_two, scale_two)

    branch_row = to_rows(low(grad_hidden).reshape(rows, span, width))
    grad_mixed = dot_nt(branch_row, w_o)
    grad_out_rows = dot_tn(mixed_row, branch_row)
    grad_q, grad_k, grad_v, grad_e, g_first, g_first_bias, g_second, g_second_bias, g_gain, g_bias = backward_inner(
        restarts, queries, keys, values, grad_mixed, e, saved, gain, bias
    )
    grad_q, grad_k, grad_v = grad_q[:length], grad_k[:length], grad_v[:length]
    grad_rates = grad_e[:blocks, :, :, 0].reshape(blocks, pairs, 2, MB).transpose(0, 3, 1, 2).reshape(length, mine)
    grad_logits = low(grad_rates * sigma * (1.0 - sigma) / head_dim)
    part = dot_nt(grad_q, w_q) + dot_nt(grad_k, w_k) + dot_nt(grad_v, w_v) + dot_nt(grad_logits, w_r)
    grad_act_one = jnp.sum(from_rows(low(part)).astype(f32), 1).reshape(count, width)
    _, unit_one, scale_one = normalize(flat_in, mixer_gain)
    input_grad = grad_hidden + norm_back(grad_act_one, mixer_gain, unit_one, scale_one)
    grad_mixer_gain = jnp.sum(grad_act_one * unit_one, 0)

    g_second = g_second.reshape(mine, head_dim, inner)
    g_second = g_second - jnp.mean(g_second, 1, keepdims=True)
    large = (
        dot_tn(act_row, grad_q),
        dot_tn(act_row, grad_k),
        dot_tn(act_row, grad_v),
        grad_out_rows,
        g_first.reshape(mine * head_dim, inner),
        g_second.reshape(mine * head_dim, inner),
    )
    large = lax.psum(tuple(low(a) for a in large), ("row", "feat"))
    join = lambda a, axis, size: lax.slice_in_dim(
        lax.all_gather(a, "group", axis=axis, tiled=True), 0, size, axis=axis
    ).astype(f32)
    g_query, g_key, g_value = (join(a, 1, width) for a in large[:3])
    g_out = join(large[3], 0, width)
    g_first, g_second = (join(a, 0, width).reshape(heads, head_dim, inner) for a in large[4:])

    g_first_bias = g_first_bias.reshape(mine, MB, inner)[:, 0]
    g_second_bias = jnp.stack(
        [g_second_bias[:, h * MB, h * head_dim : (h + 1) * head_dim] for h in range(2)], 1
    ).reshape(mine, head_dim)
    g_second_bias = g_second_bias - jnp.mean(g_second_bias, 1, keepdims=True)
    used = (group * mine + jnp.arange(mine)) < heads
    per_head = jnp.concatenate(
        [
            g_first_bias,
            g_second_bias,
            jnp.sum(g_gain, 0).reshape(mine, head_dim),
            jnp.sum(g_bias, 0).reshape(mine, head_dim),
            dot_tn(grad_logits, act_row),
            jnp.sum(grad_logits.astype(f32), 0)[:, None],
            jnp.sum(logits, 0)[:, None],
        ],
        1,
    )
    slots = lax.dynamic_update_slice(
        jnp.zeros((groups * mine, per_head.shape[1]), f32), per_head, (group * mine, 0)
    )[:heads]
    places = rows * groups * feats
    place = (row * groups + group) * feats + lax.axis_index("feat")
    top = jnp.max(jnp.where(used[None], logits, -jnp.inf))
    top = jnp.where(jnp.any(used), top, jnp.finfo(f32).min)
    tops = jnp.where(jnp.arange(places) == place, top, 0.0)
    slots, g_mixer, g_feed, tops = lax.psum((slots, grad_mixer_gain, grad_feed_gain, tops), ("row", "group", "feat"))
    at = [0, inner, inner + head_dim, inner + 2 * head_dim, inner + 3 * head_dim, inner + 3 * head_dim + width]
    total = jnp.sum(slots[:, at[5] + 1])
    stats = jnp.stack([total / (places * count * heads), jnp.max(tops)])
    return (
        block_out,
        input_grad.reshape(rows, span, width),
        g_mixer,
        g_query,
        g_key,
        g_value,
        g_out,
        slots[:, at[4] : at[5]].T,
        slots[:, at[5]],
        g_first,
        slots[:, : at[1]],
        g_second,
        slots[:, at[1] : at[2]],
        slots[:, at[2] : at[3]],
        slots[:, at[3] : at[4]],
        g_feed,
        feed_grads[0].astype(f32),
        feed_grads[1].astype(f32),
        feed_grads[2].astype(f32),
        stats,
    )


def solution(mesh):
    feats = mesh.shape["feat"]

    def run(*arrays):
        rows = arrays[0].shape[0] // feats
        grid = jax.sharding.Mesh(mesh.devices.reshape(rows, -1, feats), ("row", "group", "feat"))
        by_token = P("feat", SEQ, None)
        by_hidden = P(None, "feat")
        return jax.shard_map(
            per_device,
            mesh=grid,
            in_specs=(by_token, by_token, P("feat", None)) + (P(),) * 14 + (by_hidden,) * 3,
            out_specs=(by_token, by_token) + (P(),) * 14 + (by_hidden,) * 3 + (P(),),
            check_vma=False,
        )(*arrays)

    return run
```

```python
from functools import partial

import jax
import jax.numpy as jnp
from jax import lax
from jax.experimental import pallas as pl
from jax.experimental.pallas import tpu as pltpu
from jax.sharding import PartitionSpec as P

MB = 16
epsilon = 1e-05
f32, bf16 = jnp.float32, jnp.bfloat16


def dot(a, b):
    return lax.dot_general(a, b, (((1,), (0,)), ((), ())), preferred_element_type=f32)


def dot_nt(a, b):
    return lax.dot_general(a, b, (((1,), (1,)), ((), ())), preferred_element_type=f32)


def dot_tn(a, b):
    return lax.dot_general(a, b, (((0,), (0,)), ((), ())), preferred_element_type=f32)


def low(v):
    return v.astype(bf16)


def gelu_parts(z):
    a = jnp.abs(z)
    d = 1.0 + 0.23164189 * a
    t = pl.reciprocal(d, approx=True)
    t = t * (2.0 - d * t)
    ex = jnp.exp(-0.5 * (z * z))
    poly = t * (
        0.127414796 + t * (-0.142248368 + t * (0.7107068705 + t * (-0.7265760135 + t * 0.5307027145)))
    )
    h = poly * ex
    cdf = jnp.where(z >= 0, 1.0 - h, h)
    pdf = 0.3989422804014327 * ex
    return z * cdf, cdf + z * pdf, pdf


def lane_sum(v):
    return jnp.sum(v, -1, keepdims=True)


def masks(head_dim):
    pair = 2 * head_dim
    rows, cols = 2 * MB, pair
    r = lax.broadcasted_iota(jnp.int32, (rows, cols), 0)
    c = lax.broadcasted_iota(jnp.int32, (rows, cols), 1)
    own = ((r < MB) == (c < head_dim)).astype(f32)
    r = lax.broadcasted_iota(jnp.int32, (rows, rows), 0)
    c = lax.broadcasted_iota(jnp.int32, (rows, rows), 1)
    same = (r < MB) == (c < MB)
    causal = (same & (c <= r)).astype(f32)
    return own, causal, same.astype(bf16)


def spread(v, own):
    return jnp.concatenate([v, v], 0) * own


def fold(v):
    return v[:MB] + v[MB:]


def twice(v):
    return jnp.concatenate([v, v], 1)


def forward_kernel(pairs, head_dim, restart_ref, q_ref, k_ref, v_ref, e_ref, w1i_ref, b1i_ref, w2i_ref, b2i_ref, gain_ref, bias_ref,
                   big_ref, mid_ref, small_ref, n1_ref, pq_ref, uq_ref, n2_ref, out_ref,
                   w1, b1, w2, b2, s_q1, s_x2, s_e2, s_w2, s_b2, s_q):
    j = pl.program_id(0)
    pair = 2 * head_dim
    inv = 1.0 / head_dim
    own, causal, ones = masks(head_dim)

    @pl.when(restart_ref[j] > 0)
    def _():
        w1[...] = w1i_ref[...]
        b1[...] = b1i_ref[...]
        w2[...] = w2i_ref[...]
        b2[...] = b2i_ref[...]

    before = [(s_q1[p], s_x2[p], s_e2[p], s_w2[p], s_b2[p], s_q[p]) for p in range(pairs)]
    for p in range(pairs):
        cols = slice(p * pair, (p + 1) * pair)
        gain, bias = gain_ref[:, cols], bias_ref[:, cols]
        qc, kc, vc = q_ref[:, cols], k_ref[:, cols], v_ref[:, cols]
        kb, qb = low(spread(kc, own)), low(spread(qc, own))
        w1c, w2c = w1[p], w2[p]
        w1b, w2b = low(w1c), low(w2c)
        b1c, b2c = b1[p], b2[p]
        kq = dot(jnp.concatenate([kb, qb], 0), w1b)
        z1 = kq[: 2 * MB] + b1c
        x2, l1, pdf = gelu_parts(z1)
        x2b = low(x2)
        c = dot_nt(x2b, w2b) * own + b2c
        s = lax.rsqrt(lane_sum(c * c) * inv + epsilon)
        u = c * s
        r = u * (gain * gain) + spread((bias - (vc - kc)) * gain, own)
        mr, m2 = lane_sum(r) * inv, lane_sum(r * u) * inv
        g2 = s * (r - mr * own - u * m2)
        e = e_ref[0, p]
        h = dot(low(g2), w2b)
        g1 = h * l1
        e1b, e2b = low(twice(e) * g1), low(e * g2)
        n1 = causal * (dot_nt(qb, kb) + 1.0)
        q1 = kq[2 * MB :] + b1c - dot(low(n1), e1b)
        w1[p] = w1c - dot_tn(kb, e1b)
        b1[p] = b1c - dot(ones, e1b)
        w2[p] = w2c - dot_tn(e2b, x2b)
        b2[p] = b2c - dot(ones, e2b)
        big_ref[0, p, 0:pair] = w1b
        big_ref[0, p, pair : 2 * pair] = w2b
        big_ref[0, p, 2 * pair : 2 * pair + 2 * MB] = x2b
        big_ref[0, p, 2 * pair + 2 * MB : 2 * pair + 4 * MB] = e1b
        mid_ref[0, p, 0 : 2 * MB] = low(g1)
        mid_ref[0, p, 2 * MB : 4 * MB] = low(l1)
        mid_ref[0, p, 4 * MB : 6 * MB] = low(h * pdf * (2.0 - z1 * z1))
        small_ref[0, p, 0 : 2 * MB] = u
        small_ref[0, p, 2 * MB : 4 * MB] = jnp.broadcast_to(s, u.shape)
        small_ref[0, p, 4 * MB : 6 * MB] = r
        small_ref[0, p, 6 * MB : 8 * MB] = jnp.broadcast_to(m2, u.shape)
        small_ref[0, p, 8 * MB : 10 * MB] = g2
        n1_ref[0, p] = low(n1)
        q1p, x2p, e2p, w2p, b2p, qp = before[p]
        s_q1[p], s_x2[p], s_e2[p], s_w2[p], s_b2[p], s_q[p] = q1, x2b, e2b, w2b, b2c, qc
        p2, lq, _ = gelu_parts(q1p)
        p2b = low(p2)
        n2 = causal * (dot_nt(p2b, x2p) + 1.0)
        q2 = dot_nt(p2b, w2p) * own - dot(low(n2), e2p) + b2p
        sq = lax.rsqrt(lane_sum(q2 * q2) * inv + epsilon)
        uq = q2 * sq
        out_ref[:, cols] = qp + fold(uq) * gain + bias
        pq_ref[0, p, 0 : 2 * MB] = p2b
        pq_ref[0, p, 2 * MB : 4 * MB] = low(lq)
        uq_ref[0, p, 0 : 2 * MB] = uq
        uq_ref[0, p, 2 * MB : 4 * MB] = jnp.broadcast_to(sq, uq.shape)
        n2_ref[0, p] = low(n2)


def forward_inner(restarts, q, k, v, e, w1i, b1i, w2i, b2i, gain, bias):
    blocks, pairs, _, pair = e.shape
    head_dim = pair // 2
    inner = w1i.shape[-1]
    steps = blocks + 1
    last = blocks - 1
    tok = pl.BlockSpec((MB, pairs * pair), lambda j, r: (jnp.minimum(j, last), 0))
    whole = lambda a: pl.BlockSpec(a.shape, lambda j, r: (0,) * a.ndim)

    def per_step(rows, width, dtype):
        return (
            jax.ShapeDtypeStruct((steps, pairs, rows, width), dtype),
            pl.BlockSpec((1, pairs, rows, width), lambda j, r: (j, 0, 0, 0)),
        )

    outs = [
        per_step(2 * pair + 4 * MB, inner, bf16),
        per_step(6 * MB, inner, bf16),
        per_step(10 * MB, pair, f32),
        per_step(2 * MB, 2 * MB, bf16),
        per_step(4 * MB, inner, bf16),
        per_step(4 * MB, pair, f32),
        per_step(2 * MB, 2 * MB, bf16),
        (
            jax.ShapeDtypeStruct((steps * MB, pairs * pair), f32),
            pl.BlockSpec((MB, pairs * pair), lambda j, r: (j, 0)),
        ),
    ]
    return pl.pallas_call(
        partial(forward_kernel, pairs, head_dim),
        grid_spec=pltpu.PrefetchScalarGridSpec(
            num_scalar_prefetch=1,
            grid=(steps,),
            in_specs=[tok, tok, tok, pl.BlockSpec((1, pairs, 2 * MB, pair), lambda j, r: (jnp.minimum(j, last), 0, 0, 0))]
            + [whole(a) for a in (w1i, b1i, w2i, b2i, gain, bias)],
            out_specs=[o[1] for o in outs],
            scratch_shapes=[
                pltpu.VMEM((pairs, pair, inner), f32),
                pltpu.VMEM((pairs, 2 * MB, inner), f32),
                pltpu.VMEM((pairs, pair, inner), f32),
                pltpu.VMEM((pairs, 2 * MB, pair), f32),
                pltpu.VMEM((pairs, 2 * MB, inner), f32),
                pltpu.VMEM((pairs, 2 * MB, inner), bf16),
                pltpu.VMEM((pairs, 2 * MB, pair), bf16),
                pltpu.VMEM((pairs, pair, inner), bf16),
                pltpu.VMEM((pairs, 2 * MB, pair), f32),
                pltpu.VMEM((pairs, MB, pair), f32),
            ],
        ),
        out_shape=[o[0] for o in outs],
        compiler_params=pltpu.CompilerParams(vmem_limit_bytes=48 * 1024 * 1024),
        name="inner_forward",
    )(restarts, q, k, v, e, w1i, b1i, w2i, b2i, gain, bias)


def backward_kernel(pairs, head_dim, restart_ref,
                    qq_ref, kq_ref, doq_ref, eq_ref, bigq_ref, g2q_ref, n1_ref, pqq_ref, uqq_ref, n2_ref,
                    q_ref, k_ref, v_ref, do_ref, e_ref, big_ref, mid_ref, small_ref, pq_ref, uq_ref, gain_ref, bias_ref,
                    dq_ref, dk_ref, dv_ref, de_ref, gw1, gb1, gw2, gb2, ggain, gbias,
                    w1, b1, w2, b2, s_e1, s_e2, s_k, s_x2, s_q1, s_q2, s_q):
    j = pl.program_id(0)
    steps = pl.num_programs(0)
    pair = 2 * head_dim
    inv = 1.0 / head_dim
    own, causal, ones = masks(head_dim)

    @pl.when(j <= 1)
    def _():
        for ref in (w1, b1, w2, b2, gw1, gb1, gw2, gb2, ggain, gbias):
            ref[...] = jnp.zeros_like(ref)

    before = [(s_e1[p], s_e2[p], s_k[p], s_x2[p], s_q1[p], s_q2[p], s_q[p]) for p in range(pairs)]
    for p in range(pairs):
        cols = slice(p * pair, (p + 1) * pair)
        gain, bias = gain_ref[:, cols], bias_ref[:, cols]
        qb, kb, do = low(spread(qq_ref[:, cols], own)), low(spread(kq_ref[:, cols], own)), doq_ref[:, cols]
        w1b, w2b = bigq_ref[0, p, 0:pair], bigq_ref[0, p, pair : 2 * pair]
        x2b, e1b = bigq_ref[0, p, 2 * pair : 2 * pair + 2 * MB], bigq_ref[0, p, 2 * pair + 2 * MB : 2 * pair + 4 * MB]
        e2b = low(eq_ref[0, p] * g2q_ref[0, p])
        n1b, n2b = n1_ref[0, p], n2_ref[0, p]
        p2b, lq = pqq_ref[0, p, 0 : 2 * MB], pqq_ref[0, p, 2 * MB : 4 * MB].astype(f32)
        uq, sq = uqq_ref[0, p, 0 : 2 * MB], uqq_ref[0, p, 2 * MB : 4 * MB]
        w = spread(do * gain, own)
        new_q2 = low(sq * (w - (lane_sum(w) * inv) * own - uq * (lane_sum(w * uq) * inv)))
        dpx = low(-causal * dot_nt(new_q2, e2b))
        new_q1 = low((dot(new_q2, w2b) + dot(dpx, x2b)) * lq)
        dqk = low(-causal * dot_nt(new_q1, e1b))
        new_e1 = dot_tn(n1b, new_q1)
        new_e2 = dot_tn(n2b, new_q2)
        new_k = dot_tn(dqk, qb)
        new_x2 = dot_tn(dpx, p2b)
        new_q = do + fold((dot_nt(new_q1, w1b) + dot(dqk, kb)) * own)
        e1q, e2q, dkq, x2q, dq1, dq2, dqc = before[p]
        s_e1[p], s_e2[p], s_k[p], s_x2[p], s_q1[p], s_q2[p], s_q[p] = (
            new_e1, new_e2, new_k, new_x2, new_q1, new_q2, new_q,
        )
        qc, kc, vc, do = q_ref[:, cols], k_ref[:, cols], v_ref[:, cols], do_ref[:, cols]
        qb, kb = low(spread(qc, own)), low(spread(kc, own))
        w1b, w2b = big_ref[0, p, 0:pair], big_ref[0, p, pair : 2 * pair]
        x2b, e1b = big_ref[0, p, 2 * pair : 2 * pair + 2 * MB], big_ref[0, p, 2 * pair + 2 * MB : 2 * pair + 4 * MB]
        g1, l1, hg = (mid_ref[0, p, i * 2 * MB : (i + 1) * 2 * MB].astype(f32) for i in range(3))
        u, s, r, m2, g2 = (small_ref[0, p, i * 2 * MB : (i + 1) * 2 * MB] for i in range(5))
        p2b, uq = pq_ref[0, p, 0 : 2 * MB], uq_ref[0, p, 0 : 2 * MB]
        e = e_ref[0, p]
        e2b = low(e * g2)
        dw1, dw2, db1, db2 = w1[p], w2[p], b1[p], b2[p]
        dw1b, dw2b = low(dw1), low(dw2)
        de1 = -(e1q + dot(kb, dw1b) + db1)
        de2 = -(e2q + dot_nt(x2b, dw2b) * own + db2)
        dk = dkq - dot_nt(e1b, dw1b) * own
        dx2 = x2q - dot(e2b, dw2b)
        de_ref[0, p] = jnp.broadcast_to(lane_sum(g1 * de1) + lane_sum(g2 * de2), u.shape)
        dg1 = twice(e) * de1
        dh = low(dg1 * l1)
        dg2 = e * de2 + dot_nt(dh, w2b) * own
        ma, mg = lane_sum(dg2 * u) * inv, lane_sum(dg2) * inv
        dr = s * (dg2 - mg * own - u * ma)
        gg = gain * gain
        du = dr * gg - s * (dg2 * m2 + r * ma)
        md, mu = lane_sum(du) * inv, lane_sum(du * u + dg2 * g2) * inv
        dz2 = low(s * (du - md * own - u * mu))
        dx2 = dx2 + dot(dz2, w2b)
        dz1 = low(dg1 * hg + dx2 * l1)
        dk = dk + dot_nt(dz1, w1b) * own
        drg = fold(dr) * gain
        dq_ref[:, cols] = low(dqc)
        dk_ref[:, cols] = low(fold(dk) + drg)
        dv_ref[:, cols] = low(-drg)
        ggain[:, cols] += fold(do_spread_times(do, uq)) + fold(dr * u) * (2.0 * gain) + fold(dr) * (bias - (vc - kc))
        gbias[:, cols] += do + drg
        ndw1 = dw1 + dot_tn(jnp.concatenate([qb, kb], 0), jnp.concatenate([dq1, dz1], 0))
        ndw2 = dw2 + dot_tn(jnp.concatenate([dq2, low(g2), dz2], 0), jnp.concatenate([p2b, dh, x2b], 0))
        ndb1 = db1 + dot(ones, dq1) + dot(ones, dz1)
        ndb2 = db2 + dot(ones, dq2) + dot(ones, dz2)
        w1[p], w2[p], b1[p], b2[p] = ndw1, ndw2, ndb1, ndb2

    @pl.when(restart_ref[jnp.minimum(steps - 1 - j, steps - 2)] > 0)
    def _():
        gw1[...] += w1[...]
        gb1[...] += b1[...]
        gw2[...] += w2[...]
        gb2[...] += b2[...]
        for ref in (w1, b1, w2, b2):
            ref[...] = jnp.zeros_like(ref)


def do_spread_times(do, uq):
    return jnp.concatenate([do, do], 0) * uq


def backward_inner(restarts, q, k, v, do, e, saved, gain, bias):
    big, mid, small, n1, pq, uq, n2 = saved
    blocks, pairs, _, pair = e.shape
    head_dim = pair // 2
    inner = big.shape[-1]
    steps = blocks + 1
    now = lambda j: jnp.minimum(blocks - j, blocks - 1)
    ahead = lambda j: jnp.maximum(blocks - 1 - j, 0)
    tok = lambda at: pl.BlockSpec((MB, pairs * pair), lambda j, r: (at(j), 0))

    def block(a, at, rows=None, part=0):
        shape = (1, pairs, rows or a.shape[2], a.shape[3])
        return pl.BlockSpec(shape, lambda j, r: (at(j), 0, part, 0))

    whole = lambda a: pl.BlockSpec(a.shape, lambda j, r: (0,) * a.ndim)
    later = lambda j: ahead(j) + 1
    at_now = lambda j: now(j) + 1
    operands = [
        (q, tok(ahead)), (k, tok(ahead)), (do, tok(ahead)), (e, block(e, ahead)), (big, block(big, ahead)),
        (small, block(small, ahead, 2 * MB, 4)), (n1, block(n1, ahead)), (pq, block(pq, later)), (uq, block(uq, later)),
        (n2, block(n2, later)),
        (q, tok(now)), (k, tok(now)), (v, tok(now)), (do, tok(now)), (e, block(e, now)), (big, block(big, now)),
        (mid, block(mid, now)), (small, block(small, now)), (pq, block(pq, at_now, 2 * MB)), (uq, block(uq, at_now, 2 * MB)),
        (gain, whole(gain)), (bias, whole(bias)),
    ]
    width = pairs * pair
    tok_out = (jax.ShapeDtypeStruct((steps * MB, width), bf16), pl.BlockSpec((MB, width), lambda j, r: (blocks - j, 0)))
    state = [((pairs, pair, inner), f32), ((pairs, 2 * MB, inner), f32), ((pairs, pair, inner), f32), ((pairs, 2 * MB, pair), f32)]
    keep = lambda shape: (jax.ShapeDtypeStruct(shape, f32), pl.BlockSpec(shape, lambda j, r: (0,) * len(shape)))
    outs = [tok_out] * 3 + [
        (jax.ShapeDtypeStruct((steps, pairs, 2 * MB, pair), f32), pl.BlockSpec((1, pairs, 2 * MB, pair), lambda j, r: (blocks - j, 0, 0, 0)))
    ] + [keep(shape) for shape, _ in state] + [keep((MB, width))] * 2
    return pl.pallas_call(
        partial(backward_kernel, pairs, head_dim),
        grid_spec=pltpu.PrefetchScalarGridSpec(
            num_scalar_prefetch=1,
            grid=(steps,),
            in_specs=[o[1] for o in operands],
            out_specs=[o[1] for o in outs],
            scratch_shapes=[pltpu.VMEM(shape, kind) for shape, kind in state] + [
                pltpu.VMEM((pairs, 2 * MB, inner), f32),
                pltpu.VMEM((pairs, 2 * MB, pair), f32),
                pltpu.VMEM((pairs, 2 * MB, pair), f32),
                pltpu.VMEM((pairs, 2 * MB, inner), f32),
                pltpu.VMEM((pairs, 2 * MB, inner), bf16),
                pltpu.VMEM((pairs, 2 * MB, pair), bf16),
                pltpu.VMEM((pairs, MB, pair), f32),
            ],
        ),
        out_shape=[o[0] for o in outs],
        compiler_params=pltpu.CompilerParams(vmem_limit_bytes=48 * 1024 * 1024),
        name="inner_backward",
    )(restarts, *[o[0] for o in operands])


MESH = pl.DeviceIdType.MESH


def greet(peers):
    barrier = pltpu.get_barrier_semaphore()
    for peer in peers:
        pl.semaphore_signal(barrier, inc=1, device_id=peer, device_id_type=MESH)
    pl.semaphore_wait(barrier, len(peers))


def reduce_kernel(rows, groups, chunks, span, *refs):
    count = len(chunks)
    ins, part, small, rest = refs[:count], refs[count], refs[count + 1], refs[count + 2 :]
    outs, part_out, small_out, rest = rest[:count], rest[count], rest[count + 1], rest[count + 2 :]
    got_core, rest = rest[:count], rest[count:]
    sum_core, rest = rest[:count], rest[count:]
    got_y, rest = rest[:count], rest[count:]
    sum_y, rest = rest[:count], rest[count:]
    got_row, rest = rest[:count], rest[count:]
    part_got, part_sum, small_got, small_sum, send_sem, recv_sem = rest
    row, group, feat = lax.axis_index("row"), lax.axis_index("group"), lax.axis_index("feat")
    core, y = lax.rem(feat, 2), feat // 2
    core_mate = {"feat": feat + 1 - 2 * core}
    y_mate = {"feat": feat + 2 - 4 * y}
    row_mates = [{"row": lax.rem(row + o, rows)} for o in range(1, rows)]
    group_mates = [{"group": lax.rem(group + o, groups)} for o in range(1, groups)]
    started = []

    def send(src, dst, peer):
        i = len(started)
        copy = pltpu.make_async_remote_copy(
            src_ref=src, dst_ref=dst, send_sem=send_sem.at[i], recv_sem=recv_sem.at[i], device_id=peer, device_id_type=MESH
        )
        copy.start()
        started.append(copy)
        return copy

    def at(start, size):
        return pl.ds(pl.multiple_of(start, 16), size)

    def add(a, b):
        return (a.astype(f32) + b.astype(f32)).astype(bf16)

    greet([core_mate, y_mate] + row_mates + group_mates)
    halves = [shape[0] // 2 for shape in chunks]
    quarters = [shape[0] // 4 for shape in chunks]
    units = [shape[0] // (4 * rows) for shape in chunks]

    by_core = [send(ins[i].at[at((1 - core) * halves[i], halves[i])], got_core[i], core_mate) for i in range(count)]
    small_copy = send(small, small_got.at[0], core_mate)
    blocks = []
    for o in range(1, groups):
        blocks.append(send(part.at[lax.rem(group + o, groups)], part_got.at[o - 1], group_mates[o - 1]))
    by_y = []
    for i in range(count):
        by_core[i].wait_recv()
        sum_core[i][...] = add(ins[i][at(core * halves[i], halves[i])], got_core[i][...])
        by_y.append(send(sum_core[i].at[at((1 - y) * quarters[i], quarters[i])], got_y[i], y_mate))
    small_copy.wait_recv()
    small_sum[0] = small[...] + small_got[0]
    small_copy = send(small_sum.at[0], small_got.at[1], y_mate)
    total = part[group].astype(f32)
    for o in range(1, groups):
        blocks[o - 1].wait_recv()
        total = total + part_got[o - 1].astype(f32)
    part_sum[...] = total.astype(bf16)
    home = []
    for o in range(1, rows):
        home.append(send(part_sum.at[at(lax.rem(row + o, rows) * span, span)], part_out.at[at(row * span, span)], row_mates[o - 1]))
    part_out[at(row * span, span)] = part_sum[at(row * span, span)]
    by_row = []
    for i in range(count):
        by_y[i].wait_recv()
        sum_y[i][...] = add(sum_core[i][at(y * quarters[i], quarters[i])], got_y[i][...])
        by_row.append(
            [
                send(sum_y[i].at[at(lax.rem(row + o, rows) * units[i], units[i])], got_row[i].at[o - 1], row_mates[o - 1])
                for o in range(1, rows)
            ]
        )
    small_copy.wait_recv()
    small_sum[1] = small_sum[0] + small_got[1]
    small_copies = [send(small_sum.at[1], small_got.at[2 + row], row_mates[o - 1]) for o in range(1, rows)]
    small_got[2 + row] = small_sum[1]

    place = (core * 2 + y) * rows + row
    back_row = []
    for i in range(count):
        total = sum_y[i][at(row * units[i], units[i])].astype(f32)
        for o in range(1, rows):
            by_row[i][o - 1].wait_recv()
            total = total + got_row[i][o - 1].astype(f32)
        here = outs[i].at[group, at(place * units[i], units[i])]
        here[...] = total.astype(bf16)
        back_row.append([send(here, here, row_mates[o - 1]) for o in range(1, rows)])
    for copy in small_copies:
        copy.wait_recv()
    small_total = small_got[2]
    for r in range(1, rows):
        small_total = small_total + small_got[2 + r]
    small_out[group] = small_total
    small_copies = [send(small_out.at[group], small_out.at[group], mate) for mate in group_mates]
    first = []
    for i in range(count):
        for copy in back_row[i]:
            copy.wait_recv()
        here = outs[i].at[group, at((core * 2 + y) * quarters[i], quarters[i])]
        if i % 2 == 0:
            first.append([send(here, here, mate) for mate in group_mates])
        else:
            first.append([send(here, here, y_mate)])
    second = []
    for i in range(count):
        for copy in first[i]:
            copy.wait_recv()
        if i % 2 == 0:
            here = outs[i].at[:, at((core * 2 + y) * quarters[i], quarters[i])]
            second.append([send(here, here, y_mate)])
        else:
            here = outs[i].at[group, at(core * halves[i], halves[i])]
            second.append([send(here, here, mate) for mate in group_mates])
    third = []
    for i in range(count):
        for copy in second[i]:
            copy.wait_recv()
        here = outs[i].at[:, at(core * halves[i], halves[i])]
        third.append(send(here, here, core_mate))
    for copy in third + home + small_copies:
        copy.wait_recv()
    for copy in started:
        copy.wait_send()


def reduce_all(arrays, part, small, rows, groups, collective_id):
    chunks = [a.shape for a in arrays]
    count = len(chunks)
    span = part.shape[1] // rows
    copies = count * (2 + 2 * (rows - 1) + (groups - 1) + 2) + (groups - 1) + (rows - 1) + 2 + (rows - 1) + (groups - 1)
    vmem = pl.BlockSpec(memory_space=pltpu.VMEM)
    scratch = [pltpu.VMEM((h // 2, w), bf16) for h, w in chunks] * 2
    scratch += [pltpu.VMEM((h // 4, w), bf16) for h, w in chunks] * 2
    scratch += [pltpu.VMEM((rows - 1, h // (4 * rows), w), bf16) for h, w in chunks]
    scratch += [
        pltpu.VMEM((groups - 1,) + part.shape[1:], bf16),
        pltpu.VMEM(part.shape[1:], bf16),
        pltpu.VMEM((2 + rows,) + small.shape, f32),
        pltpu.VMEM((2,) + small.shape, f32),
        pltpu.SemaphoreType.DMA((copies,)),
        pltpu.SemaphoreType.DMA((copies,)),
    ]
    return pl.pallas_call(
        partial(reduce_kernel, rows, groups, chunks, span),
        in_specs=[vmem] * (count + 2),
        out_specs=[vmem] * (count + 2),
        out_shape=[jax.ShapeDtypeStruct((groups, h, w), bf16) for h, w in chunks]
        + [jax.ShapeDtypeStruct(part.shape[1:], bf16), jax.ShapeDtypeStruct((groups,) + small.shape, f32)],
        scratch_shapes=scratch,
        compiler_params=pltpu.CompilerParams(
            collective_id=collective_id, has_side_effects=True, vmem_limit_bytes=48 * 1024 * 1024
        ),
        name="reduce_all",
    )(*arrays, part, small)


def normalize(vector, gain):
    centered = vector - jnp.mean(vector, -1, keepdims=True)
    variance = jnp.mean(centered * centered, -1, keepdims=True)
    inv_scale = lax.rsqrt(variance + epsilon)
    normed_unit = centered * inv_scale
    return (normed_unit * gain, normed_unit, inv_scale)


def norm_back(grad_out, gain, normed_unit, inv_scale):
    scaled = grad_out * gain
    return inv_scale * (
        scaled
        - jnp.mean(scaled, -1, keepdims=True)
        - normed_unit * jnp.mean(scaled * normed_unit, -1, keepdims=True)
    )


SEQ = ("row", "group")


def per_device(
    tokens,
    cotangent,
    doc_starts,
    mixer_gain,
    query_weight,
    key_weight,
    value_weight,
    out_weight,
    rate_weight,
    rate_bias,
    first_init,
    first_bias_init,
    second_init,
    second_bias_init,
    inner_gain,
    inner_bias,
    feed_gain,
    gate_weight,
    up_weight,
    down_weight,
):
    rows, span, width = tokens.shape
    heads, head_dim, inner = first_init.shape
    groups = lax.axis_size("group")
    feats = lax.axis_size("feat")
    row, group = lax.axis_index("row"), lax.axis_index("group")
    count = rows * span
    length = span * rows * groups
    blocks = length // MB
    pairs = -(-heads // (2 * groups))
    mine = 2 * pairs
    pair = 2 * head_dim
    cols = mine * head_dim
    spare = mine * groups - heads

    def own_heads(array, axis, per_head=1):
        if spare:
            pad = [(0, 0)] * array.ndim
            pad[axis] = (0, spare * per_head)
            array = jnp.pad(array, pad)
        return lax.dynamic_slice_in_dim(array, group * mine * per_head, mine * per_head, axis)

    def to_rows(array):
        got = lax.all_to_all(jnp.repeat(array, groups, 0), SEQ, 0, 0, tiled=True)
        return got.reshape(length, array.shape[-1])

    def from_rows(array):
        parts = array.reshape(rows * groups, span, array.shape[-1])
        got = lax.all_to_all(parts, SEQ, 0, 0, tiled=True)
        return got.reshape(rows, groups, span, array.shape[-1])

    row_in = to_rows(tokens).astype(f32)
    act_row = low(normalize(row_in, mixer_gain)[0])
    w_q, w_k, w_v = (own_heads(w, 1, head_dim) for w in (query_weight, key_weight, value_weight))
    w_o = own_heads(out_weight, 0, head_dim)
    w_r = own_heads(rate_weight, 1)
    queries, keys, values = (dot(act_row, w) for w in (w_q, w_k, w_v))
    logits = dot(act_row, w_r) + own_heads(rate_bias, 0)
    sigma = jax.nn.sigmoid(logits)
    rates = sigma / head_dim
    e = jnp.broadcast_to(
        rates.reshape(blocks, MB, pairs, 2).transpose(0, 2, 3, 1).reshape(blocks, pairs, 2 * MB, 1),
        (blocks, pairs, 2 * MB, pair),
    )
    block_ids = jnp.arange(blocks, dtype=jnp.int32)
    starts = lax.dynamic_index_in_dim(doc_starts, row, 0, False)
    restarts = ((block_ids == 0) | jnp.any(starts[:, None] == block_ids[None], 0)).astype(jnp.int32)
    pack = lambda a: own_heads(a, 0).reshape(pairs, pair, inner)
    start_first = pack(first_init)
    start_second = pack(second_init - jnp.mean(second_init, 1, keepdims=True))
    start_first_bias = jnp.repeat(own_heads(first_bias_init, 0).reshape(pairs, 2, 1, inner), MB, 2).reshape(
        pairs, 2 * MB, inner
    )
    centered = own_heads(second_bias_init - jnp.mean(second_bias_init, 1, keepdims=True), 0)
    start_second_bias = (
        jnp.eye(2, dtype=f32)[None, :, None, :, None] * centered.reshape(pairs, 1, 1, 2, head_dim)
    ) * jnp.ones((1, 1, MB, 1, 1), f32)
    start_second_bias = start_second_bias.reshape(pairs, 2 * MB, pair)
    gain, bias = own_heads(inner_gain, 0).reshape(1, cols), own_heads(inner_bias, 0).reshape(1, cols)
    *saved, mixed = forward_inner(
        jnp.concatenate([restarts, jnp.zeros((1,), jnp.int32)]),
        queries, keys, values, e, start_first, start_first_bias, start_second, start_second_bias, gain, bias,
    )
    mixed_row = low(mixed[MB:])
    mixed_low = from_rows(mixed_row).transpose(0, 2, 1, 3).reshape(count, groups * cols)[:, :width]

    flat_in = tokens.astype(f32).reshape(count, width)
    hidden_in = flat_in + dot(mixed_low, out_weight)
    normed_two, unit_two, scale_two = normalize(hidden_in, feed_gain)
    act_two = low(normed_two)
    grad_low = cotangent.reshape(count, width)
    group_grad = lax.all_gather(grad_low, "feat", axis=0, tiled=True)
    grad_act = dot(group_grad, down_weight)
    group_rows = lax.all_gather(act_two, "feat", axis=0, tiled=True)
    gate_pre, up_value = dot(group_rows, gate_weight), dot(group_rows, up_weight)
    gate_sig = jax.nn.sigmoid(gate_pre)
    silu = gate_pre * gate_sig
    hidden_act = low(silu * up_value)
    grad_gate = low(grad_act * up_value * gate_sig * (1.0 + gate_pre * (1.0 - gate_sig)))
    grad_up = low(grad_act * silu)
    grad_act_two = lax.psum_scatter(
        low(dot_nt(grad_gate, gate_weight) + dot_nt(grad_up, up_weight)), "feat", scatter_dimension=0, tiled=True
    ).astype(f32)
    feed_out = lax.psum_scatter(
        low(dot_nt(hidden_act, down_weight)), "feat", scatter_dimension=0, tiled=True
    ).astype(f32)
    block_out = low(hidden_in + feed_out).reshape(rows, span, width)
    feed_terms = (low(dot_tn(group_rows, grad_gate)), low(dot_tn(group_rows, grad_up)), low(dot_tn(group_grad, hidden_act)))
    grad_feed_gain = jnp.sum(grad_act_two * unit_two, 0)
    grad_hidden = grad_low.astype(f32) + norm_back(grad_act_two, feed_gain, unit_two, scale_two)

    branch_row = to_rows(low(grad_hidden).reshape(rows, span, width))
    grad_mixed = dot_nt(branch_row, w_o)
    feed_terms, grad_mixed = lax.optimization_barrier((feed_terms, grad_mixed))
    feed_grads = lax.psum(feed_terms, SEQ)
    grad_out_rows = dot_tn(branch_row, mixed_row)
    grad_q, grad_k, grad_v, grad_e, g_first, g_first_bias, g_second, g_second_bias, g_gain, g_bias = backward_inner(
        restarts, queries, keys, values, grad_mixed, e, saved, gain, bias
    )
    grad_q, grad_k, grad_v = grad_q[:length], grad_k[:length], grad_v[:length]
    grad_rates = grad_e[:blocks, :, :, 0].reshape(blocks, pairs, 2, MB).transpose(0, 3, 1, 2).reshape(length, mine)
    grad_logits = low(grad_rates * sigma * (1.0 - sigma) / head_dim)
    part = dot_nt(grad_q, w_q) + dot_nt(grad_k, w_k) + dot_nt(grad_v, w_v) + dot_nt(grad_logits, w_r)
    _, unit_row, _ = normalize(row_in, mixer_gain)
    blocks_out = low(part).reshape(rows, groups, span, width).transpose(1, 0, 2, 3).reshape(groups, count, width)
    arrays = (
        jnp.concatenate([low(dot_tn(act_row, grad_q)), low(dot_tn(act_row, grad_k))], 1),
        jnp.concatenate([low(dot_tn(act_row, grad_v)), low(grad_out_rows)], 1),
        jnp.concatenate([low(g_first.reshape(cols, inner)), low(g_second.reshape(cols, inner))], 0),
    )
    per_head = jnp.concatenate(
        [
            g_first_bias.reshape(mine, MB, inner)[:, 0],
            jnp.stack([g_second_bias[:, h * MB, h * head_dim : (h + 1) * head_dim] for h in range(2)], 1).reshape(
                mine, head_dim
            ),
            jnp.sum(g_gain, 0).reshape(mine, head_dim),
            jnp.sum(g_bias, 0).reshape(mine, head_dim),
            dot_tn(grad_logits, act_row),
            jnp.sum(grad_logits.astype(f32), 0)[:, None],
            jnp.sum(logits, 0)[:, None],
        ],
        1,
    )
    used = (group * mine + jnp.arange(mine)) < heads
    peers = rows * feats
    top = jnp.max(jnp.where(used[None], logits, jnp.finfo(f32).min))
    tops = jnp.where(jnp.arange(peers) == row * feats + lax.axis_index("feat"), top, 0.0)
    pieces = [per_head.reshape(-1), jnp.sum(part * unit_row, 0), grad_feed_gain, tops]
    sizes = [p.shape[0] for p in pieces]
    size = sum(sizes)
    lines = -(-size // 1024) * 8
    small = jnp.pad(jnp.concatenate(pieces), (0, lines * 128 - size)).reshape(lines, 128)
    *arrays, got, small = reduce_all(arrays, blocks_out, small, rows, groups, 3)

    grad_act_one = got.astype(f32)
    _, unit_one, scale_one = normalize(flat_in, mixer_gain)
    input_grad = grad_hidden + norm_back(grad_act_one, mixer_gain, unit_one, scale_one)

    def gathered(array, part_no):
        got = lax.slice_in_dim(array, part_no * cols, (part_no + 1) * cols, axis=2).astype(f32)
        return got.transpose(1, 0, 2).reshape(width, groups * cols)[:, :width]

    g_query, g_key = (gathered(arrays[0], i) for i in range(2))
    g_value, g_out = gathered(arrays[1], 0), gathered(arrays[1], 1).T
    states = arrays[2].astype(f32).reshape(groups, 2, cols, inner)
    g_first, g_second = (
        states[:, i].reshape(groups * mine, head_dim, inner)[:heads] for i in range(2)
    )
    g_second = g_second - jnp.mean(g_second, 1, keepdims=True)
    small = small.reshape(groups, lines * 128)
    ends = [0]
    for s in sizes:
        ends.append(ends[-1] + s)
    slots = small[:, : ends[1]].reshape(groups * mine, -1)[:heads]
    g_mixer, g_feed = jnp.sum(small[:, ends[1] : ends[2]], 0), jnp.sum(small[:, ends[2] : ends[3]], 0)
    at = [0, inner, inner + head_dim, inner + 2 * head_dim, inner + 3 * head_dim, inner + 3 * head_dim + width]
    g_second_bias = slots[:, at[1] : at[2]]
    g_second_bias = g_second_bias - jnp.mean(g_second_bias, 1, keepdims=True)
    total = jnp.sum(slots[:, at[5] + 1])
    stats = jnp.stack([total / (rows * groups * feats * count * heads), jnp.max(small[:, ends[3] : ends[4]])])
    return (
        block_out,
        input_grad.reshape(rows, span, width),
        g_mixer,
        g_query,
        g_key,
        g_value,
        g_out,
        slots[:, at[4] : at[5]].T,
        slots[:, at[5]],
        g_first,
        slots[:, : at[1]],
        g_second,
        g_second_bias,
        slots[:, at[2] : at[3]],
        slots[:, at[3] : at[4]],
        g_feed,
        feed_grads[0].astype(f32),
        feed_grads[1].astype(f32),
        feed_grads[2].astype(f32),
        stats,
    )


def solution(mesh):
    feats = mesh.shape["feat"]

    def run(*arrays):
        rows = arrays[0].shape[0] // feats
        grid = jax.sharding.Mesh(mesh.devices.reshape(rows, -1, feats), ("row", "group", "feat"))
        by_token = P("feat", SEQ, None)
        by_hidden = P(None, "feat")
        return jax.shard_map(
            per_device,
            mesh=grid,
            in_specs=(by_token, by_token, P("feat", None)) + (P(),) * 14 + (by_hidden,) * 3,
            out_specs=(by_token, by_token) + (P(),) * 14 + (by_hidden,) * 3 + (P(),),
            check_vma=False,
        )(*arrays)

    return run
```

```python
from functools import partial

import jax
import jax.numpy as jnp
from jax import lax
from jax.experimental import pallas as pl
from jax.experimental.pallas import tpu as pltpu
from jax.sharding import PartitionSpec as P

MB = 16
epsilon = 1e-05
f32, bf16 = jnp.float32, jnp.bfloat16


def dot(a, b):
    return lax.dot_general(a, b, (((1,), (0,)), ((), ())), preferred_element_type=f32)


def dot_nt(a, b):
    return lax.dot_general(a, b, (((1,), (1,)), ((), ())), preferred_element_type=f32)


def dot_tn(a, b):
    return lax.dot_general(a, b, (((0,), (0,)), ((), ())), preferred_element_type=f32)


def low(v):
    return v.astype(bf16)


def gelu_parts(z):
    a = jnp.abs(z)
    d = 1.0 + 0.23164189 * a
    t = pl.reciprocal(d, approx=True)
    t = t * (2.0 - d * t)
    ex = jnp.exp(-0.5 * (z * z))
    poly = t * (
        0.127414796 + t * (-0.142248368 + t * (0.7107068705 + t * (-0.7265760135 + t * 0.5307027145)))
    )
    h = poly * ex
    cdf = jnp.where(z >= 0, 1.0 - h, h)
    pdf = 0.3989422804014327 * ex
    return z * cdf, cdf + z * pdf, pdf


def lane_sum(v):
    return jnp.sum(v, -1, keepdims=True)


def masks(head_dim):
    pair = 2 * head_dim
    rows, cols = 2 * MB, pair
    r = lax.broadcasted_iota(jnp.int32, (rows, cols), 0)
    c = lax.broadcasted_iota(jnp.int32, (rows, cols), 1)
    own = ((r < MB) == (c < head_dim)).astype(f32)
    r = lax.broadcasted_iota(jnp.int32, (rows, rows), 0)
    c = lax.broadcasted_iota(jnp.int32, (rows, rows), 1)
    same = (r < MB) == (c < MB)
    causal = (same & (c <= r)).astype(f32)
    return own, causal, same.astype(bf16)


def spread(v, own):
    return jnp.concatenate([v, v], 0) * own


def fold(v):
    return v[:MB] + v[MB:]


def twice(v):
    return jnp.concatenate([v, v], 1)


def forward_kernel(pairs, head_dim, restart_ref, q_ref, k_ref, v_ref, e_ref, w1i_ref, b1i_ref, w2i_ref, b2i_ref, gain_ref, bias_ref,
                   big_ref, mid_ref, small_ref, n1_ref, pq_ref, uq_ref, n2_ref, out_ref,
                   w1, b1, w2, b2, s_q1, s_x2, s_e2, s_w2, s_b2, s_q):
    j = pl.program_id(0)
    pair = 2 * head_dim
    inv = 1.0 / head_dim
    own, causal, ones = masks(head_dim)

    @pl.when(restart_ref[j] > 0)
    def _():
        w1[...] = w1i_ref[...]
        b1[...] = b1i_ref[...]
        w2[...] = w2i_ref[...]
        b2[...] = b2i_ref[...]

    before = [(s_q1[p], s_x2[p], s_e2[p], s_w2[p], s_b2[p], s_q[p]) for p in range(pairs)]
    for p in range(pairs):
        cols = slice(p * pair, (p + 1) * pair)
        gain, bias = gain_ref[:, cols], bias_ref[:, cols]
        qc, kc, vc = q_ref[:, cols], k_ref[:, cols], v_ref[:, cols]
        kb, qb = low(spread(kc, own)), low(spread(qc, own))
        w1c, w2c = w1[p], w2[p]
        w1b, w2b = low(w1c), low(w2c)
        b1c, b2c = b1[p], b2[p]
        kq = dot(jnp.concatenate([kb, qb], 0), w1b)
        z1 = kq[: 2 * MB] + b1c
        x2, l1, pdf = gelu_parts(z1)
        x2b = low(x2)
        c = dot_nt(x2b, w2b) * own + b2c
        s = lax.rsqrt(lane_sum(c * c) * inv + epsilon)
        u = c * s
        r = u * (gain * gain) + spread((bias - (vc - kc)) * gain, own)
        mr, m2 = lane_sum(r) * inv, lane_sum(r * u) * inv
        g2 = s * (r - mr * own - u * m2)
        e = e_ref[0, p]
        h = dot(low(g2), w2b)
        g1 = h * l1
        e1b, e2b = low(twice(e) * g1), low(e * g2)
        n1 = causal * (dot_nt(qb, kb) + 1.0)
        q1 = kq[2 * MB :] + b1c - dot(low(n1), e1b)
        w1[p] = w1c - dot_tn(kb, e1b)
        b1[p] = b1c - dot(ones, e1b)
        w2[p] = w2c - dot_tn(e2b, x2b)
        b2[p] = b2c - dot(ones, e2b)
        big_ref[0, p, 0:pair] = w1b
        big_ref[0, p, pair : 2 * pair] = w2b
        big_ref[0, p, 2 * pair : 2 * pair + 2 * MB] = x2b
        big_ref[0, p, 2 * pair + 2 * MB : 2 * pair + 4 * MB] = e1b
        mid_ref[0, p, 0 : 2 * MB] = low(g1)
        mid_ref[0, p, 2 * MB : 4 * MB] = low(l1)
        mid_ref[0, p, 4 * MB : 6 * MB] = low(h * pdf * (2.0 - z1 * z1))
        small_ref[0, p, 0 : 2 * MB] = u
        small_ref[0, p, 2 * MB : 4 * MB] = jnp.broadcast_to(s, u.shape)
        small_ref[0, p, 4 * MB : 6 * MB] = r
        small_ref[0, p, 6 * MB : 8 * MB] = jnp.broadcast_to(m2, u.shape)
        small_ref[0, p, 8 * MB : 10 * MB] = g2
        n1_ref[0, p] = low(n1)
        q1p, x2p, e2p, w2p, b2p, qp = before[p]
        s_q1[p], s_x2[p], s_e2[p], s_w2[p], s_b2[p], s_q[p] = q1, x2b, e2b, w2b, b2c, qc
        p2, lq, _ = gelu_parts(q1p)
        p2b = low(p2)
        n2 = causal * (dot_nt(p2b, x2p) + 1.0)
        q2 = dot_nt(p2b, w2p) * own - dot(low(n2), e2p) + b2p
        sq = lax.rsqrt(lane_sum(q2 * q2) * inv + epsilon)
        uq = q2 * sq
        out_ref[:, cols] = qp + fold(uq) * gain + bias
        pq_ref[0, p, 0 : 2 * MB] = p2b
        pq_ref[0, p, 2 * MB : 4 * MB] = low(lq)
        uq_ref[0, p, 0 : 2 * MB] = uq
        uq_ref[0, p, 2 * MB : 4 * MB] = jnp.broadcast_to(sq, uq.shape)
        n2_ref[0, p] = low(n2)


def forward_inner(restarts, q, k, v, e, w1i, b1i, w2i, b2i, gain, bias):
    blocks, pairs, _, pair = e.shape
    head_dim = pair // 2
    inner = w1i.shape[-1]
    steps = blocks + 1
    last = blocks - 1
    tok = pl.BlockSpec((MB, pairs * pair), lambda j, r: (jnp.minimum(j, last), 0))
    whole = lambda a: pl.BlockSpec(a.shape, lambda j, r: (0,) * a.ndim)

    def per_step(rows, width, dtype):
        return (
            jax.ShapeDtypeStruct((steps, pairs, rows, width), dtype),
            pl.BlockSpec((1, pairs, rows, width), lambda j, r: (j, 0, 0, 0)),
        )

    outs = [
        per_step(2 * pair + 4 * MB, inner, bf16),
        per_step(6 * MB, inner, bf16),
        per_step(10 * MB, pair, f32),
        per_step(2 * MB, 2 * MB, bf16),
        per_step(4 * MB, inner, bf16),
        per_step(4 * MB, pair, f32),
        per_step(2 * MB, 2 * MB, bf16),
        (
            jax.ShapeDtypeStruct((steps * MB, pairs * pair), f32),
            pl.BlockSpec((MB, pairs * pair), lambda j, r: (j, 0)),
        ),
    ]
    return pl.pallas_call(
        partial(forward_kernel, pairs, head_dim),
        grid_spec=pltpu.PrefetchScalarGridSpec(
            num_scalar_prefetch=1,
            grid=(steps,),
            in_specs=[tok, tok, tok, pl.BlockSpec((1, pairs, 2 * MB, pair), lambda j, r: (jnp.minimum(j, last), 0, 0, 0))]
            + [whole(a) for a in (w1i, b1i, w2i, b2i, gain, bias)],
            out_specs=[o[1] for o in outs],
            scratch_shapes=[
                pltpu.VMEM((pairs, pair, inner), f32),
                pltpu.VMEM((pairs, 2 * MB, inner), f32),
                pltpu.VMEM((pairs, pair, inner), f32),
                pltpu.VMEM((pairs, 2 * MB, pair), f32),
                pltpu.VMEM((pairs, 2 * MB, inner), f32),
                pltpu.VMEM((pairs, 2 * MB, inner), bf16),
                pltpu.VMEM((pairs, 2 * MB, pair), bf16),
                pltpu.VMEM((pairs, pair, inner), bf16),
                pltpu.VMEM((pairs, 2 * MB, pair), f32),
                pltpu.VMEM((pairs, MB, pair), f32),
            ],
        ),
        out_shape=[o[0] for o in outs],
        compiler_params=pltpu.CompilerParams(vmem_limit_bytes=48 * 1024 * 1024),
        name="inner_forward",
    )(restarts, q, k, v, e, w1i, b1i, w2i, b2i, gain, bias)


MESH = pl.DeviceIdType.MESH


def greet(peers):
    barrier = pltpu.get_barrier_semaphore()
    for peer in peers:
        pl.semaphore_signal(barrier, inc=1, device_id=peer, device_id_type=MESH)
    pl.semaphore_wait(barrier, len(peers))


class Copies:
    def __init__(self, send_sem, recv_sem):
        self.send_sem, self.recv_sem, self.started = send_sem, recv_sem, []

    def make(self, src, dst, peer):
        i = len(self.started)
        copy = pltpu.make_async_remote_copy(
            src_ref=src, dst_ref=dst, send_sem=self.send_sem.at[i], recv_sem=self.recv_sem.at[i],
            device_id=peer, device_id_type=MESH,
        )
        self.started.append(copy)
        return copy

    def send(self, src, dst, peer):
        copy = self.make(src, dst, peer)
        copy.start()
        return copy


def rows_at(start, size):
    return pl.ds(pl.multiple_of(start, 16), size)


def add_low(a, b):
    return (a.astype(f32) + b.astype(f32)).astype(bf16)


def mates(axis):
    size, here = lax.axis_size(axis), lax.axis_index(axis)
    return [{axis: lax.rem(here + o, size)} for o in range(1, size)]


def feed_sum_steps(ins, outs, got_group, sum_group, got_row, full, copies):
    row, group = lax.axis_index("row"), lax.axis_index("group")
    rows, groups = lax.axis_size("row"), lax.axis_size("group")
    row_mates, group_mates = mates("row"), mates("group")
    stages = {}
    for i, src in enumerate(ins):
        part = src.shape[0] // groups
        unit = part // rows

        def scatter_group(i=i, src=src, part=part):
            return [
                copies.make(src.at[rows_at(lax.rem(group + o, groups) * part, part)], got_group[i].at[o - 1], group_mates[o - 1])
                for o in range(1, groups)
            ]

        def scatter_row(i=i, unit=unit):
            return [
                copies.make(sum_group[i].at[rows_at(lax.rem(row + o, rows) * unit, unit)], got_row[i].at[o - 1], row_mates[o - 1])
                for o in range(1, rows)
            ]

        def gather_row(i=i, part=part, unit=unit):
            here = full[i].at[rows_at(group * part + row * unit, unit)]
            return [copies.make(here, here, mate) for mate in row_mates]

        def gather_group(i=i, part=part):
            here = full[i].at[rows_at(group * part, part)]
            return [copies.make(here, here, mate) for mate in group_mates]

        stages[i] = [scatter_group(), scatter_row(), gather_row(), gather_group()]

    def begin():
        greet(row_mates + group_mates)
        for i in range(len(ins)):
            for copy in stages[i][0]:
                copy.start()

    def after(i, s):
        part = ins[i].shape[0] // groups
        unit = part // rows
        for copy in stages[i][s]:
            copy.wait_recv()
        if s == 0:
            total = ins[i][rows_at(group * part, part)].astype(f32)
            for o in range(1, groups):
                total = total + got_group[i][o - 1].astype(f32)
            sum_group[i][...] = low(total)
        if s == 1:
            total = sum_group[i][rows_at(row * unit, unit)].astype(f32)
            for o in range(1, rows):
                total = total + got_row[i][o - 1].astype(f32)
            full[i][rows_at(group * part + row * unit, unit)] = low(total)
        if s < 3:
            for copy in stages[i][s + 1]:
                copy.start()
        else:
            outs[i][...] = full[i][...]
            for copy in sum(stages[i], []):
                copy.wait_send()

    return begin, after


def backward_kernel(pairs, head_dim, feeds, stage_steps, restart_ref,
                    qq_ref, kq_ref, doq_ref, eq_ref, bigq_ref, g2q_ref, n1_ref, pqq_ref, uqq_ref, n2_ref,
                    q_ref, k_ref, v_ref, do_ref, e_ref, big_ref, mid_ref, small_ref, pq_ref, uq_ref, gain_ref, bias_ref, *refs):
    j = pl.program_id(0)
    steps = pl.num_programs(0)
    pair = 2 * head_dim
    inv = 1.0 / head_dim
    own, causal, ones = masks(head_dim)
    feed_in, refs = refs[:feeds], refs[feeds:]
    dq_ref, dk_ref, dv_ref, de_ref, gw1, gb1, gw2, gb2, ggain, gbias = refs[:10]
    feed_out, refs = refs[10 : 10 + feeds], refs[10 + feeds :]
    w1, b1, w2, b2, s_e1, s_e2, s_k, s_x2, s_q1, s_q2, s_q = refs[:11]
    buffers = [refs[11 + i * feeds : 11 + (i + 1) * feeds] for i in range(4)]
    if feeds:
        begin, after = feed_sum_steps(feed_in, feed_out, *buffers, Copies(*refs[-2:]))
        pl.when(j == 0)(begin)
        for (i, s), at in stage_steps.items():
            pl.when(j == at)(partial(after, i, s))

    @pl.when(j <= 1)
    def _():
        for ref in (w1, b1, w2, b2, gw1, gb1, gw2, gb2, ggain, gbias):
            ref[...] = jnp.zeros_like(ref)

    before = [(s_e1[p], s_e2[p], s_k[p], s_x2[p], s_q1[p], s_q2[p], s_q[p]) for p in range(pairs)]
    for p in range(pairs):
        cols = slice(p * pair, (p + 1) * pair)
        gain, bias = gain_ref[:, cols], bias_ref[:, cols]
        qb, kb, do = low(spread(qq_ref[:, cols], own)), low(spread(kq_ref[:, cols], own)), doq_ref[:, cols]
        w1b, w2b = bigq_ref[0, p, 0:pair], bigq_ref[0, p, pair : 2 * pair]
        x2b, e1b = bigq_ref[0, p, 2 * pair : 2 * pair + 2 * MB], bigq_ref[0, p, 2 * pair + 2 * MB : 2 * pair + 4 * MB]
        e2b = low(eq_ref[0, p] * g2q_ref[0, p])
        n1b, n2b = n1_ref[0, p], n2_ref[0, p]
        p2b, lq = pqq_ref[0, p, 0 : 2 * MB], pqq_ref[0, p, 2 * MB : 4 * MB].astype(f32)
        uq, sq = uqq_ref[0, p, 0 : 2 * MB], uqq_ref[0, p, 2 * MB : 4 * MB]
        w = spread(do * gain, own)
        new_q2 = low(sq * (w - (lane_sum(w) * inv) * own - uq * (lane_sum(w * uq) * inv)))
        dpx = low(-causal * dot_nt(new_q2, e2b))
        new_q1 = low((dot(new_q2, w2b) + dot(dpx, x2b)) * lq)
        dqk = low(-causal * dot_nt(new_q1, e1b))
        new_e1 = dot_tn(n1b, new_q1)
        new_e2 = dot_tn(n2b, new_q2)
        new_k = dot_tn(dqk, qb)
        new_x2 = dot_tn(dpx, p2b)
        new_q = do + fold((dot_nt(new_q1, w1b) + dot(dqk, kb)) * own)
        e1q, e2q, dkq, x2q, dq1, dq2, dqc = before[p]
        s_e1[p], s_e2[p], s_k[p], s_x2[p], s_q1[p], s_q2[p], s_q[p] = (
            new_e1, new_e2, new_k, new_x2, new_q1, new_q2, new_q,
        )
        qc, kc, vc, do = q_ref[:, cols], k_ref[:, cols], v_ref[:, cols], do_ref[:, cols]
        qb, kb = low(spread(qc, own)), low(spread(kc, own))
        w1b, w2b = big_ref[0, p, 0:pair], big_ref[0, p, pair : 2 * pair]
        x2b, e1b = big_ref[0, p, 2 * pair : 2 * pair + 2 * MB], big_ref[0, p, 2 * pair + 2 * MB : 2 * pair + 4 * MB]
        g1, l1, hg = (mid_ref[0, p, i * 2 * MB : (i + 1) * 2 * MB].astype(f32) for i in range(3))
        u, s, r, m2, g2 = (small_ref[0, p, i * 2 * MB : (i + 1) * 2 * MB] for i in range(5))
        p2b, uq = pq_ref[0, p, 0 : 2 * MB], uq_ref[0, p, 0 : 2 * MB]
        e = e_ref[0, p]
        e2b = low(e * g2)
        dw1, dw2, db1, db2 = w1[p], w2[p], b1[p], b2[p]
        dw1b, dw2b = low(dw1), low(dw2)
        de1 = -(e1q + dot(kb, dw1b) + db1)
        de2 = -(e2q + dot_nt(x2b, dw2b) * own + db2)
        dk = dkq - dot_nt(e1b, dw1b) * own
        dx2 = x2q - dot(e2b, dw2b)
        de_ref[0, p] = jnp.broadcast_to(lane_sum(g1 * de1) + lane_sum(g2 * de2), u.shape)
        dg1 = twice(e) * de1
        dh = low(dg1 * l1)
        dg2 = e * de2 + dot_nt(dh, w2b) * own
        ma, mg = lane_sum(dg2 * u) * inv, lane_sum(dg2) * inv
        dr = s * (dg2 - mg * own - u * ma)
        gg = gain * gain
        du = dr * gg - s * (dg2 * m2 + r * ma)
        md, mu = lane_sum(du) * inv, lane_sum(du * u + dg2 * g2) * inv
        dz2 = low(s * (du - md * own - u * mu))
        dx2 = dx2 + dot(dz2, w2b)
        dz1 = low(dg1 * hg + dx2 * l1)
        dk = dk + dot_nt(dz1, w1b) * own
        drg = fold(dr) * gain
        dq_ref[:, cols] = low(dqc)
        dk_ref[:, cols] = low(fold(dk) + drg)
        dv_ref[:, cols] = low(-drg)
        ggain[:, cols] += fold(do_spread_times(do, uq)) + fold(dr * u) * (2.0 * gain) + fold(dr) * (bias - (vc - kc))
        gbias[:, cols] += do + drg
        ndw1 = dw1 + dot_tn(jnp.concatenate([qb, kb], 0), jnp.concatenate([dq1, dz1], 0))
        ndw2 = dw2 + dot_tn(jnp.concatenate([dq2, low(g2), dz2], 0), jnp.concatenate([p2b, dh, x2b], 0))
        ndb1 = db1 + dot(ones, dq1) + dot(ones, dz1)
        ndb2 = db2 + dot(ones, dq2) + dot(ones, dz2)
        first = restart_ref[jnp.minimum(steps - 1 - j, steps - 2)]
        go_on = 1.0 - first
        for ref, init, value in ((w1, gw1, ndw1), (w2, gw2, ndw2), (b1, gb1, ndb1), (b2, gb2, ndb2)):
            ref[p] = value * go_on
            init[p] += value * first


def do_spread_times(do, uq):
    return jnp.concatenate([do, do], 0) * uq


def backward_inner(restarts, q, k, v, do, e, saved, gain, bias, feed_terms, collective_id):
    big, mid, small, n1, pq, uq, n2 = saved
    blocks, pairs, _, pair = e.shape
    head_dim = pair // 2
    inner = big.shape[-1]
    steps = blocks + 1
    now = lambda j: jnp.minimum(blocks - j, blocks - 1)
    ahead = lambda j: jnp.maximum(blocks - 1 - j, 0)
    tok = lambda at: pl.BlockSpec((MB, pairs * pair), lambda j: (at(j), 0))

    def block(a, at, rows=None, part=0):
        shape = (1, pairs, rows or a.shape[2], a.shape[3])
        return pl.BlockSpec(shape, lambda j: (at(j), 0, part, 0))

    whole = lambda a: pl.BlockSpec(a.shape, lambda j: (0,) * a.ndim)
    later = lambda j: ahead(j) + 1
    at_now = lambda j: now(j) + 1
    operands = [
        (q, tok(ahead)), (k, tok(ahead)), (do, tok(ahead)), (e, block(e, ahead)), (big, block(big, ahead)),
        (small, block(small, ahead, 2 * MB, 4)), (n1, block(n1, ahead)), (pq, block(pq, later)), (uq, block(uq, later)),
        (n2, block(n2, later)),
        (q, tok(now)), (k, tok(now)), (v, tok(now)), (do, tok(now)), (e, block(e, now)), (big, block(big, now)),
        (mid, block(mid, now)), (small, block(small, now)), (pq, block(pq, at_now, 2 * MB)), (uq, block(uq, at_now, 2 * MB)),
        (gain, whole(gain)), (bias, whole(bias)),
    ]
    feeds = len(feed_terms)
    vmem = pl.BlockSpec(memory_space=pltpu.VMEM)
    operands += [(a, vmem) for a in feed_terms]
    width = pairs * pair
    tok_out = (jax.ShapeDtypeStruct((steps * MB, width), bf16), pl.BlockSpec((MB, width), lambda j: (blocks - j, 0)))
    state = [((pairs, pair, inner), f32), ((pairs, 2 * MB, inner), f32), ((pairs, pair, inner), f32), ((pairs, 2 * MB, pair), f32)]
    keep = lambda shape: (jax.ShapeDtypeStruct(shape, f32), pl.BlockSpec(shape, lambda j: (0,) * len(shape)))
    outs = [tok_out] * 3 + [
        (jax.ShapeDtypeStruct((steps, pairs, 2 * MB, pair), f32), pl.BlockSpec((1, pairs, 2 * MB, pair), lambda j: (blocks - j, 0, 0, 0)))
    ] + [keep(shape) for shape, _ in state] + [keep((MB, width))] * 2 + [(jax.ShapeDtypeStruct(a.shape, a.dtype), vmem) for a in feed_terms]
    stage_steps = {(i, s): (3 + 3 * (i + 2 * s)) * blocks // 32 for i in range(feeds) for s in range(4)}
    comm = []
    if feeds:
        groups, rows = lax.axis_size("group"), lax.axis_size("row")
        comm = [pltpu.VMEM((groups - 1, a.shape[0] // groups, a.shape[1]), bf16) for a in feed_terms]
        comm += [pltpu.VMEM((a.shape[0] // groups, a.shape[1]), bf16) for a in feed_terms]
        comm += [pltpu.VMEM((rows - 1, a.shape[0] // (groups * rows), a.shape[1]), bf16) for a in feed_terms]
        comm += [pltpu.VMEM(a.shape, bf16) for a in feed_terms]
        comm += [pltpu.SemaphoreType.DMA((feeds * 2 * (groups + rows - 2),))] * 2
    return pl.pallas_call(
        partial(backward_kernel, pairs, head_dim, feeds, stage_steps),
        grid_spec=pltpu.PrefetchScalarGridSpec(
            num_scalar_prefetch=0,
            grid=(steps,),
            in_specs=[pl.BlockSpec(memory_space=pltpu.SMEM)] + [o[1] for o in operands],
            out_specs=[o[1] for o in outs],
            scratch_shapes=[pltpu.VMEM(shape, kind) for shape, kind in state] + [
                pltpu.VMEM((pairs, 2 * MB, inner), f32),
                pltpu.VMEM((pairs, 2 * MB, pair), f32),
                pltpu.VMEM((pairs, 2 * MB, pair), f32),
                pltpu.VMEM((pairs, 2 * MB, inner), f32),
                pltpu.VMEM((pairs, 2 * MB, inner), bf16),
                pltpu.VMEM((pairs, 2 * MB, pair), bf16),
                pltpu.VMEM((pairs, MB, pair), f32),
            ] + comm,
        ),
        out_shape=[o[0] for o in outs],
        compiler_params=pltpu.CompilerParams(
            collective_id=collective_id if feeds else None, has_side_effects=bool(feeds), vmem_limit_bytes=56 * 1024 * 1024
        ),
        name="inner_backward",
    )(restarts.astype(f32), *[o[0] for o in operands])


def reduce_kernel(rows, groups, chunks, span, *refs):
    count = len(chunks)
    ins, part, small, rest = refs[:count], refs[count], refs[count + 1], refs[count + 2 :]
    outs, part_out, small_out, rest = rest[:count], rest[count], rest[count + 1], rest[count + 2 :]
    got_core, rest = rest[:count], rest[count:]
    sum_core, rest = rest[:count], rest[count:]
    got_y, rest = rest[:count], rest[count:]
    sum_y, rest = rest[:count], rest[count:]
    got_row, rest = rest[:count], rest[count:]
    part_got, part_sum, small_got, small_sum, send_sem, recv_sem = rest
    row, group, feat = lax.axis_index("row"), lax.axis_index("group"), lax.axis_index("feat")
    core, y = lax.rem(feat, 2), feat // 2
    core_mate = {"feat": feat + 1 - 2 * core}
    y_mate = {"feat": feat + 2 - 4 * y}
    row_mates = [{"row": lax.rem(row + o, rows)} for o in range(1, rows)]
    group_mates = [{"group": lax.rem(group + o, groups)} for o in range(1, groups)]
    started = []

    def send(src, dst, peer):
        i = len(started)
        copy = pltpu.make_async_remote_copy(
            src_ref=src, dst_ref=dst, send_sem=send_sem.at[i], recv_sem=recv_sem.at[i], device_id=peer, device_id_type=MESH
        )
        copy.start()
        started.append(copy)
        return copy

    def at(start, size):
        return pl.ds(pl.multiple_of(start, 16), size)

    def add(a, b):
        return (a.astype(f32) + b.astype(f32)).astype(bf16)

    greet([core_mate, y_mate] + row_mates + group_mates)
    halves = [shape[0] // 2 for shape in chunks]
    quarters = [shape[0] // 4 for shape in chunks]
    units = [shape[0] // (4 * rows) for shape in chunks]

    by_core = [send(ins[i].at[at((1 - core) * halves[i], halves[i])], got_core[i], core_mate) for i in range(count)]
    small_copy = send(small, small_got.at[0], core_mate)
    blocks = []
    for o in range(1, groups):
        blocks.append(send(part.at[lax.rem(group + o, groups)], part_got.at[o - 1], group_mates[o - 1]))
    by_y = []
    for i in range(count):
        by_core[i].wait_recv()
        sum_core[i][...] = add(ins[i][at(core * halves[i], halves[i])], got_core[i][...])
        by_y.append(send(sum_core[i].at[at((1 - y) * quarters[i], quarters[i])], got_y[i], y_mate))
    small_copy.wait_recv()
    small_sum[0] = small[...] + small_got[0]
    small_copy = send(small_sum.at[0], small_got.at[1], y_mate)
    total = part[group].astype(f32)
    for o in range(1, groups):
        blocks[o - 1].wait_recv()
        total = total + part_got[o - 1].astype(f32)
    part_sum[...] = total.astype(bf16)
    home = []
    for o in range(1, rows):
        home.append(send(part_sum.at[at(lax.rem(row + o, rows) * span, span)], part_out.at[at(row * span, span)], row_mates[o - 1]))
    part_out[at(row * span, span)] = part_sum[at(row * span, span)]
    by_row = []
    for i in range(count):
        by_y[i].wait_recv()
        sum_y[i][...] = add(sum_core[i][at(y * quarters[i], quarters[i])], got_y[i][...])
        by_row.append(
            [
                send(sum_y[i].at[at(lax.rem(row + o, rows) * units[i], units[i])], got_row[i].at[o - 1], row_mates[o - 1])
                for o in range(1, rows)
            ]
        )
    small_copy.wait_recv()
    small_sum[1] = small_sum[0] + small_got[1]
    small_copies = [send(small_sum.at[1], small_got.at[2 + row], row_mates[o - 1]) for o in range(1, rows)]
    small_got[2 + row] = small_sum[1]

    place = (core * 2 + y) * rows + row
    back_row = []
    for i in range(count):
        total = sum_y[i][at(row * units[i], units[i])].astype(f32)
        for o in range(1, rows):
            by_row[i][o - 1].wait_recv()
            total = total + got_row[i][o - 1].astype(f32)
        here = outs[i].at[group, at(place * units[i], units[i])]
        here[...] = total.astype(bf16)
        back_row.append([send(here, here, row_mates[o - 1]) for o in range(1, rows)])
    for copy in small_copies:
        copy.wait_recv()
    small_total = small_got[2]
    for r in range(1, rows):
        small_total = small_total + small_got[2 + r]
    small_out[group] = small_total
    small_copies = [send(small_out.at[group], small_out.at[group], mate) for mate in group_mates]
    first = []
    for i in range(count):
        for copy in back_row[i]:
            copy.wait_recv()
        here = outs[i].at[group, at((core * 2 + y) * quarters[i], quarters[i])]
        if i % 2 == 0:
            first.append([send(here, here, mate) for mate in group_mates])
        else:
            first.append([send(here, here, y_mate)])
    second = []
    for i in range(count):
        for copy in first[i]:
            copy.wait_recv()
        if i % 2 == 0:
            here = outs[i].at[:, at((core * 2 + y) * quarters[i], quarters[i])]
            second.append([send(here, here, y_mate)])
        else:
            here = outs[i].at[group, at(core * halves[i], halves[i])]
            second.append([send(here, here, mate) for mate in group_mates])
    third = []
    for i in range(count):
        for copy in second[i]:
            copy.wait_recv()
        here = outs[i].at[:, at(core * halves[i], halves[i])]
        third.append(send(here, here, core_mate))
    for copy in third + home + small_copies:
        copy.wait_recv()
    for copy in started:
        copy.wait_send()


def reduce_all(arrays, part, small, rows, groups, collective_id):
    chunks = [a.shape for a in arrays]
    count = len(chunks)
    span = part.shape[1] // rows
    copies = count * (2 + 2 * (rows - 1) + (groups - 1) + 2) + (groups - 1) + (rows - 1) + 2 + (rows - 1) + (groups - 1)
    vmem = pl.BlockSpec(memory_space=pltpu.VMEM)
    scratch = [pltpu.VMEM((h // 2, w), bf16) for h, w in chunks] * 2
    scratch += [pltpu.VMEM((h // 4, w), bf16) for h, w in chunks] * 2
    scratch += [pltpu.VMEM((rows - 1, h // (4 * rows), w), bf16) for h, w in chunks]
    scratch += [
        pltpu.VMEM((groups - 1,) + part.shape[1:], bf16),
        pltpu.VMEM(part.shape[1:], bf16),
        pltpu.VMEM((2 + rows,) + small.shape, f32),
        pltpu.VMEM((2,) + small.shape, f32),
        pltpu.SemaphoreType.DMA((copies,)),
        pltpu.SemaphoreType.DMA((copies,)),
    ]
    return pl.pallas_call(
        partial(reduce_kernel, rows, groups, chunks, span),
        in_specs=[vmem] * (count + 2),
        out_specs=[vmem] * (count + 2),
        out_shape=[jax.ShapeDtypeStruct((groups, h, w), bf16) for h, w in chunks]
        + [jax.ShapeDtypeStruct(part.shape[1:], bf16), jax.ShapeDtypeStruct((groups,) + small.shape, f32)],
        scratch_shapes=scratch,
        compiler_params=pltpu.CompilerParams(
            collective_id=collective_id, has_side_effects=True, vmem_limit_bytes=48 * 1024 * 1024
        ),
        name="reduce_all",
    )(*arrays, part, small)


def normalize(vector, gain):
    centered = vector - jnp.mean(vector, -1, keepdims=True)
    variance = jnp.mean(centered * centered, -1, keepdims=True)
    inv_scale = lax.rsqrt(variance + epsilon)
    normed_unit = centered * inv_scale
    return (normed_unit * gain, normed_unit, inv_scale)


def norm_back(grad_out, gain, normed_unit, inv_scale):
    scaled = grad_out * gain
    return inv_scale * (
        scaled
        - jnp.mean(scaled, -1, keepdims=True)
        - normed_unit * jnp.mean(scaled * normed_unit, -1, keepdims=True)
    )


SEQ = ("row", "group")


def per_device(
    tokens,
    cotangent,
    doc_starts,
    mixer_gain,
    query_weight,
    key_weight,
    value_weight,
    out_weight,
    rate_weight,
    rate_bias,
    first_init,
    first_bias_init,
    second_init,
    second_bias_init,
    inner_gain,
    inner_bias,
    feed_gain,
    gate_weight,
    up_weight,
    down_weight,
):
    rows, span, width = tokens.shape
    heads, head_dim, inner = first_init.shape
    groups = lax.axis_size("group")
    feats = lax.axis_size("feat")
    row, group = lax.axis_index("row"), lax.axis_index("group")
    count = rows * span
    length = span * rows * groups
    blocks = length // MB
    pairs = -(-heads // (2 * groups))
    mine = 2 * pairs
    pair = 2 * head_dim
    cols = mine * head_dim
    spare = mine * groups - heads

    def own_heads(array, axis, per_head=1):
        if spare:
            pad = [(0, 0)] * array.ndim
            pad[axis] = (0, spare * per_head)
            array = jnp.pad(array, pad)
        return lax.dynamic_slice_in_dim(array, group * mine * per_head, mine * per_head, axis)

    def to_rows(array):
        got = lax.all_to_all(jnp.repeat(array, groups, 0), SEQ, 0, 0, tiled=True)
        return got.reshape(length, array.shape[-1])

    def from_rows(array):
        parts = array.reshape(rows * groups, span, array.shape[-1])
        got = lax.all_to_all(parts, SEQ, 0, 0, tiled=True)
        return got.reshape(rows, groups, span, array.shape[-1])

    row_in = to_rows(tokens).astype(f32)
    act_row = low(normalize(row_in, mixer_gain)[0])
    w_q, w_k, w_v = (own_heads(w, 1, head_dim) for w in (query_weight, key_weight, value_weight))
    w_o = own_heads(out_weight, 0, head_dim)
    w_r = own_heads(rate_weight, 1)
    queries, keys, values = (dot(act_row, w) for w in (w_q, w_k, w_v))
    logits = dot(act_row, w_r) + own_heads(rate_bias, 0)
    sigma = jax.nn.sigmoid(logits)
    rates = sigma / head_dim
    e = jnp.broadcast_to(
        rates.reshape(blocks, MB, pairs, 2).transpose(0, 2, 3, 1).reshape(blocks, pairs, 2 * MB, 1),
        (blocks, pairs, 2 * MB, pair),
    )
    block_ids = jnp.arange(blocks, dtype=jnp.int32)
    starts = lax.dynamic_index_in_dim(doc_starts, row, 0, False)
    restarts = ((block_ids == 0) | jnp.any(starts[:, None] == block_ids[None], 0)).astype(jnp.int32)
    pack = lambda a: own_heads(a, 0).reshape(pairs, pair, inner)
    start_first = pack(first_init)
    start_second = pack(second_init - jnp.mean(second_init, 1, keepdims=True))
    start_first_bias = jnp.repeat(own_heads(first_bias_init, 0).reshape(pairs, 2, 1, inner), MB, 2).reshape(
        pairs, 2 * MB, inner
    )
    centered = own_heads(second_bias_init - jnp.mean(second_bias_init, 1, keepdims=True), 0)
    start_second_bias = (
        jnp.eye(2, dtype=f32)[None, :, None, :, None] * centered.reshape(pairs, 1, 1, 2, head_dim)
    ) * jnp.ones((1, 1, MB, 1, 1), f32)
    start_second_bias = start_second_bias.reshape(pairs, 2 * MB, pair)
    gain, bias = own_heads(inner_gain, 0).reshape(1, cols), own_heads(inner_bias, 0).reshape(1, cols)
    *saved, mixed = forward_inner(
        jnp.concatenate([restarts, jnp.zeros((1,), jnp.int32)]),
        queries, keys, values, e, start_first, start_first_bias, start_second, start_second_bias, gain, bias,
    )
    mixed_row = low(mixed[MB:])
    mixed_low = from_rows(mixed_row).transpose(0, 2, 1, 3).reshape(count, groups * cols)[:, :width]

    flat_in = tokens.astype(f32).reshape(count, width)
    hidden_in = flat_in + dot(mixed_low, out_weight)
    normed_two, unit_two, scale_two = normalize(hidden_in, feed_gain)
    act_two = low(normed_two)
    grad_low = cotangent.reshape(count, width)
    group_grad = lax.all_gather(grad_low, "feat", axis=0, tiled=True)
    grad_act = dot(group_grad, down_weight)
    group_rows = lax.all_gather(act_two, "feat", axis=0, tiled=True)
    gate_pre, up_value = dot(group_rows, gate_weight), dot(group_rows, up_weight)
    gate_sig = jax.nn.sigmoid(gate_pre)
    silu = gate_pre * gate_sig
    hidden_act = low(silu * up_value)
    grad_gate = low(grad_act * up_value * gate_sig * (1.0 + gate_pre * (1.0 - gate_sig)))
    grad_up = low(grad_act * silu)
    grad_act_two = lax.psum_scatter(
        low(dot_nt(grad_gate, gate_weight) + dot_nt(grad_up, up_weight)), "feat", scatter_dimension=0, tiled=True
    ).astype(f32)
    feed_out = lax.psum_scatter(
        low(dot_nt(hidden_act, down_weight)), "feat", scatter_dimension=0, tiled=True
    ).astype(f32)
    block_out = low(hidden_in + feed_out).reshape(rows, span, width)
    halves = lambda a, b: low(jnp.concatenate([dot_tn(a, half) for half in jnp.split(b, 2, 1)], 0))
    feed_terms = (halves(group_rows, grad_gate), halves(group_rows, grad_up), halves(group_grad, hidden_act))
    grad_feed_gain = jnp.sum(grad_act_two * unit_two, 0)
    grad_hidden = grad_low.astype(f32) + norm_back(grad_act_two, feed_gain, unit_two, scale_two)

    branch_row = to_rows(low(grad_hidden).reshape(rows, span, width))
    grad_mixed = dot_nt(branch_row, w_o)
    grad_out_rows = dot_tn(branch_row, mixed_row)
    grad_q, grad_k, grad_v, grad_e, g_first, g_first_bias, g_second, g_second_bias, g_gain, g_bias, *feed_grads = (
        backward_inner(restarts, queries, keys, values, grad_mixed, e, saved, gain, bias, feed_terms, 2)
    )
    grad_q, grad_k, grad_v = grad_q[:length], grad_k[:length], grad_v[:length]
    grad_rates = grad_e[:blocks, :, :, 0].reshape(blocks, pairs, 2, MB).transpose(0, 3, 1, 2).reshape(length, mine)
    grad_logits = low(grad_rates * sigma * (1.0 - sigma) / head_dim)
    part = dot_nt(grad_q, w_q) + dot_nt(grad_k, w_k) + dot_nt(grad_v, w_v) + dot_nt(grad_logits, w_r)
    _, unit_row, _ = normalize(row_in, mixer_gain)
    blocks_out = low(part).reshape(rows, groups, span, width).transpose(1, 0, 2, 3).reshape(groups, count, width)
    arrays = (
        jnp.concatenate([low(dot_tn(act_row, grad_q)), low(dot_tn(act_row, grad_k))], 1),
        jnp.concatenate([low(dot_tn(act_row, grad_v)), low(grad_out_rows)], 1),
        jnp.concatenate([low(g_first.reshape(cols, inner)), low(g_second.reshape(cols, inner))], 0),
    )
    per_head = jnp.concatenate(
        [
            g_first_bias.reshape(mine, MB, inner)[:, 0],
            jnp.stack([g_second_bias[:, h * MB, h * head_dim : (h + 1) * head_dim] for h in range(2)], 1).reshape(
                mine, head_dim
            ),
            jnp.sum(g_gain, 0).reshape(mine, head_dim),
            jnp.sum(g_bias, 0).reshape(mine, head_dim),
            dot_tn(grad_logits, act_row),
            jnp.sum(grad_logits.astype(f32), 0)[:, None],
            jnp.sum(logits, 0)[:, None],
        ],
        1,
    )
    used = (group * mine + jnp.arange(mine)) < heads
    peers = rows * feats
    top = jnp.max(jnp.where(used[None], logits, jnp.finfo(f32).min))
    tops = jnp.where(jnp.arange(peers) == row * feats + lax.axis_index("feat"), top, 0.0)
    pieces = [per_head.reshape(-1), jnp.sum(part * unit_row, 0), grad_feed_gain, tops]
    sizes = [p.shape[0] for p in pieces]
    size = sum(sizes)
    lines = -(-size // 1024) * 8
    small = jnp.pad(jnp.concatenate(pieces), (0, lines * 128 - size)).reshape(lines, 128)
    *arrays, got, small = reduce_all(arrays, blocks_out, small, rows, groups, 3)

    grad_act_one = got.astype(f32)
    _, unit_one, scale_one = normalize(flat_in, mixer_gain)
    input_grad = grad_hidden + norm_back(grad_act_one, mixer_gain, unit_one, scale_one)

    def gathered(array, part_no):
        got = lax.slice_in_dim(array, part_no * cols, (part_no + 1) * cols, axis=2).astype(f32)
        return got.transpose(1, 0, 2).reshape(width, groups * cols)[:, :width]

    g_query, g_key = (gathered(arrays[0], i) for i in range(2))
    g_value, g_out = gathered(arrays[1], 0), gathered(arrays[1], 1).T
    states = arrays[2].astype(f32).reshape(groups, 2, cols, inner)
    g_first, g_second = (
        states[:, i].reshape(groups * mine, head_dim, inner)[:heads] for i in range(2)
    )
    g_second = g_second - jnp.mean(g_second, 1, keepdims=True)
    small = small.reshape(groups, lines * 128)
    ends = [0]
    for s in sizes:
        ends.append(ends[-1] + s)
    slots = small[:, : ends[1]].reshape(groups * mine, -1)[:heads]
    g_mixer, g_feed = jnp.sum(small[:, ends[1] : ends[2]], 0), jnp.sum(small[:, ends[2] : ends[3]], 0)
    at = [0, inner, inner + head_dim, inner + 2 * head_dim, inner + 3 * head_dim, inner + 3 * head_dim + width]
    g_second_bias = slots[:, at[1] : at[2]]
    g_second_bias = g_second_bias - jnp.mean(g_second_bias, 1, keepdims=True)
    total = jnp.sum(slots[:, at[5] + 1])
    stats = jnp.stack([total / (rows * groups * feats * count * heads), jnp.max(small[:, ends[3] : ends[4]])])
    return (
        block_out,
        input_grad.reshape(rows, span, width),
        g_mixer,
        g_query,
        g_key,
        g_value,
        g_out,
        slots[:, at[4] : at[5]].T,
        slots[:, at[5]],
        g_first,
        slots[:, : at[1]],
        g_second,
        g_second_bias,
        slots[:, at[2] : at[3]],
        slots[:, at[3] : at[4]],
        g_feed,
        jnp.concatenate(jnp.split(feed_grads[0], 2, 0), 1).astype(f32),
        jnp.concatenate(jnp.split(feed_grads[1], 2, 0), 1).astype(f32),
        jnp.concatenate(jnp.split(feed_grads[2], 2, 0), 1).astype(f32),
        stats,
    )


def solution(mesh):
    feats = mesh.shape["feat"]

    def run(*arrays):
        rows = arrays[0].shape[0] // feats
        grid = jax.sharding.Mesh(mesh.devices.reshape(rows, -1, feats), ("row", "group", "feat"))
        by_token = P("feat", SEQ, None)
        by_hidden = P(None, "feat")
        return jax.shard_map(
            per_device,
            mesh=grid,
            in_specs=(by_token, by_token, P("feat", None)) + (P(),) * 14 + (by_hidden,) * 3,
            out_specs=(by_token, by_token) + (P(),) * 14 + (by_hidden,) * 3 + (P(),),
            check_vma=False,
        )(*arrays)

    return run
```

```python
from functools import partial

import jax
import jax.numpy as jnp
from jax import lax
from jax.experimental import pallas as pl
from jax.experimental.pallas import tpu as pltpu
from jax.sharding import PartitionSpec as P

MB = 16
epsilon = 1e-05
f32, bf16 = jnp.float32, jnp.bfloat16


def dot(a, b):
    return lax.dot_general(a, b, (((1,), (0,)), ((), ())), preferred_element_type=f32)


def dot_nt(a, b):
    return lax.dot_general(a, b, (((1,), (1,)), ((), ())), preferred_element_type=f32)


def dot_tn(a, b):
    return lax.dot_general(a, b, (((0,), (0,)), ((), ())), preferred_element_type=f32)


def low(v):
    return v.astype(bf16)


def gelu_parts(z):
    a = jnp.abs(z)
    d = 1.0 + 0.23164189 * a
    t = pl.reciprocal(d, approx=True)
    t = t * (2.0 - d * t)
    ex = jnp.exp(-0.5 * (z * z))
    poly = t * (
        0.127414796 + t * (-0.142248368 + t * (0.7107068705 + t * (-0.7265760135 + t * 0.5307027145)))
    )
    h = poly * ex
    cdf = jnp.where(z >= 0, 1.0 - h, h)
    pdf = 0.3989422804014327 * ex
    return z * cdf, cdf + z * pdf, pdf


def lane_sum(v):
    return jnp.sum(v, -1, keepdims=True)


def masks(head_dim):
    pair = 2 * head_dim
    rows, cols = 2 * MB, pair
    r = lax.broadcasted_iota(jnp.int32, (rows, cols), 0)
    c = lax.broadcasted_iota(jnp.int32, (rows, cols), 1)
    own = ((r < MB) == (c < head_dim)).astype(f32)
    r = lax.broadcasted_iota(jnp.int32, (rows, rows), 0)
    c = lax.broadcasted_iota(jnp.int32, (rows, rows), 1)
    same = (r < MB) == (c < MB)
    causal = (same & (c <= r)).astype(f32)
    return own, causal, same.astype(bf16)


def spread(v, own):
    return jnp.concatenate([v, v], 0) * own


def fold(v):
    return v[:MB] + v[MB:]


def twice(v):
    return jnp.concatenate([v, v], 1)


def forward_kernel(pairs, head_dim, restart_ref, q_ref, k_ref, v_ref, e_ref, w1i_ref, b1i_ref, w2i_ref, b2i_ref, gain_ref, bias_ref,
                   big_ref, mid_ref, small_ref, n1_ref, pq_ref, uq_ref, n2_ref, out_ref,
                   w1, b1, w2, b2, s_q1, s_x2, s_e2, s_w2, s_b2, s_q):
    j = pl.program_id(0)
    pair = 2 * head_dim
    inv = 1.0 / head_dim
    own, causal, ones = masks(head_dim)

    @pl.when(restart_ref[j] > 0)
    def _():
        w1[...] = w1i_ref[...]
        b1[...] = b1i_ref[...]
        w2[...] = w2i_ref[...]
        b2[...] = b2i_ref[...]

    before = [(s_q1[p], s_x2[p], s_e2[p], s_w2[p], s_b2[p], s_q[p]) for p in range(pairs)]
    for p in range(pairs):
        cols = slice(p * pair, (p + 1) * pair)
        gain, bias = gain_ref[:, cols], bias_ref[:, cols]
        qc, kc, vc = q_ref[:, cols], k_ref[:, cols], v_ref[:, cols]
        kb, qb = low(spread(kc, own)), low(spread(qc, own))
        w1c, w2c = w1[p], w2[p]
        w1b, w2b = low(w1c), low(w2c)
        b1c, b2c = b1[p], b2[p]
        kq = dot(jnp.concatenate([kb, qb], 0), w1b)
        z1 = kq[: 2 * MB] + b1c
        x2, l1, pdf = gelu_parts(z1)
        x2b = low(x2)
        c = dot_nt(x2b, w2b) * own + b2c
        s = lax.rsqrt(lane_sum(c * c) * inv + epsilon)
        u = c * s
        r = u * (gain * gain) + spread((bias - (vc - kc)) * gain, own)
        mr, m2 = lane_sum(r) * inv, lane_sum(r * u) * inv
        g2 = s * (r - mr * own - u * m2)
        e = e_ref[0, p]
        h = dot(low(g2), w2b)
        g1 = h * l1
        e1b, e2b = low(twice(e) * g1), low(e * g2)
        n1 = causal * (dot_nt(qb, kb) + 1.0)
        q1 = kq[2 * MB :] + b1c - dot(low(n1), e1b)
        w1[p] = w1c - dot_tn(kb, e1b)
        b1[p] = b1c - dot(ones, e1b)
        w2[p] = w2c - dot_tn(e2b, x2b)
        b2[p] = b2c - dot(ones, e2b)
        big_ref[0, p, 0:pair] = w1b
        big_ref[0, p, pair : 2 * pair] = w2b
        big_ref[0, p, 2 * pair : 2 * pair + 2 * MB] = x2b
        big_ref[0, p, 2 * pair + 2 * MB : 2 * pair + 4 * MB] = e1b
        mid_ref[0, p, 0 : 2 * MB] = low(g1)
        mid_ref[0, p, 2 * MB : 4 * MB] = low(l1)
        mid_ref[0, p, 4 * MB : 6 * MB] = low(h * pdf * (2.0 - z1 * z1))
        small_ref[0, p, 0 : 2 * MB] = u
        small_ref[0, p, 2 * MB : 4 * MB] = jnp.broadcast_to(s, u.shape)
        small_ref[0, p, 4 * MB : 6 * MB] = r
        small_ref[0, p, 6 * MB : 8 * MB] = jnp.broadcast_to(m2, u.shape)
        small_ref[0, p, 8 * MB : 10 * MB] = g2
        n1_ref[0, p] = low(n1)
        q1p, x2p, e2p, w2p, b2p, qp = before[p]
        s_q1[p], s_x2[p], s_e2[p], s_w2[p], s_b2[p], s_q[p] = q1, x2b, e2b, w2b, b2c, qc
        p2, lq, _ = gelu_parts(q1p)
        p2b = low(p2)
        n2 = causal * (dot_nt(p2b, x2p) + 1.0)
        q2 = dot_nt(p2b, w2p) * own - dot(low(n2), e2p) + b2p
        sq = lax.rsqrt(lane_sum(q2 * q2) * inv + epsilon)
        uq = q2 * sq
        out_ref[:, cols] = qp + fold(uq) * gain + bias
        pq_ref[0, p, 0 : 2 * MB] = p2b
        pq_ref[0, p, 2 * MB : 4 * MB] = low(lq)
        uq_ref[0, p, 0 : 2 * MB] = uq
        uq_ref[0, p, 2 * MB : 4 * MB] = jnp.broadcast_to(sq, uq.shape)
        n2_ref[0, p] = low(n2)


def forward_inner(restarts, q, k, v, e, w1i, b1i, w2i, b2i, gain, bias):
    blocks, pairs, _, pair = e.shape
    head_dim = pair // 2
    inner = w1i.shape[-1]
    steps = blocks + 1
    last = blocks - 1
    tok = pl.BlockSpec((MB, pairs * pair), lambda j, r: (jnp.minimum(j, last), 0))
    whole = lambda a: pl.BlockSpec(a.shape, lambda j, r: (0,) * a.ndim)

    def per_step(rows, width, dtype):
        return (
            jax.ShapeDtypeStruct((steps, pairs, rows, width), dtype),
            pl.BlockSpec((1, pairs, rows, width), lambda j, r: (j, 0, 0, 0)),
        )

    outs = [
        per_step(2 * pair + 4 * MB, inner, bf16),
        per_step(6 * MB, inner, bf16),
        per_step(10 * MB, pair, f32),
        per_step(2 * MB, 2 * MB, bf16),
        per_step(4 * MB, inner, bf16),
        per_step(4 * MB, pair, f32),
        per_step(2 * MB, 2 * MB, bf16),
        (
            jax.ShapeDtypeStruct((steps * MB, pairs * pair), f32),
            pl.BlockSpec((MB, pairs * pair), lambda j, r: (j, 0)),
        ),
    ]
    return pl.pallas_call(
        partial(forward_kernel, pairs, head_dim),
        grid_spec=pltpu.PrefetchScalarGridSpec(
            num_scalar_prefetch=1,
            grid=(steps,),
            in_specs=[tok, tok, tok, pl.BlockSpec((1, pairs, 2 * MB, pair), lambda j, r: (jnp.minimum(j, last), 0, 0, 0))]
            + [whole(a) for a in (w1i, b1i, w2i, b2i, gain, bias)],
            out_specs=[o[1] for o in outs],
            scratch_shapes=[
                pltpu.VMEM((pairs, pair, inner), f32),
                pltpu.VMEM((pairs, 2 * MB, inner), f32),
                pltpu.VMEM((pairs, pair, inner), f32),
                pltpu.VMEM((pairs, 2 * MB, pair), f32),
                pltpu.VMEM((pairs, 2 * MB, inner), f32),
                pltpu.VMEM((pairs, 2 * MB, inner), bf16),
                pltpu.VMEM((pairs, 2 * MB, pair), bf16),
                pltpu.VMEM((pairs, pair, inner), bf16),
                pltpu.VMEM((pairs, 2 * MB, pair), f32),
                pltpu.VMEM((pairs, MB, pair), f32),
            ],
        ),
        out_shape=[o[0] for o in outs],
        compiler_params=pltpu.CompilerParams(vmem_limit_bytes=48 * 1024 * 1024),
        name="inner_forward",
    )(restarts, q, k, v, e, w1i, b1i, w2i, b2i, gain, bias)


MESH = pl.DeviceIdType.MESH


def greet(peers):
    barrier = pltpu.get_barrier_semaphore()
    for peer in peers:
        pl.semaphore_signal(barrier, inc=1, device_id=peer, device_id_type=MESH)
    pl.semaphore_wait(barrier, len(peers))


class Copies:
    def __init__(self, send_sem, recv_sem):
        self.send_sem, self.recv_sem, self.started = send_sem, recv_sem, []

    def make(self, src, dst, peer):
        i = len(self.started)
        copy = pltpu.make_async_remote_copy(
            src_ref=src, dst_ref=dst, send_sem=self.send_sem.at[i], recv_sem=self.recv_sem.at[i],
            device_id=peer, device_id_type=MESH,
        )
        self.started.append(copy)
        return copy

    def send(self, src, dst, peer):
        copy = self.make(src, dst, peer)
        copy.start()
        return copy


def rows_at(start, size):
    return pl.ds(pl.multiple_of(start, 16), size)


def add_low(a, b):
    return (a.astype(f32) + b.astype(f32)).astype(bf16)


def mates(axis):
    size, here = lax.axis_size(axis), lax.axis_index(axis)
    return [{axis: lax.rem(here + o, size)} for o in range(1, size)]


def feed_sum_steps(ins, outs, got_group, sum_group, got_row, full, copies):
    row, group = lax.axis_index("row"), lax.axis_index("group")
    rows, groups = lax.axis_size("row"), lax.axis_size("group")
    row_mates, group_mates = mates("row"), mates("group")
    stages = {}
    for i, src in enumerate(ins):
        part = src.shape[0] // groups
        unit = part // rows

        def scatter_group(i=i, src=src, part=part):
            return [
                copies.make(src.at[rows_at(lax.rem(group + o, groups) * part, part)], got_group[i].at[o - 1], group_mates[o - 1])
                for o in range(1, groups)
            ]

        def scatter_row(i=i, unit=unit):
            return [
                copies.make(sum_group[i].at[rows_at(lax.rem(row + o, rows) * unit, unit)], got_row[i].at[o - 1], row_mates[o - 1])
                for o in range(1, rows)
            ]

        def gather_row(i=i, part=part, unit=unit):
            here = full[i].at[rows_at(group * part + row * unit, unit)]
            return [copies.make(here, here, mate) for mate in row_mates]

        def gather_group(i=i, part=part):
            here = full[i].at[rows_at(group * part, part)]
            return [copies.make(here, here, mate) for mate in group_mates]

        stages[i] = [scatter_group(), scatter_row(), gather_row(), gather_group()]

    def begin():
        greet(row_mates + group_mates)
        for i in range(len(ins)):
            for copy in stages[i][0]:
                copy.start()

    def after(i, s):
        part = ins[i].shape[0] // groups
        unit = part // rows
        for copy in stages[i][s]:
            copy.wait_recv()
        if s == 0:
            total = ins[i][rows_at(group * part, part)].astype(f32)
            for o in range(1, groups):
                total = total + got_group[i][o - 1].astype(f32)
            sum_group[i][...] = low(total)
        if s == 1:
            total = sum_group[i][rows_at(row * unit, unit)].astype(f32)
            for o in range(1, rows):
                total = total + got_row[i][o - 1].astype(f32)
            full[i][rows_at(group * part + row * unit, unit)] = low(total)
        if s < 3:
            for copy in stages[i][s + 1]:
                copy.start()
        else:
            outs[i][...] = full[i][...]
            for copy in sum(stages[i], []):
                copy.wait_send()

    return begin, after


def backward_kernel(pairs, head_dim, feeds, stage_steps, restart_ref,
                    qq_ref, kq_ref, doq_ref, eq_ref, bigq_ref, g2q_ref, n1_ref, pqq_ref, uqq_ref, n2_ref,
                    q_ref, k_ref, v_ref, do_ref, e_ref, big_ref, mid_ref, small_ref, pq_ref, uq_ref, gain_ref, bias_ref, *refs):
    j = pl.program_id(0)
    steps = pl.num_programs(0)
    pair = 2 * head_dim
    inv = 1.0 / head_dim
    own, causal, ones = masks(head_dim)
    feed_in, refs = refs[:feeds], refs[feeds:]
    dq_ref, dk_ref, dv_ref, de_ref, gw1, gb1, gw2, gb2, ggain, gbias = refs[:10]
    feed_out, refs = refs[10 : 10 + feeds], refs[10 + feeds :]
    w1, b1, w2, b2, s_e1, s_e2, s_k, s_x2, s_q1, s_q2, s_q = refs[:11]
    buffers = [refs[11 + i * feeds : 11 + (i + 1) * feeds] for i in range(4)]
    if feeds:
        begin, after = feed_sum_steps(feed_in, feed_out, *buffers, Copies(*refs[-2:]))
        pl.when(j == 0)(begin)
        for (i, s), at in stage_steps.items():
            pl.when(j == at)(partial(after, i, s))

    @pl.when(j <= 1)
    def _():
        for ref in (w1, b1, w2, b2, gw1, gb1, gw2, gb2, ggain, gbias):
            ref[...] = jnp.zeros_like(ref)

    before = [(s_e1[p], s_e2[p], s_k[p], s_x2[p], s_q1[p], s_q2[p], s_q[p]) for p in range(pairs)]
    for p in range(pairs):
        cols = slice(p * pair, (p + 1) * pair)
        gain, bias = gain_ref[:, cols], bias_ref[:, cols]
        qb, kb, do = low(spread(qq_ref[:, cols], own)), low(spread(kq_ref[:, cols], own)), doq_ref[:, cols]
        w1b, w2b = bigq_ref[0, p, 0:pair], bigq_ref[0, p, pair : 2 * pair]
        x2b, e1b = bigq_ref[0, p, 2 * pair : 2 * pair + 2 * MB], bigq_ref[0, p, 2 * pair + 2 * MB : 2 * pair + 4 * MB]
        e2b = low(eq_ref[0, p] * g2q_ref[0, p])
        n1b, n2b = n1_ref[0, p], n2_ref[0, p]
        p2b, lq = pqq_ref[0, p, 0 : 2 * MB], pqq_ref[0, p, 2 * MB : 4 * MB].astype(f32)
        uq, sq = uqq_ref[0, p, 0 : 2 * MB], uqq_ref[0, p, 2 * MB : 4 * MB]
        w = spread(do * gain, own)
        new_q2 = low(sq * (w - (lane_sum(w) * inv) * own - uq * (lane_sum(w * uq) * inv)))
        dpx = low(-causal * dot_nt(new_q2, e2b))
        new_q1 = low((dot(new_q2, w2b) + dot(dpx, x2b)) * lq)
        dqk = low(-causal * dot_nt(new_q1, e1b))
        new_e1 = dot_tn(n1b, new_q1)
        new_e2 = dot_tn(n2b, new_q2)
        new_k = dot_tn(dqk, qb)
        new_x2 = dot_tn(dpx, p2b)
        new_q = do + fold((dot_nt(new_q1, w1b) + dot(dqk, kb)) * own)
        e1q, e2q, dkq, x2q, dq1, dq2, dqc = before[p]
        s_e1[p], s_e2[p], s_k[p], s_x2[p], s_q1[p], s_q2[p], s_q[p] = (
            new_e1, new_e2, new_k, new_x2, new_q1, new_q2, new_q,
        )
        qc, kc, vc, do = q_ref[:, cols], k_ref[:, cols], v_ref[:, cols], do_ref[:, cols]
        qb, kb = low(spread(qc, own)), low(spread(kc, own))
        w1b, w2b = big_ref[0, p, 0:pair], big_ref[0, p, pair : 2 * pair]
        x2b, e1b = big_ref[0, p, 2 * pair : 2 * pair + 2 * MB], big_ref[0, p, 2 * pair + 2 * MB : 2 * pair + 4 * MB]
        g1, l1, hg = (mid_ref[0, p, i * 2 * MB : (i + 1) * 2 * MB].astype(f32) for i in range(3))
        u, s, r, m2, g2 = (small_ref[0, p, i * 2 * MB : (i + 1) * 2 * MB] for i in range(5))
        p2b, uq = pq_ref[0, p, 0 : 2 * MB], uq_ref[0, p, 0 : 2 * MB]
        e = e_ref[0, p]
        e2b = low(e * g2)
        dw1, dw2, db1, db2 = w1[p], w2[p], b1[p], b2[p]
        dw1b, dw2b = low(dw1), low(dw2)
        de1 = -(e1q + dot(kb, dw1b) + db1)
        de2 = -(e2q + dot_nt(x2b, dw2b) * own + db2)
        dk = dkq - dot_nt(e1b, dw1b) * own
        dx2 = x2q - dot(e2b, dw2b)
        de_ref[0, p] = jnp.broadcast_to(lane_sum(g1 * de1) + lane_sum(g2 * de2), u.shape)
        dg1 = twice(e) * de1
        dh = low(dg1 * l1)
        dg2 = e * de2 + dot_nt(dh, w2b) * own
        ma, mg = lane_sum(dg2 * u) * inv, lane_sum(dg2) * inv
        dr = s * (dg2 - mg * own - u * ma)
        gg = gain * gain
        du = dr * gg - s * (dg2 * m2 + r * ma)
        md, mu = lane_sum(du) * inv, lane_sum(du * u + dg2 * g2) * inv
        dz2 = low(s * (du - md * own - u * mu))
        dx2 = dx2 + dot(dz2, w2b)
        dz1 = low(dg1 * hg + dx2 * l1)
        dk = dk + dot_nt(dz1, w1b) * own
        drg = fold(dr) * gain
        dq_ref[:, cols] = low(dqc)
        dk_ref[:, cols] = low(fold(dk) + drg)
        dv_ref[:, cols] = low(-drg)
        ggain[:, cols] += fold(do_spread_times(do, uq)) + fold(dr * u) * (2.0 * gain) + fold(dr) * (bias - (vc - kc))
        gbias[:, cols] += do + drg
        ndw1 = dw1 + dot_tn(jnp.concatenate([qb, kb], 0), jnp.concatenate([dq1, dz1], 0))
        ndw2 = dw2 + dot_tn(jnp.concatenate([dq2, low(g2), dz2], 0), jnp.concatenate([p2b, dh, x2b], 0))
        ndb1 = db1 + dot(ones, dq1) + dot(ones, dz1)
        ndb2 = db2 + dot(ones, dq2) + dot(ones, dz2)
        first = restart_ref[jnp.minimum(steps - 1 - j, steps - 2)]
        go_on = 1.0 - first
        for ref, init, value in ((w1, gw1, ndw1), (w2, gw2, ndw2), (b1, gb1, ndb1), (b2, gb2, ndb2)):
            ref[p] = value * go_on
            init[p] += value * first


def do_spread_times(do, uq):
    return jnp.concatenate([do, do], 0) * uq


def backward_inner(restarts, q, k, v, do, e, saved, gain, bias, feed_terms, collective_id):
    big, mid, small, n1, pq, uq, n2 = saved
    blocks, pairs, _, pair = e.shape
    head_dim = pair // 2
    inner = big.shape[-1]
    steps = blocks + 1
    now = lambda j: jnp.minimum(blocks - j, blocks - 1)
    ahead = lambda j: jnp.maximum(blocks - 1 - j, 0)
    tok = lambda at: pl.BlockSpec((MB, pairs * pair), lambda j: (at(j), 0))

    def block(a, at, rows=None, part=0):
        shape = (1, pairs, rows or a.shape[2], a.shape[3])
        return pl.BlockSpec(shape, lambda j: (at(j), 0, part, 0))

    whole = lambda a: pl.BlockSpec(a.shape, lambda j: (0,) * a.ndim)
    later = lambda j: ahead(j) + 1
    at_now = lambda j: now(j) + 1
    operands = [
        (q, tok(ahead)), (k, tok(ahead)), (do, tok(ahead)), (e, block(e, ahead)), (big, block(big, ahead)),
        (small, block(small, ahead, 2 * MB, 4)), (n1, block(n1, ahead)), (pq, block(pq, later)), (uq, block(uq, later)),
        (n2, block(n2, later)),
        (q, tok(now)), (k, tok(now)), (v, tok(now)), (do, tok(now)), (e, block(e, now)), (big, block(big, now)),
        (mid, block(mid, now)), (small, block(small, now)), (pq, block(pq, at_now, 2 * MB)), (uq, block(uq, at_now, 2 * MB)),
        (gain, whole(gain)), (bias, whole(bias)),
    ]
    feeds = len(feed_terms)
    vmem = pl.BlockSpec(memory_space=pltpu.VMEM)
    operands += [(a, vmem) for a in feed_terms]
    width = pairs * pair
    tok_out = (jax.ShapeDtypeStruct((steps * MB, width), bf16), pl.BlockSpec((MB, width), lambda j: (blocks - j, 0)))
    state = [((pairs, pair, inner), f32), ((pairs, 2 * MB, inner), f32), ((pairs, pair, inner), f32), ((pairs, 2 * MB, pair), f32)]
    keep = lambda shape: (jax.ShapeDtypeStruct(shape, f32), pl.BlockSpec(shape, lambda j: (0,) * len(shape)))
    outs = [tok_out] * 3 + [
        (jax.ShapeDtypeStruct((steps, pairs, 2 * MB, pair), f32), pl.BlockSpec((1, pairs, 2 * MB, pair), lambda j: (blocks - j, 0, 0, 0)))
    ] + [keep(shape) for shape, _ in state] + [keep((MB, width))] * 2 + [(jax.ShapeDtypeStruct(a.shape, a.dtype), vmem) for a in feed_terms]
    stage_steps = {(i, s): (3 + 3 * (i + 2 * s)) * blocks // 32 for i in range(feeds) for s in range(4)}
    comm = []
    if feeds:
        groups, rows = lax.axis_size("group"), lax.axis_size("row")
        comm = [pltpu.VMEM((groups - 1, a.shape[0] // groups, a.shape[1]), bf16) for a in feed_terms]
        comm += [pltpu.VMEM((a.shape[0] // groups, a.shape[1]), bf16) for a in feed_terms]
        comm += [pltpu.VMEM((rows - 1, a.shape[0] // (groups * rows), a.shape[1]), bf16) for a in feed_terms]
        comm += [pltpu.VMEM(a.shape, bf16) for a in feed_terms]
        comm += [pltpu.SemaphoreType.DMA((feeds * 2 * (groups + rows - 2),))] * 2
    return pl.pallas_call(
        partial(backward_kernel, pairs, head_dim, feeds, stage_steps),
        grid_spec=pltpu.PrefetchScalarGridSpec(
            num_scalar_prefetch=0,
            grid=(steps,),
            in_specs=[pl.BlockSpec(memory_space=pltpu.SMEM)] + [o[1] for o in operands],
            out_specs=[o[1] for o in outs],
            scratch_shapes=[pltpu.VMEM(shape, kind) for shape, kind in state] + [
                pltpu.VMEM((pairs, 2 * MB, inner), f32),
                pltpu.VMEM((pairs, 2 * MB, pair), f32),
                pltpu.VMEM((pairs, 2 * MB, pair), f32),
                pltpu.VMEM((pairs, 2 * MB, inner), f32),
                pltpu.VMEM((pairs, 2 * MB, inner), bf16),
                pltpu.VMEM((pairs, 2 * MB, pair), bf16),
                pltpu.VMEM((pairs, MB, pair), f32),
            ] + comm,
        ),
        out_shape=[o[0] for o in outs],
        compiler_params=pltpu.CompilerParams(
            collective_id=collective_id if feeds else None, has_side_effects=bool(feeds), vmem_limit_bytes=56 * 1024 * 1024
        ),
        name="inner_backward",
    )(restarts.astype(f32), *[o[0] for o in operands])


def norm_parts(v, width):
    centered = v - jnp.sum(v, -1, keepdims=True) * (1.0 / width)
    scale = lax.rsqrt(jnp.sum(centered * centered, -1, keepdims=True) * (1.0 / width) + epsilon)
    return centered * scale, scale


def middle_kernel(span, mixed_ref, tok_ref, cot_ref, wout_ref, gate_ref, up_ref, down_ref, gain_ref,
                  block_ref, hid_ref, gmix_ref, gwo_ref, tgate_ref, tup_ref, tdown_ref, gfeed_ref,
                  mixed_got, acts, cots, unit, scales, h_in, gg, gu, ha, pg0, po0, out_core, in_core, out_diag, in_diag, out_y, in_y,
                  branch, branch_row, send_sem, recv_sem, local_sem):
    rows, groups = lax.axis_size("row"), lax.axis_size("group")
    row, group, feat = lax.axis_index("row"), lax.axis_index("group"), lax.axis_index("feat")
    count, width = tok_ref.shape
    cols = mixed_ref.shape[1]
    core, y = lax.rem(feat, 2), feat // 2
    core_mate, y_mate = {"feat": feat + 1 - 2 * core}, {"feat": feat + 2 - 4 * y}
    here = row * groups + group
    places = rows * groups
    others = [lax.rem(here + o, places) for o in range(1, places)]
    seq_mates = [{"row": t // groups, "group": lax.rem(t, groups)} for t in others]
    copies = Copies(send_sem, recv_sem)
    send = copies.send
    slot = lambda ref, s: ref.at[s * count : (s + 1) * count]

    greet([core_mate, y_mate] + seq_mates)
    lanes = pl.ds(pl.multiple_of(group * cols, 128), cols)
    moves = [
        send(mixed_ref.at[rows_at(t * span, span)], mixed_got.at[rows_at(row * span, span), lanes], mate)
        for t, mate in zip(others, seq_mates)
    ]
    own = pltpu.make_async_copy(
        mixed_ref.at[rows_at(here * span, span)], mixed_got.at[rows_at(row * span, span), lanes], local_sem.at[0]
    )
    own.start()
    cot_core = send(cot_ref, slot(cots, 1), core_mate)
    cot_y = send(cot_ref, slot(cots, 2), y_mate)
    cots[0:count] = cot_ref[...]
    own.wait()
    for copy in moves:
        copy.wait_recv()
    hidden = tok_ref[...].astype(f32) + dot(mixed_got[:, :width], wout_ref[:width])
    h_in[...] = hidden
    unit_two, scale_two = norm_parts(hidden, width)
    unit[...] = unit_two
    scales[...] = jnp.broadcast_to(scale_two, scales.shape)
    acts[0:count] = low(unit_two * gain_ref[...])
    act_core = send(slot(acts, 0), slot(acts, 1), core_mate)
    act_y = send(slot(acts, 0), slot(acts, 2), y_mate)
    cot_y.wait_recv()
    cot_diag = send(slot(cots, 2), slot(cots, 3), core_mate)

    def feed(s):
        part = slice(s * count, (s + 1) * count)
        gate_pre, up_value = dot(acts[part], gate_ref[...]), dot(acts[part], up_ref[...])
        grad = dot(cots[part], down_ref[...])
        sig = jax.nn.sigmoid(gate_pre)
        silu = gate_pre * sig
        ha[part] = low(silu * up_value)
        gg[part] = low(grad * up_value * sig * (1.0 + gate_pre * (1.0 - sig)))
        gu[part] = low(grad * silu)
        back = dot_nt(gg[part], gate_ref[...]) + dot_nt(gu[part], up_ref[...])
        return back, dot_nt(ha[part], down_ref[...])

    pg0[...], po0[...] = feed(0)
    act_core.wait_recv()
    cot_core.wait_recv()
    back, forth = feed(1)
    out_core[0], out_core[1] = low(back), low(forth)
    core_sums = [send(out_core.at[i], in_core.at[i], core_mate) for i in range(2)]
    act_y.wait_recv()
    act_diag = send(slot(acts, 2), slot(acts, 3), core_mate)
    act_diag.wait_recv()
    cot_diag.wait_recv()
    back, forth = feed(3)
    out_diag[0], out_diag[1] = low(back), low(forth)
    diag_sums = [send(out_diag.at[i], in_diag.at[i], core_mate) for i in range(2)]
    back, forth = feed(2)
    y_sums = []
    for i, value in enumerate((back, forth)):
        diag_sums[i].wait_recv()
        out_y[i] = low(value + in_diag[i].astype(f32))
        y_sums.append(send(out_y.at[i], in_y.at[i], y_mate))
    half = gg.shape[1] // 2
    for out, left, right in ((tgate_ref, acts, gg), (tup_ref, acts, gu), (tdown_ref, cots, ha)):
        for h in range(2):
            out[h * width : (h + 1) * width] = low(dot_tn(left[...], right[:, h * half : (h + 1) * half]))
    core_sums[0].wait_recv()
    y_sums[0].wait_recv()
    grad_act = pg0[...] + in_core[0].astype(f32) + in_y[0].astype(f32)
    unit_two = unit[...]
    gfeed_ref[...] = jnp.sum(grad_act * unit_two, 0, keepdims=True)
    w = grad_act * gain_ref[...]
    inv = 1.0 / width
    grad = cot_ref[...].astype(f32) + scales[:, 0:1] * (
        w - jnp.sum(w, -1, keepdims=True) * inv - unit_two * (jnp.sum(w * unit_two, -1, keepdims=True) * inv)
    )
    hid_ref[...] = grad
    branch[...] = low(grad)
    moves = [
        send(branch.at[rows_at((t // groups) * span, span)], branch_row.at[rows_at(here * span, span)], mate)
        for t, mate in zip(others, seq_mates)
    ]
    branch_row[rows_at(here * span, span)] = branch[rows_at(row * span, span)]
    core_sums[1].wait_recv()
    y_sums[1].wait_recv()
    block_ref[...] = low(h_in[...] + po0[...] + in_core[1].astype(f32) + in_y[1].astype(f32))
    for copy in moves:
        copy.wait_recv()
    gmix_ref[...] = dot_nt(branch_row[...], wout_ref[rows_at(group * cols, cols)])
    gwo_ref[...] = low(dot_tn(branch_row[...], mixed_ref[...]))
    for copy in copies.started:
        copy.wait_send()


def middle(mixed_row, tokens, cotangent, out_weight, gate_weight, up_weight, down_weight, gain, span, collective_id):
    rows, groups = lax.axis_size("row"), lax.axis_size("group")
    length, cols = mixed_row.shape
    count, width = tokens.shape
    hidden = gate_weight.shape[1]
    copies = 2 * (rows * groups - 1) + 12
    vmem = pl.BlockSpec(memory_space=pltpu.VMEM)
    outs = [
        ((count, width), bf16), ((count, width), f32), ((length, cols), f32), ((width, cols), bf16),
        ((2 * width, hidden // 2), bf16), ((2 * width, hidden // 2), bf16), ((2 * width, hidden // 2), bf16), ((1, width), f32),
    ]
    two = pltpu.VMEM((2, count, width), bf16)
    return pl.pallas_call(
        partial(middle_kernel, span),
        in_specs=[vmem] * 8,
        out_specs=[vmem] * len(outs),
        out_shape=[jax.ShapeDtypeStruct(*o) for o in outs],
        scratch_shapes=[
            pltpu.VMEM((count, groups * cols), bf16),
            pltpu.VMEM((4 * count, width), bf16),
            pltpu.VMEM((4 * count, width), bf16),
            pltpu.VMEM((count, width), f32),
            pltpu.VMEM((count, 128), f32),
            pltpu.VMEM((count, width), f32),
            pltpu.VMEM((4 * count, hidden), bf16),
            pltpu.VMEM((4 * count, hidden), bf16),
            pltpu.VMEM((4 * count, hidden), bf16),
            pltpu.VMEM((count, width), f32),
            pltpu.VMEM((count, width), f32),
            two, two, two, two, two, two,
            pltpu.VMEM((count, width), bf16),
            pltpu.VMEM((length, width), bf16),
            pltpu.SemaphoreType.DMA((copies,)),
            pltpu.SemaphoreType.DMA((copies,)),
            pltpu.SemaphoreType.DMA((1,)),
        ],
        compiler_params=pltpu.CompilerParams(
            collective_id=collective_id, has_side_effects=True, vmem_limit_bytes=56 * 1024 * 1024
        ),
        name="middle",
    )(mixed_row, tokens, cotangent, out_weight, gate_weight, up_weight, down_weight, gain)


def reduce_kernel(rows, groups, chunks, span, *refs):
    count = len(chunks)
    ins, part, small, rest = refs[:count], refs[count], refs[count + 1], refs[count + 2 :]
    outs, part_out, small_out, rest = rest[:count], rest[count], rest[count + 1], rest[count + 2 :]
    got_core, rest = rest[:count], rest[count:]
    sum_core, rest = rest[:count], rest[count:]
    got_y, rest = rest[:count], rest[count:]
    sum_y, rest = rest[:count], rest[count:]
    got_row, rest = rest[:count], rest[count:]
    part_got, part_sum, small_got, small_sum, send_sem, recv_sem = rest
    row, group, feat = lax.axis_index("row"), lax.axis_index("group"), lax.axis_index("feat")
    core, y = lax.rem(feat, 2), feat // 2
    core_mate = {"feat": feat + 1 - 2 * core}
    y_mate = {"feat": feat + 2 - 4 * y}
    row_mates = [{"row": lax.rem(row + o, rows)} for o in range(1, rows)]
    group_mates = [{"group": lax.rem(group + o, groups)} for o in range(1, groups)]
    started = []

    def send(src, dst, peer):
        i = len(started)
        copy = pltpu.make_async_remote_copy(
            src_ref=src, dst_ref=dst, send_sem=send_sem.at[i], recv_sem=recv_sem.at[i], device_id=peer, device_id_type=MESH
        )
        copy.start()
        started.append(copy)
        return copy

    def at(start, size):
        return pl.ds(pl.multiple_of(start, 16), size)

    def add(a, b):
        return (a.astype(f32) + b.astype(f32)).astype(bf16)

    greet([core_mate, y_mate] + row_mates + group_mates)
    halves = [shape[0] // 2 for shape in chunks]
    quarters = [shape[0] // 4 for shape in chunks]
    units = [shape[0] // (4 * rows) for shape in chunks]

    by_core = [send(ins[i].at[at((1 - core) * halves[i], halves[i])], got_core[i], core_mate) for i in range(count)]
    small_copy = send(small, small_got.at[0], core_mate)
    blocks = []
    for o in range(1, groups):
        blocks.append(send(part.at[lax.rem(group + o, groups)], part_got.at[o - 1], group_mates[o - 1]))
    by_y = []
    for i in range(count):
        by_core[i].wait_recv()
        sum_core[i][...] = add(ins[i][at(core * halves[i], halves[i])], got_core[i][...])
        by_y.append(send(sum_core[i].at[at((1 - y) * quarters[i], quarters[i])], got_y[i], y_mate))
    small_copy.wait_recv()
    small_sum[0] = small[...] + small_got[0]
    small_copy = send(small_sum.at[0], small_got.at[1], y_mate)
    total = part[group].astype(f32)
    for o in range(1, groups):
        blocks[o - 1].wait_recv()
        total = total + part_got[o - 1].astype(f32)
    part_sum[...] = total.astype(bf16)
    home = []
    for o in range(1, rows):
        home.append(send(part_sum.at[at(lax.rem(row + o, rows) * span, span)], part_out.at[at(row * span, span)], row_mates[o - 1]))
    part_out[at(row * span, span)] = part_sum[at(row * span, span)]
    by_row = []
    for i in range(count):
        by_y[i].wait_recv()
        sum_y[i][...] = add(sum_core[i][at(y * quarters[i], quarters[i])], got_y[i][...])
        by_row.append(
            [
                send(sum_y[i].at[at(lax.rem(row + o, rows) * units[i], units[i])], got_row[i].at[o - 1], row_mates[o - 1])
                for o in range(1, rows)
            ]
        )
    small_copy.wait_recv()
    small_sum[1] = small_sum[0] + small_got[1]
    small_copies = [send(small_sum.at[1], small_got.at[2 + row], row_mates[o - 1]) for o in range(1, rows)]
    small_got[2 + row] = small_sum[1]

    place = (core * 2 + y) * rows + row
    back_row = []
    for i in range(count):
        total = sum_y[i][at(row * units[i], units[i])].astype(f32)
        for o in range(1, rows):
            by_row[i][o - 1].wait_recv()
            total = total + got_row[i][o - 1].astype(f32)
        here = outs[i].at[group, at(place * units[i], units[i])]
        here[...] = total.astype(bf16)
        back_row.append([send(here, here, row_mates[o - 1]) for o in range(1, rows)])
    for copy in small_copies:
        copy.wait_recv()
    small_total = small_got[2]
    for r in range(1, rows):
        small_total = small_total + small_got[2 + r]
    small_out[group] = small_total
    small_copies = [send(small_out.at[group], small_out.at[group], mate) for mate in group_mates]
    first = []
    for i in range(count):
        for copy in back_row[i]:
            copy.wait_recv()
        here = outs[i].at[group, at((core * 2 + y) * quarters[i], quarters[i])]
        if i % 2 == 0:
            first.append([send(here, here, mate) for mate in group_mates])
        else:
            first.append([send(here, here, y_mate)])
    second = []
    for i in range(count):
        for copy in first[i]:
            copy.wait_recv()
        if i % 2 == 0:
            here = outs[i].at[:, at((core * 2 + y) * quarters[i], quarters[i])]
            second.append([send(here, here, y_mate)])
        else:
            here = outs[i].at[group, at(core * halves[i], halves[i])]
            second.append([send(here, here, mate) for mate in group_mates])
    third = []
    for i in range(count):
        for copy in second[i]:
            copy.wait_recv()
        here = outs[i].at[:, at(core * halves[i], halves[i])]
        third.append(send(here, here, core_mate))
    for copy in third + home + small_copies:
        copy.wait_recv()
    for copy in started:
        copy.wait_send()


def reduce_all(arrays, part, small, rows, groups, collective_id):
    chunks = [a.shape for a in arrays]
    count = len(chunks)
    span = part.shape[1] // rows
    copies = count * (2 + 2 * (rows - 1) + (groups - 1) + 2) + (groups - 1) + (rows - 1) + 2 + (rows - 1) + (groups - 1)
    vmem = pl.BlockSpec(memory_space=pltpu.VMEM)
    scratch = [pltpu.VMEM((h // 2, w), bf16) for h, w in chunks] * 2
    scratch += [pltpu.VMEM((h // 4, w), bf16) for h, w in chunks] * 2
    scratch += [pltpu.VMEM((rows - 1, h // (4 * rows), w), bf16) for h, w in chunks]
    scratch += [
        pltpu.VMEM((groups - 1,) + part.shape[1:], bf16),
        pltpu.VMEM(part.shape[1:], bf16),
        pltpu.VMEM((2 + rows,) + small.shape, f32),
        pltpu.VMEM((2,) + small.shape, f32),
        pltpu.SemaphoreType.DMA((copies,)),
        pltpu.SemaphoreType.DMA((copies,)),
    ]
    return pl.pallas_call(
        partial(reduce_kernel, rows, groups, chunks, span),
        in_specs=[vmem] * (count + 2),
        out_specs=[vmem] * (count + 2),
        out_shape=[jax.ShapeDtypeStruct((groups, h, w), bf16) for h, w in chunks]
        + [jax.ShapeDtypeStruct(part.shape[1:], bf16), jax.ShapeDtypeStruct((groups,) + small.shape, f32)],
        scratch_shapes=scratch,
        compiler_params=pltpu.CompilerParams(
            collective_id=collective_id, has_side_effects=True, vmem_limit_bytes=48 * 1024 * 1024
        ),
        name="reduce_all",
    )(*arrays, part, small)


def normalize(vector, gain):
    centered = vector - jnp.mean(vector, -1, keepdims=True)
    variance = jnp.mean(centered * centered, -1, keepdims=True)
    inv_scale = lax.rsqrt(variance + epsilon)
    normed_unit = centered * inv_scale
    return (normed_unit * gain, normed_unit, inv_scale)


def norm_back(grad_out, gain, normed_unit, inv_scale):
    scaled = grad_out * gain
    return inv_scale * (
        scaled
        - jnp.mean(scaled, -1, keepdims=True)
        - normed_unit * jnp.mean(scaled * normed_unit, -1, keepdims=True)
    )


SEQ = ("row", "group")


def per_device(
    tokens,
    cotangent,
    doc_starts,
    mixer_gain,
    query_weight,
    key_weight,
    value_weight,
    out_weight,
    rate_weight,
    rate_bias,
    first_init,
    first_bias_init,
    second_init,
    second_bias_init,
    inner_gain,
    inner_bias,
    feed_gain,
    gate_weight,
    up_weight,
    down_weight,
):
    rows, span, width = tokens.shape
    heads, head_dim, inner = first_init.shape
    groups = lax.axis_size("group")
    feats = lax.axis_size("feat")
    row, group = lax.axis_index("row"), lax.axis_index("group")
    count = rows * span
    length = span * rows * groups
    blocks = length // MB
    pairs = -(-heads // (2 * groups))
    mine = 2 * pairs
    pair = 2 * head_dim
    cols = mine * head_dim
    spare = mine * groups - heads

    def own_heads(array, axis, per_head=1):
        if spare:
            pad = [(0, 0)] * array.ndim
            pad[axis] = (0, spare * per_head)
            array = jnp.pad(array, pad)
        return lax.dynamic_slice_in_dim(array, group * mine * per_head, mine * per_head, axis)

    def to_rows(array):
        got = lax.all_to_all(jnp.repeat(array, groups, 0), SEQ, 0, 0, tiled=True)
        return got.reshape(length, array.shape[-1])

    row_in = to_rows(tokens).astype(f32)
    act_row = low(normalize(row_in, mixer_gain)[0])
    w_q, w_k, w_v = (own_heads(w, 1, head_dim) for w in (query_weight, key_weight, value_weight))
    w_r = own_heads(rate_weight, 1)
    queries, keys, values = (dot(act_row, w) for w in (w_q, w_k, w_v))
    logits = dot(act_row, w_r) + own_heads(rate_bias, 0)
    sigma = jax.nn.sigmoid(logits)
    rates = sigma / head_dim
    e = jnp.broadcast_to(
        rates.reshape(blocks, MB, pairs, 2).transpose(0, 2, 3, 1).reshape(blocks, pairs, 2 * MB, 1),
        (blocks, pairs, 2 * MB, pair),
    )
    block_ids = jnp.arange(blocks, dtype=jnp.int32)
    starts = lax.dynamic_index_in_dim(doc_starts, row, 0, False)
    restarts = ((block_ids == 0) | jnp.any(starts[:, None] == block_ids[None], 0)).astype(jnp.int32)
    pack = lambda a: own_heads(a, 0).reshape(pairs, pair, inner)
    start_first = pack(first_init)
    start_second = pack(second_init - jnp.mean(second_init, 1, keepdims=True))
    start_first_bias = jnp.repeat(own_heads(first_bias_init, 0).reshape(pairs, 2, 1, inner), MB, 2).reshape(
        pairs, 2 * MB, inner
    )
    centered = own_heads(second_bias_init - jnp.mean(second_bias_init, 1, keepdims=True), 0)
    start_second_bias = (
        jnp.eye(2, dtype=f32)[None, :, None, :, None] * centered.reshape(pairs, 1, 1, 2, head_dim)
    ) * jnp.ones((1, 1, MB, 1, 1), f32)
    start_second_bias = start_second_bias.reshape(pairs, 2 * MB, pair)
    gain, bias = own_heads(inner_gain, 0).reshape(1, cols), own_heads(inner_bias, 0).reshape(1, cols)
    *saved, mixed = forward_inner(
        jnp.concatenate([restarts, jnp.zeros((1,), jnp.int32)]),
        queries, keys, values, e, start_first, start_first_bias, start_second, start_second_bias, gain, bias,
    )
    mixed_row = low(mixed[MB:])

    flat_in = tokens.astype(f32).reshape(count, width)
    all_heads = jnp.pad(out_weight, ((0, spare * head_dim), (0, 0))) if spare else out_weight
    block_out, grad_hidden, grad_mixed, grad_out_rows, *feed_terms, grad_feed_gain = middle(
        mixed_row, tokens.reshape(count, width), cotangent.reshape(count, width), all_heads,
        gate_weight, up_weight, down_weight, feed_gain.reshape(1, width), span, 1,
    )

    grad_q, grad_k, grad_v, grad_e, g_first, g_first_bias, g_second, g_second_bias, g_gain, g_bias, *feed_grads = (
        backward_inner(restarts, queries, keys, values, grad_mixed, e, saved, gain, bias, feed_terms, 2)
    )
    grad_q, grad_k, grad_v = grad_q[:length], grad_k[:length], grad_v[:length]
    grad_rates = grad_e[:blocks, :, :, 0].reshape(blocks, pairs, 2, MB).transpose(0, 3, 1, 2).reshape(length, mine)
    grad_logits = low(grad_rates * sigma * (1.0 - sigma) / head_dim)
    part = dot_nt(grad_q, w_q) + dot_nt(grad_k, w_k) + dot_nt(grad_v, w_v) + dot_nt(grad_logits, w_r)
    _, unit_row, _ = normalize(row_in, mixer_gain)
    blocks_out = low(part).reshape(rows, groups, span, width).transpose(1, 0, 2, 3).reshape(groups, count, width)
    arrays = (
        jnp.concatenate([low(dot_tn(act_row, grad_q)), low(dot_tn(act_row, grad_k))], 1),
        jnp.concatenate([low(dot_tn(act_row, grad_v)), grad_out_rows], 1),
        jnp.concatenate([low(g_first.reshape(cols, inner)), low(g_second.reshape(cols, inner))], 0),
    )
    per_head = jnp.concatenate(
        [
            g_first_bias.reshape(mine, MB, inner)[:, 0],
            jnp.stack([g_second_bias[:, h * MB, h * head_dim : (h + 1) * head_dim] for h in range(2)], 1).reshape(
                mine, head_dim
            ),
            jnp.sum(g_gain, 0).reshape(mine, head_dim),
            jnp.sum(g_bias, 0).reshape(mine, head_dim),
            dot_tn(grad_logits, act_row),
            jnp.sum(grad_logits.astype(f32), 0)[:, None],
            jnp.sum(logits, 0)[:, None],
        ],
        1,
    )
    used = (group * mine + jnp.arange(mine)) < heads
    peers = rows * feats
    top = jnp.max(jnp.where(used[None], logits, jnp.finfo(f32).min))
    tops = jnp.where(jnp.arange(peers) == row * feats + lax.axis_index("feat"), top, 0.0)
    pieces = [per_head.reshape(-1), jnp.sum(part * unit_row, 0), grad_feed_gain.reshape(-1), tops]
    sizes = [p.shape[0] for p in pieces]
    size = sum(sizes)
    lines = -(-size // 1024) * 8
    small = jnp.pad(jnp.concatenate(pieces), (0, lines * 128 - size)).reshape(lines, 128)
    *arrays, got, small = reduce_all(arrays, blocks_out, small, rows, groups, 3)

    grad_act_one = got.astype(f32)
    _, unit_one, scale_one = normalize(flat_in, mixer_gain)
    input_grad = grad_hidden + norm_back(grad_act_one, mixer_gain, unit_one, scale_one)

    def gathered(array, part_no):
        cut = slice(part_no * cols, (part_no + 1) * cols)
        return jnp.concatenate([array[g, :, cut] for g in range(groups)], 1)[:, :width].astype(f32)

    g_query, g_key = (gathered(arrays[0], i) for i in range(2))
    g_value, g_out = gathered(arrays[1], 0), gathered(arrays[1], 1).T
    states = arrays[2].astype(f32).reshape(groups, 2, cols, inner)
    g_first, g_second = (
        states[:, i].reshape(groups * mine, head_dim, inner)[:heads] for i in range(2)
    )
    g_second = g_second - jnp.mean(g_second, 1, keepdims=True)
    small = small.reshape(groups, lines * 128)
    ends = [0]
    for s in sizes:
        ends.append(ends[-1] + s)
    slots = small[:, : ends[1]].reshape(groups * mine, -1)[:heads]
    g_mixer, g_feed = jnp.sum(small[:, ends[1] : ends[2]], 0), jnp.sum(small[:, ends[2] : ends[3]], 0)
    at = [0, inner, inner + head_dim, inner + 2 * head_dim, inner + 3 * head_dim, inner + 3 * head_dim + width]
    g_second_bias = slots[:, at[1] : at[2]]
    g_second_bias = g_second_bias - jnp.mean(g_second_bias, 1, keepdims=True)
    total = jnp.sum(slots[:, at[5] + 1])
    stats = jnp.stack([total / (rows * groups * feats * count * heads), jnp.max(small[:, ends[3] : ends[4]])])
    return (
        block_out.reshape(rows, span, width),
        input_grad.reshape(rows, span, width),
        g_mixer,
        g_query,
        g_key,
        g_value,
        g_out,
        slots[:, at[4] : at[5]].T,
        slots[:, at[5]],
        g_first,
        slots[:, : at[1]],
        g_second,
        g_second_bias,
        slots[:, at[2] : at[3]],
        slots[:, at[3] : at[4]],
        g_feed,
        jnp.concatenate(jnp.split(feed_grads[0], 2, 0), 1).astype(f32),
        jnp.concatenate(jnp.split(feed_grads[1], 2, 0), 1).astype(f32),
        jnp.concatenate(jnp.split(feed_grads[2], 2, 0), 1).astype(f32),
        stats,
    )


def solution(mesh):
    feats = mesh.shape["feat"]

    def run(*arrays):
        rows = arrays[0].shape[0] // feats
        grid = jax.sharding.Mesh(mesh.devices.reshape(rows, -1, feats), ("row", "group", "feat"))
        by_token = P("feat", SEQ, None)
        by_hidden = P(None, "feat")
        return jax.shard_map(
            per_device,
            mesh=grid,
            in_specs=(by_token, by_token, P("feat", None)) + (P(),) * 14 + (by_hidden,) * 3,
            out_specs=(by_token, by_token) + (P(),) * 14 + (by_hidden,) * 3 + (P(),),
            check_vma=False,
        )(*arrays)

    return run
```

```python
from functools import partial

import jax
import jax.numpy as jnp
from jax import lax
from jax.experimental import pallas as pl
from jax.experimental.pallas import tpu as pltpu
from jax.sharding import PartitionSpec as P

MB = 16
epsilon = 1e-05
f32, bf16 = jnp.float32, jnp.bfloat16


def dot(a, b):
    return lax.dot_general(a, b, (((1,), (0,)), ((), ())), preferred_element_type=f32)


def dot_nt(a, b):
    return lax.dot_general(a, b, (((1,), (1,)), ((), ())), preferred_element_type=f32)


def dot_tn(a, b):
    return lax.dot_general(a, b, (((0,), (0,)), ((), ())), preferred_element_type=f32)


def low(v):
    return v.astype(bf16)


def gelu_parts(z):
    a = jnp.abs(z)
    d = 1.0 + 0.23164189 * a
    t = pl.reciprocal(d, approx=True)
    t = t * (2.0 - d * t)
    ex = jnp.exp(-0.5 * (z * z))
    poly = t * (
        0.127414796 + t * (-0.142248368 + t * (0.7107068705 + t * (-0.7265760135 + t * 0.5307027145)))
    )
    h = poly * ex
    cdf = jnp.where(z >= 0, 1.0 - h, h)
    pdf = 0.3989422804014327 * ex
    return z * cdf, cdf + z * pdf, pdf


def lane_sum(v):
    return jnp.sum(v, -1, keepdims=True)


def masks(head_dim):
    pair = 2 * head_dim
    rows, cols = 2 * MB, pair
    r = lax.broadcasted_iota(jnp.int32, (rows, cols), 0)
    c = lax.broadcasted_iota(jnp.int32, (rows, cols), 1)
    own = ((r < MB) == (c < head_dim)).astype(f32)
    r = lax.broadcasted_iota(jnp.int32, (rows, rows), 0)
    c = lax.broadcasted_iota(jnp.int32, (rows, rows), 1)
    same = (r < MB) == (c < MB)
    causal = (same & (c <= r)).astype(f32)
    return own, causal, same.astype(bf16)


def spread(v, own):
    return jnp.concatenate([v, v], 0) * own


def fold(v):
    return v[:MB] + v[MB:]


def twice(v):
    return jnp.concatenate([v, v], 1)


def in_turn(parts):
    while parts:
        parts = [part for part in parts if next(part, parts) is not parts]


def forward_kernel(pairs, head_dim, restart_ref, q_ref, k_ref, v_ref, e_ref, w1i_ref, b1i_ref, w2i_ref, b2i_ref, gain_ref, bias_ref,
                   big_ref, mid_ref, small_ref, n1_ref, pq_ref, uq_ref, n2_ref, out_ref,
                   w1, b1, w2, b2, s_q1, s_x2, s_e2, s_w2, s_b2, s_q):
    j = pl.program_id(0)
    pair = 2 * head_dim
    inv = 1.0 / head_dim
    own, causal, ones = masks(head_dim)

    @pl.when(restart_ref[j] > 0)
    def _():
        w1[...] = w1i_ref[...]
        b1[...] = b1i_ref[...]
        w2[...] = w2i_ref[...]
        b2[...] = b2i_ref[...]

    loaded = [
        (s_q1[p], s_x2[p], s_e2[p], s_w2[p], s_b2[p], s_q[p], w1[p], w2[p], b1[p], b2[p], e_ref[0, p]) for p in range(pairs)
    ]
    tokens = [[ref[:, p * pair : (p + 1) * pair] for ref in (q_ref, k_ref, v_ref, gain_ref, bias_ref)] for p in range(pairs)]
    writes = []

    def write(ref, index, value):
        writes.append((ref, index, value))

    def outputs_before(p):
        q1p, x2p, e2p, w2p, b2p, qp = loaded[p][:6]
        gain, bias = tokens[p][3:]
        p2, lq, _ = gelu_parts(q1p)
        p2b = low(p2)
        yield
        n2 = causal * (dot_nt(p2b, x2p) + 1.0)
        q2 = dot_nt(p2b, w2p)
        yield
        q2 = q2 * own - dot(low(n2), e2p) + b2p
        yield
        sq = lax.rsqrt(lane_sum(q2 * q2) * inv + epsilon)
        uq = q2 * sq
        write(out_ref, (slice(None), slice(p * pair, (p + 1) * pair)), qp + fold(uq) * gain + bias)
        write(pq_ref, (0, p, slice(0, 2 * MB)), p2b)
        write(pq_ref, (0, p, slice(2 * MB, 4 * MB)), low(lq))
        write(uq_ref, (0, p, slice(0, 2 * MB)), uq)
        write(uq_ref, (0, p, slice(2 * MB, 4 * MB)), jnp.broadcast_to(sq, uq.shape))
        write(n2_ref, (0, p), low(n2))

    def inner_step(p):
        w1c, w2c, b1c, b2c, e = loaded[p][6:]
        qc, kc, vc, gain, bias = tokens[p]
        kb, qb = low(spread(kc, own)), low(spread(qc, own))
        w1b, w2b = low(w1c), low(w2c)
        kq = dot(jnp.concatenate([kb, qb], 0), w1b)
        yield
        z1 = kq[: 2 * MB] + b1c
        x2, l1, pdf = gelu_parts(z1)
        x2b = low(x2)
        yield
        c = dot_nt(x2b, w2b)
        n1 = causal * (dot_nt(qb, kb) + 1.0)
        yield
        c = c * own + b2c
        s = lax.rsqrt(lane_sum(c * c) * inv + epsilon)
        u = c * s
        r = u * (gain * gain) + spread((bias - (vc - kc)) * gain, own)
        yield
        mr, m2 = lane_sum(r) * inv, lane_sum(r * u) * inv
        g2 = s * (r - mr * own - u * m2)
        yield
        h = dot(low(g2), w2b)
        e2b = low(e * g2)
        yield
        g1 = h * l1
        e1b = low(twice(e) * g1)
        yield
        u1 = dot_tn(kb, e1b)
        yield
        q1 = kq[2 * MB :] + b1c - dot(low(n1), e1b)
        yield
        write(w1, p, w1c - u1)
        write(b1, p, b1c - dot(ones, e1b))
        write(w2, p, w2c - dot_tn(e2b, x2b))
        write(b2, p, b2c - dot(ones, e2b))
        write(big_ref, (0, p, slice(0, pair)), w1b)
        write(big_ref, (0, p, slice(pair, 2 * pair)), w2b)
        write(big_ref, (0, p, slice(2 * pair, 2 * pair + 2 * MB)), x2b)
        write(big_ref, (0, p, slice(2 * pair + 2 * MB, 2 * pair + 4 * MB)), e1b)
        write(mid_ref, (0, p, slice(0, 2 * MB)), low(g1))
        write(mid_ref, (0, p, slice(2 * MB, 4 * MB)), low(l1))
        write(mid_ref, (0, p, slice(4 * MB, 6 * MB)), low(h * pdf * (2.0 - z1 * z1)))
        for i, value in enumerate((u, s, r, m2, g2)):
            write(small_ref, (0, p, slice(i * 2 * MB, (i + 1) * 2 * MB)), jnp.broadcast_to(value, u.shape))
        write(n1_ref, (0, p), low(n1))
        for ref, value in ((s_q1, q1), (s_x2, x2b), (s_e2, e2b), (s_w2, w2b), (s_b2, b2c), (s_q, qc)):
            write(ref, p, value)

    in_turn([inner_step(p) for p in range(pairs)] + [outputs_before(p) for p in range(pairs)])
    for ref, index, value in writes:
        ref[index] = value


def forward_inner(restarts, q, k, v, e, w1i, b1i, w2i, b2i, gain, bias):
    blocks, pairs, _, pair = e.shape
    head_dim = pair // 2
    inner = w1i.shape[-1]
    steps = blocks + 1
    last = blocks - 1
    tok = pl.BlockSpec((MB, pairs * pair), lambda j, r: (jnp.minimum(j, last), 0))
    whole = lambda a: pl.BlockSpec(a.shape, lambda j, r: (0,) * a.ndim)

    def per_step(rows, width, dtype):
        return (
            jax.ShapeDtypeStruct((steps, pairs, rows, width), dtype),
            pl.BlockSpec((1, pairs, rows, width), lambda j, r: (j, 0, 0, 0)),
        )

    outs = [
        per_step(2 * pair + 4 * MB, inner, bf16),
        per_step(6 * MB, inner, bf16),
        per_step(10 * MB, pair, f32),
        per_step(2 * MB, 2 * MB, bf16),
        per_step(4 * MB, inner, bf16),
        per_step(4 * MB, pair, f32),
        per_step(2 * MB, 2 * MB, bf16),
        (
            jax.ShapeDtypeStruct((steps * MB, pairs * pair), f32),
            pl.BlockSpec((MB, pairs * pair), lambda j, r: (j, 0)),
        ),
    ]
    return pl.pallas_call(
        partial(forward_kernel, pairs, head_dim),
        grid_spec=pltpu.PrefetchScalarGridSpec(
            num_scalar_prefetch=1,
            grid=(steps,),
            in_specs=[tok, tok, tok, pl.BlockSpec((1, pairs, 2 * MB, pair), lambda j, r: (jnp.minimum(j, last), 0, 0, 0))]
            + [whole(a) for a in (w1i, b1i, w2i, b2i, gain, bias)],
            out_specs=[o[1] for o in outs],
            scratch_shapes=[
                pltpu.VMEM((pairs, pair, inner), f32),
                pltpu.VMEM((pairs, 2 * MB, inner), f32),
                pltpu.VMEM((pairs, pair, inner), f32),
                pltpu.VMEM((pairs, 2 * MB, pair), f32),
                pltpu.VMEM((pairs, 2 * MB, inner), f32),
                pltpu.VMEM((pairs, 2 * MB, inner), bf16),
                pltpu.VMEM((pairs, 2 * MB, pair), bf16),
                pltpu.VMEM((pairs, pair, inner), bf16),
                pltpu.VMEM((pairs, 2 * MB, pair), f32),
                pltpu.VMEM((pairs, MB, pair), f32),
            ],
        ),
        out_shape=[o[0] for o in outs],
        compiler_params=pltpu.CompilerParams(vmem_limit_bytes=48 * 1024 * 1024),
        name="inner_forward",
    )(restarts, q, k, v, e, w1i, b1i, w2i, b2i, gain, bias)


MESH = pl.DeviceIdType.MESH


def greet(peers):
    barrier = pltpu.get_barrier_semaphore()
    for peer in peers:
        pl.semaphore_signal(barrier, inc=1, device_id=peer, device_id_type=MESH)
    pl.semaphore_wait(barrier, len(peers))


class Copies:
    def __init__(self, send_sem, recv_sem):
        self.send_sem, self.recv_sem, self.started = send_sem, recv_sem, []

    def make(self, src, dst, peer):
        i = len(self.started)
        copy = pltpu.make_async_remote_copy(
            src_ref=src, dst_ref=dst, send_sem=self.send_sem.at[i], recv_sem=self.recv_sem.at[i],
            device_id=peer, device_id_type=MESH,
        )
        self.started.append(copy)
        return copy

    def send(self, src, dst, peer):
        copy = self.make(src, dst, peer)
        copy.start()
        return copy


def rows_at(start, size):
    return pl.ds(pl.multiple_of(start, 16), size)


def add_low(a, b):
    return (a.astype(f32) + b.astype(f32)).astype(bf16)


def mates(axis):
    size, here = lax.axis_size(axis), lax.axis_index(axis)
    return [{axis: lax.rem(here + o, size)} for o in range(1, size)]


def feed_sum_steps(ins, outs, got_group, sum_group, got_row, full, copies):
    row, group = lax.axis_index("row"), lax.axis_index("group")
    rows, groups = lax.axis_size("row"), lax.axis_size("group")
    row_mates, group_mates = mates("row"), mates("group")
    stages = []
    for i, src in enumerate(ins):
        part = src.shape[0] // groups
        unit = part // rows
        here = full[i].at[rows_at(row * unit, unit)]
        stages.append(
            [
                [
                    copies.make(src.at[rows_at(lax.rem(group + o, groups) * part, part)], got_group[i].at[o - 1], group_mates[o - 1])
                    for o in range(1, groups)
                ],
                [
                    copies.make(sum_group[i].at[rows_at(lax.rem(row + o, rows) * unit, unit)], got_row[i].at[o - 1], row_mates[o - 1])
                    for o in range(1, rows)
                ],
                [copies.make(here, here, mate) for mate in row_mates],
            ]
        )

    def begin():
        greet(row_mates + group_mates)
        for i in range(len(ins)):
            for copy in stages[i][0]:
                copy.start()

    def after(i, s):
        part = ins[i].shape[0] // groups
        unit = part // rows
        for copy in stages[i][s]:
            copy.wait_recv()
        if s == 0:
            total = ins[i][rows_at(group * part, part)].astype(f32)
            for o in range(1, groups):
                total = total + got_group[i][o - 1].astype(f32)
            sum_group[i][...] = low(total)
        if s == 1:
            total = sum_group[i][rows_at(row * unit, unit)].astype(f32)
            for o in range(1, rows):
                total = total + got_row[i][o - 1].astype(f32)
            full[i][rows_at(row * unit, unit)] = low(total)
        if s < 2:
            for copy in stages[i][s + 1]:
                copy.start()
        else:
            outs[i][...] = full[i][...]
            for copy in sum(stages[i], []):
                copy.wait_send()

    return begin, after


def backward_kernel(pairs, head_dim, feeds, stage_steps, restart_ref,
                    qq_ref, kq_ref, doq_ref, eq_ref, bigq_ref, g2q_ref, n1_ref, pqq_ref, uqq_ref, n2_ref,
                    q_ref, k_ref, v_ref, do_ref, e_ref, big_ref, mid_ref, small_ref, pq_ref, uq_ref, gain_ref, bias_ref, *refs):
    j = pl.program_id(0)
    steps = pl.num_programs(0)
    pair = 2 * head_dim
    inv = 1.0 / head_dim
    own, causal, ones = masks(head_dim)
    feed_in, refs = refs[:feeds], refs[feeds:]
    dq_ref, dk_ref, dv_ref, de_ref, gw1, gb1, gw2, gb2, ggain, gbias = refs[:10]
    feed_out, refs = refs[10 : 10 + feeds], refs[10 + feeds :]
    w1, b1, w2, b2, s_e1, s_e2, s_k, s_x2, s_q1, s_q2, s_q = refs[:11]
    buffers = [refs[11 + i * feeds : 11 + (i + 1) * feeds] for i in range(4)]
    if feeds:
        begin, after = feed_sum_steps(feed_in, feed_out, *buffers, Copies(*refs[-2:]))
        pl.when(j == 0)(begin)
        for (i, s), at in stage_steps.items():
            pl.when(j == at)(partial(after, i, s))

    @pl.when(j <= 1)
    def _():
        for ref in (w1, b1, w2, b2, gw1, gb1, gw2, gb2, ggain, gbias):
            ref[...] = jnp.zeros_like(ref)

    rows2 = 2 * MB
    piece = lambda ref, p, i: ref[0, p, i * rows2 : (i + 1) * rows2]
    token = lambda ref, p: ref[:, p * pair : (p + 1) * pair]
    first = restart_ref[jnp.minimum(steps - 1 - j, steps - 2)]
    go_on = 1.0 - first
    writes = []

    def write(ref, index, value):
        writes.append((ref, index, value))

    def load_outputs(p):
        return (
            [token(ref, p) for ref in (qq_ref, kq_ref, doq_ref, gain_ref)]
            + [bigq_ref[0, p, 0:pair], bigq_ref[0, p, pair : 2 * pair]]
            + [bigq_ref[0, p, 2 * pair : 2 * pair + rows2], bigq_ref[0, p, 2 * pair + rows2 : 2 * pair + 2 * rows2]]
            + [eq_ref[0, p], g2q_ref[0, p], n1_ref[0, p], n2_ref[0, p]]
            + [piece(ref, p, i) for ref in (pqq_ref, uqq_ref) for i in range(2)]
        )

    def load_step(p):
        return (
            [ref[p] for ref in (s_e1, s_e2, s_k, s_x2, s_q1, s_q2, s_q, w1, w2, b1, b2)]
            + [token(ref, p) for ref in (q_ref, k_ref, v_ref, do_ref, gain_ref, bias_ref)]
            + [big_ref[0, p, 0:pair], big_ref[0, p, pair : 2 * pair]]
            + [big_ref[0, p, 2 * pair : 2 * pair + rows2], big_ref[0, p, 2 * pair + rows2 : 2 * pair + 2 * rows2]]
            + [piece(mid_ref, p, i).astype(f32) for i in range(3)]
            + [piece(small_ref, p, i) for i in range(5)]
            + [pq_ref[0, p], uq_ref[0, p], e_ref[0, p]]
        )

    def outputs_ahead(p, loaded):
        qc, kc, do, gain, w1b, w2b, x2b, e1b, e, g2, n1b, n2b, p2b, lq, uq, sq = loaded
        qb, kb = low(spread(qc, own)), low(spread(kc, own))
        e2b = low(e * g2)
        w = spread(do * gain, own)
        dq2 = low(sq * (w - (lane_sum(w) * inv) * own - uq * (lane_sum(w * uq) * inv)))
        yield
        dn2 = dot_nt(dq2, e2b)
        dp2 = dot(dq2, w2b)
        yield
        dpx = low(-causal * dn2)
        new_e2 = dot_tn(n2b, dq2)
        dp2 = dp2 + dot(dpx, x2b)
        yield
        dq1 = low(dp2 * lq.astype(f32))
        new_x2 = dot_tn(dpx, p2b)
        yield
        dn1 = dot_nt(dq1, e1b)
        new_q = dot_nt(dq1, w1b)
        yield
        new_e1 = dot_tn(n1b, dq1)
        dqk = low(-causal * dn1)
        yield
        new_k = dot_tn(dqk, qb)
        new_q = do + fold((new_q + dot(dqk, kb)) * own)
        for ref, value in zip((s_e1, s_e2, s_k, s_x2, s_q1, s_q2, s_q), (new_e1, new_e2, new_k, new_x2, dq1, dq2, new_q)):
            write(ref, p, value)

    def step_back(p, loaded):
        e1q, e2q, dkq, x2q, dq1, dq2, dqc, dw1, dw2, db1, db2, qc, kc, vc, do, gain, bias, w1b, w2b, x2b, e1b = loaded[:21]
        g1, l1, hg, u, s, r, m2, g2, p2b, uq, e = loaded[21:]
        cols = (slice(None), slice(p * pair, (p + 1) * pair))
        dw1b, dw2b = low(dw1), low(dw2)
        qb, kb = low(spread(qc, own)), low(spread(kc, own))
        e2b = low(e * g2)
        de1 = dot(kb, dw1b)
        de2 = dot_nt(x2b, dw2b)
        yield
        de1 = -(e1q + de1 + db1)
        de2 = -(e2q + de2 * own + db2)
        dg1 = twice(e) * de1
        dh = low(dg1 * l1)
        yield
        dg2 = dot_nt(dh, w2b)
        dx2 = x2q - dot(e2b, dw2b)
        yield
        dg2 = e * de2 + dg2 * own
        dk = dkq - dot_nt(e1b, dw1b) * own
        ma, mg = lane_sum(dg2 * u) * inv, lane_sum(dg2) * inv
        write(de_ref, (0, p), jnp.broadcast_to(lane_sum(g1 * de1) + lane_sum(g2 * de2), u.shape))
        yield
        dr = s * (dg2 - mg * own - u * ma)
        du = dr * (gain * gain) - s * (dg2 * m2 + r * ma)
        yield
        md, mu = lane_sum(du) * inv, lane_sum(du * u + dg2 * g2) * inv
        dz2 = low(s * (du - md * own - u * mu))
        yield
        dx2 = dx2 + dot(dz2, w2b)
        yield
        dz1 = low(dg1 * hg + dx2 * l1)
        drg = fold(dr) * gain
        write(dq_ref, cols, low(dqc))
        write(dv_ref, cols, low(-drg))
        more_gain = fold(spread_by(do, uq)) + fold(dr * u) * (2.0 * gain) + fold(dr) * (bias - (vc - kc))
        yield
        ndw1 = dw1 + dot_tn(jnp.concatenate([qb, kb], 0), jnp.concatenate([dq1, dz1], 0))
        yield
        dk = dk + dot_nt(dz1, w1b) * own
        write(dk_ref, cols, low(fold(dk) + drg))
        ndw2 = dw2 + dot_tn(jnp.concatenate([dq2, low(g2), dz2], 0), jnp.concatenate([p2b, dh, x2b], 0))
        ndb1 = db1 + dot(ones, dq1) + dot(ones, dz1)
        ndb2 = db2 + dot(ones, dq2) + dot(ones, dz2)
        for ref, value in ((w1, ndw1), (w2, ndw2), (b1, ndb1), (b2, ndb2)):
            write(ref, p, value * go_on)
        more.append((cols, more_gain, do + drg))
        starts.append((p, ndw1, ndw2, ndb1, ndb2))

    more, starts = [], []
    ahead_in = [load_outputs(p) for p in range(pairs)]
    step_in = [load_step(p) for p in range(pairs)]
    in_turn([step_back(p, step_in[p]) for p in range(pairs)] + [outputs_ahead(p, ahead_in[p]) for p in range(pairs)])
    for ref, index, value in writes:
        ref[index] = value
    for cols, more_gain, more_bias in more:
        ggain[cols] += more_gain
        gbias[cols] += more_bias
    for p, *values in starts:
        for ref, value in zip((gw1, gw2, gb1, gb2), values):
            ref[p] += value * first


def spread_by(do, uq):
    return jnp.concatenate([do, do], 0) * uq


def backward_inner(restarts, q, k, v, do, e, saved, gain, bias, feed_terms, collective_id):
    big, mid, small, n1, pq, uq, n2 = saved
    blocks, pairs, _, pair = e.shape
    head_dim = pair // 2
    inner = big.shape[-1]
    steps = blocks + 1
    now = lambda j: jnp.minimum(blocks - j, blocks - 1)
    ahead = lambda j: jnp.maximum(blocks - 1 - j, 0)
    tok = lambda at: pl.BlockSpec((MB, pairs * pair), lambda j: (at(j), 0))

    def block(a, at, rows=None, part=0):
        shape = (1, pairs, rows or a.shape[2], a.shape[3])
        return pl.BlockSpec(shape, lambda j: (at(j), 0, part, 0))

    whole = lambda a: pl.BlockSpec(a.shape, lambda j: (0,) * a.ndim)
    later = lambda j: ahead(j) + 1
    at_now = lambda j: now(j) + 1
    operands = [
        (q, tok(ahead)), (k, tok(ahead)), (do, tok(ahead)), (e, block(e, ahead)), (big, block(big, ahead)),
        (small, block(small, ahead, 2 * MB, 4)), (n1, block(n1, ahead)), (pq, block(pq, later)), (uq, block(uq, later)),
        (n2, block(n2, later)),
        (q, tok(now)), (k, tok(now)), (v, tok(now)), (do, tok(now)), (e, block(e, now)), (big, block(big, now)),
        (mid, block(mid, now)), (small, block(small, now)), (pq, block(pq, at_now, 2 * MB)), (uq, block(uq, at_now, 2 * MB)),
        (gain, whole(gain)), (bias, whole(bias)),
    ]
    feeds = len(feed_terms)
    vmem = pl.BlockSpec(memory_space=pltpu.VMEM)
    operands += [(a, vmem) for a in feed_terms]
    width = pairs * pair
    tok_out = (jax.ShapeDtypeStruct((steps * MB, width), bf16), pl.BlockSpec((MB, width), lambda j: (blocks - j, 0)))
    state = [((pairs, pair, inner), f32), ((pairs, 2 * MB, inner), f32), ((pairs, pair, inner), f32), ((pairs, 2 * MB, pair), f32)]
    keep = lambda shape: (jax.ShapeDtypeStruct(shape, f32), pl.BlockSpec(shape, lambda j: (0,) * len(shape)))
    outs = [tok_out] * 3 + [
        (jax.ShapeDtypeStruct((steps, pairs, 2 * MB, pair), f32), pl.BlockSpec((1, pairs, 2 * MB, pair), lambda j: (blocks - j, 0, 0, 0)))
    ] + [keep(shape) for shape, _ in state] + [keep((MB, width))] * 2 + [
        (jax.ShapeDtypeStruct((a.shape[0] // lax.axis_size("group"), a.shape[1]), bf16), vmem) for a in feed_terms
    ]
    stage_steps = {(i, s): at * blocks // 32 for s, steps_of in enumerate(((6, 11, 16), (13, 19, 25), (21, 28, 32))) for i, at in enumerate(steps_of[:feeds])}
    comm = []
    if feeds:
        groups, rows = lax.axis_size("group"), lax.axis_size("row")
        comm = [pltpu.VMEM((groups - 1, a.shape[0] // groups, a.shape[1]), bf16) for a in feed_terms]
        comm += [pltpu.VMEM((a.shape[0] // groups, a.shape[1]), bf16) for a in feed_terms]
        comm += [pltpu.VMEM((rows - 1, a.shape[0] // (groups * rows), a.shape[1]), bf16) for a in feed_terms]
        comm += [pltpu.VMEM((a.shape[0] // groups, a.shape[1]), bf16) for a in feed_terms]
        comm += [pltpu.SemaphoreType.DMA((feeds * (groups + 2 * rows - 3),))] * 2
    return pl.pallas_call(
        partial(backward_kernel, pairs, head_dim, feeds, stage_steps),
        grid_spec=pltpu.PrefetchScalarGridSpec(
            num_scalar_prefetch=0,
            grid=(steps,),
            in_specs=[pl.BlockSpec(memory_space=pltpu.SMEM)] + [o[1] for o in operands],
            out_specs=[o[1] for o in outs],
            scratch_shapes=[pltpu.VMEM(shape, kind) for shape, kind in state] + [
                pltpu.VMEM((pairs, 2 * MB, inner), f32),
                pltpu.VMEM((pairs, 2 * MB, pair), f32),
                pltpu.VMEM((pairs, 2 * MB, pair), f32),
                pltpu.VMEM((pairs, 2 * MB, inner), f32),
                pltpu.VMEM((pairs, 2 * MB, inner), bf16),
                pltpu.VMEM((pairs, 2 * MB, pair), bf16),
                pltpu.VMEM((pairs, MB, pair), f32),
            ] + comm,
        ),
        out_shape=[o[0] for o in outs],
        compiler_params=pltpu.CompilerParams(
            collective_id=collective_id if feeds else None, has_side_effects=bool(feeds), vmem_limit_bytes=56 * 1024 * 1024
        ),
        name="inner_backward",
    )(restarts.astype(f32), *[o[0] for o in operands])


def norm_parts(v, width):
    centered = v - jnp.sum(v, -1, keepdims=True) * (1.0 / width)
    scale = lax.rsqrt(jnp.sum(centered * centered, -1, keepdims=True) * (1.0 / width) + epsilon)
    return centered * scale, scale


def middle_kernel(span, mixed_ref, tok_ref, cot_ref, wout_ref, gate_ref, up_ref, down_ref, gain_ref,
                  block_ref, hid_ref, gmix_ref, gwo_ref, tgate_ref, tup_ref, tdown_ref, gfeed_ref,
                  mixed_got, acts, cots, unit, scales, h_in, gg, gu, ha, pg0, po0, out_core, in_core, out_diag, in_diag, out_y, in_y,
                  branch, branch_row, send_sem, recv_sem, local_sem):
    rows, groups = lax.axis_size("row"), lax.axis_size("group")
    row, group, feat = lax.axis_index("row"), lax.axis_index("group"), lax.axis_index("feat")
    count, width = tok_ref.shape
    cols = mixed_ref.shape[1]
    core, y = lax.rem(feat, 2), feat // 2
    core_mate, y_mate = {"feat": feat + 1 - 2 * core}, {"feat": feat + 2 - 4 * y}
    here = row * groups + group
    places = rows * groups
    others = [lax.rem(here + o, places) for o in range(1, places)]
    seq_mates = [{"row": t // groups, "group": lax.rem(t, groups)} for t in others]
    copies = Copies(send_sem, recv_sem)
    send = copies.send
    slot = lambda ref, s: ref.at[s * count : (s + 1) * count]

    greet([core_mate, y_mate] + seq_mates)
    lanes = pl.ds(pl.multiple_of(group * cols, 128), cols)
    moves = [
        send(mixed_ref.at[rows_at(t * span, span)], mixed_got.at[rows_at(row * span, span), lanes], mate)
        for t, mate in zip(others, seq_mates)
    ]
    own = pltpu.make_async_copy(
        mixed_ref.at[rows_at(here * span, span)], mixed_got.at[rows_at(row * span, span), lanes], local_sem.at[0]
    )
    own.start()
    cot_core = send(cot_ref, slot(cots, 1), core_mate)
    cot_y = send(cot_ref, slot(cots, 2), y_mate)
    cots[0:count] = cot_ref[...]
    own.wait()
    for copy in moves:
        copy.wait_recv()
    hidden = tok_ref[...].astype(f32) + dot(mixed_got[:, :width], wout_ref[:width])
    h_in[...] = hidden
    unit_two, scale_two = norm_parts(hidden, width)
    unit[...] = unit_two
    scales[...] = jnp.broadcast_to(scale_two, scales.shape)
    acts[0:count] = low(unit_two * gain_ref[...])
    act_core = send(slot(acts, 0), slot(acts, 1), core_mate)
    act_y = send(slot(acts, 0), slot(acts, 2), y_mate)
    cot_y.wait_recv()
    cot_diag = send(slot(cots, 2), slot(cots, 3), core_mate)

    def feed(s):
        part = slice(s * count, (s + 1) * count)
        gate_pre, up_value = dot(acts[part], gate_ref[...]), dot(acts[part], up_ref[...])
        grad = dot(cots[part], down_ref[...])
        sig = jax.nn.sigmoid(gate_pre)
        silu = gate_pre * sig
        ha[part] = low(silu * up_value)
        gg[part] = low(grad * up_value * sig * (1.0 + gate_pre * (1.0 - sig)))
        gu[part] = low(grad * silu)
        back = dot_nt(gg[part], gate_ref[...]) + dot_nt(gu[part], up_ref[...])
        return back, dot_nt(ha[part], down_ref[...])

    pg0[...], po0[...] = feed(0)
    act_core.wait_recv()
    cot_core.wait_recv()
    back, forth = feed(1)
    out_core[0], out_core[1] = low(back), low(forth)
    core_sums = [send(out_core.at[i], in_core.at[i], core_mate) for i in range(2)]
    act_y.wait_recv()
    act_diag = send(slot(acts, 2), slot(acts, 3), core_mate)
    act_diag.wait_recv()
    cot_diag.wait_recv()
    back, forth = feed(3)
    out_diag[0], out_diag[1] = low(back), low(forth)
    diag_sums = [send(out_diag.at[i], in_diag.at[i], core_mate) for i in range(2)]
    back, forth = feed(2)
    y_sums = []
    for i, value in enumerate((back, forth)):
        diag_sums[i].wait_recv()
        out_y[i] = low(value + in_diag[i].astype(f32))
        y_sums.append(send(out_y.at[i], in_y.at[i], y_mate))
    half = gg.shape[1] // 2
    for out, left, right in ((tgate_ref, acts, gg), (tup_ref, acts, gu), (tdown_ref, cots, ha)):
        for h in range(2):
            out[h * width : (h + 1) * width] = low(dot_tn(left[...], right[:, h * half : (h + 1) * half]))
    core_sums[0].wait_recv()
    y_sums[0].wait_recv()
    grad_act = pg0[...] + in_core[0].astype(f32) + in_y[0].astype(f32)
    unit_two = unit[...]
    gfeed_ref[...] = jnp.sum(grad_act * unit_two, 0, keepdims=True)
    w = grad_act * gain_ref[...]
    inv = 1.0 / width
    grad = cot_ref[...].astype(f32) + scales[:, 0:1] * (
        w - jnp.sum(w, -1, keepdims=True) * inv - unit_two * (jnp.sum(w * unit_two, -1, keepdims=True) * inv)
    )
    hid_ref[...] = grad
    branch[...] = low(grad)
    moves = [
        send(branch.at[rows_at((t // groups) * span, span)], branch_row.at[rows_at(here * span, span)], mate)
        for t, mate in zip(others, seq_mates)
    ]
    branch_row[rows_at(here * span, span)] = branch[rows_at(row * span, span)]
    core_sums[1].wait_recv()
    y_sums[1].wait_recv()
    block_ref[...] = low(h_in[...] + po0[...] + in_core[1].astype(f32) + in_y[1].astype(f32))
    for copy in moves:
        copy.wait_recv()
    gmix_ref[...] = dot_nt(branch_row[...], wout_ref[rows_at(group * cols, cols)])
    gwo_ref[...] = low(dot_tn(branch_row[...], mixed_ref[...]))
    for copy in copies.started:
        copy.wait_send()


def middle(mixed_row, tokens, cotangent, out_weight, gate_weight, up_weight, down_weight, gain, span, collective_id):
    rows, groups = lax.axis_size("row"), lax.axis_size("group")
    length, cols = mixed_row.shape
    count, width = tokens.shape
    hidden = gate_weight.shape[1]
    copies = 2 * (rows * groups - 1) + 12
    vmem = pl.BlockSpec(memory_space=pltpu.VMEM)
    outs = [
        ((count, width), bf16), ((count, width), f32), ((length, cols), f32), ((width, cols), bf16),
        ((2 * width, hidden // 2), bf16), ((2 * width, hidden // 2), bf16), ((2 * width, hidden // 2), bf16), ((1, width), f32),
    ]
    two = pltpu.VMEM((2, count, width), bf16)
    return pl.pallas_call(
        partial(middle_kernel, span),
        in_specs=[vmem] * 8,
        out_specs=[vmem] * len(outs),
        out_shape=[jax.ShapeDtypeStruct(*o) for o in outs],
        scratch_shapes=[
            pltpu.VMEM((count, groups * cols), bf16),
            pltpu.VMEM((4 * count, width), bf16),
            pltpu.VMEM((4 * count, width), bf16),
            pltpu.VMEM((count, width), f32),
            pltpu.VMEM((count, 128), f32),
            pltpu.VMEM((count, width), f32),
            pltpu.VMEM((4 * count, hidden), bf16),
            pltpu.VMEM((4 * count, hidden), bf16),
            pltpu.VMEM((4 * count, hidden), bf16),
            pltpu.VMEM((count, width), f32),
            pltpu.VMEM((count, width), f32),
            two, two, two, two, two, two,
            pltpu.VMEM((count, width), bf16),
            pltpu.VMEM((length, width), bf16),
            pltpu.SemaphoreType.DMA((copies,)),
            pltpu.SemaphoreType.DMA((copies,)),
            pltpu.SemaphoreType.DMA((1,)),
        ],
        compiler_params=pltpu.CompilerParams(
            collective_id=collective_id, has_side_effects=True, vmem_limit_bytes=56 * 1024 * 1024
        ),
        name="middle",
    )(mixed_row, tokens, cotangent, out_weight, gate_weight, up_weight, down_weight, gain)


def reduce_kernel(rows, groups, chunks, span, feeds, *refs):
    count = len(chunks)
    ins, part, small, rest = refs[:count], refs[count], refs[count + 1], refs[count + 2 :]
    feed_in, rest = rest[:feeds], rest[feeds:]
    outs, part_out, small_out, rest = rest[:count], rest[count], rest[count + 1], rest[count + 2 :]
    feed_out, rest = rest[:feeds], rest[feeds:]
    got_core, rest = rest[:count], rest[count:]
    sum_core, rest = rest[:count], rest[count:]
    got_y, rest = rest[:count], rest[count:]
    sum_y, rest = rest[:count], rest[count:]
    got_row, rest = rest[:count], rest[count:]
    part_got, part_sum, small_got, small_sum, send_sem, recv_sem = rest
    row, group, feat = lax.axis_index("row"), lax.axis_index("group"), lax.axis_index("feat")
    core, y = lax.rem(feat, 2), feat // 2
    core_mate = {"feat": feat + 1 - 2 * core}
    y_mate = {"feat": feat + 2 - 4 * y}
    row_mates, group_mates = mates("row"), mates("group")
    copies = Copies(send_sem, recv_sem)
    send = copies.send

    at, add = rows_at, add_low
    greet([core_mate, y_mate] + row_mates + group_mates)
    halves = [shape[0] // 2 for shape in chunks]
    quarters = [shape[0] // 4 for shape in chunks]
    units = [shape[0] // (4 * rows) for shape in chunks]

    by_core = [send(ins[i].at[at((1 - core) * halves[i], halves[i])], got_core[i], core_mate) for i in range(count)]
    small_copy = send(small, small_got.at[0], core_mate)
    blocks = []
    for o in range(1, groups):
        blocks.append(send(part.at[lax.rem(group + o, groups)], part_got.at[o - 1], group_mates[o - 1]))
    feed_moves = [send(feed_in[i], feed_out[i].at[group], mate) for i in range(feeds) for mate in group_mates]
    for i in range(feeds):
        feed_out[i][group] = feed_in[i][...]
    by_y = []
    for i in range(count):
        by_core[i].wait_recv()
        sum_core[i][...] = add(ins[i][at(core * halves[i], halves[i])], got_core[i][...])
        by_y.append(send(sum_core[i].at[at((1 - y) * quarters[i], quarters[i])], got_y[i], y_mate))
    small_copy.wait_recv()
    small_sum[0] = small[...] + small_got[0]
    small_copy = send(small_sum.at[0], small_got.at[1], y_mate)
    total = part[group].astype(f32)
    for o in range(1, groups):
        blocks[o - 1].wait_recv()
        total = total + part_got[o - 1].astype(f32)
    part_sum[...] = total.astype(bf16)
    home = []
    for o in range(1, rows):
        home.append(send(part_sum.at[at(lax.rem(row + o, rows) * span, span)], part_out.at[at(row * span, span)], row_mates[o - 1]))
    part_out[at(row * span, span)] = part_sum[at(row * span, span)]
    by_row = []
    for i in range(count):
        by_y[i].wait_recv()
        sum_y[i][...] = add(sum_core[i][at(y * quarters[i], quarters[i])], got_y[i][...])
        by_row.append(
            [
                send(sum_y[i].at[at(lax.rem(row + o, rows) * units[i], units[i])], got_row[i].at[o - 1], row_mates[o - 1])
                for o in range(1, rows)
            ]
        )
    small_copy.wait_recv()
    small_sum[1] = small_sum[0] + small_got[1]
    small_copies = [send(small_sum.at[1], small_got.at[2 + row], row_mates[o - 1]) for o in range(1, rows)]
    small_got[2 + row] = small_sum[1]

    place = (core * 2 + y) * rows + row
    back_row = []
    for i in range(count):
        total = sum_y[i][at(row * units[i], units[i])].astype(f32)
        for o in range(1, rows):
            by_row[i][o - 1].wait_recv()
            total = total + got_row[i][o - 1].astype(f32)
        here = outs[i].at[group, at(place * units[i], units[i])]
        here[...] = total.astype(bf16)
        back_row.append([send(here, here, row_mates[o - 1]) for o in range(1, rows)])
    for copy in small_copies:
        copy.wait_recv()
    small_total = small_got[2]
    for r in range(1, rows):
        small_total = small_total + small_got[2 + r]
    small_out[group] = small_total
    small_copies = [send(small_out.at[group], small_out.at[group], mate) for mate in group_mates]
    first = []
    for i in range(count):
        for copy in back_row[i]:
            copy.wait_recv()
        here = outs[i].at[group, at((core * 2 + y) * quarters[i], quarters[i])]
        if i % 2 == 0:
            first.append([send(here, here, mate) for mate in group_mates])
        else:
            first.append([send(here, here, y_mate)])
    second = []
    for i in range(count):
        for copy in first[i]:
            copy.wait_recv()
        if i % 2 == 0:
            here = outs[i].at[:, at((core * 2 + y) * quarters[i], quarters[i])]
            second.append([send(here, here, y_mate)])
        else:
            here = outs[i].at[group, at(core * halves[i], halves[i])]
            second.append([send(here, here, mate) for mate in group_mates])
    third = []
    for i in range(count):
        for copy in second[i]:
            copy.wait_recv()
        here = outs[i].at[:, at(core * halves[i], halves[i])]
        third.append(send(here, here, core_mate))
    for copy in third + home + small_copies + feed_moves:
        copy.wait_recv()
    for copy in copies.started:
        copy.wait_send()


def reduce_all(arrays, part, small, feed_parts, rows, groups, collective_id):
    chunks = [a.shape for a in arrays]
    count = len(chunks)
    span = part.shape[1] // rows
    copies = count * (2 + 2 * (rows - 1) + (groups - 1) + 2) + (groups - 1) + (rows - 1) + 2 + (rows - 1) + (groups - 1)
    feeds = len(feed_parts)
    copies += feeds * (groups - 1)
    vmem = pl.BlockSpec(memory_space=pltpu.VMEM)
    scratch = [pltpu.VMEM((h // 2, w), bf16) for h, w in chunks] * 2
    scratch += [pltpu.VMEM((h // 4, w), bf16) for h, w in chunks] * 2
    scratch += [pltpu.VMEM((rows - 1, h // (4 * rows), w), bf16) for h, w in chunks]
    scratch += [
        pltpu.VMEM((groups - 1,) + part.shape[1:], bf16),
        pltpu.VMEM(part.shape[1:], bf16),
        pltpu.VMEM((2 + rows,) + small.shape, f32),
        pltpu.VMEM((2,) + small.shape, f32),
        pltpu.SemaphoreType.DMA((copies,)),
        pltpu.SemaphoreType.DMA((copies,)),
    ]
    return pl.pallas_call(
        partial(reduce_kernel, rows, groups, chunks, span, feeds),
        in_specs=[vmem] * (count + 2 + feeds),
        out_specs=[vmem] * (count + 2 + feeds),
        out_shape=[jax.ShapeDtypeStruct((groups, h, w), bf16) for h, w in chunks]
        + [jax.ShapeDtypeStruct(part.shape[1:], bf16), jax.ShapeDtypeStruct((groups,) + small.shape, f32)]
        + [jax.ShapeDtypeStruct((groups,) + a.shape, bf16) for a in feed_parts],
        scratch_shapes=scratch,
        compiler_params=pltpu.CompilerParams(
            collective_id=collective_id, has_side_effects=True, vmem_limit_bytes=48 * 1024 * 1024
        ),
        name="reduce_all",
    )(*arrays, part, small, *feed_parts)


def normalize(vector, gain):
    centered = vector - jnp.mean(vector, -1, keepdims=True)
    variance = jnp.mean(centered * centered, -1, keepdims=True)
    inv_scale = lax.rsqrt(variance + epsilon)
    normed_unit = centered * inv_scale
    return (normed_unit * gain, normed_unit, inv_scale)


def norm_back(grad_out, gain, normed_unit, inv_scale):
    scaled = grad_out * gain
    return inv_scale * (
        scaled
        - jnp.mean(scaled, -1, keepdims=True)
        - normed_unit * jnp.mean(scaled * normed_unit, -1, keepdims=True)
    )


SEQ = ("row", "group")


def per_device(
    tokens,
    cotangent,
    doc_starts,
    mixer_gain,
    query_weight,
    key_weight,
    value_weight,
    out_weight,
    rate_weight,
    rate_bias,
    first_init,
    first_bias_init,
    second_init,
    second_bias_init,
    inner_gain,
    inner_bias,
    feed_gain,
    gate_weight,
    up_weight,
    down_weight,
):
    rows, span, width = tokens.shape
    heads, head_dim, inner = first_init.shape
    groups = lax.axis_size("group")
    feats = lax.axis_size("feat")
    row, group = lax.axis_index("row"), lax.axis_index("group")
    count = rows * span
    length = span * rows * groups
    blocks = length // MB
    pairs = -(-heads // (2 * groups))
    mine = 2 * pairs
    pair = 2 * head_dim
    cols = mine * head_dim
    spare = mine * groups - heads

    def own_heads(array, axis, per_head=1):
        if spare:
            pad = [(0, 0)] * array.ndim
            pad[axis] = (0, spare * per_head)
            array = jnp.pad(array, pad)
        return lax.dynamic_slice_in_dim(array, group * mine * per_head, mine * per_head, axis)

    def to_rows(array):
        got = lax.all_to_all(jnp.repeat(array, groups, 0), SEQ, 0, 0, tiled=True)
        return got.reshape(length, array.shape[-1])

    row_in = to_rows(tokens).astype(f32)
    act_row = low(normalize(row_in, mixer_gain)[0])
    w_q, w_k, w_v = (own_heads(w, 1, head_dim) for w in (query_weight, key_weight, value_weight))
    w_r = own_heads(rate_weight, 1)
    queries, keys, values = (dot(act_row, w) for w in (w_q, w_k, w_v))
    logits = dot(act_row, w_r) + own_heads(rate_bias, 0)
    sigma = jax.nn.sigmoid(logits)
    rates = sigma / head_dim
    e = jnp.broadcast_to(
        rates.reshape(blocks, MB, pairs, 2).transpose(0, 2, 3, 1).reshape(blocks, pairs, 2 * MB, 1),
        (blocks, pairs, 2 * MB, pair),
    )
    block_ids = jnp.arange(blocks, dtype=jnp.int32)
    starts = lax.dynamic_index_in_dim(doc_starts, row, 0, False)
    restarts = ((block_ids == 0) | jnp.any(starts[:, None] == block_ids[None], 0)).astype(jnp.int32)
    pack = lambda a: own_heads(a, 0).reshape(pairs, pair, inner)
    start_first = pack(first_init)
    start_second = pack(second_init - jnp.mean(second_init, 1, keepdims=True))
    start_first_bias = jnp.repeat(own_heads(first_bias_init, 0).reshape(pairs, 2, 1, inner), MB, 2).reshape(
        pairs, 2 * MB, inner
    )
    centered = own_heads(second_bias_init - jnp.mean(second_bias_init, 1, keepdims=True), 0)
    start_second_bias = (
        jnp.eye(2, dtype=f32)[None, :, None, :, None] * centered.reshape(pairs, 1, 1, 2, head_dim)
    ) * jnp.ones((1, 1, MB, 1, 1), f32)
    start_second_bias = start_second_bias.reshape(pairs, 2 * MB, pair)
    gain, bias = own_heads(inner_gain, 0).reshape(1, cols), own_heads(inner_bias, 0).reshape(1, cols)
    *saved, mixed = forward_inner(
        jnp.concatenate([restarts, jnp.zeros((1,), jnp.int32)]),
        queries, keys, values, e, start_first, start_first_bias, start_second, start_second_bias, gain, bias,
    )
    mixed_row = low(mixed[MB:])

    flat_in = tokens.astype(f32).reshape(count, width)
    all_heads = jnp.pad(out_weight, ((0, spare * head_dim), (0, 0))) if spare else out_weight
    block_out, grad_hidden, grad_mixed, grad_out_rows, *feed_terms, grad_feed_gain = middle(
        mixed_row, tokens.reshape(count, width), cotangent.reshape(count, width), all_heads,
        gate_weight, up_weight, down_weight, feed_gain.reshape(1, width), span, 1,
    )

    grad_q, grad_k, grad_v, grad_e, g_first, g_first_bias, g_second, g_second_bias, g_gain, g_bias, *feed_grads = (
        backward_inner(restarts, queries, keys, values, grad_mixed, e, saved, gain, bias, feed_terms, 2)
    )
    grad_q, grad_k, grad_v = grad_q[:length], grad_k[:length], grad_v[:length]
    grad_rates = grad_e[:blocks, :, :, 0].reshape(blocks, pairs, 2, MB).transpose(0, 3, 1, 2).reshape(length, mine)
    grad_logits = low(grad_rates * sigma * (1.0 - sigma) / head_dim)
    part = dot_nt(grad_q, w_q) + dot_nt(grad_k, w_k) + dot_nt(grad_v, w_v) + dot_nt(grad_logits, w_r)
    _, unit_row, _ = normalize(row_in, mixer_gain)
    blocks_out = low(part).reshape(rows, groups, span, width).transpose(1, 0, 2, 3).reshape(groups, count, width)
    arrays = (
        jnp.concatenate([low(dot_tn(act_row, grad_q)), low(dot_tn(act_row, grad_k))], 1),
        jnp.concatenate([low(dot_tn(act_row, grad_v)), grad_out_rows], 1),
        jnp.concatenate([low(g_first.reshape(cols, inner)), low(g_second.reshape(cols, inner))], 0),
    )
    per_head = jnp.concatenate(
        [
            g_first_bias.reshape(mine, MB, inner)[:, 0],
            jnp.stack([g_second_bias[:, h * MB, h * head_dim : (h + 1) * head_dim] for h in range(2)], 1).reshape(
                mine, head_dim
            ),
            jnp.sum(g_gain, 0).reshape(mine, head_dim),
            jnp.sum(g_bias, 0).reshape(mine, head_dim),
            dot_tn(grad_logits, act_row),
            jnp.sum(grad_logits.astype(f32), 0)[:, None],
            jnp.sum(logits, 0)[:, None],
        ],
        1,
    )
    used = (group * mine + jnp.arange(mine)) < heads
    peers = rows * feats
    top = jnp.max(jnp.where(used[None], logits, jnp.finfo(f32).min))
    tops = jnp.where(jnp.arange(peers) == row * feats + lax.axis_index("feat"), top, 0.0)
    pieces = [per_head.reshape(-1), jnp.sum(part * unit_row, 0), grad_feed_gain.reshape(-1), tops]
    sizes = [p.shape[0] for p in pieces]
    size = sum(sizes)
    lines = -(-size // 1024) * 8
    small = jnp.pad(jnp.concatenate(pieces), (0, lines * 128 - size)).reshape(lines, 128)
    def feed_joined(array):
        flat = array.reshape(2 * width, -1)
        return jnp.concatenate([flat[:width], flat[width:]], 1).astype(f32)

    reduced = reduce_all(arrays, blocks_out, small, feed_grads, rows, groups, 3)
    arrays, (got, small), feed_grads = reduced[:3], reduced[3:5], reduced[5:]

    grad_act_one = got.astype(f32)
    _, unit_one, scale_one = normalize(flat_in, mixer_gain)
    input_grad = grad_hidden + norm_back(grad_act_one, mixer_gain, unit_one, scale_one)

    def gathered(array, part_no):
        cut = slice(part_no * cols, (part_no + 1) * cols)
        return jnp.concatenate([array[g, :, cut] for g in range(groups)], 1)[:, :width].astype(f32)

    g_query, g_key = (gathered(arrays[0], i) for i in range(2))
    g_value, g_out = gathered(arrays[1], 0), gathered(arrays[1], 1).T
    states = arrays[2].astype(f32).reshape(groups, 2, cols, inner)
    g_first, g_second = (
        states[:, i].reshape(groups * mine, head_dim, inner)[:heads] for i in range(2)
    )
    g_second = g_second - jnp.mean(g_second, 1, keepdims=True)
    small = small.reshape(groups, lines * 128)
    ends = [0]
    for s in sizes:
        ends.append(ends[-1] + s)
    slots = small[:, : ends[1]].reshape(groups * mine, -1)[:heads]
    g_mixer, g_feed = jnp.sum(small[:, ends[1] : ends[2]], 0), jnp.sum(small[:, ends[2] : ends[3]], 0)
    at = [0, inner, inner + head_dim, inner + 2 * head_dim, inner + 3 * head_dim, inner + 3 * head_dim + width]
    g_second_bias = slots[:, at[1] : at[2]]
    g_second_bias = g_second_bias - jnp.mean(g_second_bias, 1, keepdims=True)
    total = jnp.sum(slots[:, at[5] + 1])
    stats = jnp.stack([total / (rows * groups * feats * count * heads), jnp.max(small[:, ends[3] : ends[4]])])
    return (
        block_out.reshape(rows, span, width),
        input_grad.reshape(rows, span, width),
        g_mixer,
        g_query,
        g_key,
        g_value,
        g_out,
        slots[:, at[4] : at[5]].T,
        slots[:, at[5]],
        g_first,
        slots[:, : at[1]],
        g_second,
        g_second_bias,
        slots[:, at[2] : at[3]],
        slots[:, at[3] : at[4]],
        g_feed,
        feed_joined(feed_grads[0]),
        feed_joined(feed_grads[1]),
        feed_joined(feed_grads[2]),
        stats,
    )


def solution(mesh):
    feats = mesh.shape["feat"]

    def run(*arrays):
        rows = arrays[0].shape[0] // feats
        grid = jax.sharding.Mesh(mesh.devices.reshape(rows, -1, feats), ("row", "group", "feat"))
        by_token = P("feat", SEQ, None)
        by_hidden = P(None, "feat")
        return jax.shard_map(
            per_device,
            mesh=grid,
            in_specs=(by_token, by_token, P("feat", None)) + (P(),) * 14 + (by_hidden,) * 3,
            out_specs=(by_token, by_token) + (P(),) * 14 + (by_hidden,) * 3 + (P(),),
            check_vma=False,
        )(*arrays)

    return run
```

```python
from functools import partial

import jax
import jax.numpy as jnp
from jax import lax
from jax.experimental import pallas as pl
from jax.experimental.pallas import tpu as pltpu
from jax.sharding import PartitionSpec as P

MB = 16
epsilon = 1e-05
f32, bf16 = jnp.float32, jnp.bfloat16


def dot(a, b):
    return lax.dot_general(a, b, (((1,), (0,)), ((), ())), preferred_element_type=f32)


def dot_nt(a, b):
    return lax.dot_general(a, b, (((1,), (1,)), ((), ())), preferred_element_type=f32)


def dot_tn(a, b):
    return lax.dot_general(a, b, (((0,), (0,)), ((), ())), preferred_element_type=f32)


def low(v):
    return v.astype(bf16)


def gelu_parts(z):
    a = jnp.abs(z)
    d = 1.0 + 0.23164189 * a
    t = pl.reciprocal(d, approx=True)
    t = t * (2.0 - d * t)
    ex = jnp.exp(-0.5 * (z * z))
    poly = t * (
        0.127414796 + t * (-0.142248368 + t * (0.7107068705 + t * (-0.7265760135 + t * 0.5307027145)))
    )
    h = poly * ex
    cdf = jnp.where(z >= 0, 1.0 - h, h)
    pdf = 0.3989422804014327 * ex
    return z * cdf, cdf + z * pdf, pdf


def lane_sum(v):
    return jnp.sum(v, -1, keepdims=True)


def masks(head_dim):
    pair = 2 * head_dim
    rows, cols = 2 * MB, pair
    r = lax.broadcasted_iota(jnp.int32, (rows, cols), 0)
    c = lax.broadcasted_iota(jnp.int32, (rows, cols), 1)
    own = ((r < MB) == (c < head_dim)).astype(f32)
    r = lax.broadcasted_iota(jnp.int32, (rows, rows), 0)
    c = lax.broadcasted_iota(jnp.int32, (rows, rows), 1)
    same = (r < MB) == (c < MB)
    causal = (same & (c <= r)).astype(f32)
    return own, causal, same.astype(bf16)


def spread(v, own):
    return jnp.concatenate([v, v], 0) * own


def fold(v):
    return v[:MB] + v[MB:]


def twice(v):
    return jnp.concatenate([v, v], 1)


def in_turn(parts):
    while parts:
        parts = [part for part in parts if next(part, parts) is not parts]


def forward_kernel(pairs, head_dim, restart_ref, q_ref, k_ref, v_ref, e_ref, w1i_ref, b1i_ref, w2i_ref, b2i_ref, gain_ref, bias_ref,
                   big_ref, mid_ref, small_ref, n1_ref, pq_ref, uq_ref, n2_ref, out_ref,
                   w1, b1, w2, b2, s_q1, s_x2, s_e2, s_w2, s_b2, s_q):
    j = pl.program_id(0)
    pair = 2 * head_dim
    inv = 1.0 / head_dim
    own, causal, ones = masks(head_dim)

    @pl.when(restart_ref[j] > 0)
    def _():
        w1[...] = w1i_ref[...]
        b1[...] = b1i_ref[...]
        w2[...] = w2i_ref[...]
        b2[...] = b2i_ref[...]

    loaded = [
        (s_q1[p], s_x2[p], s_e2[p], s_w2[p], s_b2[p], s_q[p], w1[p], w2[p], b1[p], b2[p], e_ref[0, p]) for p in range(pairs)
    ]
    tokens = [[ref[:, p * pair : (p + 1) * pair] for ref in (q_ref, k_ref, v_ref, gain_ref, bias_ref)] for p in range(pairs)]
    writes = []

    def write(ref, index, value):
        writes.append((ref, index, value))

    def outputs_before(p):
        q1p, x2p, e2p, w2p, b2p, qp = loaded[p][:6]
        gain, bias = tokens[p][3:]
        p2, lq, _ = gelu_parts(q1p)
        p2b = low(p2)
        yield
        n2 = causal * (dot_nt(p2b, x2p) + 1.0)
        q2 = dot_nt(p2b, w2p)
        yield
        q2 = q2 * own - dot(low(n2), e2p) + b2p
        yield
        sq = lax.rsqrt(lane_sum(q2 * q2) * inv + epsilon)
        uq = q2 * sq
        write(out_ref, (slice(None), slice(p * pair, (p + 1) * pair)), qp + fold(uq) * gain + bias)
        write(pq_ref, (0, p, slice(0, 2 * MB)), p2b)
        write(pq_ref, (0, p, slice(2 * MB, 4 * MB)), low(lq))
        write(uq_ref, (0, p, slice(0, 2 * MB)), uq)
        write(uq_ref, (0, p, slice(2 * MB, 4 * MB)), jnp.broadcast_to(sq, uq.shape))
        write(n2_ref, (0, p), low(n2))

    def inner_step(p):
        w1c, w2c, b1c, b2c, e = loaded[p][6:]
        qc, kc, vc, gain, bias = tokens[p]
        kb, qb = low(spread(kc, own)), low(spread(qc, own))
        w1b, w2b = low(w1c), low(w2c)
        kq = dot(jnp.concatenate([kb, qb], 0), w1b)
        yield
        z1 = kq[: 2 * MB] + b1c
        x2, l1, pdf = gelu_parts(z1)
        x2b = low(x2)
        yield
        c = dot_nt(x2b, w2b)
        n1 = causal * (dot_nt(qb, kb) + 1.0)
        yield
        c = c * own + b2c
        s = lax.rsqrt(lane_sum(c * c) * inv + epsilon)
        u = c * s
        r = u * (gain * gain) + spread((bias - (vc - kc)) * gain, own)
        yield
        mr, m2 = lane_sum(r) * inv, lane_sum(r * u) * inv
        g2 = s * (r - mr * own - u * m2)
        yield
        h = dot(low(g2), w2b)
        e2b = low(e * g2)
        yield
        g1 = h * l1
        e1b = low(twice(e) * g1)
        yield
        u1 = dot_tn(kb, e1b)
        yield
        q1 = kq[2 * MB :] + b1c - dot(low(n1), e1b)
        yield
        write(w1, p, w1c - u1)
        write(b1, p, b1c - dot(ones, e1b))
        write(w2, p, w2c - dot_tn(e2b, x2b))
        write(b2, p, b2c - dot(ones, e2b))
        write(big_ref, (0, p, slice(0, pair)), w1b)
        write(big_ref, (0, p, slice(pair, 2 * pair)), w2b)
        write(big_ref, (0, p, slice(2 * pair, 2 * pair + 2 * MB)), x2b)
        write(big_ref, (0, p, slice(2 * pair + 2 * MB, 2 * pair + 4 * MB)), e1b)
        write(mid_ref, (0, p, slice(0, 2 * MB)), low(g1))
        write(mid_ref, (0, p, slice(2 * MB, 4 * MB)), low(l1))
        write(mid_ref, (0, p, slice(4 * MB, 6 * MB)), low(h * pdf * (2.0 - z1 * z1)))
        for i, value in enumerate((u, s, r, m2, g2)):
            write(small_ref, (0, p, slice(i * 2 * MB, (i + 1) * 2 * MB)), jnp.broadcast_to(value, u.shape))
        write(n1_ref, (0, p), low(n1))
        for ref, value in ((s_q1, q1), (s_x2, x2b), (s_e2, e2b), (s_w2, w2b), (s_b2, b2c), (s_q, qc)):
            write(ref, p, value)

    in_turn([inner_step(p) for p in range(pairs)] + [outputs_before(p) for p in range(pairs)])
    for ref, index, value in writes:
        ref[index] = value


def forward_inner(restarts, q, k, v, e, w1i, b1i, w2i, b2i, gain, bias):
    blocks, pairs, _, pair = e.shape
    head_dim = pair // 2
    inner = w1i.shape[-1]
    steps = blocks + 1
    last = blocks - 1
    tok = pl.BlockSpec((MB, pairs * pair), lambda j, r: (jnp.minimum(j, last), 0))
    whole = lambda a: pl.BlockSpec(a.shape, lambda j, r: (0,) * a.ndim)

    def per_step(rows, width, dtype):
        return (
            jax.ShapeDtypeStruct((steps, pairs, rows, width), dtype),
            pl.BlockSpec((1, pairs, rows, width), lambda j, r: (j, 0, 0, 0)),
        )

    outs = [
        per_step(2 * pair + 4 * MB, inner, bf16),
        per_step(6 * MB, inner, bf16),
        per_step(10 * MB, pair, f32),
        per_step(2 * MB, 2 * MB, bf16),
        per_step(4 * MB, inner, bf16),
        per_step(4 * MB, pair, f32),
        per_step(2 * MB, 2 * MB, bf16),
        (
            jax.ShapeDtypeStruct((steps * MB, pairs * pair), f32),
            pl.BlockSpec((MB, pairs * pair), lambda j, r: (j, 0)),
        ),
    ]
    return pl.pallas_call(
        partial(forward_kernel, pairs, head_dim),
        grid_spec=pltpu.PrefetchScalarGridSpec(
            num_scalar_prefetch=1,
            grid=(steps,),
            in_specs=[tok, tok, tok, pl.BlockSpec((1, pairs, 2 * MB, pair), lambda j, r: (jnp.minimum(j, last), 0, 0, 0))]
            + [whole(a) for a in (w1i, b1i, w2i, b2i, gain, bias)],
            out_specs=[o[1] for o in outs],
            scratch_shapes=[
                pltpu.VMEM((pairs, pair, inner), f32),
                pltpu.VMEM((pairs, 2 * MB, inner), f32),
                pltpu.VMEM((pairs, pair, inner), f32),
                pltpu.VMEM((pairs, 2 * MB, pair), f32),
                pltpu.VMEM((pairs, 2 * MB, inner), f32),
                pltpu.VMEM((pairs, 2 * MB, inner), bf16),
                pltpu.VMEM((pairs, 2 * MB, pair), bf16),
                pltpu.VMEM((pairs, pair, inner), bf16),
                pltpu.VMEM((pairs, 2 * MB, pair), f32),
                pltpu.VMEM((pairs, MB, pair), f32),
            ],
        ),
        out_shape=[o[0] for o in outs],
        compiler_params=pltpu.CompilerParams(vmem_limit_bytes=48 * 1024 * 1024),
        name="inner_forward",
    )(restarts, q, k, v, e, w1i, b1i, w2i, b2i, gain, bias)


MESH = pl.DeviceIdType.MESH


def greet(peers):
    barrier = pltpu.get_barrier_semaphore()
    for peer in peers:
        pl.semaphore_signal(barrier, inc=1, device_id=peer, device_id_type=MESH)
    pl.semaphore_wait(barrier, len(peers))


class Copies:
    def __init__(self, send_sem, recv_sem):
        self.send_sem, self.recv_sem, self.started = send_sem, recv_sem, []

    def make(self, src, dst, peer):
        i = len(self.started)
        copy = pltpu.make_async_remote_copy(
            src_ref=src, dst_ref=dst, send_sem=self.send_sem.at[i], recv_sem=self.recv_sem.at[i],
            device_id=peer, device_id_type=MESH,
        )
        self.started.append(copy)
        return copy

    def send(self, src, dst, peer):
        copy = self.make(src, dst, peer)
        copy.start()
        return copy


def rows_at(start, size):
    return pl.ds(pl.multiple_of(start, 16), size)


def add_low(a, b):
    return (a.astype(f32) + b.astype(f32)).astype(bf16)


def mates(axis):
    size, here = lax.axis_size(axis), lax.axis_index(axis)
    return [{axis: lax.rem(here + o, size)} for o in range(1, size)]


def feed_sum_steps(ins, outs, got_group, sum_group, got_row, full, copies, whole):
    row, group = lax.axis_index("row"), lax.axis_index("group")
    rows, groups = lax.axis_size("row"), lax.axis_size("group")
    row_mates, group_mates = mates("row"), mates("group")
    count = len(ins)
    part = ins[0].shape[0] // groups
    unit = part // rows
    mine = rows_at(row * unit, unit)
    moves = {}
    for i in range(count):
        moves["X", i] = [
            copies.make(ins[i].at[rows_at(lax.rem(group + o, groups) * part, part)], got_group[i].at[o - 1], group_mates[o - 1])
            for o in range(1, groups)
        ]
        moves["Z", i] = [
            copies.make(sum_group[i].at[rows_at(lax.rem(row + o, rows) * unit, unit)], got_row[i].at[o - 1], row_mates[o - 1])
            for o in range(1, rows)
        ]
        if i < whole:
            here = full[i].at[group, mine]
            moves["ZA", i] = [copies.make(here, here, mate) for mate in row_mates]
            here = full[i].at[group]
            moves["XA", i] = [copies.make(here, here, mate) for mate in group_mates]

    def finish(kind, i):
        for copy in moves[kind, i]:
            copy.wait_recv()
        if kind == "X":
            total = ins[i][rows_at(group * part, part)].astype(f32)
            for o in range(1, groups):
                total = total + got_group[i][o - 1].astype(f32)
            sum_group[i][...] = low(total)
        if kind == "Z":
            total = sum_group[i][mine].astype(f32)
            for o in range(1, rows):
                total = total + got_row[i][o - 1].astype(f32)
            if i < whole:
                full[i][group, mine] = low(total)
            else:
                outs[i][...] = low(total)

    def run(slot):
        _, done, begun = FEED_SLOTS[slot]
        if slot == 0:
            greet(row_mates + group_mates)
        for name in done:
            finish(name[:-1], int(name[-1]))
        for name in begun:
            for copy in moves[name[:-1], int(name[-1])]:
                copy.start()
        if slot == len(FEED_SLOTS) - 1:
            for i in range(whole):
                outs[i][...] = full[i][...]
            for copy in copies.started:
                copy.wait_send()

    return [partial(run, slot) for slot in range(len(FEED_SLOTS))]


def backward_kernel(pairs, head_dim, feeds, restart_ref,
                    qq_ref, kq_ref, doq_ref, eq_ref, bigq_ref, g2q_ref, n1_ref, pqq_ref, uqq_ref, n2_ref,
                    q_ref, k_ref, v_ref, do_ref, e_ref, big_ref, mid_ref, small_ref, pq_ref, uq_ref, gain_ref, bias_ref, *refs):
    j = pl.program_id(0)
    steps = pl.num_programs(0)
    pair = 2 * head_dim
    inv = 1.0 / head_dim
    own, causal, ones = masks(head_dim)
    feed_in, refs = refs[:feeds], refs[feeds:]
    dq_ref, dk_ref, dv_ref, de_ref, gw1, gb1, gw2, gb2, ggain, gbias = refs[:10]
    feed_out, refs = refs[10 : 10 + feeds], refs[10 + feeds :]
    w1, b1, w2, b2, s_e1, s_e2, s_k, s_x2, s_q1, s_q2, s_q = refs[:11]
    if feeds:
        refs, sems = refs[11:-2], refs[-2:]
        buffers = [refs[i * feeds : (i + 1) * feeds] for i in range(3)] + [refs[3 * feeds :]]
        slots = feed_sum_steps(feed_in, feed_out, *buffers, Copies(*sems), FEED_WHOLE)
        for i, run in enumerate(slots):
            pl.when(j == FEED_SLOTS[i][0] * (steps - 1) // 32)(run)

    @pl.when(j <= 1)
    def _():
        for ref in (w1, b1, w2, b2, gw1, gb1, gw2, gb2, ggain, gbias):
            ref[...] = jnp.zeros_like(ref)

    rows2 = 2 * MB
    piece = lambda ref, p, i: ref[0, p, i * rows2 : (i + 1) * rows2]
    token = lambda ref, p: ref[:, p * pair : (p + 1) * pair]
    first = restart_ref[jnp.minimum(steps - 1 - j, steps - 2)]
    go_on = 1.0 - first
    writes = []

    def write(ref, index, value):
        writes.append((ref, index, value))

    def load_outputs(p):
        return (
            [token(ref, p) for ref in (qq_ref, kq_ref, doq_ref, gain_ref)]
            + [bigq_ref[0, p, 0:pair], bigq_ref[0, p, pair : 2 * pair]]
            + [bigq_ref[0, p, 2 * pair : 2 * pair + rows2], bigq_ref[0, p, 2 * pair + rows2 : 2 * pair + 2 * rows2]]
            + [eq_ref[0, p], g2q_ref[0, p], n1_ref[0, p], n2_ref[0, p]]
            + [piece(ref, p, i) for ref in (pqq_ref, uqq_ref) for i in range(2)]
        )

    def load_step(p):
        return (
            [ref[p] for ref in (s_e1, s_e2, s_k, s_x2, s_q1, s_q2, s_q, w1, w2, b1, b2)]
            + [token(ref, p) for ref in (q_ref, k_ref, v_ref, do_ref, gain_ref, bias_ref)]
            + [big_ref[0, p, 0:pair], big_ref[0, p, pair : 2 * pair]]
            + [big_ref[0, p, 2 * pair : 2 * pair + rows2], big_ref[0, p, 2 * pair + rows2 : 2 * pair + 2 * rows2]]
            + [piece(mid_ref, p, i).astype(f32) for i in range(3)]
            + [piece(small_ref, p, i) for i in range(5)]
            + [pq_ref[0, p], uq_ref[0, p], e_ref[0, p]]
        )

    def outputs_ahead(p, loaded):
        qc, kc, do, gain, w1b, w2b, x2b, e1b, e, g2, n1b, n2b, p2b, lq, uq, sq = loaded
        qb, kb = low(spread(qc, own)), low(spread(kc, own))
        e2b = low(e * g2)
        w = spread(do * gain, own)
        dq2 = low(sq * (w - (lane_sum(w) * inv) * own - uq * (lane_sum(w * uq) * inv)))
        yield
        dn2 = dot_nt(dq2, e2b)
        dp2 = dot(dq2, w2b)
        yield
        dpx = low(-causal * dn2)
        new_e2 = dot_tn(n2b, dq2)
        dp2 = dp2 + dot(dpx, x2b)
        yield
        dq1 = low(dp2 * lq.astype(f32))
        new_x2 = dot_tn(dpx, p2b)
        yield
        dn1 = dot_nt(dq1, e1b)
        new_q = dot_nt(dq1, w1b)
        yield
        new_e1 = dot_tn(n1b, dq1)
        dqk = low(-causal * dn1)
        yield
        new_k = dot_tn(dqk, qb)
        new_q = do + fold((new_q + dot(dqk, kb)) * own)
        for ref, value in zip((s_e1, s_e2, s_k, s_x2, s_q1, s_q2, s_q), (new_e1, new_e2, new_k, new_x2, dq1, dq2, new_q)):
            write(ref, p, value)

    def step_back(p, loaded):
        e1q, e2q, dkq, x2q, dq1, dq2, dqc, dw1, dw2, db1, db2, qc, kc, vc, do, gain, bias, w1b, w2b, x2b, e1b = loaded[:21]
        g1, l1, hg, u, s, r, m2, g2, p2b, uq, e = loaded[21:]
        cols = (slice(None), slice(p * pair, (p + 1) * pair))
        dw1b, dw2b = low(dw1), low(dw2)
        qb, kb = low(spread(qc, own)), low(spread(kc, own))
        e2b = low(e * g2)
        de1 = dot(kb, dw1b)
        de2 = dot_nt(x2b, dw2b)
        yield
        de1 = -(e1q + de1 + db1)
        de2 = -(e2q + de2 * own + db2)
        dg1 = twice(e) * de1
        dh = low(dg1 * l1)
        yield
        dg2 = dot_nt(dh, w2b)
        dx2 = x2q - dot(e2b, dw2b)
        yield
        dg2 = e * de2 + dg2 * own
        dk = dkq - dot_nt(e1b, dw1b) * own
        ma, mg = lane_sum(dg2 * u) * inv, lane_sum(dg2) * inv
        rate = jnp.broadcast_to(lane_sum(g1 * de1) + lane_sum(g2 * de2), u.shape)
        rates.append(jnp.where(head == 2 * p, rate[:MB], 0.0) + jnp.where(head == 2 * p + 1, rate[MB:], 0.0))
        yield
        dr = s * (dg2 - mg * own - u * ma)
        du = dr * (gain * gain) - s * (dg2 * m2 + r * ma)
        yield
        md, mu = lane_sum(du) * inv, lane_sum(du * u + dg2 * g2) * inv
        dz2 = low(s * (du - md * own - u * mu))
        yield
        dx2 = dx2 + dot(dz2, w2b)
        yield
        dz1 = low(dg1 * hg + dx2 * l1)
        drg = fold(dr) * gain
        write(dq_ref, cols, low(dqc))
        write(dv_ref, cols, low(-drg))
        more_gain = fold(spread_by(do, uq)) + fold(dr * u) * (2.0 * gain) + fold(dr) * (bias - (vc - kc))
        yield
        ndw1 = dw1 + dot_tn(jnp.concatenate([qb, kb], 0), jnp.concatenate([dq1, dz1], 0))
        yield
        dk = dk + dot_nt(dz1, w1b) * own
        write(dk_ref, cols, low(fold(dk) + drg))
        ndw2 = dw2 + dot_tn(jnp.concatenate([dq2, low(g2), dz2], 0), jnp.concatenate([p2b, dh, x2b], 0))
        ndb1 = db1 + dot(ones, dq1) + dot(ones, dz1)
        ndb2 = db2 + dot(ones, dq2) + dot(ones, dz2)
        for ref, value in ((w1, ndw1), (w2, ndw2), (b1, ndb1), (b2, ndb2)):
            write(ref, p, value * go_on)
        more.append((cols, more_gain, do + drg))
        starts.append((p, ndw1, ndw2, ndb1, ndb2))

    more, starts, rates = [], [], []
    head = lax.broadcasted_iota(jnp.int32, (MB, pair), 1)
    ahead_in = [load_outputs(p) for p in range(pairs)]
    step_in = [load_step(p) for p in range(pairs)]
    in_turn([step_back(p, step_in[p]) for p in range(pairs)] + [outputs_ahead(p, ahead_in[p]) for p in range(pairs)])
    for ref, index, value in writes:
        ref[index] = value
    de_ref[...] = sum(rates)
    for cols, more_gain, more_bias in more:
        ggain[cols] += more_gain
        gbias[cols] += more_bias
    for p, *values in starts:
        for ref, value in zip((gw1, gw2, gb1, gb2), values):
            ref[p] += value * first


def spread_by(do, uq):
    return jnp.concatenate([do, do], 0) * uq


def backward_inner(restarts, q, k, v, do, e, saved, gain, bias, feed_terms, collective_id):
    big, mid, small, n1, pq, uq, n2 = saved
    blocks, pairs, _, pair = e.shape
    head_dim = pair // 2
    inner = big.shape[-1]
    steps = blocks + 1
    now = lambda j: jnp.minimum(blocks - j, blocks - 1)
    ahead = lambda j: jnp.maximum(blocks - 1 - j, 0)
    tok = lambda at: pl.BlockSpec((MB, pairs * pair), lambda j: (at(j), 0))

    def block(a, at, rows=None, part=0):
        shape = (1, pairs, rows or a.shape[2], a.shape[3])
        return pl.BlockSpec(shape, lambda j: (at(j), 0, part, 0))

    whole = lambda a: pl.BlockSpec(a.shape, lambda j: (0,) * a.ndim)
    later = lambda j: ahead(j) + 1
    at_now = lambda j: now(j) + 1
    operands = [
        (q, tok(ahead)), (k, tok(ahead)), (do, tok(ahead)), (e, block(e, ahead)), (big, block(big, ahead)),
        (small, block(small, ahead, 2 * MB, 4)), (n1, block(n1, ahead)), (pq, block(pq, later)), (uq, block(uq, later)),
        (n2, block(n2, later)),
        (q, tok(now)), (k, tok(now)), (v, tok(now)), (do, tok(now)), (e, block(e, now)), (big, block(big, now)),
        (mid, block(mid, now)), (small, block(small, now)), (pq, block(pq, at_now, 2 * MB)), (uq, block(uq, at_now, 2 * MB)),
        (gain, whole(gain)), (bias, whole(bias)),
    ]
    feeds = len(feed_terms)
    vmem = pl.BlockSpec(memory_space=pltpu.VMEM)
    operands += [(a, vmem) for a in feed_terms]
    width = pairs * pair
    tok_out = (jax.ShapeDtypeStruct((steps * MB, width), bf16), pl.BlockSpec((MB, width), lambda j: (blocks - j, 0)))
    state = [((pairs, pair, inner), f32), ((pairs, 2 * MB, inner), f32), ((pairs, pair, inner), f32), ((pairs, 2 * MB, pair), f32)]
    keep = lambda shape: (jax.ShapeDtypeStruct(shape, f32), pl.BlockSpec(shape, lambda j: (0,) * len(shape)))
    outs = [tok_out] * 3 + [
        (jax.ShapeDtypeStruct((steps * MB, pair), f32), pl.BlockSpec((MB, pair), lambda j: (blocks - j, 0)))
    ] + [keep(shape) for shape, _ in state] + [keep((MB, width))] * 2
    comm = []
    if feeds:
        groups, rows = lax.axis_size("group"), lax.axis_size("row")
        part, wide = feed_terms[0].shape[0] // groups, feed_terms[0].shape[1]
        unit = part // rows
        outs += [
            (jax.ShapeDtypeStruct((groups, part, wide) if i < FEED_WHOLE else (unit, wide), bf16), vmem) for i in range(feeds)
        ]
        comm = [pltpu.VMEM((groups - 1, part, wide), bf16)] * feeds + [pltpu.VMEM((part, wide), bf16)] * feeds
        comm += [pltpu.VMEM((rows - 1, unit, wide), bf16)] * feeds + [pltpu.VMEM((groups, part, wide), bf16)] * FEED_WHOLE
        copies = (feeds + FEED_WHOLE) * (groups + rows - 2)
        comm += [pltpu.SemaphoreType.DMA((copies,))] * 2
    return pl.pallas_call(
        partial(backward_kernel, pairs, head_dim, feeds),
        grid_spec=pltpu.PrefetchScalarGridSpec(
            num_scalar_prefetch=0,
            grid=(steps,),
            in_specs=[pl.BlockSpec(memory_space=pltpu.SMEM)] + [o[1] for o in operands],
            out_specs=[o[1] for o in outs],
            scratch_shapes=[pltpu.VMEM(shape, kind) for shape, kind in state] + [
                pltpu.VMEM((pairs, 2 * MB, inner), f32),
                pltpu.VMEM((pairs, 2 * MB, pair), f32),
                pltpu.VMEM((pairs, 2 * MB, pair), f32),
                pltpu.VMEM((pairs, 2 * MB, inner), f32),
                pltpu.VMEM((pairs, 2 * MB, inner), bf16),
                pltpu.VMEM((pairs, 2 * MB, pair), bf16),
                pltpu.VMEM((pairs, MB, pair), f32),
            ] + comm,
        ),
        out_shape=[o[0] for o in outs],
        compiler_params=pltpu.CompilerParams(
            collective_id=collective_id if feeds else None, has_side_effects=bool(feeds), vmem_limit_bytes=56 * 1024 * 1024
        ),
        name="inner_backward",
    )(restarts.astype(f32), *[o[0] for o in operands])


def norm_parts(v, width):
    centered = v - jnp.sum(v, -1, keepdims=True) * (1.0 / width)
    scale = lax.rsqrt(jnp.sum(centered * centered, -1, keepdims=True) * (1.0 / width) + epsilon)
    return centered * scale, scale


def feed_terms(*items):
    for outs, left, right in items:
        width = left.shape[1]
        for i, out in enumerate(outs):
            both = low(dot_tn(left[...], right[:, i * 256 : (i + 1) * 256]))
            out[0:width] = both[:, :128]
            out[width : 2 * width] = both[:, 128:]


def middle_kernel(span, mixed_ref, tok_ref, cot_ref, wout_ref, gate_ref, up_ref, down_ref, gain_ref,
                  block_ref, hid_ref, gmix_ref, gwo_ref, t0, t1, t2, t3, t4, t5, gfeed_ref,
                  mixed_got, acts, cots, unit, scales, h_in, gg, gu, ha, pg0, po0, out_core, in_core, out_diag, in_diag, out_y, in_y,
                  branch, branch_row, send_sem, recv_sem, local_sem):
    rows, groups = lax.axis_size("row"), lax.axis_size("group")
    row, group, feat = lax.axis_index("row"), lax.axis_index("group"), lax.axis_index("feat")
    count, width = tok_ref.shape
    cols = mixed_ref.shape[1]
    core, y = lax.rem(feat, 2), feat // 2
    core_mate, y_mate = {"feat": feat + 1 - 2 * core}, {"feat": feat + 2 - 4 * y}
    here = row * groups + group
    places = rows * groups
    others = [lax.rem(here + o, places) for o in range(1, places)]
    seq_mates = [{"row": t // groups, "group": lax.rem(t, groups)} for t in others]
    copies = Copies(send_sem, recv_sem)
    send = copies.send
    slot = lambda ref, s: ref.at[s * count : (s + 1) * count]

    greet([core_mate, y_mate] + seq_mates)
    lanes = pl.ds(pl.multiple_of(group * cols, 128), cols)
    moves = [
        send(mixed_ref.at[rows_at(t * span, span)], mixed_got.at[rows_at(row * span, span), lanes], mate)
        for t, mate in zip(others, seq_mates)
    ]
    own = pltpu.make_async_copy(
        mixed_ref.at[rows_at(here * span, span)], mixed_got.at[rows_at(row * span, span), lanes], local_sem.at[0]
    )
    own.start()
    cot_core = send(cot_ref, slot(cots, 1), core_mate)
    cot_y = send(cot_ref, slot(cots, 2), y_mate)
    cots[0:count] = cot_ref[...]
    own.wait()
    for copy in moves:
        copy.wait_recv()
    hidden = tok_ref[...].astype(f32) + dot(mixed_got[:, :width], wout_ref[:width])
    h_in[...] = hidden
    unit_two, scale_two = norm_parts(hidden, width)
    unit[...] = unit_two
    scales[...] = jnp.broadcast_to(scale_two, scales.shape)
    acts[0:count] = low(unit_two * gain_ref[...])
    act_core = send(slot(acts, 0), slot(acts, 1), core_mate)
    act_y = send(slot(acts, 0), slot(acts, 2), y_mate)
    cot_y.wait_recv()
    cot_diag = send(slot(cots, 2), slot(cots, 3), core_mate)

    def feed(s):
        part = slice(s * count, (s + 1) * count)
        gate_pre, up_value = dot(acts[part], gate_ref[...]), dot(acts[part], up_ref[...])
        grad = dot(cots[part], down_ref[...])
        sig = jax.nn.sigmoid(gate_pre)
        silu = gate_pre * sig
        ha[part] = low(silu * up_value)
        gg[part] = low(grad * up_value * sig * (1.0 + gate_pre * (1.0 - sig)))
        gu[part] = low(grad * silu)
        back = dot_nt(gg[part], gate_ref[...]) + dot_nt(gu[part], up_ref[...])
        return back, dot_nt(ha[part], down_ref[...])

    pg0[...], po0[...] = feed(0)
    act_core.wait_recv()
    cot_core.wait_recv()
    back, forth = feed(1)
    out_core[0], out_core[1] = low(back), low(forth)
    core_sums = [send(out_core.at[i], in_core.at[i], core_mate) for i in range(2)]
    act_y.wait_recv()
    act_diag = send(slot(acts, 2), slot(acts, 3), core_mate)
    act_diag.wait_recv()
    cot_diag.wait_recv()
    back, forth = feed(3)
    out_diag[0], out_diag[1] = low(back), low(forth)
    diag_sums = [send(out_diag.at[i], in_diag.at[i], core_mate) for i in range(2)]
    back, forth = feed(2)
    y_sums = []
    for i, value in enumerate((back, forth)):
        diag_sums[i].wait_recv()
        out_y[i] = low(value + in_diag[i].astype(f32))
        y_sums.append(send(out_y.at[i], in_y.at[i], y_mate))
    feed_terms(((t0, t1), acts, gg), ((t2, t3), acts, gu), ((t4, t5), cots, ha))
    core_sums[0].wait_recv()
    y_sums[0].wait_recv()
    grad_act = pg0[...] + in_core[0].astype(f32) + in_y[0].astype(f32)
    unit_two = unit[...]
    gfeed_ref[...] = jnp.sum(grad_act * unit_two, 0, keepdims=True)
    w = grad_act * gain_ref[...]
    inv = 1.0 / width
    grad = cot_ref[...].astype(f32) + scales[:, 0:1] * (
        w - jnp.sum(w, -1, keepdims=True) * inv - unit_two * (jnp.sum(w * unit_two, -1, keepdims=True) * inv)
    )
    hid_ref[...] = grad
    branch[...] = low(grad)
    moves = [
        send(branch.at[rows_at((t // groups) * span, span)], branch_row.at[rows_at(here * span, span)], mate)
        for t, mate in zip(others, seq_mates)
    ]
    branch_row[rows_at(here * span, span)] = branch[rows_at(row * span, span)]
    core_sums[1].wait_recv()
    y_sums[1].wait_recv()
    block_ref[...] = low(h_in[...] + po0[...] + in_core[1].astype(f32) + in_y[1].astype(f32))
    for copy in moves:
        copy.wait_recv()
    gmix_ref[...] = dot_nt(branch_row[...], wout_ref[rows_at(group * cols, cols)])
    gwo_ref[...] = low(dot_tn(branch_row[...], mixed_ref[...]))
    for copy in copies.started:
        copy.wait_send()


def middle(mixed_row, tokens, cotangent, out_weight, gate_weight, up_weight, down_weight, gain, span, collective_id):
    rows, groups = lax.axis_size("row"), lax.axis_size("group")
    length, cols = mixed_row.shape
    count, width = tokens.shape
    hidden = gate_weight.shape[1]
    copies = 2 * (rows * groups - 1) + 12
    vmem = pl.BlockSpec(memory_space=pltpu.VMEM)
    outs = [
        ((count, width), bf16), ((count, width), f32), ((length, cols), f32), ((width, cols), bf16),
        *[((2 * width, 128), bf16)] * 6, ((1, width), f32),
    ]
    two = pltpu.VMEM((2, count, width), bf16)
    return pl.pallas_call(
        partial(middle_kernel, span),
        in_specs=[vmem] * 8,
        out_specs=[vmem] * len(outs),
        out_shape=[jax.ShapeDtypeStruct(*o) for o in outs],
        scratch_shapes=[
            pltpu.VMEM((count, groups * cols), bf16),
            pltpu.VMEM((4 * count, width), bf16),
            pltpu.VMEM((4 * count, width), bf16),
            pltpu.VMEM((count, width), f32),
            pltpu.VMEM((count, 128), f32),
            pltpu.VMEM((count, width), f32),
            pltpu.VMEM((4 * count, hidden), bf16),
            pltpu.VMEM((4 * count, hidden), bf16),
            pltpu.VMEM((4 * count, hidden), bf16),
            pltpu.VMEM((count, width), f32),
            pltpu.VMEM((count, width), f32),
            two, two, two, two, two, two,
            pltpu.VMEM((count, width), bf16),
            pltpu.VMEM((length, width), bf16),
            pltpu.SemaphoreType.DMA((copies,)),
            pltpu.SemaphoreType.DMA((copies,)),
            pltpu.SemaphoreType.DMA((1,)),
        ],
        compiler_params=pltpu.CompilerParams(
            collective_id=collective_id, has_side_effects=True, vmem_limit_bytes=56 * 1024 * 1024
        ),
        name="middle",
    )(mixed_row, tokens, cotangent, out_weight, gate_weight, up_weight, down_weight, gain)


TAIL_SLOTS = [
    ([], ["FZ1", "FZ2", "FZ0"]),
    ([], ["CORE4", "CORE3"]),
    ([], ["CORE0"]),
    (["CORE4"], ["CORE1", "Y4"]),
    (["CORE3"], ["CORE2", "Y3"]),
    (["CORE0"], ["Y0"]),
    (["FZ1"], ["FX1"]),
    (["CORE1"], []),
    (["CORE2"], []),
    ([], ["PART0"]),
    ([], ["SC0"]),
    (["Y4"], ["Y2", "Z4"]),
    (["SC0"], []),
    (["FZ2"], ["FX2"]),
    (["Y3"], ["Y1", "Z3"]),
    (["FX1"], []),
    (["FZ0"], ["FX0"]),
    (["Y0"], ["SY0", "Z0"]),
    (["Z4"], ["ZA4"]),
    (["Y2"], []),
    (["Z3"], ["ZA3"]),
    (["PART0"], []),
    (["Y1"], []),
    (["Z0"], ["Z1"]),
    (["SY0"], []),
    (["ZA4"], ["P4", "Z2"]),
    (["FX2"], []),
    (["ZA3"], ["P3", "ZA0"]),
    (["P4"], ["Q4"]),
    (["FX0"], []),
    (["Z1"], ["ZA1"]),
    (["P3"], ["Q3"]),
    (["Z2"], ["ZA2"]),
    (["ZA0"], ["P0", "SZ0"]),
    (["Q4"], ["C4"]),
    (["C4"], []),
    (["ZA1"], ["P1", "HOME0"]),
    (["Q3"], ["C3"]),
    (["P0"], ["Q0"]),
    (["ZA2"], ["P2"]),
    (["C3"], []),
    (["P1"], ["Q1"]),
    (["SZ0"], ["SX0"]),
    (["P2"], ["Q2"]),
    (["Q0"], ["C0"]),
    (["C0"], []),
    (["Q1"], ["C1"]),
    (["HOME0"], []),
    (["SX0"], []),
    (["C1"], []),
    (["Q2"], ["C2"]),
    (["C2"], []),
]
TAIL_GROUP_FIRST = (True, False, True, True, False)


FEED_SLOTS = [
    (0, [], ["X1", "X2"]),
    (8, ["X1"], ["X0", "Z1"]),
    (11, ["X2"], ["X4", "Z2"]),
    (13, ["Z1"], ["ZA1"]),
    (14, ["X0"], ["X3"]),
    (16, ["Z2"], ["Z0"]),
    (18, ["X4"], ["X5"]),
    (19, ["ZA1"], ["ZA2"]),
    (21, ["X3"], ["XA1"]),
    (22, ["Z0"], ["ZA0"]),
    (24, ["X5"], []),
    (25, ["ZA2"], ["XA2", "Z5"]),
    (27, ["XA1"], []),
    (28, ["ZA0"], ["XA0", "Z3"]),
    (30, ["XA2"], []),
    (31, ["Z5"], ["Z4"]),
    (32, ["XA0", "Z3", "Z4"], []),
]
FEED_WHOLE = 3


def tail_kernel(span, shapes, feeds, act_ref, unit_ref, gq_ref, gk_ref, gv_ref, de_ref, slope_ref, wq_ref, wk_ref, wv_ref, wr_ref,
                gwo_ref, gw1, gb1, gw2, gb2, ggain, gbias, gfeed, stat_ref, *refs):
    rows, groups = lax.axis_size("row"), lax.axis_size("group")
    row, group, feat = lax.axis_index("row"), lax.axis_index("group"), lax.axis_index("feat")
    core, y = lax.rem(feat, 2), feat // 2
    core_mate, y_mate = {"feat": feat + 1 - 2 * core}, {"feat": feat + 2 - 4 * y}
    row_mates, group_mates = mates("row"), mates("group")
    count = len(shapes)
    feed_in, refs = refs[:feeds], refs[feeds:]
    outs, (home_out, small_out), refs = refs[:count], refs[count : count + 2], refs[count + 2 :]
    feed_out, refs = refs[:feeds], refs[feeds:]
    own, got_core, sum_core, got_y, sum_y, got_row = (refs[i * count : (i + 1) * count] for i in range(6))
    part, part_got, part_sum, small, small_core, small_got, send_sem, recv_sem = refs[6 * count :]
    length, width = act_ref.shape
    cols = gwo_ref.shape[1]
    pairs, pair, inner = gw1.shape
    head_dim = pair // 2
    copies = Copies(send_sem, recv_sem)
    moves = {}

    def start(name, *what):
        moves[name] = [copies.send(*w) for w in what]

    greet([core_mate, y_mate] + row_mates + group_mates)

    half = [h // 2 for h, _ in shapes]
    quarter = [h // 4 for h, _ in shapes]
    piece = [h // (4 * rows) for h, _ in shapes]
    unit = feed_in[0].shape[0]
    place = (core * 2 + y) * rows + row
    source = list(own[:3]) + [gwo_ref, own[4]]
    grad_refs = (gq_ref, gk_ref, gv_ref)
    lanes = pl.ds(pl.multiple_of(group * cols, 128), cols)

    def token_gradient():
        logits = low(de_ref[0:length] * slope_ref[...])
        total = dot_nt(logits, wr_ref[...])
        for grad, weight in zip(grad_refs, (wq_ref, wk_ref, wv_ref)):
            total = total + dot_nt(grad[0:length], weight[:, lanes])
        for r in range(rows):
            for g in range(groups):
                part[g, r * span : (r + 1) * span] = low(total[(r * groups + g) * span : (r * groups + g + 1) * span])
        start("PART0", *[(part.at[lax.rem(group + o, groups)], part_got.at[o - 1], group_mates[o - 1]) for o in range(1, groups)])
        small[...] = jnp.zeros_like(small)
        small[0 : 2 * pairs] = dot_tn(logits, act_ref[...])[0 : 2 * pairs]
        for p in range(pairs):
            for h in range(2):
                n = 2 * p + h
                small[6 + n // 3 : 7 + n // 3, (n % 3) * inner : (n % 3 + 1) * inner] = gb1[p, h * MB : h * MB + 1]
            small[9:10, p * pair : (p + 1) * pair] = gb2[p, 0:1] + gb2[p, MB : MB + 1]
        small[8:9, 0:cols] = jnp.sum(ggain[...], 0, keepdims=True)
        small[8:9, cols : 2 * cols] = jnp.sum(gbias[...], 0, keepdims=True)
        small[9:10, width - 384 : width - 256] = jnp.sum(logits.astype(f32), 0, keepdims=True)
        small[9:10, width - 256 : width - 128] = stat_ref[0:1]
        small[9:10, width - 128 : width] = stat_ref[1:2]
        small[10:11] = jnp.sum(total * unit_ref[...], 0, keepdims=True)
        small[11:12] = gfeed[...]

    def finish(name):
        for copy in moves[name]:
            copy.wait_recv()
        kind, i = name[:-1], int(name[-1])
        if kind == "CORE":
            sum_core[i][...] = add_low(source[i][rows_at(core * half[i], half[i])], got_core[i][...])
        if kind == "Y":
            sum_y[i][...] = add_low(sum_core[i][rows_at(y * quarter[i], quarter[i])], got_y[i][...])
        if kind == "Z":
            value = sum_y[i][rows_at(row * piece[i], piece[i])].astype(f32)
            for o in range(1, rows):
                value = value + got_row[i][o - 1].astype(f32)
            outs[i][group, rows_at(place * piece[i], piece[i])] = low(value)
        if kind == "PART":
            value = part[group].astype(f32)
            for o in range(1, groups):
                value = value + part_got[o - 1].astype(f32)
            part_sum[...] = low(value)
            home_out[rows_at(row * span, span)] = part_sum[rows_at(row * span, span)]
        if kind == "SC":
            small_core[...] = small[...] + small_got[0]
        if kind == "SY":
            small_got[2 + row] = small_core[...] + small_got[1]
        if kind == "SZ":
            value = small_got[2]
            for r in range(1, rows):
                value = value + small_got[2 + r]
            small_out[group] = value

    def begin(name):
        kind, i = name[:-1], int(name[-1])
        if kind == "PART":
            token_gradient()
        if kind == "HOME":
            here = home_out.at[rows_at(row * span, span)]
            start(name, *[
                (part_sum.at[rows_at(lax.rem(row + o, rows) * span, span)], here, row_mates[o - 1]) for o in range(1, rows)
            ])
        if kind == "SC":
            start(name, (small, small_got.at[0], core_mate))
        if kind == "SY":
            start(name, (small_core, small_got.at[1], y_mate))
        if kind == "SZ":
            here = small_got.at[2 + row]
            start(name, *[(here, here, mate) for mate in row_mates])
        if kind == "SX":
            here = small_out.at[group]
            start(name, *[(here, here, mate) for mate in group_mates])
        if kind == "FZ":
            here = feed_out[i].at[group, rows_at(row * unit, unit)]
            here[...] = feed_in[i][...]
            start(name, *[(here, here, mate) for mate in row_mates])
        if kind == "FX":
            here = feed_out[i].at[group]
            start(name, *[(here, here, mate) for mate in group_mates])
        if kind == "CORE":
            if i < 3:
                own[i][...] = low(dot_tn(act_ref[...], grad_refs[i][0:length]))
            if i == 4:
                for p in range(pairs):
                    own[4][p * pair : (p + 1) * pair] = low(gw1[p])
                    own[4][cols + p * pair : cols + (p + 1) * pair] = low(gw2[p])
            start(name, (source[i].at[rows_at((1 - core) * half[i], half[i])], got_core[i], core_mate))
        if kind == "Y":
            start(name, (sum_core[i].at[rows_at((1 - y) * quarter[i], quarter[i])], got_y[i], y_mate))
        if kind == "Z":
            start(name, *[
                (sum_y[i].at[rows_at(lax.rem(row + o, rows) * piece[i], piece[i])], got_row[i].at[o - 1], row_mates[o - 1])
                for o in range(1, rows)
            ])
        if kind == "ZA":
            here = outs[i].at[group, rows_at(place * piece[i], piece[i])]
            start(name, *[(here, here, mate) for mate in row_mates])
        if kind in ("P", "Q", "C"):
            quarters = rows_at((core * 2 + y) * quarter[i], quarter[i])
            halves = rows_at(core * half[i], half[i])
            by_group = TAIL_GROUP_FIRST[i] == (kind == "P")
            if kind == "C":
                here, to = outs[i].at[:, halves], [core_mate]
            elif by_group:
                here, to = outs[i].at[group, quarters if kind == "P" else halves], group_mates
            else:
                here, to = (outs[i].at[group, quarters] if kind == "P" else outs[i].at[:, quarters]), [y_mate]
            start(name, *[(here, here, mate) for mate in to])

    for done, begun in TAIL_SLOTS:
        for name in done:
            finish(name)
        for name in begun:
            begin(name)
    for copy in copies.started:
        copy.wait_send()


def tail(act_row, unit_row, grads, de, slope, weights, rate_weight, grad_out, states, grad_feed_gain, stat, feed_parts, span, collective_id):
    rows, groups = lax.axis_size("row"), lax.axis_size("group")
    length, width = act_row.shape
    cols = grad_out.shape[1]
    inner = states[0].shape[-1]
    shapes = [(width, cols)] * 4 + [(2 * cols, inner)]
    count, feeds = len(shapes), len(feed_parts)
    unit, wide = feed_parts[0].shape
    copies = count * (2 + 2 * (rows - 1) + (groups - 1) + 2) + (groups - 1) + (rows - 1) + 2 + (rows - 1) + (groups - 1)
    copies += feeds * (rows + groups - 2)
    vmem = pl.BlockSpec(memory_space=pltpu.VMEM)
    operands = [act_row, unit_row, *grads, de, slope, *weights, rate_weight, grad_out, *states, grad_feed_gain, stat, *feed_parts]
    outs = [((groups, h, w), bf16) for h, w in shapes]
    outs += [((rows * span, width), bf16), ((groups, 16, width), f32)]
    outs += [((groups, rows * unit, wide), bf16)] * feeds
    scratch = [pltpu.VMEM((h, w), bf16) for h, w in shapes]
    scratch += [pltpu.VMEM((h // 2, w), bf16) for h, w in shapes] * 2
    scratch += [pltpu.VMEM((h // 4, w), bf16) for h, w in shapes] * 2
    scratch += [pltpu.VMEM((rows - 1, h // (4 * rows), w), bf16) for h, w in shapes]
    scratch += [
        pltpu.VMEM((groups, rows * span, width), bf16),
        pltpu.VMEM((groups - 1, rows * span, width), bf16),
        pltpu.VMEM((rows * span, width), bf16),
        pltpu.VMEM((16, width), f32),
        pltpu.VMEM((16, width), f32),
        pltpu.VMEM((2 + rows, 16, width), f32),
        pltpu.SemaphoreType.DMA((copies,)),
        pltpu.SemaphoreType.DMA((copies,)),
    ]
    return pl.pallas_call(
        partial(tail_kernel, span, shapes, feeds),
        in_specs=[vmem] * len(operands),
        out_specs=[vmem] * len(outs),
        out_shape=[jax.ShapeDtypeStruct(*o) for o in outs],
        scratch_shapes=scratch,
        compiler_params=pltpu.CompilerParams(
            collective_id=collective_id, has_side_effects=True, vmem_limit_bytes=60 * 1024 * 1024
        ),
        name="tail",
    )(*operands)


def normalize(vector, gain):
    centered = vector - jnp.mean(vector, -1, keepdims=True)
    variance = jnp.mean(centered * centered, -1, keepdims=True)
    inv_scale = lax.rsqrt(variance + epsilon)
    normed_unit = centered * inv_scale
    return (normed_unit * gain, normed_unit, inv_scale)


def norm_back(grad_out, gain, normed_unit, inv_scale):
    scaled = grad_out * gain
    return inv_scale * (
        scaled
        - jnp.mean(scaled, -1, keepdims=True)
        - normed_unit * jnp.mean(scaled * normed_unit, -1, keepdims=True)
    )


SEQ = ("row", "group")


def per_device(
    tokens,
    cotangent,
    doc_starts,
    mixer_gain,
    query_weight,
    key_weight,
    value_weight,
    out_weight,
    rate_weight,
    rate_bias,
    first_init,
    first_bias_init,
    second_init,
    second_bias_init,
    inner_gain,
    inner_bias,
    feed_gain,
    gate_weight,
    up_weight,
    down_weight,
):
    rows, span, width = tokens.shape
    heads, head_dim, inner = first_init.shape
    groups = lax.axis_size("group")
    feats = lax.axis_size("feat")
    row, group = lax.axis_index("row"), lax.axis_index("group")
    count = rows * span
    length = span * rows * groups
    blocks = length // MB
    pairs = -(-heads // (2 * groups))
    mine = 2 * pairs
    pair = 2 * head_dim
    cols = mine * head_dim
    spare = mine * groups - heads

    def own_heads(array, axis, per_head=1):
        if spare:
            pad = [(0, 0)] * array.ndim
            pad[axis] = (0, spare * per_head)
            array = jnp.pad(array, pad)
        return lax.dynamic_slice_in_dim(array, group * mine * per_head, mine * per_head, axis)

    def to_rows(array):
        got = lax.all_to_all(jnp.repeat(array, groups, 0), SEQ, 0, 0, tiled=True)
        return got.reshape(length, array.shape[-1])

    row_in = to_rows(tokens).astype(f32)
    act_row = low(normalize(row_in, mixer_gain)[0])
    w_q, w_k, w_v = (own_heads(w, 1, head_dim) for w in (query_weight, key_weight, value_weight))
    w_r = own_heads(rate_weight, 1)
    queries, keys, values = (dot(act_row, w) for w in (w_q, w_k, w_v))
    logits = dot(act_row, w_r) + own_heads(rate_bias, 0)
    sigma = jax.nn.sigmoid(logits)
    rates = sigma / head_dim
    e = jnp.broadcast_to(
        rates.reshape(blocks, MB, pairs, 2).transpose(0, 2, 3, 1).reshape(blocks, pairs, 2 * MB, 1),
        (blocks, pairs, 2 * MB, pair),
    )
    block_ids = jnp.arange(blocks, dtype=jnp.int32)
    starts = lax.dynamic_index_in_dim(doc_starts, row, 0, False)
    restarts = ((block_ids == 0) | jnp.any(starts[:, None] == block_ids[None], 0)).astype(jnp.int32)
    pack = lambda a: own_heads(a, 0).reshape(pairs, pair, inner)
    start_first = pack(first_init)
    start_second = pack(second_init - jnp.mean(second_init, 1, keepdims=True))
    start_first_bias = jnp.repeat(own_heads(first_bias_init, 0).reshape(pairs, 2, 1, inner), MB, 2).reshape(
        pairs, 2 * MB, inner
    )
    centered = own_heads(second_bias_init - jnp.mean(second_bias_init, 1, keepdims=True), 0)
    start_second_bias = (
        jnp.eye(2, dtype=f32)[None, :, None, :, None] * centered.reshape(pairs, 1, 1, 2, head_dim)
    ) * jnp.ones((1, 1, MB, 1, 1), f32)
    start_second_bias = start_second_bias.reshape(pairs, 2 * MB, pair)
    gain, bias = own_heads(inner_gain, 0).reshape(1, cols), own_heads(inner_bias, 0).reshape(1, cols)
    *saved, mixed = forward_inner(
        jnp.concatenate([restarts, jnp.zeros((1,), jnp.int32)]),
        queries, keys, values, e, start_first, start_first_bias, start_second, start_second_bias, gain, bias,
    )
    mixed_row = low(mixed[MB:])

    flat_in = tokens.astype(f32).reshape(count, width)
    all_heads = jnp.pad(out_weight, ((0, spare * head_dim), (0, 0))) if spare else out_weight
    block_out, grad_hidden, grad_mixed, grad_out_rows, *feed_terms, grad_feed_gain = middle(
        mixed_row, tokens.reshape(count, width), cotangent.reshape(count, width), all_heads,
        gate_weight, up_weight, down_weight, feed_gain.reshape(1, width), span, 1,
    )

    grad_q, grad_k, grad_v, grad_e, g_first, g_first_bias, g_second, g_second_bias, g_gain, g_bias, *feed_sums = (
        backward_inner(restarts, queries, keys, values, grad_mixed, e, saved, gain, bias, feed_terms, 2)
    )

    lanes = lambda array: jnp.pad(array, ((0, 0), (0, 128 - mine)))
    _, unit_row, _ = normalize(row_in, mixer_gain)
    all_cols = lambda w: jnp.pad(w, ((0, 0), (0, spare * head_dim))) if spare else w
    used = (group * mine + jnp.arange(mine)) < heads
    top = jnp.max(jnp.where(used[None], logits, jnp.finfo(f32).min))
    place = row * feats + lax.axis_index("feat")
    stat = jnp.stack([lanes(jnp.sum(logits, 0, keepdims=True))[0], jnp.where(jnp.arange(128) == place, top, 0.0)])
    *reduced, = tail(
        act_row, unit_row, (grad_q, grad_k, grad_v), grad_e, lanes(sigma * (1.0 - sigma) / head_dim),
        [all_cols(w) for w in (query_weight, key_weight, value_weight)], lanes(w_r), grad_out_rows,
        (g_first, g_first_bias, g_second, g_second_bias, g_gain, g_bias), grad_feed_gain, stat,
        feed_sums[FEED_WHOLE:], span, 3,
    )
    arrays, (got, small), feed_sums = reduced[:5], reduced[5:7], feed_sums[:FEED_WHOLE] + reduced[7:]

    grad_act_one = got.astype(f32)
    _, unit_one, scale_one = normalize(flat_in, mixer_gain)
    input_grad = grad_hidden + norm_back(grad_act_one, mixer_gain, unit_one, scale_one)

    def feed_joined(*cuts):
        flat = [cut.reshape(2 * width, 128) for cut in cuts]
        return jnp.concatenate([cut[i * width : (i + 1) * width] for cut in flat for i in range(2)], 1).astype(f32)

    feed_grads = [feed_joined(*feed_sums[2 * i : 2 * i + 2]) for i in range(3)]
    joined = lambda array: jnp.concatenate([array[g] for g in range(groups)], 1)[:, :width].astype(f32)
    g_query, g_key, g_value, g_out = (joined(array) for array in arrays[:4])
    states = arrays[4].reshape(groups, 2, cols, inner)
    g_first, g_second = (
        states[:, i].reshape(groups * mine, head_dim, inner)[:heads].astype(f32) for i in range(2)
    )
    g_second = g_second - jnp.mean(g_second, 1, keepdims=True)
    per_head = lambda array, size: array.reshape(groups * mine, size)[:heads]
    g_rate = small[:, :mine].reshape(groups * mine, width)[:heads].T
    g_first_bias = per_head(small[:, 6:8].reshape(groups, -1)[:, : mine * inner], inner)
    g_gain, g_bias = per_head(small[:, 8, :cols], head_dim), per_head(small[:, 8, cols : 2 * cols], head_dim)
    g_second_bias = per_head(small[:, 9, :cols], head_dim)
    g_second_bias = g_second_bias - jnp.mean(g_second_bias, 1, keepdims=True)
    g_rate_bias = small[:, 9, width - 384 : width - 384 + mine].reshape(-1)[:heads]
    total = jnp.sum(small[:, 9, width - 256 : width - 256 + mine].reshape(-1)[:heads])
    g_mixer, g_feed = jnp.sum(small[:, 10], 0), jnp.sum(small[:, 11], 0)
    tops = small[:, 9, width - 128 : width - 128 + rows * feats]
    stats = jnp.stack([total / (rows * groups * feats * count * heads), jnp.max(tops)])
    return (
        block_out.reshape(rows, span, width),
        input_grad.reshape(rows, span, width),
        g_mixer,
        g_query,
        g_key,
        g_value,
        g_out.T,
        g_rate,
        g_rate_bias,
        g_first,
        g_first_bias,
        g_second,
        g_second_bias,
        g_gain,
        g_bias,
        g_feed,
        *feed_grads,
        stats,
    )


def solution(mesh):
    feats = mesh.shape["feat"]

    def run(*arrays):
        rows = arrays[0].shape[0] // feats
        grid = jax.sharding.Mesh(mesh.devices.reshape(rows, -1, feats), ("row", "group", "feat"))
        by_token = P("feat", SEQ, None)
        by_hidden = P(None, "feat")
        return jax.shard_map(
            per_device,
            mesh=grid,
            in_specs=(by_token, by_token, P("feat", None)) + (P(),) * 14 + (by_hidden,) * 3,
            out_specs=(by_token, by_token) + (P(),) * 14 + (by_hidden,) * 3 + (P(),),
            check_vma=False,
        )(*arrays)

    return run
```

```python
from functools import partial

import jax
import jax.numpy as jnp
from jax import lax
from jax.experimental import pallas as pl
from jax.experimental.pallas import tpu as pltpu
from jax.sharding import PartitionSpec as P

MB = 16
epsilon = 1e-05
f32, bf16 = jnp.float32, jnp.bfloat16


def dot(a, b):
    return lax.dot_general(a, b, (((1,), (0,)), ((), ())), preferred_element_type=f32)


def dot_nt(a, b):
    return lax.dot_general(a, b, (((1,), (1,)), ((), ())), preferred_element_type=f32)


def dot_tn(a, b):
    return lax.dot_general(a, b, (((0,), (0,)), ((), ())), preferred_element_type=f32)


def low(v):
    return v.astype(bf16)


def gelu_parts(z):
    a = jnp.abs(z)
    d = 1.0 + 0.23164189 * a
    t = pl.reciprocal(d, approx=True)
    t = t * (2.0 - d * t)
    ex = jnp.exp(-0.5 * (z * z))
    poly = t * (
        0.127414796 + t * (-0.142248368 + t * (0.7107068705 + t * (-0.7265760135 + t * 0.5307027145)))
    )
    h = poly * ex
    cdf = jnp.where(z >= 0, 1.0 - h, h)
    pdf = 0.3989422804014327 * ex
    return z * cdf, cdf + z * pdf, pdf


def lane_sum(v):
    return jnp.sum(v, -1, keepdims=True)


def masks(head_dim):
    pair = 2 * head_dim
    rows, cols = 2 * MB, pair
    r = lax.broadcasted_iota(jnp.int32, (rows, cols), 0)
    c = lax.broadcasted_iota(jnp.int32, (rows, cols), 1)
    own = ((r < MB) == (c < head_dim)).astype(f32)
    r = lax.broadcasted_iota(jnp.int32, (rows, rows), 0)
    c = lax.broadcasted_iota(jnp.int32, (rows, rows), 1)
    same = (r < MB) == (c < MB)
    causal = (same & (c <= r)).astype(f32)
    return own, causal, same.astype(bf16)


def spread(v, own):
    return jnp.concatenate([v, v], 0) * own


def fold(v):
    return v[:MB] + v[MB:]


def twice(v):
    return jnp.concatenate([v, v], 1)


def pair_index(p, pairs, array):
    return jnp.minimum(lax.axis_index("group") * pairs + p, array.shape[0] - 1)


def rate_rows(rates, p):
    return jnp.concatenate([jnp.broadcast_to(rates[:, n : n + 1], rates.shape) for n in (2 * p, 2 * p + 1)], 0)


def in_turn(parts):
    while parts:
        parts = [part for part in parts if next(part, parts) is not parts]


def forward_kernel(pairs, head_dim, restart_ref, q_ref, k_ref, v_ref, rate_ref, w1i_ref, b1i_ref, w2i_ref, par_ref,
                   big_ref, mid_ref, small_ref, n1_ref, pq_ref, uq_ref, n2_ref, out_ref,
                   w1, b1, w2, b2, s_q1, s_x2, s_e2, s_w2, s_b2, s_q):
    j = pl.program_id(0)
    pair = 2 * head_dim
    inv = 1.0 / head_dim
    own, causal, ones = masks(head_dim)

    @pl.when(restart_ref[j] > 0)
    def _():
        for p in range(pairs):
            n = pair_index(p, pairs, w1i_ref)
            first_bias = b1i_ref[n]
            second = w2i_ref[n]
            second_bias = par_ref[0, n] * own
            w1[p] = w1i_ref[n]
            for h in range(2):
                b1[p, h * MB : (h + 1) * MB] = jnp.broadcast_to(first_bias[h : h + 1], (MB, first_bias.shape[1]))
                half = second[h * head_dim : (h + 1) * head_dim]
                w2[p, h * head_dim : (h + 1) * head_dim] = half - jnp.sum(half, 0, keepdims=True) * inv
            b2[p] = second_bias - (lane_sum(second_bias) * inv) * own

    loaded = [
        (s_q1[p], s_x2[p], s_e2[p], s_w2[p], s_b2[p], s_q[p], w1[p], w2[p], b1[p], b2[p], rate_rows(rate_ref[...], p))
        for p in range(pairs)
    ]
    tokens = [
        [ref[:, p * pair : (p + 1) * pair] for ref in (q_ref, k_ref, v_ref)]
        + [par_ref[i, pair_index(p, pairs, w1i_ref)] for i in (1, 2)]
        for p in range(pairs)
    ]
    writes = []

    def write(ref, index, value):
        writes.append((ref, index, value))

    def outputs_before(p):
        q1p, x2p, e2p, w2p, b2p, qp = loaded[p][:6]
        gain, bias = tokens[p][3:]
        p2, lq, _ = gelu_parts(q1p)
        p2b = low(p2)
        yield
        n2 = causal * (dot_nt(p2b, x2p) + 1.0)
        q2 = dot_nt(p2b, w2p)
        yield
        q2 = q2 * own - dot(low(n2), e2p) + b2p
        yield
        sq = lax.rsqrt(lane_sum(q2 * q2) * inv + epsilon)
        uq = q2 * sq
        write(out_ref, (slice(None), slice(p * pair, (p + 1) * pair)), qp + fold(uq) * gain + bias)
        write(pq_ref, (0, p, slice(0, 2 * MB)), p2b)
        write(pq_ref, (0, p, slice(2 * MB, 4 * MB)), low(lq))
        write(uq_ref, (0, p, slice(0, 2 * MB)), uq)
        write(uq_ref, (0, p, slice(2 * MB, 4 * MB)), jnp.broadcast_to(sq, uq.shape))
        write(n2_ref, (0, p), low(n2))

    def inner_step(p):
        w1c, w2c, b1c, b2c, e = loaded[p][6:]
        qc, kc, vc, gain, bias = tokens[p]
        kb, qb = low(spread(kc, own)), low(spread(qc, own))
        w1b, w2b = low(w1c), low(w2c)
        kq = dot(jnp.concatenate([kb, qb], 0), w1b)
        yield
        z1 = kq[: 2 * MB] + b1c
        x2, l1, pdf = gelu_parts(z1)
        x2b = low(x2)
        yield
        c = dot_nt(x2b, w2b)
        n1 = causal * (dot_nt(qb, kb) + 1.0)
        yield
        c = c * own + b2c
        s = lax.rsqrt(lane_sum(c * c) * inv + epsilon)
        u = c * s
        r = u * (gain * gain) + spread((bias - (vc - kc)) * gain, own)
        yield
        mr, m2 = lane_sum(r) * inv, lane_sum(r * u) * inv
        g2 = s * (r - mr * own - u * m2)
        yield
        h = dot(low(g2), w2b)
        e2b = low(e * g2)
        yield
        g1 = h * l1
        e1b = low(twice(e) * g1)
        yield
        u1 = dot_tn(kb, e1b)
        yield
        q1 = kq[2 * MB :] + b1c - dot(low(n1), e1b)
        yield
        write(w1, p, w1c - u1)
        write(b1, p, b1c - dot(ones, e1b))
        write(w2, p, w2c - dot_tn(e2b, x2b))
        write(b2, p, b2c - dot(ones, e2b))
        write(big_ref, (0, p, slice(0, pair)), w1b)
        write(big_ref, (0, p, slice(pair, 2 * pair)), w2b)
        write(big_ref, (0, p, slice(2 * pair, 2 * pair + 2 * MB)), x2b)
        write(big_ref, (0, p, slice(2 * pair + 2 * MB, 2 * pair + 4 * MB)), e1b)
        write(mid_ref, (0, p, slice(0, 2 * MB)), low(g1))
        write(mid_ref, (0, p, slice(2 * MB, 4 * MB)), low(l1))
        write(mid_ref, (0, p, slice(4 * MB, 6 * MB)), low(h * pdf * (2.0 - z1 * z1)))
        for i, value in enumerate((u, s, r, m2, g2)):
            write(small_ref, (0, p, slice(i * 2 * MB, (i + 1) * 2 * MB)), jnp.broadcast_to(value, u.shape))
        write(n1_ref, (0, p), low(n1))
        for ref, value in ((s_q1, q1), (s_x2, x2b), (s_e2, e2b), (s_w2, w2b), (s_b2, b2c), (s_q, qc)):
            write(ref, p, value)

    in_turn([inner_step(p) for p in range(pairs)] + [outputs_before(p) for p in range(pairs)])
    for ref, index, value in writes:
        ref[index] = value


def forward_inner(restarts, q, k, v, rates, w1i, b1i, w2i, params):
    _, pair, inner = w1i.shape
    blocks, pairs = q.shape[0] // MB, q.shape[1] // pair
    head_dim = pair // 2
    steps = blocks + 1
    last = blocks - 1
    tok = pl.BlockSpec((MB, pairs * pair), lambda j, r: (jnp.minimum(j, last), 0))
    whole = lambda a: pl.BlockSpec(a.shape, lambda j, r: (0,) * a.ndim)

    def per_step(rows, width, dtype):
        return (
            jax.ShapeDtypeStruct((steps, pairs, rows, width), dtype),
            pl.BlockSpec((1, pairs, rows, width), lambda j, r: (j, 0, 0, 0)),
        )

    outs = [
        per_step(2 * pair + 4 * MB, inner, bf16),
        per_step(6 * MB, inner, bf16),
        per_step(10 * MB, pair, f32),
        per_step(2 * MB, 2 * MB, bf16),
        per_step(4 * MB, inner, bf16),
        per_step(4 * MB, pair, f32),
        per_step(2 * MB, 2 * MB, bf16),
        (
            jax.ShapeDtypeStruct((steps * MB, pairs * pair), f32),
            pl.BlockSpec((MB, pairs * pair), lambda j, r: (j, 0)),
        ),
    ]
    return pl.pallas_call(
        partial(forward_kernel, pairs, head_dim),
        grid_spec=pltpu.PrefetchScalarGridSpec(
            num_scalar_prefetch=1,
            grid=(steps,),
            in_specs=[tok, tok, tok, pl.BlockSpec((MB, 128), lambda j, r: (jnp.minimum(j, last), 0))]
            + [whole(a) for a in (w1i, b1i, w2i, params)],
            out_specs=[o[1] for o in outs],
            scratch_shapes=[
                pltpu.VMEM((pairs, pair, inner), f32),
                pltpu.VMEM((pairs, 2 * MB, inner), f32),
                pltpu.VMEM((pairs, pair, inner), f32),
                pltpu.VMEM((pairs, 2 * MB, pair), f32),
                pltpu.VMEM((pairs, 2 * MB, inner), f32),
                pltpu.VMEM((pairs, 2 * MB, inner), bf16),
                pltpu.VMEM((pairs, 2 * MB, pair), bf16),
                pltpu.VMEM((pairs, pair, inner), bf16),
                pltpu.VMEM((pairs, 2 * MB, pair), f32),
                pltpu.VMEM((pairs, MB, pair), f32),
            ],
        ),
        out_shape=[o[0] for o in outs],
        compiler_params=pltpu.CompilerParams(vmem_limit_bytes=48 * 1024 * 1024),
        name="inner_forward",
    )(restarts, q, k, v, rates, w1i, b1i, w2i, params)


MESH = pl.DeviceIdType.MESH


def greet(peers):
    barrier = pltpu.get_barrier_semaphore()
    for peer in peers:
        pl.semaphore_signal(barrier, inc=1, device_id=peer, device_id_type=MESH)
    pl.semaphore_wait(barrier, len(peers))


class Copies:
    def __init__(self, send_sem, recv_sem):
        self.send_sem, self.recv_sem, self.started = send_sem, recv_sem, []

    def make(self, src, dst, peer):
        i = len(self.started)
        copy = pltpu.make_async_remote_copy(
            src_ref=src, dst_ref=dst, send_sem=self.send_sem.at[i], recv_sem=self.recv_sem.at[i],
            device_id=peer, device_id_type=MESH,
        )
        self.started.append(copy)
        return copy

    def send(self, src, dst, peer):
        copy = self.make(src, dst, peer)
        copy.start()
        return copy


def rows_at(start, size):
    return pl.ds(pl.multiple_of(start, 16), size)


def add_low(a, b):
    return (a.astype(f32) + b.astype(f32)).astype(bf16)


def mates(axis):
    size, here = lax.axis_size(axis), lax.axis_index(axis)
    return [{axis: lax.rem(here + o, size)} for o in range(1, size)]


def feed_sum_steps(ins, outs, got_group, sum_group, got_row, full, copies, whole):
    row, group = lax.axis_index("row"), lax.axis_index("group")
    rows, groups = lax.axis_size("row"), lax.axis_size("group")
    row_mates, group_mates = mates("row"), mates("group")
    count = len(ins)
    part = ins[0].shape[0] // groups
    unit = part // rows
    mine = rows_at(row * unit, unit)
    moves = {}
    for i in range(count):
        moves["X", i] = [
            copies.make(ins[i].at[rows_at(lax.rem(group + o, groups) * part, part)], got_group[i].at[o - 1], group_mates[o - 1])
            for o in range(1, groups)
        ]
        moves["Z", i] = [
            copies.make(sum_group[i].at[rows_at(lax.rem(row + o, rows) * unit, unit)], got_row[i].at[o - 1], row_mates[o - 1])
            for o in range(1, rows)
        ]
        if i < whole:
            here = full[i].at[group, mine]
            moves["ZA", i] = [copies.make(here, here, mate) for mate in row_mates]
            here = full[i].at[group]
            moves["XA", i] = [copies.make(here, here, mate) for mate in group_mates]

    def finish(kind, i):
        for copy in moves[kind, i]:
            copy.wait_recv()
        if kind == "X":
            total = ins[i][rows_at(group * part, part)].astype(f32)
            for o in range(1, groups):
                total = total + got_group[i][o - 1].astype(f32)
            sum_group[i][...] = low(total)
        if kind == "Z":
            total = sum_group[i][mine].astype(f32)
            for o in range(1, rows):
                total = total + got_row[i][o - 1].astype(f32)
            if i < whole:
                full[i][group, mine] = low(total)
            else:
                outs[i][...] = low(total)

    def run(slot):
        _, done, begun = FEED_SLOTS[slot]
        if slot == 0:
            greet(row_mates + group_mates)
        for name in done:
            finish(name[:-1], int(name[-1]))
        for name in begun:
            for copy in moves[name[:-1], int(name[-1])]:
                copy.start()
        if slot == len(FEED_SLOTS) - 1:
            for i in range(whole):
                outs[i][...] = full[i][...]
            for copy in copies.started:
                copy.wait_send()

    return [partial(run, slot) for slot in range(len(FEED_SLOTS))]


def backward_kernel(pairs, head_dim, feeds, restart_ref,
                    qq_ref, kq_ref, doq_ref, eq_ref, bigq_ref, g2q_ref, n1_ref, pqq_ref, uqq_ref, n2_ref,
                    q_ref, k_ref, v_ref, do_ref, e_ref, big_ref, mid_ref, small_ref, pq_ref, uq_ref, par_ref, *refs):
    j = pl.program_id(0)
    steps = pl.num_programs(0)
    pair = 2 * head_dim
    inv = 1.0 / head_dim
    own, causal, ones = masks(head_dim)
    feed_in, refs = refs[:feeds], refs[feeds:]
    dq_ref, dk_ref, dv_ref, de_ref, gw1, gb1, gw2, gb2, ggain, gbias = refs[:10]
    feed_out, refs = refs[10 : 10 + feeds], refs[10 + feeds :]
    w1, b1, w2, b2, s_e1, s_e2, s_k, s_x2, s_q1, s_q2, s_q = refs[:11]
    if feeds:
        refs, sems = refs[11:-2], refs[-2:]
        buffers = [refs[i * feeds : (i + 1) * feeds] for i in range(3)] + [refs[3 * feeds :]]
        slots = feed_sum_steps(feed_in, feed_out, *buffers, Copies(*sems), FEED_WHOLE)
        for i, run in enumerate(slots):
            pl.when(j == FEED_SLOTS[i][0] * (steps - 1) // 32)(run)

    @pl.when(j <= 1)
    def _():
        for ref in (w1, b1, w2, b2, gw1, gb1, gw2, gb2, ggain, gbias):
            ref[...] = jnp.zeros_like(ref)

    rows2 = 2 * MB
    piece = lambda ref, p, i: ref[0, p, i * rows2 : (i + 1) * rows2]
    token = lambda ref, p: ref[:, p * pair : (p + 1) * pair]
    place = lambda p: jnp.minimum(lax.axis_index("group") * pairs + p, par_ref.shape[1] - 1)
    first = restart_ref[jnp.minimum(steps - 1 - j, steps - 2)]
    go_on = 1.0 - first
    writes = []

    def write(ref, index, value):
        writes.append((ref, index, value))

    def load_outputs(p):
        return (
            [token(ref, p) for ref in (qq_ref, kq_ref, doq_ref)]
            + [par_ref[1, place(p)]]
            + [bigq_ref[0, p, 0:pair], bigq_ref[0, p, pair : 2 * pair]]
            + [bigq_ref[0, p, 2 * pair : 2 * pair + rows2], bigq_ref[0, p, 2 * pair + rows2 : 2 * pair + 2 * rows2]]
            + [rate_rows(eq_ref[...], p), g2q_ref[0, p], n1_ref[0, p], n2_ref[0, p]]
            + [piece(ref, p, i) for ref in (pqq_ref, uqq_ref) for i in range(2)]
        )

    def load_step(p):
        return (
            [ref[p] for ref in (s_e1, s_e2, s_k, s_x2, s_q1, s_q2, s_q, w1, w2, b1, b2)]
            + [token(ref, p) for ref in (q_ref, k_ref, v_ref, do_ref)]
            + [par_ref[i, place(p)] for i in (1, 2)]
            + [big_ref[0, p, 0:pair], big_ref[0, p, pair : 2 * pair]]
            + [big_ref[0, p, 2 * pair : 2 * pair + rows2], big_ref[0, p, 2 * pair + rows2 : 2 * pair + 2 * rows2]]
            + [piece(mid_ref, p, i).astype(f32) for i in range(3)]
            + [piece(small_ref, p, i) for i in range(5)]
            + [pq_ref[0, p], uq_ref[0, p], rate_rows(e_ref[...], p)]
        )

    def outputs_ahead(p, loaded):
        qc, kc, do, gain, w1b, w2b, x2b, e1b, e, g2, n1b, n2b, p2b, lq, uq, sq = loaded
        qb, kb = low(spread(qc, own)), low(spread(kc, own))
        e2b = low(e * g2)
        w = spread(do * gain, own)
        dq2 = low(sq * (w - (lane_sum(w) * inv) * own - uq * (lane_sum(w * uq) * inv)))
        yield
        dn2 = dot_nt(dq2, e2b)
        dp2 = dot(dq2, w2b)
        yield
        dpx = low(-causal * dn2)
        new_e2 = dot_tn(n2b, dq2)
        dp2 = dp2 + dot(dpx, x2b)
        yield
        dq1 = low(dp2 * lq.astype(f32))
        new_x2 = dot_tn(dpx, p2b)
        yield
        dn1 = dot_nt(dq1, e1b)
        new_q = dot_nt(dq1, w1b)
        yield
        new_e1 = dot_tn(n1b, dq1)
        dqk = low(-causal * dn1)
        yield
        new_k = dot_tn(dqk, qb)
        new_q = do + fold((new_q + dot(dqk, kb)) * own)
        for ref, value in zip((s_e1, s_e2, s_k, s_x2, s_q1, s_q2, s_q), (new_e1, new_e2, new_k, new_x2, dq1, dq2, new_q)):
            write(ref, p, value)

    def step_back(p, loaded):
        e1q, e2q, dkq, x2q, dq1, dq2, dqc, dw1, dw2, db1, db2, qc, kc, vc, do, gain, bias, w1b, w2b, x2b, e1b = loaded[:21]
        g1, l1, hg, u, s, r, m2, g2, p2b, uq, e = loaded[21:]
        cols = (slice(None), slice(p * pair, (p + 1) * pair))
        dw1b, dw2b = low(dw1), low(dw2)
        qb, kb = low(spread(qc, own)), low(spread(kc, own))
        e2b = low(e * g2)
        de1 = dot(kb, dw1b)
        de2 = dot_nt(x2b, dw2b)
        yield
        de1 = -(e1q + de1 + db1)
        de2 = -(e2q + de2 * own + db2)
        dg1 = twice(e) * de1
        dh = low(dg1 * l1)
        yield
        dg2 = dot_nt(dh, w2b)
        dx2 = x2q - dot(e2b, dw2b)
        yield
        dg2 = e * de2 + dg2 * own
        dk = dkq - dot_nt(e1b, dw1b) * own
        ma, mg = lane_sum(dg2 * u) * inv, lane_sum(dg2) * inv
        rate = jnp.broadcast_to(lane_sum(g1 * de1) + lane_sum(g2 * de2), u.shape)
        rates.append(jnp.where(head == 2 * p, rate[:MB], 0.0) + jnp.where(head == 2 * p + 1, rate[MB:], 0.0))
        yield
        dr = s * (dg2 - mg * own - u * ma)
        du = dr * (gain * gain) - s * (dg2 * m2 + r * ma)
        yield
        md, mu = lane_sum(du) * inv, lane_sum(du * u + dg2 * g2) * inv
        dz2 = low(s * (du - md * own - u * mu))
        yield
        dx2 = dx2 + dot(dz2, w2b)
        yield
        dz1 = low(dg1 * hg + dx2 * l1)
        drg = fold(dr) * gain
        write(dq_ref, cols, low(dqc))
        write(dv_ref, cols, low(-drg))
        more_gain = fold(spread_by(do, uq)) + fold(dr * u) * (2.0 * gain) + fold(dr) * (bias - (vc - kc))
        yield
        ndw1 = dw1 + dot_tn(jnp.concatenate([qb, kb], 0), jnp.concatenate([dq1, dz1], 0))
        yield
        dk = dk + dot_nt(dz1, w1b) * own
        write(dk_ref, cols, low(fold(dk) + drg))
        ndw2 = dw2 + dot_tn(jnp.concatenate([dq2, low(g2), dz2], 0), jnp.concatenate([p2b, dh, x2b], 0))
        ndb1 = db1 + dot(ones, dq1) + dot(ones, dz1)
        ndb2 = db2 + dot(ones, dq2) + dot(ones, dz2)
        for ref, value in ((w1, ndw1), (w2, ndw2), (b1, ndb1), (b2, ndb2)):
            write(ref, p, value * go_on)
        more.append((cols, more_gain, do + drg))
        starts.append((p, ndw1, ndw2, ndb1, ndb2))

    more, starts, rates = [], [], []
    head = lax.broadcasted_iota(jnp.int32, (MB, pair), 1)
    ahead_in = [load_outputs(p) for p in range(pairs)]
    step_in = [load_step(p) for p in range(pairs)]
    in_turn([step_back(p, step_in[p]) for p in range(pairs)] + [outputs_ahead(p, ahead_in[p]) for p in range(pairs)])
    for ref, index, value in writes:
        ref[index] = value
    de_ref[...] = sum(rates)
    for cols, more_gain, more_bias in more:
        ggain[cols] += more_gain
        gbias[cols] += more_bias
    for p, *values in starts:
        for ref, value in zip((gw1, gw2, gb1, gb2), values):
            ref[p] += value * first


def spread_by(do, uq):
    return jnp.concatenate([do, do], 0) * uq


def backward_inner(restarts, q, k, v, do, rates, saved, params, feed_terms, collective_id):
    big, mid, small, n1, pq, uq, n2 = saved
    pairs, pair, inner = big.shape[1], params.shape[3], big.shape[3]
    blocks = q.shape[0] // MB
    head_dim = pair // 2
    steps = blocks + 1
    rate = lambda at: pl.BlockSpec((MB, 128), lambda j: (at(j), 0))
    now = lambda j: jnp.minimum(blocks - j, blocks - 1)
    ahead = lambda j: jnp.maximum(blocks - 1 - j, 0)
    tok = lambda at: pl.BlockSpec((MB, pairs * pair), lambda j: (at(j), 0))

    def block(a, at, rows=None, part=0):
        shape = (1, pairs, rows or a.shape[2], a.shape[3])
        return pl.BlockSpec(shape, lambda j: (at(j), 0, part, 0))

    whole = lambda a: pl.BlockSpec(a.shape, lambda j: (0,) * a.ndim)
    later = lambda j: ahead(j) + 1
    at_now = lambda j: now(j) + 1
    operands = [
        (q, tok(ahead)), (k, tok(ahead)), (do, tok(ahead)), (rates, rate(ahead)), (big, block(big, ahead)),
        (small, block(small, ahead, 2 * MB, 4)), (n1, block(n1, ahead)), (pq, block(pq, later)), (uq, block(uq, later)),
        (n2, block(n2, later)),
        (q, tok(now)), (k, tok(now)), (v, tok(now)), (do, tok(now)), (rates, rate(now)), (big, block(big, now)),
        (mid, block(mid, now)), (small, block(small, now)), (pq, block(pq, at_now, 2 * MB)), (uq, block(uq, at_now, 2 * MB)),
        (params, whole(params)),
    ]
    feeds = len(feed_terms)
    vmem = pl.BlockSpec(memory_space=pltpu.VMEM)
    operands += [(a, vmem) for a in feed_terms]
    width = pairs * pair
    tok_out = (jax.ShapeDtypeStruct((steps * MB, width), bf16), pl.BlockSpec((MB, width), lambda j: (blocks - j, 0)))
    state = [((pairs, pair, inner), f32), ((pairs, 2 * MB, inner), f32), ((pairs, pair, inner), f32), ((pairs, 2 * MB, pair), f32)]
    keep = lambda shape: (jax.ShapeDtypeStruct(shape, f32), pl.BlockSpec(shape, lambda j: (0,) * len(shape)))
    outs = [tok_out] * 3 + [
        (jax.ShapeDtypeStruct((steps * MB, pair), f32), pl.BlockSpec((MB, pair), lambda j: (blocks - j, 0)))
    ] + [keep(shape) for shape, _ in state] + [keep((MB, width))] * 2
    comm = []
    if feeds:
        groups, rows = lax.axis_size("group"), lax.axis_size("row")
        part, wide = feed_terms[0].shape[0] // groups, feed_terms[0].shape[1]
        unit = part // rows
        outs += [
            (jax.ShapeDtypeStruct((groups, part, wide) if i < FEED_WHOLE else (unit, wide), bf16), vmem) for i in range(feeds)
        ]
        comm = [pltpu.VMEM((groups - 1, part, wide), bf16)] * feeds + [pltpu.VMEM((part, wide), bf16)] * feeds
        comm += [pltpu.VMEM((rows - 1, unit, wide), bf16)] * feeds + [pltpu.VMEM((groups, part, wide), bf16)] * FEED_WHOLE
        copies = (feeds + FEED_WHOLE) * (groups + rows - 2)
        comm += [pltpu.SemaphoreType.DMA((copies,))] * 2
    return pl.pallas_call(
        partial(backward_kernel, pairs, head_dim, feeds),
        grid_spec=pltpu.PrefetchScalarGridSpec(
            num_scalar_prefetch=0,
            grid=(steps,),
            in_specs=[pl.BlockSpec(memory_space=pltpu.SMEM)] + [o[1] for o in operands],
            out_specs=[o[1] for o in outs],
            scratch_shapes=[pltpu.VMEM(shape, kind) for shape, kind in state] + [
                pltpu.VMEM((pairs, 2 * MB, inner), f32),
                pltpu.VMEM((pairs, 2 * MB, pair), f32),
                pltpu.VMEM((pairs, 2 * MB, pair), f32),
                pltpu.VMEM((pairs, 2 * MB, inner), f32),
                pltpu.VMEM((pairs, 2 * MB, inner), bf16),
                pltpu.VMEM((pairs, 2 * MB, pair), bf16),
                pltpu.VMEM((pairs, MB, pair), f32),
            ] + comm,
        ),
        out_shape=[o[0] for o in outs],
        compiler_params=pltpu.CompilerParams(
            collective_id=collective_id if feeds else None, has_side_effects=bool(feeds), vmem_limit_bytes=56 * 1024 * 1024
        ),
        name="inner_backward",
    )(restarts.astype(f32), *[o[0] for o in operands])


def norm_parts(v, width):
    centered = v - jnp.sum(v, -1, keepdims=True) * (1.0 / width)
    scale = lax.rsqrt(jnp.sum(centered * centered, -1, keepdims=True) * (1.0 / width) + epsilon)
    return centered * scale, scale


def feed_terms(*items):
    for outs, left, right in items:
        width = left.shape[1]
        for i, out in enumerate(outs):
            both = low(dot_tn(left[...], right[:, i * 256 : (i + 1) * 256]))
            out[0:width] = both[:, :128]
            out[width : 2 * width] = both[:, 128:]


def middle_kernel(span, mixed_in, tok_ref, cot_ref, wout_ref, gate_ref, up_ref, down_ref, gain_ref,
                  block_ref, hid_ref, gmix_ref, gwo_ref, t0, t1, t2, t3, t4, t5, gfeed_ref,
                  mixed_ref, mixed_got, acts, cots, unit, scales, h_in, gg, gu, ha, pg0, po0, out_core, in_core, out_diag, in_diag, out_y, in_y,
                  branch, branch_row, send_sem, recv_sem, local_sem):
    rows, groups = lax.axis_size("row"), lax.axis_size("group")
    row, group, feat = lax.axis_index("row"), lax.axis_index("group"), lax.axis_index("feat")
    count, width = tok_ref.shape
    cols = mixed_ref.shape[1]
    core, y = lax.rem(feat, 2), feat // 2
    core_mate, y_mate = {"feat": feat + 1 - 2 * core}, {"feat": feat + 2 - 4 * y}
    here = row * groups + group
    places = rows * groups
    others = [lax.rem(here + o, places) for o in range(1, places)]
    seq_mates = [{"row": t // groups, "group": lax.rem(t, groups)} for t in others]
    copies = Copies(send_sem, recv_sem)
    send = copies.send
    slot = lambda ref, s: ref.at[s * count : (s + 1) * count]

    mixed_ref[...] = low(mixed_in[MB:])
    greet([core_mate, y_mate] + seq_mates)
    lanes = pl.ds(pl.multiple_of(group * cols, 128), cols)
    moves = [
        send(mixed_ref.at[rows_at(t * span, span)], mixed_got.at[rows_at(row * span, span), lanes], mate)
        for t, mate in zip(others, seq_mates)
    ]
    own = pltpu.make_async_copy(
        mixed_ref.at[rows_at(here * span, span)], mixed_got.at[rows_at(row * span, span), lanes], local_sem.at[0]
    )
    own.start()
    cot_core = send(cot_ref, slot(cots, 1), core_mate)
    cot_y = send(cot_ref, slot(cots, 2), y_mate)
    cots[0:count] = cot_ref[...]
    own.wait()
    for copy in moves:
        copy.wait_recv()
    hidden = tok_ref[...].astype(f32) + dot(mixed_got[:, :width], wout_ref[:width])
    h_in[...] = hidden
    unit_two, scale_two = norm_parts(hidden, width)
    unit[...] = unit_two
    scales[...] = jnp.broadcast_to(scale_two, scales.shape)
    acts[0:count] = low(unit_two * gain_ref[...])
    act_core = send(slot(acts, 0), slot(acts, 1), core_mate)
    act_y = send(slot(acts, 0), slot(acts, 2), y_mate)
    cot_y.wait_recv()
    cot_diag = send(slot(cots, 2), slot(cots, 3), core_mate)

    def feed(s):
        part = slice(s * count, (s + 1) * count)
        gate_pre, up_value = dot(acts[part], gate_ref[...]), dot(acts[part], up_ref[...])
        grad = dot(cots[part], down_ref[...])
        sig = jax.nn.sigmoid(gate_pre)
        silu = gate_pre * sig
        ha[part] = low(silu * up_value)
        gg[part] = low(grad * up_value * sig * (1.0 + gate_pre * (1.0 - sig)))
        gu[part] = low(grad * silu)
        back = dot_nt(gg[part], gate_ref[...]) + dot_nt(gu[part], up_ref[...])
        return back, dot_nt(ha[part], down_ref[...])

    pg0[...], po0[...] = feed(0)
    act_core.wait_recv()
    cot_core.wait_recv()
    back, forth = feed(1)
    out_core[0], out_core[1] = low(back), low(forth)
    core_sums = [send(out_core.at[i], in_core.at[i], core_mate) for i in range(2)]
    act_y.wait_recv()
    act_diag = send(slot(acts, 2), slot(acts, 3), core_mate)
    act_diag.wait_recv()
    cot_diag.wait_recv()
    back, forth = feed(3)
    out_diag[0], out_diag[1] = low(back), low(forth)
    diag_sums = [send(out_diag.at[i], in_diag.at[i], core_mate) for i in range(2)]
    back, forth = feed(2)
    y_sums = []
    for i, value in enumerate((back, forth)):
        diag_sums[i].wait_recv()
        out_y[i] = low(value + in_diag[i].astype(f32))
        y_sums.append(send(out_y.at[i], in_y.at[i], y_mate))
    feed_terms(((t0, t1), acts, gg), ((t2, t3), acts, gu), ((t4, t5), cots, ha))
    core_sums[0].wait_recv()
    y_sums[0].wait_recv()
    grad_act = pg0[...] + in_core[0].astype(f32) + in_y[0].astype(f32)
    unit_two = unit[...]
    gfeed_ref[...] = jnp.sum(grad_act * unit_two, 0, keepdims=True)
    w = grad_act * gain_ref[...]
    inv = 1.0 / width
    grad = cot_ref[...].astype(f32) + scales[:, 0:1] * (
        w - jnp.sum(w, -1, keepdims=True) * inv - unit_two * (jnp.sum(w * unit_two, -1, keepdims=True) * inv)
    )
    hid_ref[...] = grad
    branch[...] = low(grad)
    row_mates, group_mates = mates("row"), mates("group")
    block = lambda r: branch_row.at[rows_at((r * groups + group) * span, span)]
    by_row = [
        send(branch.at[rows_at(lax.rem(row + o, rows) * span, span)], block(row), row_mates[o - 1]) for o in range(1, rows)
    ]
    block(row)[...] = branch[rows_at(row * span, span)]
    moves = [send(block(row), block(row), mate) for mate in group_mates]
    for o in range(1, rows):
        by_row[o - 1].wait_recv()
        from_row = block(lax.rem(row - o + rows, rows))
        moves += [send(from_row, from_row, mate) for mate in group_mates]
    core_sums[1].wait_recv()
    y_sums[1].wait_recv()
    block_ref[...] = low(h_in[...] + po0[...] + in_core[1].astype(f32) + in_y[1].astype(f32))
    for copy in moves:
        copy.wait_recv()
    gmix_ref[...] = dot_nt(branch_row[...], wout_ref[rows_at(group * cols, cols)])
    for h in range(2):
        half = branch_row[:, h * (width // 2) : (h + 1) * (width // 2)]
        gwo_ref[h * cols : (h + 1) * cols] = low(dot_tn(mixed_ref[...], half))
    for copy in copies.started:
        copy.wait_send()


def middle(mixed_row, tokens, cotangent, out_weight, gate_weight, up_weight, down_weight, gain, span, collective_id):
    rows, groups = lax.axis_size("row"), lax.axis_size("group")
    length, cols = mixed_row.shape[0] - MB, mixed_row.shape[1]
    count, width = tokens.shape
    hidden = gate_weight.shape[1]
    copies = (rows * groups - 1) + (rows - 1) + rows * (groups - 1) + 12
    vmem = pl.BlockSpec(memory_space=pltpu.VMEM)
    outs = [
        ((count, width), bf16), ((count, width), f32), ((length, cols), f32), ((2 * cols, width // 2), bf16),
        *[((2 * width, 128), bf16)] * 6, ((1, width), f32),
    ]
    two = pltpu.VMEM((2, count, width), bf16)
    return pl.pallas_call(
        partial(middle_kernel, span),
        in_specs=[vmem] * 8,
        out_specs=[vmem] * len(outs),
        out_shape=[jax.ShapeDtypeStruct(*o) for o in outs],
        scratch_shapes=[
            pltpu.VMEM((length, cols), bf16),
            pltpu.VMEM((count, groups * cols), bf16),
            pltpu.VMEM((4 * count, width), bf16),
            pltpu.VMEM((4 * count, width), bf16),
            pltpu.VMEM((count, width), f32),
            pltpu.VMEM((count, 128), f32),
            pltpu.VMEM((count, width), f32),
            pltpu.VMEM((4 * count, hidden), bf16),
            pltpu.VMEM((4 * count, hidden), bf16),
            pltpu.VMEM((4 * count, hidden), bf16),
            pltpu.VMEM((count, width), f32),
            pltpu.VMEM((count, width), f32),
            two, two, two, two, two, two,
            pltpu.VMEM((count, width), bf16),
            pltpu.VMEM((length, width), bf16),
            pltpu.SemaphoreType.DMA((copies,)),
            pltpu.SemaphoreType.DMA((copies,)),
            pltpu.SemaphoreType.DMA((1,)),
        ],
        compiler_params=pltpu.CompilerParams(
            collective_id=collective_id, has_side_effects=True, vmem_limit_bytes=56 * 1024 * 1024
        ),
        name="middle",
    )(mixed_row, tokens, cotangent, out_weight, gate_weight, up_weight, down_weight, gain)


def head_kernel(span, heads, mine, head_dim, tok_ref, gain_ref, wq_ref, wk_ref, wv_ref, wr_ref, rb_ref,
                q_ref, k_ref, v_ref, act_ref, unit_ref, rate_ref, slope_ref, stat_ref, row_tok, send_sem, recv_sem):
    rows, groups = lax.axis_size("row"), lax.axis_size("group")
    row, group, feat = lax.axis_index("row"), lax.axis_index("group"), lax.axis_index("feat")
    row_mates, group_mates = mates("row"), mates("group")
    width = tok_ref.shape[2]
    cols = q_ref.shape[1]
    copies = Copies(send_sem, recv_sem)
    block = lambda r: row_tok.at[rows_at((r * groups + group) * span, span)]

    greet(row_mates + group_mates)
    by_row = [
        copies.send(tok_ref.at[lax.rem(row + o, rows)], block(row), row_mates[o - 1]) for o in range(1, rows)
    ]
    block(row)[...] = tok_ref[row]
    by_group = [copies.send(block(row), block(row), mate) for mate in group_mates]
    for o in range(1, rows):
        by_row[o - 1].wait_recv()
        here = block(lax.rem(row - o + rows, rows))
        by_group += [copies.send(here, here, mate) for mate in group_mates]
    for copy in by_group:
        copy.wait_recv()
    unit, _ = norm_parts(row_tok[...].astype(f32), width)
    unit_ref[...] = unit
    act = low(unit * gain_ref[...])
    act_ref[...] = act
    lanes = pl.ds(pl.multiple_of(group * cols, 128), cols)
    for out, weight in ((q_ref, wq_ref), (k_ref, wk_ref), (v_ref, wv_ref)):
        out[...] = dot(act, weight[:, lanes])
    logits = dot(act, wr_ref[...]) + rb_ref[...]
    sigma = jax.nn.sigmoid(logits)
    lane = lax.broadcasted_iota(jnp.int32, logits.shape, 1)
    used = (lane < mine) & (group * mine + lane < heads)
    rate_ref[...] = sigma * (1.0 / head_dim)
    slope_ref[...] = jnp.where(used, sigma * (1.0 - sigma) * (1.0 / head_dim), 0.0)
    stat_ref[0:1] = jnp.sum(logits, 0, keepdims=True)
    top = jnp.max(jnp.max(jnp.where(used, logits, -3e38), 0, keepdims=True), 1, keepdims=True)
    place = row * lax.axis_size("feat") + feat
    stat_ref[1:2] = jnp.where(lane[0:1] == place, top, 0.0)
    for copy in copies.started:
        copy.wait_send()


def head(tokens, gain, weights, rate_weight, rate_bias, heads, mine, head_dim, collective_id):
    rows, groups = lax.axis_size("row"), lax.axis_size("group")
    _, span, width = tokens.shape
    length, cols = rows * groups * span, mine * head_dim
    vmem = pl.BlockSpec(memory_space=pltpu.VMEM)
    copies = (rows - 1) + rows * (groups - 1)
    outs = [((length, cols), f32)] * 3 + [((length, width), bf16), ((length, width), f32)]
    outs += [((length, 128), f32)] * 2 + [((2, 128), f32)]
    return pl.pallas_call(
        partial(head_kernel, span, heads, mine, head_dim),
        in_specs=[vmem] * 7,
        out_specs=[vmem] * len(outs),
        out_shape=[jax.ShapeDtypeStruct(*o) for o in outs],
        scratch_shapes=[
            pltpu.VMEM((length, width), bf16),
            pltpu.SemaphoreType.DMA((copies,)),
            pltpu.SemaphoreType.DMA((copies,)),
        ],
        compiler_params=pltpu.CompilerParams(
            collective_id=collective_id, has_side_effects=True, vmem_limit_bytes=48 * 1024 * 1024
        ),
        name="head",
    )(tokens, gain, *weights, rate_weight, rate_bias)


TAIL_SLOTS = [
    ([], ["FZ1", "FZ2", "FZ0"]),
    ([], ["CORE4", "CORE3"]),
    ([], ["CORE0"]),
    (["CORE4"], ["CORE1", "Y4"]),
    (["CORE3"], ["CORE2", "Y3"]),
    (["CORE0"], ["Y0"]),
    (["FZ1"], ["FX1"]),
    (["CORE1"], []),
    (["CORE2"], []),
    ([], ["PART0"]),
    ([], ["SC0"]),
    (["Y4"], ["Y2", "Z4"]),
    (["SC0"], []),
    (["FZ2"], ["FX2"]),
    (["Y3"], ["Y1", "Z3"]),
    (["FX1"], []),
    (["FZ0"], ["FX0"]),
    (["Y0"], ["SY0", "Z0"]),
    (["Z4"], ["ZA4"]),
    (["Y2"], []),
    (["Z3"], ["ZA3"]),
    (["PART0"], []),
    (["Y1"], []),
    (["Z0"], ["Z1"]),
    (["SY0"], []),
    (["ZA4"], ["P4", "Z2"]),
    (["FX2"], []),
    (["ZA3"], ["P3", "ZA0"]),
    (["P4"], ["Q4"]),
    (["FX0"], []),
    (["Z1"], ["ZA1"]),
    (["P3"], ["Q3"]),
    (["Z2"], ["ZA2"]),
    (["ZA0"], ["P0", "SZ0"]),
    (["Q4"], ["C4"]),
    (["C4"], []),
    (["ZA1"], ["P1", "HOME0"]),
    (["Q3"], ["C3"]),
    (["P0"], ["Q0"]),
    (["ZA2"], ["P2"]),
    (["C3"], []),
    (["P1"], ["Q1"]),
    (["SZ0"], ["SX0"]),
    (["P2"], ["Q2"]),
    (["Q0"], ["C0"]),
    (["C0"], []),
    (["Q1"], ["C1"]),
    (["HOME0"], []),
    (["SX0"], []),
    (["C1"], []),
    (["Q2"], ["C2"]),
    (["C2"], []),
]
TAIL_GROUP_FIRST = (True, False, True, True, False)


FEED_SLOTS = [
    (0, [], ["X1", "X2"]),
    (8, ["X1"], ["X0", "Z1"]),
    (11, ["X2"], ["X4", "Z2"]),
    (13, ["Z1"], ["ZA1"]),
    (14, ["X0"], ["X3"]),
    (16, ["Z2"], ["Z0"]),
    (18, ["X4"], ["X5"]),
    (19, ["ZA1"], ["ZA2"]),
    (21, ["X3"], ["XA1"]),
    (22, ["Z0"], ["ZA0"]),
    (24, ["X5"], []),
    (25, ["ZA2"], ["XA2", "Z5"]),
    (27, ["XA1"], []),
    (28, ["ZA0"], ["XA0", "Z3"]),
    (30, ["XA2"], []),
    (31, ["Z5"], ["Z4"]),
    (32, ["XA0", "Z3", "Z4"], []),
]
FEED_WHOLE = 3


def tail_kernel(span, shapes, feeds, act_ref, unit_ref, gq_ref, gk_ref, gv_ref, de_ref, slope_ref, wq_ref, wk_ref, wv_ref, wr_ref,
                gwo_ref, gw1, gb1, gw2, gb2, ggain, gbias, gfeed, stat_ref, *refs):
    rows, groups = lax.axis_size("row"), lax.axis_size("group")
    row, group, feat = lax.axis_index("row"), lax.axis_index("group"), lax.axis_index("feat")
    core, y = lax.rem(feat, 2), feat // 2
    core_mate, y_mate = {"feat": feat + 1 - 2 * core}, {"feat": feat + 2 - 4 * y}
    row_mates, group_mates = mates("row"), mates("group")
    count = len(shapes)
    feed_in, refs = refs[:feeds], refs[feeds:]
    outs, (home_out, small_out), refs = refs[:count], refs[count : count + 2], refs[count + 2 :]
    feed_out, refs = refs[:feeds], refs[feeds:]
    own, got_core, sum_core, got_y, sum_y, got_row = (refs[i * count : (i + 1) * count] for i in range(6))
    part, part_got, part_sum, small, small_core, small_got, send_sem, recv_sem = refs[6 * count :]
    length, width = act_ref.shape
    cols = gwo_ref.shape[0] // 2
    pairs, pair, inner = gw1.shape
    head_dim = pair // 2
    copies = Copies(send_sem, recv_sem)
    moves = {}

    def start(name, *what):
        moves[name] = [copies.send(*w) for w in what]

    greet([core_mate, y_mate] + row_mates + group_mates)

    half = [h // 2 for h, _ in shapes]
    quarter = [h // 4 for h, _ in shapes]
    piece = [h // (4 * rows) for h, _ in shapes]
    unit = feed_in[0].shape[0]
    place = (core * 2 + y) * rows + row
    source = list(own[:3]) + [gwo_ref, own[4]]
    grad_refs = (gq_ref, gk_ref, gv_ref)
    lanes = pl.ds(pl.multiple_of(group * cols, 128), cols)

    def token_gradient():
        logits = low(de_ref[0:length] * slope_ref[...])
        total = dot_nt(logits, wr_ref[...])
        for grad, weight in zip(grad_refs, (wq_ref, wk_ref, wv_ref)):
            total = total + dot_nt(grad[0:length], weight[:, lanes])
        for r in range(rows):
            for g in range(groups):
                part[g, r * span : (r + 1) * span] = low(total[(r * groups + g) * span : (r * groups + g + 1) * span])
        start("PART0", *[(part.at[lax.rem(group + o, groups)], part_got.at[o - 1], group_mates[o - 1]) for o in range(1, groups)])
        small[...] = jnp.zeros_like(small)
        small[0 : 2 * pairs] = dot_tn(logits, act_ref[...])[0 : 2 * pairs]
        for p in range(pairs):
            for h in range(2):
                n = 2 * p + h
                small[6 + n // 3 : 7 + n // 3, (n % 3) * inner : (n % 3 + 1) * inner] = gb1[p, h * MB : h * MB + 1]
            small[9:10, p * pair : (p + 1) * pair] = gb2[p, 0:1] + gb2[p, MB : MB + 1]
        small[8:9, 0:cols] = jnp.sum(ggain[...], 0, keepdims=True)
        small[8:9, cols : 2 * cols] = jnp.sum(gbias[...], 0, keepdims=True)
        small[9:10, width - 384 : width - 256] = jnp.sum(logits.astype(f32), 0, keepdims=True)
        small[9:10, width - 256 : width - 128] = stat_ref[0:1]
        small[9:10, width - 128 : width] = stat_ref[1:2]
        small[10:11] = jnp.sum(total * unit_ref[...], 0, keepdims=True)
        small[11:12] = gfeed[...]

    def finish(name):
        for copy in moves[name]:
            copy.wait_recv()
        kind, i = name[:-1], int(name[-1])
        if kind == "CORE":
            sum_core[i][...] = add_low(source[i][rows_at(core * half[i], half[i])], got_core[i][...])
        if kind == "Y":
            sum_y[i][...] = add_low(sum_core[i][rows_at(y * quarter[i], quarter[i])], got_y[i][...])
        if kind == "Z":
            value = sum_y[i][rows_at(row * piece[i], piece[i])].astype(f32)
            for o in range(1, rows):
                value = value + got_row[i][o - 1].astype(f32)
            outs[i][group, rows_at(place * piece[i], piece[i])] = low(value)
        if kind == "PART":
            value = part[group].astype(f32)
            for o in range(1, groups):
                value = value + part_got[o - 1].astype(f32)
            part_sum[...] = low(value)
            home_out[rows_at(row * span, span)] = part_sum[rows_at(row * span, span)]
        if kind == "SC":
            small_core[...] = small[...] + small_got[0]
        if kind == "SY":
            small_got[2 + row] = small_core[...] + small_got[1]
        if kind == "SZ":
            value = small_got[2]
            for r in range(1, rows):
                value = value + small_got[2 + r]
            small_out[group] = value

    def begin(name):
        kind, i = name[:-1], int(name[-1])
        if kind == "PART":
            token_gradient()
        if kind == "HOME":
            here = home_out.at[rows_at(row * span, span)]
            start(name, *[
                (part_sum.at[rows_at(lax.rem(row + o, rows) * span, span)], here, row_mates[o - 1]) for o in range(1, rows)
            ])
        if kind == "SC":
            start(name, (small, small_got.at[0], core_mate))
        if kind == "SY":
            start(name, (small_core, small_got.at[1], y_mate))
        if kind == "SZ":
            here = small_got.at[2 + row]
            start(name, *[(here, here, mate) for mate in row_mates])
        if kind == "SX":
            here = small_out.at[group]
            start(name, *[(here, here, mate) for mate in group_mates])
        if kind == "FZ":
            here = feed_out[i].at[group, rows_at(row * unit, unit)]
            here[...] = feed_in[i][...]
            start(name, *[(here, here, mate) for mate in row_mates])
        if kind == "FX":
            here = feed_out[i].at[group]
            start(name, *[(here, here, mate) for mate in group_mates])
        if kind == "CORE":
            if i < 3:
                own[i][...] = low(dot_tn(act_ref[...], grad_refs[i][0:length]))
            if i == 4:
                for p in range(pairs):
                    own[4][p * pair : (p + 1) * pair] = low(gw1[p])
                    own[4][cols + p * pair : cols + (p + 1) * pair] = low(gw2[p])
            start(name, (source[i].at[rows_at((1 - core) * half[i], half[i])], got_core[i], core_mate))
        if kind == "Y":
            start(name, (sum_core[i].at[rows_at((1 - y) * quarter[i], quarter[i])], got_y[i], y_mate))
        if kind == "Z":
            start(name, *[
                (sum_y[i].at[rows_at(lax.rem(row + o, rows) * piece[i], piece[i])], got_row[i].at[o - 1], row_mates[o - 1])
                for o in range(1, rows)
            ])
        if kind == "ZA":
            here = outs[i].at[group, rows_at(place * piece[i], piece[i])]
            start(name, *[(here, here, mate) for mate in row_mates])
        if kind in ("P", "Q", "C"):
            quarters = rows_at((core * 2 + y) * quarter[i], quarter[i])
            halves = rows_at(core * half[i], half[i])
            by_group = TAIL_GROUP_FIRST[i] == (kind == "P")
            if kind == "C":
                here, to = outs[i].at[:, halves], [core_mate]
            elif by_group:
                here, to = outs[i].at[group, quarters if kind == "P" else halves], group_mates
            else:
                here, to = (outs[i].at[group, quarters] if kind == "P" else outs[i].at[:, quarters]), [y_mate]
            start(name, *[(here, here, mate) for mate in to])

    for done, begun in TAIL_SLOTS:
        for name in done:
            finish(name)
        for name in begun:
            begin(name)
    for copy in copies.started:
        copy.wait_send()


def tail(act_row, unit_row, grads, de, slope, weights, rate_weight, grad_out, states, grad_feed_gain, stat, feed_parts, span, collective_id):
    rows, groups = lax.axis_size("row"), lax.axis_size("group")
    length, width = act_row.shape
    cols = grad_out.shape[0] // 2
    inner = states[0].shape[-1]
    shapes = [(width, cols)] * 3 + [(2 * cols, width // 2), (2 * cols, inner)]
    count, feeds = len(shapes), len(feed_parts)
    unit, wide = feed_parts[0].shape
    copies = count * (2 + 2 * (rows - 1) + (groups - 1) + 2) + (groups - 1) + (rows - 1) + 2 + (rows - 1) + (groups - 1)
    copies += feeds * (rows + groups - 2)
    vmem = pl.BlockSpec(memory_space=pltpu.VMEM)
    operands = [act_row, unit_row, *grads, de, slope, *weights, rate_weight, grad_out, *states, grad_feed_gain, stat, *feed_parts]
    outs = [((groups, h, w), bf16) for h, w in shapes]
    outs += [((rows * span, width), bf16), ((groups, 16, width), f32)]
    outs += [((groups, rows * unit, wide), bf16)] * feeds
    scratch = [pltpu.VMEM((h, w), bf16) for h, w in shapes]
    scratch += [pltpu.VMEM((h // 2, w), bf16) for h, w in shapes] * 2
    scratch += [pltpu.VMEM((h // 4, w), bf16) for h, w in shapes] * 2
    scratch += [pltpu.VMEM((rows - 1, h // (4 * rows), w), bf16) for h, w in shapes]
    scratch += [
        pltpu.VMEM((groups, rows * span, width), bf16),
        pltpu.VMEM((groups - 1, rows * span, width), bf16),
        pltpu.VMEM((rows * span, width), bf16),
        pltpu.VMEM((16, width), f32),
        pltpu.VMEM((16, width), f32),
        pltpu.VMEM((2 + rows, 16, width), f32),
        pltpu.SemaphoreType.DMA((copies,)),
        pltpu.SemaphoreType.DMA((copies,)),
    ]
    return pl.pallas_call(
        partial(tail_kernel, span, shapes, feeds),
        in_specs=[vmem] * len(operands),
        out_specs=[vmem] * len(outs),
        out_shape=[jax.ShapeDtypeStruct(*o) for o in outs],
        scratch_shapes=scratch,
        compiler_params=pltpu.CompilerParams(
            collective_id=collective_id, has_side_effects=True, vmem_limit_bytes=60 * 1024 * 1024
        ),
        name="tail",
    )(*operands)


def finish_kernel(heads, mine, head_dim, inner, total_logits, q_in, k_in, v_in, o_in, s_in, got_ref, small_ref, tok_ref, hid_ref, gain_ref,
                  f0, f1, f2, f3, f4, f5, rate_ref, rbias_ref, fbias_ref, sbias_ref, gain_out, bias_out, mixer_ref, feed_ref, stat_ref,
                  q_out, k_out, v_out, o_out, first_out, second_out, gate_out, up_out, down_out, in_out,
                  sq, sk, sv, so, s1, s2, sg, su, sd, si, sems):
    groups, width = q_in.shape[0], q_in.shape[1]
    cols = mine * head_dim
    sent = []

    def give(value_ref, out):
        copy = pltpu.make_async_copy(value_ref, out, sems.at[len(sent)])
        copy.start()
        sent.append(copy)

    for out, scratch, left, right in ((gate_out, sg, f0, f1), (up_out, su, f2, f3), (down_out, sd, f4, f5)):
        for i, cut in enumerate((left, right)):
            value = cut[...].reshape(2 * width, 128)
            for h in range(2):
                scratch[:, (2 * i + h) * 128 : (2 * i + h + 1) * 128] = value[h * width : (h + 1) * width].astype(f32)
        give(scratch, out)
    for out, scratch, array in ((q_out, sq, q_in), (k_out, sk, k_in), (v_out, sv, v_in)):
        for g in range(groups):
            size = min(cols, width - g * cols)
            if size > 0:
                scratch[:, g * cols : g * cols + size] = array[g, :, 0:size].astype(f32)
        give(scratch, out)
    for g in range(groups):
        size = min(cols, width - g * cols)
        if size > 0:
            for h in range(2):
                scratch = so.at[g * cols : g * cols + size, h * (width // 2) : (h + 1) * (width // 2)]
                scratch[...] = o_in[g, h * cols : h * cols + size].astype(f32)
    give(so, o_out)
    for n in range(heads):
        g, i = n // mine, n % mine
        s1[n] = s_in[g, i * head_dim : (i + 1) * head_dim].astype(f32)
        second = s_in[g, cols + i * head_dim : cols + (i + 1) * head_dim].astype(f32)
        s2[n] = second - jnp.sum(second, 0, keepdims=True) * (1.0 / head_dim)
    give(s1, first_out)
    give(s2, second_out)
    unit, scale = norm_parts(tok_ref[...].astype(f32), width)
    w = got_ref[...].astype(f32) * gain_ref[...]
    inv = 1.0 / width
    si[...] = hid_ref[...] + scale * (
        w - jnp.sum(w, -1, keepdims=True) * inv - unit * (jnp.sum(w * unit, -1, keepdims=True) * inv)
    )
    give(si, in_out)
    rates, total, top = [], 0.0, None
    for n in range(heads):
        g, i = n // mine, n % mine
        rates.append(small_ref[g, i : i + 1])
        rbias_ref[:, n : n + 1] = small_ref[g, 9:10, width - 384 + i : width - 383 + i]
        total = total + small_ref[g, 9:10, width - 256 + i : width - 255 + i]
        fbias_ref[n : n + 1] = small_ref[g, 6 + i // 3 : 7 + i // 3, (i % 3) * inner : (i % 3 + 1) * inner]
        own = slice(i * head_dim, (i + 1) * head_dim)
        second = small_ref[g, 9:10, own]
        sbias_ref[n : n + 1] = second - jnp.sum(second, -1, keepdims=True) * (1.0 / head_dim)
        gain_out[n : n + 1] = small_ref[g, 8:9, own]
        bias_out[n : n + 1] = small_ref[g, 8:9, cols + i * head_dim : cols + (i + 1) * head_dim]
    rates = jnp.concatenate(rates + [jnp.zeros((-heads % 8, width), f32)], 0) if heads % 8 else jnp.concatenate(rates, 0)
    rate_ref[...] = rates.T[:, :heads]
    mixer, feed = small_ref[0, 10:11], small_ref[0, 11:12]
    tops = small_ref[0, 9:10, width - 128 : width]
    peers = lax.axis_size("row") * lax.axis_size("feat")
    for g in range(1, groups):
        mixer, feed = mixer + small_ref[g, 10:11], feed + small_ref[g, 11:12]
        tops = jnp.maximum(tops, small_ref[g, 9:10, width - 128 : width])
    mixer_ref[...], feed_ref[...] = mixer, feed
    lane = lax.broadcasted_iota(jnp.int32, tops.shape, 1)
    top = jnp.max(jnp.where(lane < peers, tops, -3e38), 1, keepdims=True)
    stat_ref[...] = jnp.where(lane == 0, total * (1.0 / total_logits), top)
    for copy in sent:
        copy.wait()


def finish(arrays, got, small, tokens, grad_hidden, gain, feed_sums, heads, mine, head_dim, inner, total_logits):
    count, width = tokens.shape
    hidden = 2 * 2 * 128
    vmem, anywhere = pl.BlockSpec(memory_space=pltpu.VMEM), pl.BlockSpec(memory_space=pl.ANY)
    little = [(width, heads), (1, heads), (heads, inner), (heads, head_dim), (heads, head_dim), (heads, head_dim)]
    little += [(1, width), (1, width), (1, 128)]
    large = [(width, width)] * 4 + [(heads, head_dim, inner)] * 2 + [(width, hidden)] * 3 + [(count, width)]
    operands = [*arrays, got, small, tokens, grad_hidden, gain, *feed_sums]
    return pl.pallas_call(
        partial(finish_kernel, heads, mine, head_dim, inner, total_logits),
        in_specs=[vmem] * len(operands),
        out_specs=[vmem] * len(little) + [anywhere] * len(large),
        out_shape=[jax.ShapeDtypeStruct(s, f32) for s in little + large],
        scratch_shapes=[pltpu.VMEM(s, f32) for s in large] + [pltpu.SemaphoreType.DMA((len(large),))],
        compiler_params=pltpu.CompilerParams(vmem_limit_bytes=56 * 1024 * 1024),
        name="finish",
    )(*operands)


SEQ = ("row", "group")


def per_device(
    tokens,
    cotangent,
    doc_starts,
    mixer_gain,
    query_weight,
    key_weight,
    value_weight,
    out_weight,
    rate_weight,
    rate_bias,
    first_init,
    first_bias_init,
    second_init,
    second_bias_init,
    inner_gain,
    inner_bias,
    feed_gain,
    gate_weight,
    up_weight,
    down_weight,
):
    rows, span, width = tokens.shape
    heads, head_dim, inner = first_init.shape
    groups = lax.axis_size("group")
    feats = lax.axis_size("feat")
    row, group = lax.axis_index("row"), lax.axis_index("group")
    count = rows * span
    blocks = span * rows * groups // MB
    pairs = -(-heads // (2 * groups))
    mine = 2 * pairs
    pair = 2 * head_dim
    spare = mine * groups - heads

    def padded(array, axis, size):
        edges = [(0, 0)] * array.ndim
        edges[axis] = (0, spare * size)
        return jnp.pad(array, edges) if spare else array

    def own_lanes(array):
        own = lax.dynamic_slice_in_dim(padded(array, 1, 1), group * mine, mine, 1)
        return jnp.pad(own, ((0, 0), (0, 128 - mine)))

    weights = [padded(w, 1, head_dim) for w in (query_weight, key_weight, value_weight)]
    rate_lanes = own_lanes(rate_weight)
    flat_tokens = tokens.reshape(count, width)
    mixer_gain = mixer_gain.reshape(1, width)
    queries, keys, values, act_row, unit_row, rates, slope, stat = head(
        tokens, mixer_gain, weights, rate_lanes, own_lanes(rate_bias[None]), heads, mine, head_dim, 4
    )
    block_ids = jnp.arange(blocks + 1, dtype=jnp.int32)
    starts = lax.dynamic_index_in_dim(doc_starts, row, 0, False)
    restarts = ((block_ids == 0) | jnp.any(starts[:, None] == block_ids[None], 0)).astype(jnp.int32)
    params = jnp.stack([second_bias_init, inner_gain, inner_bias]).reshape(3, heads // 2, 1, pair)
    by_pair = lambda a: a.reshape(heads // 2, pair, inner)
    *saved, mixed = forward_inner(
        restarts, queries, keys, values, rates, by_pair(first_init), first_bias_init.reshape(heads // 2, 2, inner),
        by_pair(second_init), params,
    )

    block_out, grad_hidden, grad_mixed, grad_out_rows, *feed_terms, grad_feed_gain = middle(
        mixed, flat_tokens, cotangent.reshape(count, width), padded(out_weight, 0, head_dim),
        gate_weight, up_weight, down_weight, feed_gain.reshape(1, width), span, 1,
    )

    grad_q, grad_k, grad_v, grad_e, g_first, g_first_bias, g_second, g_second_bias, g_gain, g_bias, *feed_sums = (
        backward_inner(restarts, queries, keys, values, grad_mixed, rates, saved, params, feed_terms, 2)
    )
    reduced = tail(
        act_row, unit_row, (grad_q, grad_k, grad_v), grad_e, slope, weights, rate_lanes, grad_out_rows,
        (g_first, g_first_bias, g_second, g_second_bias, g_gain, g_bias), grad_feed_gain, stat,
        feed_sums[FEED_WHOLE:], span, 3,
    )
    arrays, (got, small), feed_sums = reduced[:5], reduced[5:7], [*feed_sums[:FEED_WHOLE], *reduced[7:]]
    (
        g_rate, g_rate_bias, g_first_bias, g_second_bias, g_gain, g_bias, g_mixer, g_feed, stats,
        g_query, g_key, g_value, g_out, g_first, g_second, g_gate, g_up, g_down, input_grad,
    ) = finish(
        arrays, got, small, flat_tokens, grad_hidden, mixer_gain, feed_sums, heads, mine, head_dim, inner,
        rows * groups * feats * count * heads,
    )
    return (
        block_out.reshape(rows, span, width),
        input_grad.reshape(rows, span, width),
        g_mixer[0],
        g_query,
        g_key,
        g_value,
        g_out,
        g_rate,
        g_rate_bias[0],
        g_first,
        g_first_bias,
        g_second,
        g_second_bias,
        g_gain,
        g_bias,
        g_feed[0],
        g_gate,
        g_up,
        g_down,
        stats[0, :2],
    )


def solution(mesh):
    feats = mesh.shape["feat"]

    def run(*arrays):
        rows = arrays[0].shape[0] // feats
        grid = jax.sharding.Mesh(mesh.devices.reshape(rows, -1, feats), ("row", "group", "feat"))
        by_token = P("feat", SEQ, None)
        by_hidden = P(None, "feat")
        return jax.shard_map(
            per_device,
            mesh=grid,
            in_specs=(by_token, by_token, P("feat", None)) + (P(),) * 14 + (by_hidden,) * 3,
            out_specs=(by_token, by_token) + (P(),) * 14 + (by_hidden,) * 3 + (P(),),
            check_vma=False,
        )(*arrays)

    return run
```

```python
from functools import partial

import jax
import jax.numpy as jnp
from jax import lax
from jax.experimental import pallas as pl
from jax.experimental.pallas import tpu as pltpu
from jax.sharding import PartitionSpec as P

MB = 16
epsilon = 1e-05
f32, bf16 = jnp.float32, jnp.bfloat16


def dot(a, b):
    return lax.dot_general(a, b, (((1,), (0,)), ((), ())), preferred_element_type=f32)


def dot_nt(a, b):
    return lax.dot_general(a, b, (((1,), (1,)), ((), ())), preferred_element_type=f32)


def dot_tn(a, b):
    return lax.dot_general(a, b, (((0,), (0,)), ((), ())), preferred_element_type=f32)


def low(v):
    return v.astype(bf16)


def gelu_parts(z):
    a = jnp.abs(z)
    d = 1.0 + 0.23164189 * a
    t = pl.reciprocal(d, approx=True)
    t = t * (2.0 - d * t)
    ex = jnp.exp(-0.5 * (z * z))
    poly = t * (
        0.127414796 + t * (-0.142248368 + t * (0.7107068705 + t * (-0.7265760135 + t * 0.5307027145)))
    )
    h = poly * ex
    cdf = jnp.where(z >= 0, 1.0 - h, h)
    pdf = 0.3989422804014327 * ex
    return z * cdf, cdf + z * pdf, pdf


def lane_sum(v):
    return jnp.sum(v, -1, keepdims=True)


def masks(head_dim):
    pair = 2 * head_dim
    rows, cols = 2 * MB, pair
    r = lax.broadcasted_iota(jnp.int32, (rows, cols), 0)
    c = lax.broadcasted_iota(jnp.int32, (rows, cols), 1)
    own = ((r < MB) == (c < head_dim)).astype(f32)
    r = lax.broadcasted_iota(jnp.int32, (rows, rows), 0)
    c = lax.broadcasted_iota(jnp.int32, (rows, rows), 1)
    same = (r < MB) == (c < MB)
    causal = (same & (c <= r)).astype(f32)
    return own, causal, same.astype(bf16)


def spread(v, own):
    return jnp.concatenate([v, v], 0) * own


def fold(v):
    return v[:MB] + v[MB:]


def twice(v):
    return jnp.concatenate([v, v], 1)


def pair_index(p, pairs, array):
    return jnp.minimum(lax.axis_index("group") * pairs + p, array.shape[0] - 1)


def load_params(par_ref, sources, places):
    for i, source in enumerate(sources):
        for p, n in enumerate(places):
            par_ref[i, p] = jnp.concatenate([source[pl.ds(2 * n + h, 1)] for h in range(2)], 1)


def rate_rows(rates, p):
    return jnp.concatenate([jnp.broadcast_to(rates[:, n : n + 1], rates.shape) for n in (2 * p, 2 * p + 1)], 0)


def in_turn(parts):
    while parts:
        parts = [part for part in parts if next(part, parts) is not parts]


def forward_kernel(pairs, head_dim, restart_ref, q_ref, k_ref, v_ref, rate_ref, w1i_ref, b1i_ref, w2i_ref, b2i_ref, gain_in, bias_in,
                   big_ref, mid_ref, small_ref, n1_ref, pq_ref, uq_ref, n2_ref, out_ref,
                   w1, b1, w2, b2, s_q1, s_x2, s_e2, s_w2, s_b2, s_q, par_ref):
    j = pl.program_id(0)
    pair = 2 * head_dim
    inv = 1.0 / head_dim
    own, causal, ones = masks(head_dim)

    @pl.when(j == 0)
    def _():
        load_params(par_ref, (b2i_ref, gain_in, bias_in), [pair_index(p, pairs, w1i_ref) for p in range(pairs)])

    @pl.when(restart_ref[j] > 0)
    def _():
        for p in range(pairs):
            n = pair_index(p, pairs, w1i_ref)
            second = w2i_ref[n]
            second_bias = par_ref[0, p] * own
            w1[p] = w1i_ref[n]
            for h in range(2):
                b1[p, h * MB : (h + 1) * MB] = jnp.broadcast_to(b1i_ref[pl.ds(2 * n + h, 1)], (MB, b1i_ref.shape[1]))
                half = second[h * head_dim : (h + 1) * head_dim]
                w2[p, h * head_dim : (h + 1) * head_dim] = half - jnp.sum(half, 0, keepdims=True) * inv
            b2[p] = second_bias - (lane_sum(second_bias) * inv) * own

    loaded = [
        (s_q1[p], s_x2[p], s_e2[p], s_w2[p], s_b2[p], s_q[p], w1[p], w2[p], b1[p], b2[p], rate_rows(rate_ref[...], p))
        for p in range(pairs)
    ]
    tokens = [
        [ref[:, p * pair : (p + 1) * pair] for ref in (q_ref, k_ref, v_ref)]
        + [par_ref[i, p] for i in (1, 2)]
        for p in range(pairs)
    ]
    writes = []

    def write(ref, index, value):
        writes.append((ref, index, value))

    def outputs_before(p):
        q1p, x2p, e2p, w2p, b2p, qp = loaded[p][:6]
        gain, bias = tokens[p][3:]
        p2, lq, _ = gelu_parts(q1p)
        p2b = low(p2)
        yield
        n2 = causal * (dot_nt(p2b, x2p) + 1.0)
        q2 = dot_nt(p2b, w2p)
        yield
        q2 = q2 * own - dot(low(n2), e2p) + b2p
        yield
        sq = lax.rsqrt(lane_sum(q2 * q2) * inv + epsilon)
        uq = q2 * sq
        write(out_ref, (slice(None), slice(p * pair, (p + 1) * pair)), qp + fold(uq) * gain + bias)
        write(pq_ref, (0, p, slice(0, 2 * MB)), p2b)
        write(pq_ref, (0, p, slice(2 * MB, 4 * MB)), low(lq))
        write(uq_ref, (0, p, slice(0, 2 * MB)), uq)
        write(uq_ref, (0, p, slice(2 * MB, 4 * MB)), jnp.broadcast_to(sq, uq.shape))
        write(n2_ref, (0, p), low(n2))

    def inner_step(p):
        w1c, w2c, b1c, b2c, e = loaded[p][6:]
        qc, kc, vc, gain, bias = tokens[p]
        kb, qb = low(spread(kc, own)), low(spread(qc, own))
        w1b, w2b = low(w1c), low(w2c)
        kq = dot(jnp.concatenate([kb, qb], 0), w1b)
        yield
        z1 = kq[: 2 * MB] + b1c
        x2, l1, pdf = gelu_parts(z1)
        x2b = low(x2)
        yield
        c = dot_nt(x2b, w2b)
        n1 = causal * (dot_nt(qb, kb) + 1.0)
        yield
        c = c * own + b2c
        s = lax.rsqrt(lane_sum(c * c) * inv + epsilon)
        u = c * s
        r = u * (gain * gain) + spread((bias - (vc - kc)) * gain, own)
        yield
        mr, m2 = lane_sum(r) * inv, lane_sum(r * u) * inv
        g2 = s * (r - mr * own - u * m2)
        yield
        h = dot(low(g2), w2b)
        e2b = low(e * g2)
        yield
        g1 = h * l1
        e1b = low(twice(e) * g1)
        yield
        u1 = dot_tn(kb, e1b)
        yield
        q1 = kq[2 * MB :] + b1c - dot(low(n1), e1b)
        yield
        write(w1, p, w1c - u1)
        write(b1, p, b1c - dot(ones, e1b))
        write(w2, p, w2c - dot_tn(e2b, x2b))
        write(b2, p, b2c - dot(ones, e2b))
        write(big_ref, (0, p, slice(0, pair)), w1b)
        write(big_ref, (0, p, slice(pair, 2 * pair)), w2b)
        write(big_ref, (0, p, slice(2 * pair, 2 * pair + 2 * MB)), x2b)
        write(big_ref, (0, p, slice(2 * pair + 2 * MB, 2 * pair + 4 * MB)), e1b)
        write(mid_ref, (0, p, slice(0, 2 * MB)), low(g1))
        write(mid_ref, (0, p, slice(2 * MB, 4 * MB)), low(l1))
        write(mid_ref, (0, p, slice(4 * MB, 6 * MB)), low(h * pdf * (2.0 - z1 * z1)))
        for i, value in enumerate((u, s, r, m2, g2)):
            write(small_ref, (0, p, slice(i * 2 * MB, (i + 1) * 2 * MB)), jnp.broadcast_to(value, u.shape))
        write(n1_ref, (0, p), low(n1))
        for ref, value in ((s_q1, q1), (s_x2, x2b), (s_e2, e2b), (s_w2, w2b), (s_b2, b2c), (s_q, qc)):
            write(ref, p, value)

    in_turn([inner_step(p) for p in range(pairs)] + [outputs_before(p) for p in range(pairs)])
    for ref, index, value in writes:
        ref[index] = value


def forward_inner(restarts, q, k, v, rates, w1i, b1i, w2i, b2i, gain, bias):
    _, pair, inner = w1i.shape
    blocks, pairs = q.shape[0] // MB, q.shape[1] // pair
    head_dim = pair // 2
    steps = blocks + 1
    last = blocks - 1
    tok = pl.BlockSpec((MB, pairs * pair), lambda j, r: (jnp.minimum(j, last), 0))
    whole = lambda a: pl.BlockSpec(a.shape, lambda j, r: (0,) * a.ndim)

    def per_step(rows, width, dtype):
        return (
            jax.ShapeDtypeStruct((steps, pairs, rows, width), dtype),
            pl.BlockSpec((1, pairs, rows, width), lambda j, r: (j, 0, 0, 0)),
        )

    outs = [
        per_step(2 * pair + 4 * MB, inner, bf16),
        per_step(6 * MB, inner, bf16),
        per_step(10 * MB, pair, f32),
        per_step(2 * MB, 2 * MB, bf16),
        per_step(4 * MB, inner, bf16),
        per_step(4 * MB, pair, f32),
        per_step(2 * MB, 2 * MB, bf16),
        (
            jax.ShapeDtypeStruct((steps * MB, pairs * pair), f32),
            pl.BlockSpec((MB, pairs * pair), lambda j, r: (j, 0)),
        ),
    ]
    return pl.pallas_call(
        partial(forward_kernel, pairs, head_dim),
        grid_spec=pltpu.PrefetchScalarGridSpec(
            num_scalar_prefetch=1,
            grid=(steps,),
            in_specs=[tok, tok, tok, pl.BlockSpec((MB, 128), lambda j, r: (jnp.minimum(j, last), 0))]
            + [whole(a) for a in (w1i, b1i, w2i, b2i, gain, bias)],
            out_specs=[o[1] for o in outs],
            scratch_shapes=[
                pltpu.VMEM((pairs, pair, inner), f32),
                pltpu.VMEM((pairs, 2 * MB, inner), f32),
                pltpu.VMEM((pairs, pair, inner), f32),
                pltpu.VMEM((pairs, 2 * MB, pair), f32),
                pltpu.VMEM((pairs, 2 * MB, inner), f32),
                pltpu.VMEM((pairs, 2 * MB, inner), bf16),
                pltpu.VMEM((pairs, 2 * MB, pair), bf16),
                pltpu.VMEM((pairs, pair, inner), bf16),
                pltpu.VMEM((pairs, 2 * MB, pair), f32),
                pltpu.VMEM((pairs, MB, pair), f32),
                pltpu.VMEM((3, pairs, 1, pair), f32),
            ],
        ),
        out_shape=[o[0] for o in outs],
        compiler_params=pltpu.CompilerParams(vmem_limit_bytes=48 * 1024 * 1024),
        name="inner_forward",
    )(restarts, q, k, v, rates, w1i, b1i, w2i, b2i, gain, bias)


MESH = pl.DeviceIdType.MESH


def greet(peers):
    barrier = pltpu.get_barrier_semaphore()
    for peer in peers:
        pl.semaphore_signal(barrier, inc=1, device_id=peer, device_id_type=MESH)
    pl.semaphore_wait(barrier, len(peers))


class Copies:
    def __init__(self, send_sem, recv_sem):
        self.send_sem, self.recv_sem, self.started = send_sem, recv_sem, []

    def make(self, src, dst, peer):
        i = len(self.started)
        copy = pltpu.make_async_remote_copy(
            src_ref=src, dst_ref=dst, send_sem=self.send_sem.at[i], recv_sem=self.recv_sem.at[i],
            device_id=peer, device_id_type=MESH,
        )
        self.started.append(copy)
        return copy

    def send(self, src, dst, peer):
        copy = self.make(src, dst, peer)
        copy.start()
        return copy


def rows_at(start, size):
    return pl.ds(pl.multiple_of(start, 16), size)


def add_low(a, b):
    return (a.astype(f32) + b.astype(f32)).astype(bf16)


def mates(axis):
    size, here = lax.axis_size(axis), lax.axis_index(axis)
    return [{axis: lax.rem(here + o, size)} for o in range(1, size)]


def feed_sum_steps(ins, outs, got_group, sum_group, got_row, full, copies, whole):
    row, group = lax.axis_index("row"), lax.axis_index("group")
    rows, groups = lax.axis_size("row"), lax.axis_size("group")
    row_mates, group_mates = mates("row"), mates("group")
    count = len(ins)
    part = ins[0].shape[0] // groups
    unit = part // rows
    mine = rows_at(row * unit, unit)
    moves = {}
    for i in range(count):
        moves["X", i] = [
            copies.make(ins[i].at[rows_at(lax.rem(group + o, groups) * part, part)], got_group[i].at[o - 1], group_mates[o - 1])
            for o in range(1, groups)
        ]
        moves["Z", i] = [
            copies.make(sum_group[i].at[rows_at(lax.rem(row + o, rows) * unit, unit)], got_row[i].at[o - 1], row_mates[o - 1])
            for o in range(1, rows)
        ]
        if i < whole:
            here = full[i].at[group, mine]
            moves["ZA", i] = [copies.make(here, here, mate) for mate in row_mates]
            here = full[i].at[group]
            moves["XA", i] = [copies.make(here, here, mate) for mate in group_mates]

    def finish(kind, i):
        for copy in moves[kind, i]:
            copy.wait_recv()
        if kind == "X":
            total = ins[i][rows_at(group * part, part)].astype(f32)
            for o in range(1, groups):
                total = total + got_group[i][o - 1].astype(f32)
            sum_group[i][...] = low(total)
        if kind == "Z":
            total = sum_group[i][mine].astype(f32)
            for o in range(1, rows):
                total = total + got_row[i][o - 1].astype(f32)
            if i < whole:
                full[i][group, mine] = low(total)
            else:
                outs[i][...] = low(total)

    def run(slot):
        _, done, begun = FEED_SLOTS[slot]
        if slot == 0:
            greet(row_mates + group_mates)
        for name in done:
            finish(name[:-1], int(name[-1]))
        for name in begun:
            for copy in moves[name[:-1], int(name[-1])]:
                copy.start()
        if slot == len(FEED_SLOTS) - 1:
            for i in range(whole):
                outs[i][...] = full[i][...]
            for copy in copies.started:
                copy.wait_send()

    return [partial(run, slot) for slot in range(len(FEED_SLOTS))]


def backward_kernel(pairs, head_dim, feeds, restart_ref,
                    qq_ref, kq_ref, doq_ref, eq_ref, bigq_ref, g2q_ref, n1_ref, pqq_ref, uqq_ref, n2_ref,
                    q_ref, k_ref, v_ref, do_ref, e_ref, big_ref, mid_ref, small_ref, pq_ref, uq_ref, gain_in, bias_in, *refs):
    j = pl.program_id(0)
    steps = pl.num_programs(0)
    pair = 2 * head_dim
    inv = 1.0 / head_dim
    own, causal, ones = masks(head_dim)
    feed_in, refs = refs[:feeds], refs[feeds:]
    dq_ref, dk_ref, dv_ref, de_ref, gw1, gb1, gw2, gb2, ggain, gbias = refs[:10]
    feed_out, refs = refs[10 : 10 + feeds], refs[10 + feeds :]
    w1, b1, w2, b2, s_e1, s_e2, s_k, s_x2, s_q1, s_q2, s_q, par_ref = refs[:12]
    if feeds:
        refs, sems = refs[12:-2], refs[-2:]
        buffers = [refs[i * feeds : (i + 1) * feeds] for i in range(3)] + [refs[3 * feeds :]]
        slots = feed_sum_steps(feed_in, feed_out, *buffers, Copies(*sems), FEED_WHOLE)
        for i, run in enumerate(slots):
            pl.when(j == FEED_SLOTS[i][0] * (steps - 1) // 32)(run)

    @pl.when(j == 0)
    def _():
        places = [jnp.minimum(lax.axis_index("group") * pairs + p, gain_in.shape[0] // 2 - 1) for p in range(pairs)]
        load_params(par_ref, (gain_in, bias_in), places)

    @pl.when(j <= 1)
    def _():
        for ref in (w1, b1, w2, b2, gw1, gb1, gw2, gb2, ggain, gbias):
            ref[...] = jnp.zeros_like(ref)

    rows2 = 2 * MB
    piece = lambda ref, p, i: ref[0, p, i * rows2 : (i + 1) * rows2]
    token = lambda ref, p: ref[:, p * pair : (p + 1) * pair]
    first = restart_ref[jnp.minimum(steps - 1 - j, steps - 2)]
    go_on = 1.0 - first
    writes = []

    def write(ref, index, value):
        writes.append((ref, index, value))

    def load_outputs(p):
        return (
            [token(ref, p) for ref in (qq_ref, kq_ref, doq_ref)]
            + [par_ref[0, p]]
            + [bigq_ref[0, p, 0:pair], bigq_ref[0, p, pair : 2 * pair]]
            + [bigq_ref[0, p, 2 * pair : 2 * pair + rows2], bigq_ref[0, p, 2 * pair + rows2 : 2 * pair + 2 * rows2]]
            + [rate_rows(eq_ref[...], p), g2q_ref[0, p], n1_ref[0, p], n2_ref[0, p]]
            + [piece(ref, p, i) for ref in (pqq_ref, uqq_ref) for i in range(2)]
        )

    def load_step(p):
        return (
            [ref[p] for ref in (s_e1, s_e2, s_k, s_x2, s_q1, s_q2, s_q, w1, w2, b1, b2)]
            + [token(ref, p) for ref in (q_ref, k_ref, v_ref, do_ref)]
            + [par_ref[i, p] for i in (0, 1)]
            + [big_ref[0, p, 0:pair], big_ref[0, p, pair : 2 * pair]]
            + [big_ref[0, p, 2 * pair : 2 * pair + rows2], big_ref[0, p, 2 * pair + rows2 : 2 * pair + 2 * rows2]]
            + [piece(mid_ref, p, i).astype(f32) for i in range(3)]
            + [piece(small_ref, p, i) for i in range(5)]
            + [pq_ref[0, p], uq_ref[0, p], rate_rows(e_ref[...], p)]
        )

    def outputs_ahead(p, loaded):
        qc, kc, do, gain, w1b, w2b, x2b, e1b, e, g2, n1b, n2b, p2b, lq, uq, sq = loaded
        qb, kb = low(spread(qc, own)), low(spread(kc, own))
        e2b = low(e * g2)
        w = spread(do * gain, own)
        dq2 = low(sq * (w - (lane_sum(w) * inv) * own - uq * (lane_sum(w * uq) * inv)))
        yield
        dn2 = dot_nt(dq2, e2b)
        dp2 = dot(dq2, w2b)
        yield
        dpx = low(-causal * dn2)
        new_e2 = dot_tn(n2b, dq2)
        dp2 = dp2 + dot(dpx, x2b)
        yield
        dq1 = low(dp2 * lq.astype(f32))
        new_x2 = dot_tn(dpx, p2b)
        yield
        dn1 = dot_nt(dq1, e1b)
        new_q = dot_nt(dq1, w1b)
        yield
        new_e1 = dot_tn(n1b, dq1)
        dqk = low(-causal * dn1)
        yield
        new_k = dot_tn(dqk, qb)
        new_q = do + fold((new_q + dot(dqk, kb)) * own)
        for ref, value in zip((s_e1, s_e2, s_k, s_x2, s_q1, s_q2, s_q), (new_e1, new_e2, new_k, new_x2, dq1, dq2, new_q)):
            write(ref, p, value)

    def step_back(p, loaded):
        e1q, e2q, dkq, x2q, dq1, dq2, dqc, dw1, dw2, db1, db2, qc, kc, vc, do, gain, bias, w1b, w2b, x2b, e1b = loaded[:21]
        g1, l1, hg, u, s, r, m2, g2, p2b, uq, e = loaded[21:]
        cols = (slice(None), slice(p * pair, (p + 1) * pair))
        dw1b, dw2b = low(dw1), low(dw2)
        qb, kb = low(spread(qc, own)), low(spread(kc, own))
        e2b = low(e * g2)
        de1 = dot(kb, dw1b)
        de2 = dot_nt(x2b, dw2b)
        yield
        de1 = -(e1q + de1 + db1)
        de2 = -(e2q + de2 * own + db2)
        dg1 = twice(e) * de1
        dh = low(dg1 * l1)
        yield
        dg2 = dot_nt(dh, w2b)
        dx2 = x2q - dot(e2b, dw2b)
        yield
        dg2 = e * de2 + dg2 * own
        dk = dkq - dot_nt(e1b, dw1b) * own
        ma, mg = lane_sum(dg2 * u) * inv, lane_sum(dg2) * inv
        rate = jnp.broadcast_to(lane_sum(g1 * de1) + lane_sum(g2 * de2), u.shape)
        rates.append(jnp.where(head == 2 * p, rate[:MB], 0.0) + jnp.where(head == 2 * p + 1, rate[MB:], 0.0))
        yield
        dr = s * (dg2 - mg * own - u * ma)
        du = dr * (gain * gain) - s * (dg2 * m2 + r * ma)
        yield
        md, mu = lane_sum(du) * inv, lane_sum(du * u + dg2 * g2) * inv
        dz2 = low(s * (du - md * own - u * mu))
        yield
        dx2 = dx2 + dot(dz2, w2b)
        yield
        dz1 = low(dg1 * hg + dx2 * l1)
        drg = fold(dr) * gain
        write(dq_ref, cols, low(dqc))
        write(dv_ref, cols, low(-drg))
        more_gain = fold(spread_by(do, uq)) + fold(dr * u) * (2.0 * gain) + fold(dr) * (bias - (vc - kc))
        yield
        ndw1 = dw1 + dot_tn(jnp.concatenate([qb, kb], 0), jnp.concatenate([dq1, dz1], 0))
        yield
        dk = dk + dot_nt(dz1, w1b) * own
        write(dk_ref, cols, low(fold(dk) + drg))
        ndw2 = dw2 + dot_tn(jnp.concatenate([dq2, low(g2), dz2], 0), jnp.concatenate([p2b, dh, x2b], 0))
        ndb1 = db1 + dot(ones, dq1) + dot(ones, dz1)
        ndb2 = db2 + dot(ones, dq2) + dot(ones, dz2)
        for ref, value in ((w1, ndw1), (w2, ndw2), (b1, ndb1), (b2, ndb2)):
            write(ref, p, value * go_on)
        more.append((cols, more_gain, do + drg))
        starts.append((p, ndw1, ndw2, ndb1, ndb2))

    more, starts, rates = [], [], []
    head = lax.broadcasted_iota(jnp.int32, (MB, pair), 1)
    ahead_in = [load_outputs(p) for p in range(pairs)]
    step_in = [load_step(p) for p in range(pairs)]
    in_turn([step_back(p, step_in[p]) for p in range(pairs)] + [outputs_ahead(p, ahead_in[p]) for p in range(pairs)])
    for ref, index, value in writes:
        ref[index] = value
    de_ref[...] = sum(rates)
    for cols, more_gain, more_bias in more:
        ggain[cols] += more_gain
        gbias[cols] += more_bias
    for p, *values in starts:
        for ref, value in zip((gw1, gw2, gb1, gb2), values):
            ref[p] += value * first


def spread_by(do, uq):
    return jnp.concatenate([do, do], 0) * uq


def backward_inner(restarts, q, k, v, do, rates, saved, gain, bias, feed_terms, collective_id):
    big, mid, small, n1, pq, uq, n2 = saved
    pairs, pair, inner = big.shape[1], 2 * gain.shape[1], big.shape[3]
    blocks = q.shape[0] // MB
    head_dim = pair // 2
    steps = blocks + 1
    rate = lambda at: pl.BlockSpec((MB, 128), lambda j: (at(j), 0))
    now = lambda j: jnp.minimum(blocks - j, blocks - 1)
    ahead = lambda j: jnp.maximum(blocks - 1 - j, 0)
    tok = lambda at: pl.BlockSpec((MB, pairs * pair), lambda j: (at(j), 0))

    def block(a, at, rows=None, part=0):
        shape = (1, pairs, rows or a.shape[2], a.shape[3])
        return pl.BlockSpec(shape, lambda j: (at(j), 0, part, 0))

    whole = lambda a: pl.BlockSpec(a.shape, lambda j: (0,) * a.ndim)
    later = lambda j: ahead(j) + 1
    at_now = lambda j: now(j) + 1
    operands = [
        (q, tok(ahead)), (k, tok(ahead)), (do, tok(ahead)), (rates, rate(ahead)), (big, block(big, ahead)),
        (small, block(small, ahead, 2 * MB, 4)), (n1, block(n1, ahead)), (pq, block(pq, later)), (uq, block(uq, later)),
        (n2, block(n2, later)),
        (q, tok(now)), (k, tok(now)), (v, tok(now)), (do, tok(now)), (rates, rate(now)), (big, block(big, now)),
        (mid, block(mid, now)), (small, block(small, now)), (pq, block(pq, at_now, 2 * MB)), (uq, block(uq, at_now, 2 * MB)),
        (gain, whole(gain)), (bias, whole(bias)),
    ]
    feeds = len(feed_terms)
    vmem = pl.BlockSpec(memory_space=pltpu.VMEM)
    operands += [(a, vmem) for a in feed_terms]
    width = pairs * pair
    tok_out = (jax.ShapeDtypeStruct((steps * MB, width), bf16), pl.BlockSpec((MB, width), lambda j: (blocks - j, 0)))
    state = [((pairs, pair, inner), f32), ((pairs, 2 * MB, inner), f32), ((pairs, pair, inner), f32), ((pairs, 2 * MB, pair), f32)]
    keep = lambda shape: (jax.ShapeDtypeStruct(shape, f32), pl.BlockSpec(shape, lambda j: (0,) * len(shape)))
    outs = [tok_out] * 3 + [
        (jax.ShapeDtypeStruct((steps * MB, pair), f32), pl.BlockSpec((MB, pair), lambda j: (blocks - j, 0)))
    ] + [keep(shape) for shape, _ in state] + [keep((MB, width))] * 2
    comm = []
    if feeds:
        groups, rows = lax.axis_size("group"), lax.axis_size("row")
        part, wide = feed_terms[0].shape[0] // groups, feed_terms[0].shape[1]
        unit = part // rows
        outs += [
            (jax.ShapeDtypeStruct((groups, part, wide) if i < FEED_WHOLE else (unit, wide), bf16), vmem) for i in range(feeds)
        ]
        comm = [pltpu.VMEM((groups - 1, part, wide), bf16)] * feeds + [pltpu.VMEM((part, wide), bf16)] * feeds
        comm += [pltpu.VMEM((rows - 1, unit, wide), bf16)] * feeds + [pltpu.VMEM((groups, part, wide), bf16)] * FEED_WHOLE
        copies = (feeds + FEED_WHOLE) * (groups + rows - 2)
        comm += [pltpu.SemaphoreType.DMA((copies,))] * 2
    return pl.pallas_call(
        partial(backward_kernel, pairs, head_dim, feeds),
        grid_spec=pltpu.PrefetchScalarGridSpec(
            num_scalar_prefetch=0,
            grid=(steps,),
            in_specs=[pl.BlockSpec(memory_space=pltpu.SMEM)] + [o[1] for o in operands],
            out_specs=[o[1] for o in outs],
            scratch_shapes=[pltpu.VMEM(shape, kind) for shape, kind in state] + [
                pltpu.VMEM((pairs, 2 * MB, inner), f32),
                pltpu.VMEM((pairs, 2 * MB, pair), f32),
                pltpu.VMEM((pairs, 2 * MB, pair), f32),
                pltpu.VMEM((pairs, 2 * MB, inner), f32),
                pltpu.VMEM((pairs, 2 * MB, inner), bf16),
                pltpu.VMEM((pairs, 2 * MB, pair), bf16),
                pltpu.VMEM((pairs, MB, pair), f32),
                pltpu.VMEM((2, pairs, 1, pair), f32),
            ] + comm,
        ),
        out_shape=[o[0] for o in outs],
        compiler_params=pltpu.CompilerParams(
            collective_id=collective_id if feeds else None, has_side_effects=bool(feeds), vmem_limit_bytes=56 * 1024 * 1024
        ),
        name="inner_backward",
    )(restarts.astype(f32), *[o[0] for o in operands])


def norm_parts(v, width):
    centered = v - jnp.sum(v, -1, keepdims=True) * (1.0 / width)
    scale = lax.rsqrt(jnp.sum(centered * centered, -1, keepdims=True) * (1.0 / width) + epsilon)
    return centered * scale, scale


def feed_terms(*items):
    for outs, left, right in items:
        width = left.shape[1]
        for i, out in enumerate(outs):
            both = low(dot_tn(left[...], right[:, i * 256 : (i + 1) * 256]))
            out[0:width] = both[:, :128]
            out[width : 2 * width] = both[:, 128:]


def middle_kernel(span, mixed_in, tok_ref, cot_ref, wout_in, gate_in, up_in, down_in, gain_ref,
                  block_ref, hid_ref, gmix_ref, gwo_ref, t0, t1, t2, t3, t4, t5, gfeed_ref,
                  wout_ref, gate_ref, up_ref, down_ref, downs, mixed_ref, mixed_got, acts, cots, unit, scales, h_in, gg, gu, ha, pg0, po0, out_core, in_core, out_diag, in_diag, out_y, in_y,
                  branch, branch_row, send_sem, recv_sem, local_sem):
    rows, groups = lax.axis_size("row"), lax.axis_size("group")
    row, group, feat = lax.axis_index("row"), lax.axis_index("group"), lax.axis_index("feat")
    count, width = tok_ref.shape
    cols = mixed_ref.shape[1]
    core, y = lax.rem(feat, 2), feat // 2
    core_mate, y_mate = {"feat": feat + 1 - 2 * core}, {"feat": feat + 2 - 4 * y}
    here = row * groups + group
    places = rows * groups
    others = [lax.rem(here + o, places) for o in range(1, places)]
    seq_mates = [{"row": t // groups, "group": lax.rem(t, groups)} for t in others]
    copies = Copies(send_sem, recv_sem)
    send = copies.send
    slot = lambda ref, s: ref.at[s * count : (s + 1) * count]

    loads = [
        pltpu.make_async_copy(src, dst, local_sem.at[1 + i])
        for i, (src, dst) in enumerate(((down_in, down_ref), (wout_in, wout_ref), (gate_in, gate_ref), (up_in, up_ref)))
    ]
    for load in loads:
        load.start()
    mixed_ref[...] = low(mixed_in[MB:])
    greet([core_mate, y_mate] + seq_mates)
    lanes = pl.ds(pl.multiple_of(group * cols, 128), cols)
    moves = [
        send(mixed_ref.at[rows_at(t * span, span)], mixed_got.at[rows_at(row * span, span), lanes], mate)
        for t, mate in zip(others, seq_mates)
    ]
    own = pltpu.make_async_copy(
        mixed_ref.at[rows_at(here * span, span)], mixed_got.at[rows_at(row * span, span), lanes], local_sem.at[0]
    )
    own.start()
    cot_core = send(cot_ref, slot(cots, 1), core_mate)
    cot_y = send(cot_ref, slot(cots, 2), y_mate)
    cots[0:count] = cot_ref[...]
    loads[0].wait()
    cot_core.wait_recv()
    downs[0 : 2 * count] = dot(cots[0 : 2 * count], down_ref[...])
    own.wait()
    loads[1].wait()
    for copy in moves:
        copy.wait_recv()
    hidden = tok_ref[...].astype(f32) + dot(mixed_got[:, :width], wout_ref[:width])
    h_in[...] = hidden
    unit_two, scale_two = norm_parts(hidden, width)
    unit[...] = unit_two
    scales[...] = jnp.broadcast_to(scale_two, scales.shape)
    gain = gain_ref[...].reshape(1, width)
    acts[0:count] = low(unit_two * gain)
    cut = count // 2
    span_of = lambda s, h: slice(s * count + h * cut, s * count + (h + 1) * cut)
    act_y = [send(acts.at[span_of(0, h)], acts.at[span_of(2, h)], y_mate) for h in range(2)]
    act_core = send(slot(acts, 0), slot(acts, 1), core_mate)
    cot_y.wait_recv()
    cot_diag = send(slot(cots, 2), slot(cots, 3), core_mate)
    loads[2].wait()
    loads[3].wait()

    def feed(part):
        gate_pre, up_value = dot(acts[part], gate_ref[...]), dot(acts[part], up_ref[...])
        grad = downs[part]
        sig = jax.nn.sigmoid(gate_pre)
        silu = gate_pre * sig
        ha[part] = low(silu * up_value)
        gg[part] = low(grad * up_value * sig * (1.0 + gate_pre * (1.0 - sig)))
        gu[part] = low(grad * silu)
        return dot_nt(gg[part], gate_ref[...]) + dot_nt(gu[part], up_ref[...])

    def forth(s):
        return dot_nt(ha[s * count : (s + 1) * count], down_ref[...])

    pg0[...] = feed(slice(0, count))
    act_core.wait_recv()
    out_core[0] = low(feed(slice(count, 2 * count)))
    core_sums = [send(out_core.at[0], in_core.at[0], core_mate)]
    cot_diag.wait_recv()
    downs[2 * count : 4 * count] = dot(cots[2 * count : 4 * count], down_ref[...])
    y_sums = []
    for h in range(2):
        rows_h = slice(h * cut, (h + 1) * cut)
        act_y[h].wait_recv()
        act_diag = send(acts.at[span_of(2, h)], acts.at[span_of(3, h)], core_mate)
        ahead = feed(span_of(2, h))
        act_diag.wait_recv()
        out_diag[0, rows_h] = low(feed(span_of(3, h)))
        diag_sum = send(out_diag.at[0, rows_h], in_diag.at[0, rows_h], core_mate)
        diag_sum.wait_recv()
        out_y[0, rows_h] = low(ahead + in_diag[0, rows_h].astype(f32))
        y_sums.append(send(out_y.at[0, rows_h], in_y.at[0, rows_h], y_mate))
    out_diag[1] = low(forth(3))
    diag_sum = send(out_diag.at[1], in_diag.at[1], core_mate)
    out_core[1] = low(forth(1))
    core_sums.append(send(out_core.at[1], in_core.at[1], core_mate))
    ahead = forth(2)
    diag_sum.wait_recv()
    out_y[1] = low(ahead + in_diag[1].astype(f32))
    y_sums.append(send(out_y.at[1], in_y.at[1], y_mate))
    po0[...] = forth(0)
    core_sums[0].wait_recv()
    y_sums[0].wait_recv()
    y_sums[1].wait_recv()
    grad_act = pg0[...] + in_core[0].astype(f32) + in_y[0].astype(f32)
    unit_two = unit[...]
    gfeed_ref[...] = jnp.sum(grad_act * unit_two, 0, keepdims=True)
    w = grad_act * gain
    inv = 1.0 / width
    grad = cot_ref[...].astype(f32) + scales[:, 0:1] * (
        w - jnp.sum(w, -1, keepdims=True) * inv - unit_two * (jnp.sum(w * unit_two, -1, keepdims=True) * inv)
    )
    hid_ref[...] = grad
    branch[...] = low(grad)
    row_mates, group_mates = mates("row"), mates("group")
    block = lambda r: branch_row.at[rows_at((r * groups + group) * span, span)]
    by_row = [
        send(branch.at[rows_at(lax.rem(row + o, rows) * span, span)], block(row), row_mates[o - 1]) for o in range(1, rows)
    ]
    block(row)[...] = branch[rows_at(row * span, span)]
    moves = [send(block(row), block(row), mate) for mate in group_mates]
    feed_terms(((t0, t1), acts, gg), ((t2, t3), acts, gu), ((t4, t5), cots, ha))
    for o in range(1, rows):
        by_row[o - 1].wait_recv()
        from_row = block(lax.rem(row - o + rows, rows))
        moves += [send(from_row, from_row, mate) for mate in group_mates]
    core_sums[1].wait_recv()
    y_sums[2].wait_recv()
    block_ref[...] = low(h_in[...] + po0[...] + in_core[1].astype(f32) + in_y[1].astype(f32))
    for copy in moves:
        copy.wait_recv()
    gmix_ref[...] = dot_nt(branch_row[...], wout_ref[rows_at(group * cols, cols)])
    for h in range(2):
        half = branch_row[:, h * (width // 2) : (h + 1) * (width // 2)]
        gwo_ref[h * cols : (h + 1) * cols] = low(dot_tn(mixed_ref[...], half))
    for copy in copies.started:
        copy.wait_send()


def middle(mixed_row, tokens, cotangent, out_weight, gate_weight, up_weight, down_weight, gain, span, collective_id):
    rows, groups = lax.axis_size("row"), lax.axis_size("group")
    length, cols = mixed_row.shape[0] - MB, mixed_row.shape[1]
    count, width = tokens.shape
    hidden = gate_weight.shape[1]
    copies = (rows * groups - 1) + (rows - 1) + rows * (groups - 1) + 18
    vmem = pl.BlockSpec(memory_space=pltpu.VMEM)
    outs = [
        ((count, width), bf16), ((count, width), f32), ((length, cols), f32), ((2 * cols, width // 2), bf16),
        *[((2 * width, 128), bf16)] * 6, ((1, width), f32),
    ]
    two = pltpu.VMEM((2, count, width), bf16)
    return pl.pallas_call(
        partial(middle_kernel, span),
        in_specs=[vmem] * 3 + [pl.BlockSpec(memory_space=pl.ANY)] * 4 + [vmem],
        out_specs=[vmem] * len(outs),
        out_shape=[jax.ShapeDtypeStruct(*o) for o in outs],
        scratch_shapes=[
            pltpu.VMEM(out_weight.shape, bf16),
            *[pltpu.VMEM((width, hidden), bf16)] * 3,
            pltpu.VMEM((4 * count, hidden), f32),
            pltpu.VMEM((length, cols), bf16),
            pltpu.VMEM((count, groups * cols), bf16),
            pltpu.VMEM((4 * count, width), bf16),
            pltpu.VMEM((4 * count, width), bf16),
            pltpu.VMEM((count, width), f32),
            pltpu.VMEM((count, 128), f32),
            pltpu.VMEM((count, width), f32),
            pltpu.VMEM((4 * count, hidden), bf16),
            pltpu.VMEM((4 * count, hidden), bf16),
            pltpu.VMEM((4 * count, hidden), bf16),
            pltpu.VMEM((count, width), f32),
            pltpu.VMEM((count, width), f32),
            two, two, two, two, two, two,
            pltpu.VMEM((count, width), bf16),
            pltpu.VMEM((length, width), bf16),
            pltpu.SemaphoreType.DMA((copies,)),
            pltpu.SemaphoreType.DMA((copies,)),
            pltpu.SemaphoreType.DMA((5,)),
        ],
        compiler_params=pltpu.CompilerParams(
            collective_id=collective_id, has_side_effects=True, vmem_limit_bytes=56 * 1024 * 1024
        ),
        name="middle",
    )(mixed_row, tokens, cotangent, out_weight, gate_weight, up_weight, down_weight, gain)


def own_lanes(array, mine):
    total = None
    for g in range(lax.axis_size("group")):
        part = array[:, g * mine : (g + 1) * mine].astype(f32)
        if part.shape[1]:
            part = jnp.concatenate([part, jnp.zeros((array.shape[0], 128 - part.shape[1]), f32)], 1)
            part = jnp.where(lax.axis_index("group") == g, part, 0.0)
            total = part if total is None else total + part
    return total.astype(array.dtype)


def head_kernel(span, heads, mine, head_dim, tok_ref, gain_ref, wq_ref, wk_ref, wv_ref, wr_ref, rb_ref,
                q_ref, k_ref, v_ref, act_ref, unit_ref, rate_ref, slope_ref, stat_ref, wown_ref, row_tok, send_sem, recv_sem):
    rows, groups = lax.axis_size("row"), lax.axis_size("group")
    row, group, feat = lax.axis_index("row"), lax.axis_index("group"), lax.axis_index("feat")
    row_mates, group_mates = mates("row"), mates("group")
    width = tok_ref.shape[2]
    cols = q_ref.shape[1]
    copies = Copies(send_sem, recv_sem)
    block = lambda r: row_tok.at[rows_at((r * groups + group) * span, span)]

    greet(row_mates + group_mates)
    by_row = [
        copies.send(tok_ref.at[lax.rem(row + o, rows)], block(row), row_mates[o - 1]) for o in range(1, rows)
    ]
    block(row)[...] = tok_ref[row]
    by_group = [copies.send(block(row), block(row), mate) for mate in group_mates]
    for o in range(1, rows):
        by_row[o - 1].wait_recv()
        here = block(lax.rem(row - o + rows, rows))
        by_group += [copies.send(here, here, mate) for mate in group_mates]
    for copy in by_group:
        copy.wait_recv()
    unit, _ = norm_parts(row_tok[...].astype(f32), width)
    unit_ref[...] = unit
    act = low(unit * gain_ref[...].reshape(1, width))
    act_ref[...] = act
    lanes = pl.ds(pl.multiple_of(group * cols, 128), cols)
    for out, weight in ((q_ref, wq_ref), (k_ref, wk_ref), (v_ref, wv_ref)):
        out[...] = dot(act, weight[:, lanes])
    rate_weight, rate_bias = own_lanes(wr_ref[...], mine), own_lanes(rb_ref[...].reshape(1, heads), mine)
    wown_ref[...] = rate_weight
    logits = dot(act, rate_weight) + rate_bias
    sigma = jax.nn.sigmoid(logits)
    lane = lax.broadcasted_iota(jnp.int32, logits.shape, 1)
    used = (lane < mine) & (group * mine + lane < heads)
    rate_ref[...] = sigma * (1.0 / head_dim)
    slope_ref[...] = jnp.where(used, sigma * (1.0 - sigma) * (1.0 / head_dim), 0.0)
    stat_ref[0:1] = jnp.sum(logits, 0, keepdims=True)
    top = jnp.max(jnp.max(jnp.where(used, logits, -3e38), 0, keepdims=True), 1, keepdims=True)
    place = row * lax.axis_size("feat") + feat
    stat_ref[1:2] = jnp.where(lane[0:1] == place, top, 0.0)
    for copy in copies.started:
        copy.wait_send()


def head(tokens, gain, weights, rate_weight, rate_bias, heads, mine, head_dim, collective_id):
    rows, groups = lax.axis_size("row"), lax.axis_size("group")
    _, span, width = tokens.shape
    length, cols = rows * groups * span, mine * head_dim
    vmem = pl.BlockSpec(memory_space=pltpu.VMEM)
    copies = (rows - 1) + rows * (groups - 1)
    outs = [((length, cols), f32)] * 3 + [((length, width), bf16), ((length, width), f32)]
    outs += [((length, 128), f32)] * 2 + [((2, 128), f32), ((width, 128), bf16)]
    return pl.pallas_call(
        partial(head_kernel, span, heads, mine, head_dim),
        in_specs=[vmem] * 7,
        out_specs=[vmem] * len(outs),
        out_shape=[jax.ShapeDtypeStruct(*o) for o in outs],
        scratch_shapes=[
            pltpu.VMEM((length, width), bf16),
            pltpu.SemaphoreType.DMA((copies,)),
            pltpu.SemaphoreType.DMA((copies,)),
        ],
        compiler_params=pltpu.CompilerParams(
            collective_id=collective_id, has_side_effects=True, vmem_limit_bytes=48 * 1024 * 1024
        ),
        name="head",
    )(tokens, gain, *weights, rate_weight, rate_bias)


TAIL_SLOTS = [
    ([], ["FZ3", "FZ0"]),
    ([], ["CORE4", "CORE3"]),
    (["CORE4"], ["CORE1", "Y4"]),
    (["CORE3"], ["CORE0", "Y3"]),
    (["CORE1"], ["CORE2"]),
    (["CORE0"], []),
    (["FZ3"], ["FX3", "FZ2"]),
    (["CORE2"], []),
    ([], ["PART0"]),
    ([], ["SC0"]),
    (["Y4"], ["Y2"]),
    (["SC0"], []),
    (["FZ0"], ["Z4"]),
    (["Y3"], ["Y0"]),
    (["FX3"], ["FX0"]),
    (["FZ2"], ["Z3"]),
    (["Y2"], ["Y1"]),
    (["Z4"], ["Z2"]),
    (["Y0"], ["SY0"]),
    (["Z3"], ["Z0"]),
    (["PART0"], ["FX2"]),
    (["Y1"], []),
    (["SY0"], []),
    (["Z2"], ["ZA2"]),
    (["FX0"], []),
    (["Z0"], ["ZA0"]),
    (["ZA2"], ["P2", "ZA3"]),
    (["FX2"], []),
    (["ZA0"], ["P0", "Z1"]),
    (["P2"], ["Q2"]),
    (["ZA3"], ["P3", "ZA4"]),
    (["P0"], ["Q0"]),
    (["Z1"], ["ZA1"]),
    (["ZA4"], ["P4", "FZ1"]),
    (["P3"], []),
    (["ZA1"], ["HOME0"]),
    (["Q2"], ["C2", "P1"]),
    (["C2"], []),
    (["P4"], ["Q3", "Q4"]),
    (["Q0"], ["C0"]),
    (["FZ1"], ["SZ0"]),
    (["C0"], []),
    (["P1"], ["FX1", "Q1"]),
    (["Q4"], ["C4"]),
    (["C4"], []),
    (["HOME0"], []),
    (["Q3"], ["C3"]),
    (["C3"], []),
    (["Q1"], ["C1"]),
    (["SZ0"], ["SX0"]),
    (["FX1"], []),
    (["C1"], []),
    (["SX0"], []),
]
TAIL_GROUP_FIRST = (True, True, False, False, True)


FEED_SLOTS = [
    (0, [], ["X0", "X1"]),
    (7, ["X0"], ["X5", "Z0"]),
    (10, ["X1"], ["X4", "Z1"]),
    (12, ["Z0"], ["ZA0"]),
    (13, ["X5"], ["X2"]),
    (15, ["Z1"], ["ZA1"]),
    (16, ["X4"], ["X3"]),
    (18, ["ZA0"], ["Z5"]),
    (19, ["X2"], ["XA0"]),
    (21, ["ZA1"], ["Z2"]),
    (22, ["X3"], ["XA1"]),
    (24, ["Z5"], ["Z4"]),
    (25, ["XA0"], []),
    (27, ["Z2"], ["Z3"]),
    (29, ["XA1"], []),
    (30, ["Z4"], []),
    (32, ["Z3"], []),
]
FEED_WHOLE = 2


def tail_kernel(span, shapes, feeds, act_ref, unit_ref, gq_ref, gk_ref, gv_ref, de_ref, slope_ref, wq_ref, wk_ref, wv_ref, wr_ref,
                gwo_ref, gw1, gb1, gw2, gb2, ggain, gbias, gfeed, stat_ref, *refs):
    rows, groups = lax.axis_size("row"), lax.axis_size("group")
    row, group, feat = lax.axis_index("row"), lax.axis_index("group"), lax.axis_index("feat")
    core, y = lax.rem(feat, 2), feat // 2
    core_mate, y_mate = {"feat": feat + 1 - 2 * core}, {"feat": feat + 2 - 4 * y}
    row_mates, group_mates = mates("row"), mates("group")
    count = len(shapes)
    feed_in, refs = refs[:feeds], refs[feeds:]
    outs, (home_out, small_out), refs = refs[:count], refs[count : count + 2], refs[count + 2 :]
    feed_out, refs = refs[:feeds], refs[feeds:]
    own, got_core, sum_core, got_y, sum_y, got_row = (refs[i * count : (i + 1) * count] for i in range(6))
    part, part_got, part_sum, small, small_core, small_got, send_sem, recv_sem = refs[6 * count :]
    length, width = act_ref.shape
    cols = gwo_ref.shape[0] // 2
    pairs, pair, inner = gw1.shape
    head_dim = pair // 2
    copies = Copies(send_sem, recv_sem)
    moves = {}

    def start(name, *what):
        moves[name] = [copies.send(*w) for w in what]

    greet([core_mate, y_mate] + row_mates + group_mates)

    half = [h // 2 for h, _ in shapes]
    quarter = [h // 4 for h, _ in shapes]
    piece = [h // (4 * rows) for h, _ in shapes]
    unit = feed_in[0].shape[0]
    place = (core * 2 + y) * rows + row
    source = list(own[:3]) + [gwo_ref, own[4]]
    grad_refs = (gq_ref, gk_ref, gv_ref)
    lanes = pl.ds(pl.multiple_of(group * cols, 128), cols)

    def token_gradient():
        logits = low(de_ref[0:length] * slope_ref[...])
        total = dot_nt(logits, wr_ref[...])
        for grad, weight in zip(grad_refs, (wq_ref, wk_ref, wv_ref)):
            total = total + dot_nt(grad[0:length], weight[:, lanes])
        for r in range(rows):
            for g in range(groups):
                part[g, r * span : (r + 1) * span] = low(total[(r * groups + g) * span : (r * groups + g + 1) * span])
        start("PART0", *[(part.at[lax.rem(group + o, groups)], part_got.at[o - 1], group_mates[o - 1]) for o in range(1, groups)])
        small[...] = jnp.zeros_like(small)
        small[0 : 2 * pairs] = dot_tn(logits, act_ref[...])[0 : 2 * pairs]
        for p in range(pairs):
            for h in range(2):
                n = 2 * p + h
                small[6 + n // 3 : 7 + n // 3, (n % 3) * inner : (n % 3 + 1) * inner] = gb1[p, h * MB : h * MB + 1]
            small[9:10, p * pair : (p + 1) * pair] = gb2[p, 0:1] + gb2[p, MB : MB + 1]
        small[8:9, 0:cols] = jnp.sum(ggain[...], 0, keepdims=True)
        small[8:9, cols : 2 * cols] = jnp.sum(gbias[...], 0, keepdims=True)
        small[9:10, width - 384 : width - 256] = jnp.sum(logits.astype(f32), 0, keepdims=True)
        small[9:10, width - 256 : width - 128] = stat_ref[0:1]
        small[9:10, width - 128 : width] = stat_ref[1:2]
        small[10:11] = jnp.sum(total * unit_ref[...], 0, keepdims=True)
        small[11:12] = gfeed[...]

    def finish(name):
        for copy in moves[name]:
            copy.wait_recv()
        kind, i = name[:-1], int(name[-1])
        if kind == "CORE":
            sum_core[i][...] = add_low(source[i][rows_at(core * half[i], half[i])], got_core[i][...])
        if kind == "Y":
            sum_y[i][...] = add_low(sum_core[i][rows_at(y * quarter[i], quarter[i])], got_y[i][...])
        if kind == "Z":
            value = sum_y[i][rows_at(row * piece[i], piece[i])].astype(f32)
            for o in range(1, rows):
                value = value + got_row[i][o - 1].astype(f32)
            outs[i][group, rows_at(place * piece[i], piece[i])] = low(value)
        if kind == "PART":
            value = part[group].astype(f32)
            for o in range(1, groups):
                value = value + part_got[o - 1].astype(f32)
            part_sum[...] = low(value)
            home_out[rows_at(row * span, span)] = part_sum[rows_at(row * span, span)]
        if kind == "SC":
            small_core[...] = small[...] + small_got[0]
        if kind == "SY":
            small_got[2 + row] = small_core[...] + small_got[1]
        if kind == "SZ":
            value = small_got[2]
            for r in range(1, rows):
                value = value + small_got[2 + r]
            small_out[group] = value

    def begin(name):
        kind, i = name[:-1], int(name[-1])
        if kind == "PART":
            token_gradient()
        if kind == "HOME":
            here = home_out.at[rows_at(row * span, span)]
            start(name, *[
                (part_sum.at[rows_at(lax.rem(row + o, rows) * span, span)], here, row_mates[o - 1]) for o in range(1, rows)
            ])
        if kind == "SC":
            start(name, (small, small_got.at[0], core_mate))
        if kind == "SY":
            start(name, (small_core, small_got.at[1], y_mate))
        if kind == "SZ":
            here = small_got.at[2 + row]
            start(name, *[(here, here, mate) for mate in row_mates])
        if kind == "SX":
            here = small_out.at[group]
            start(name, *[(here, here, mate) for mate in group_mates])
        if kind == "FZ":
            here = feed_out[i].at[group, rows_at(row * unit, unit)]
            here[...] = feed_in[i][...]
            start(name, *[(here, here, mate) for mate in row_mates])
        if kind == "FX":
            here = feed_out[i].at[group]
            start(name, *[(here, here, mate) for mate in group_mates])
        if kind == "CORE":
            if i < 3:
                own[i][...] = low(dot_tn(act_ref[...], grad_refs[i][0:length]))
            if i == 4:
                for p in range(pairs):
                    own[4][p * pair : (p + 1) * pair] = low(gw1[p])
                    own[4][cols + p * pair : cols + (p + 1) * pair] = low(gw2[p])
            start(name, (source[i].at[rows_at((1 - core) * half[i], half[i])], got_core[i], core_mate))
        if kind == "Y":
            start(name, (sum_core[i].at[rows_at((1 - y) * quarter[i], quarter[i])], got_y[i], y_mate))
        if kind == "Z":
            start(name, *[
                (sum_y[i].at[rows_at(lax.rem(row + o, rows) * piece[i], piece[i])], got_row[i].at[o - 1], row_mates[o - 1])
                for o in range(1, rows)
            ])
        if kind == "ZA":
            here = outs[i].at[group, rows_at(place * piece[i], piece[i])]
            start(name, *[(here, here, mate) for mate in row_mates])
        if kind in ("P", "Q", "C"):
            quarters = rows_at((core * 2 + y) * quarter[i], quarter[i])
            halves = rows_at(core * half[i], half[i])
            by_group = TAIL_GROUP_FIRST[i] == (kind == "P")
            if kind == "C":
                here, to = outs[i].at[:, halves], [core_mate]
            elif by_group:
                here, to = outs[i].at[group, quarters if kind == "P" else halves], group_mates
            else:
                here, to = (outs[i].at[group, quarters] if kind == "P" else outs[i].at[:, quarters]), [y_mate]
            start(name, *[(here, here, mate) for mate in to])

    for done, begun in TAIL_SLOTS:
        for name in done:
            finish(name)
        for name in begun:
            begin(name)
    for copy in copies.started:
        copy.wait_send()


def tail(act_row, unit_row, grads, de, slope, weights, rate_weight, grad_out, states, grad_feed_gain, stat, feed_parts, span, collective_id):
    rows, groups = lax.axis_size("row"), lax.axis_size("group")
    length, width = act_row.shape
    cols = grad_out.shape[0] // 2
    inner = states[0].shape[-1]
    shapes = [(width, cols)] * 3 + [(2 * cols, width // 2), (2 * cols, inner)]
    count, feeds = len(shapes), len(feed_parts)
    unit, wide = feed_parts[0].shape
    copies = count * (2 + 2 * (rows - 1) + (groups - 1) + 2) + (groups - 1) + (rows - 1) + 2 + (rows - 1) + (groups - 1)
    copies += feeds * (rows + groups - 2)
    vmem = pl.BlockSpec(memory_space=pltpu.VMEM)
    operands = [act_row, unit_row, *grads, de, slope, *weights, rate_weight, grad_out, *states, grad_feed_gain, stat, *feed_parts]
    outs = [((groups, h, w), bf16) for h, w in shapes]
    outs += [((rows * span, width), bf16), ((groups, 16, width), f32)]
    outs += [((groups, rows * unit, wide), bf16)] * feeds
    scratch = [pltpu.VMEM((h, w), bf16) for h, w in shapes]
    scratch += [pltpu.VMEM((h // 2, w), bf16) for h, w in shapes] * 2
    scratch += [pltpu.VMEM((h // 4, w), bf16) for h, w in shapes] * 2
    scratch += [pltpu.VMEM((rows - 1, h // (4 * rows), w), bf16) for h, w in shapes]
    scratch += [
        pltpu.VMEM((groups, rows * span, width), bf16),
        pltpu.VMEM((groups - 1, rows * span, width), bf16),
        pltpu.VMEM((rows * span, width), bf16),
        pltpu.VMEM((16, width), f32),
        pltpu.VMEM((16, width), f32),
        pltpu.VMEM((2 + rows, 16, width), f32),
        pltpu.SemaphoreType.DMA((copies,)),
        pltpu.SemaphoreType.DMA((copies,)),
    ]
    return pl.pallas_call(
        partial(tail_kernel, span, shapes, feeds),
        in_specs=[vmem] * len(operands),
        out_specs=[vmem] * len(outs),
        out_shape=[jax.ShapeDtypeStruct(*o) for o in outs],
        scratch_shapes=scratch,
        compiler_params=pltpu.CompilerParams(
            collective_id=collective_id, has_side_effects=True, vmem_limit_bytes=60 * 1024 * 1024
        ),
        name="tail",
    )(*operands)


def finish_kernel(heads, mine, head_dim, inner, total_logits, q_in, k_in, v_in, o_in, s_in, got_ref, small_ref, tok_ref, hid_ref, gain_ref,
                  f0, f1, f2, f3, f4, f5, rate_ref, rbias_ref, fbias_ref, sbias_ref, gain_out, bias_out, mixer_ref, feed_ref, stat_ref,
                  q_out, k_out, v_out, o_out, first_out, second_out, gate_out, up_out, down_out, in_out,
                  sq, sk, sv, so, s1, s2, sg, su, sd, si, sems):
    groups, width = q_in.shape[0], q_in.shape[1]
    cols = mine * head_dim
    sent = []

    def give(value_ref, out):
        copy = pltpu.make_async_copy(value_ref, out, sems.at[len(sent)])
        copy.start()
        sent.append(copy)

    for out, scratch, left, right in ((gate_out, sg, f0, f1), (up_out, su, f2, f3), (down_out, sd, f4, f5)):
        for i, cut in enumerate((left, right)):
            value = cut[...].reshape(2 * width, 128)
            for h in range(2):
                scratch[:, (2 * i + h) * 128 : (2 * i + h + 1) * 128] = value[h * width : (h + 1) * width].astype(f32)
        give(scratch, out)
    for out, scratch, array in ((q_out, sq, q_in), (k_out, sk, k_in), (v_out, sv, v_in)):
        for g in range(groups):
            size = min(cols, width - g * cols)
            if size > 0:
                scratch[:, g * cols : g * cols + size] = array[g, :, 0:size].astype(f32)
        give(scratch, out)
    for g in range(groups):
        size = min(cols, width - g * cols)
        if size > 0:
            for h in range(2):
                scratch = so.at[g * cols : g * cols + size, h * (width // 2) : (h + 1) * (width // 2)]
                scratch[...] = o_in[g, h * cols : h * cols + size].astype(f32)
    give(so, o_out)
    for n in range(heads):
        g, i = n // mine, n % mine
        s1[n] = s_in[g, i * head_dim : (i + 1) * head_dim].astype(f32)
        second = s_in[g, cols + i * head_dim : cols + (i + 1) * head_dim].astype(f32)
        s2[n] = second - jnp.sum(second, 0, keepdims=True) * (1.0 / head_dim)
    give(s1, first_out)
    give(s2, second_out)
    unit, scale = norm_parts(tok_ref[...].astype(f32), width)
    w = got_ref[...].astype(f32) * gain_ref[...].reshape(1, width)
    inv = 1.0 / width
    si[...] = hid_ref[...] + scale * (
        w - jnp.sum(w, -1, keepdims=True) * inv - unit * (jnp.sum(w * unit, -1, keepdims=True) * inv)
    )
    give(si, in_out)
    rates, total, top = [], 0.0, None
    for n in range(heads):
        g, i = n // mine, n % mine
        rates.append(small_ref[g, i : i + 1])
        rbias_ref[:, n : n + 1] = small_ref[g, 9:10, width - 384 + i : width - 383 + i]
        total = total + small_ref[g, 9:10, width - 256 + i : width - 255 + i]
        fbias_ref[n : n + 1] = small_ref[g, 6 + i // 3 : 7 + i // 3, (i % 3) * inner : (i % 3 + 1) * inner]
        own = slice(i * head_dim, (i + 1) * head_dim)
        second = small_ref[g, 9:10, own]
        sbias_ref[n : n + 1] = second - jnp.sum(second, -1, keepdims=True) * (1.0 / head_dim)
        gain_out[n : n + 1] = small_ref[g, 8:9, own]
        bias_out[n : n + 1] = small_ref[g, 8:9, cols + i * head_dim : cols + (i + 1) * head_dim]
    rates = jnp.concatenate(rates + [jnp.zeros((-heads % 8, width), f32)], 0) if heads % 8 else jnp.concatenate(rates, 0)
    rate_ref[...] = rates.T[:, :heads]
    mixer, feed = small_ref[0, 10:11], small_ref[0, 11:12]
    tops = small_ref[0, 9:10, width - 128 : width]
    peers = lax.axis_size("row") * lax.axis_size("feat")
    for g in range(1, groups):
        mixer, feed = mixer + small_ref[g, 10:11], feed + small_ref[g, 11:12]
        tops = jnp.maximum(tops, small_ref[g, 9:10, width - 128 : width])
    mixer_ref[...], feed_ref[...] = mixer.reshape(width), feed.reshape(width)
    lane = lax.broadcasted_iota(jnp.int32, tops.shape, 1)
    top = jnp.max(jnp.where(lane < peers, tops, -3e38), 1, keepdims=True)
    stat_ref[...] = jnp.where(lane == 0, total * (1.0 / total_logits), top)
    for copy in sent:
        copy.wait()


def finish(arrays, got, small, tokens, grad_hidden, gain, feed_sums, heads, mine, head_dim, inner, total_logits):
    count, width = tokens.shape
    hidden = 2 * 2 * 128
    vmem, anywhere = pl.BlockSpec(memory_space=pltpu.VMEM), pl.BlockSpec(memory_space=pl.ANY)
    little = [(width, heads), (1, heads), (heads, inner), (heads, head_dim), (heads, head_dim), (heads, head_dim)]
    little += [(width,), (width,), (1, 128)]
    large = [(width, width)] * 4 + [(heads, head_dim, inner)] * 2 + [(width, hidden)] * 3 + [(count, width)]
    operands = [*arrays, got, small, tokens, grad_hidden, gain, *feed_sums]
    return pl.pallas_call(
        partial(finish_kernel, heads, mine, head_dim, inner, total_logits),
        in_specs=[vmem] * len(operands),
        out_specs=[vmem] * len(little) + [anywhere] * len(large),
        out_shape=[jax.ShapeDtypeStruct(s, f32) for s in little + large],
        scratch_shapes=[pltpu.VMEM(s, f32) for s in large] + [pltpu.SemaphoreType.DMA((len(large),))],
        compiler_params=pltpu.CompilerParams(vmem_limit_bytes=56 * 1024 * 1024),
        name="finish",
    )(*operands)


SEQ = ("row", "group")


def per_device(
    tokens,
    cotangent,
    doc_starts,
    mixer_gain,
    query_weight,
    key_weight,
    value_weight,
    out_weight,
    rate_weight,
    rate_bias,
    first_init,
    first_bias_init,
    second_init,
    second_bias_init,
    inner_gain,
    inner_bias,
    feed_gain,
    gate_weight,
    up_weight,
    down_weight,
):
    rows, span, width = tokens.shape
    heads, head_dim, inner = first_init.shape
    groups = lax.axis_size("group")
    feats = lax.axis_size("feat")
    row, group = lax.axis_index("row"), lax.axis_index("group")
    count = rows * span
    blocks = span * rows * groups // MB
    pairs = -(-heads // (2 * groups))
    mine = 2 * pairs
    pair = 2 * head_dim
    spare = mine * groups - heads

    def padded(array, axis, size):
        edges = [(0, 0)] * array.ndim
        edges[axis] = (0, spare * size)
        return jnp.pad(array, edges) if spare else array

    weights = [padded(w, 1, head_dim) for w in (query_weight, key_weight, value_weight)]
    flat_tokens = tokens.reshape(count, width)
    queries, keys, values, act_row, unit_row, rates, slope, stat, rate_lanes = head(
        tokens, mixer_gain, weights, rate_weight, rate_bias, heads, mine, head_dim, 4
    )
    block_ids = jnp.arange(blocks + 1, dtype=jnp.int32)
    starts = lax.dynamic_index_in_dim(doc_starts, row, 0, False)
    restarts = ((block_ids == 0) | jnp.any(starts[:, None] == block_ids[None], 0)).astype(jnp.int32)
    by_pair = lambda a: a.reshape(heads // 2, pair, inner)
    *saved, mixed = forward_inner(
        restarts, queries, keys, values, rates, by_pair(first_init), first_bias_init, by_pair(second_init),
        second_bias_init, inner_gain, inner_bias,
    )

    block_out, grad_hidden, grad_mixed, grad_out_rows, *feed_terms, grad_feed_gain = middle(
        mixed, flat_tokens, cotangent.reshape(count, width), padded(out_weight, 0, head_dim),
        gate_weight, up_weight, down_weight, feed_gain, span, 1,
    )

    grad_q, grad_k, grad_v, grad_e, g_first, g_first_bias, g_second, g_second_bias, g_gain, g_bias, *feed_sums = (
        backward_inner(restarts, queries, keys, values, grad_mixed, rates, saved, inner_gain, inner_bias, feed_terms, 2)
    )
    reduced = tail(
        act_row, unit_row, (grad_q, grad_k, grad_v), grad_e, slope, weights, rate_lanes, grad_out_rows,
        (g_first, g_first_bias, g_second, g_second_bias, g_gain, g_bias), grad_feed_gain, stat,
        feed_sums[FEED_WHOLE:], span, 3,
    )
    arrays, (got, small), feed_sums = reduced[:5], reduced[5:7], [*feed_sums[:FEED_WHOLE], *reduced[7:]]
    (
        g_rate, g_rate_bias, g_first_bias, g_second_bias, g_gain, g_bias, g_mixer, g_feed, stats,
        g_query, g_key, g_value, g_out, g_first, g_second, g_gate, g_up, g_down, input_grad,
    ) = finish(
        arrays, got, small, flat_tokens, grad_hidden, mixer_gain, feed_sums, heads, mine, head_dim, inner,
        rows * groups * feats * count * heads,
    )
    return (
        block_out.reshape(rows, span, width),
        input_grad.reshape(rows, span, width),
        g_mixer,
        g_query,
        g_key,
        g_value,
        g_out,
        g_rate,
        g_rate_bias[0],
        g_first,
        g_first_bias,
        g_second,
        g_second_bias,
        g_gain,
        g_bias,
        g_feed,
        g_gate,
        g_up,
        g_down,
        stats[0, :2],
    )


def solution(mesh):
    feats = mesh.shape["feat"]

    def run(*arrays):
        rows = arrays[0].shape[0] // feats
        grid = jax.sharding.Mesh(mesh.devices.reshape(rows, -1, feats), ("row", "group", "feat"))
        by_token = P("feat", SEQ, None)
        by_hidden = P(None, "feat")
        return jax.shard_map(
            per_device,
            mesh=grid,
            in_specs=(by_token, by_token, P("feat", None)) + (P(),) * 14 + (by_hidden,) * 3,
            out_specs=(by_token, by_token) + (P(),) * 14 + (by_hidden,) * 3 + (P(),),
            check_vma=False,
        )(*arrays)

    return run
```

```python
from functools import partial

import jax
import jax.numpy as jnp
from jax import lax
from jax.experimental import pallas as pl
from jax.experimental.pallas import tpu as pltpu
from jax.sharding import PartitionSpec as P

MB = 16
epsilon = 1e-05
f32, bf16 = jnp.float32, jnp.bfloat16


def dot(a, b):
    return lax.dot_general(a, b, (((1,), (0,)), ((), ())), preferred_element_type=f32)


def dot_nt(a, b):
    return lax.dot_general(a, b, (((1,), (1,)), ((), ())), preferred_element_type=f32)


def dot_tn(a, b):
    return lax.dot_general(a, b, (((0,), (0,)), ((), ())), preferred_element_type=f32)


def low(v):
    return v.astype(bf16)


def gelu_parts(z):
    a = jnp.abs(z)
    d = 1.0 + 0.23164189 * a
    t = pl.reciprocal(d, approx=True)
    t = t * (2.0 - d * t)
    ex = jnp.exp(-0.5 * (z * z))
    poly = t * (
        0.127414796 + t * (-0.142248368 + t * (0.7107068705 + t * (-0.7265760135 + t * 0.5307027145)))
    )
    h = poly * ex
    cdf = jnp.where(z >= 0, 1.0 - h, h)
    pdf = 0.3989422804014327 * ex
    return z * cdf, cdf + z * pdf, pdf


def lane_sum(v):
    return jnp.sum(v, -1, keepdims=True)


def masks(head_dim):
    pair = 2 * head_dim
    rows, cols = 2 * MB, pair
    r = lax.broadcasted_iota(jnp.int32, (rows, cols), 0)
    c = lax.broadcasted_iota(jnp.int32, (rows, cols), 1)
    own = ((r < MB) == (c < head_dim)).astype(f32)
    r = lax.broadcasted_iota(jnp.int32, (rows, rows), 0)
    c = lax.broadcasted_iota(jnp.int32, (rows, rows), 1)
    same = (r < MB) == (c < MB)
    causal = (same & (c <= r)).astype(f32)
    return own, causal, same.astype(bf16)


def spread(v, own):
    return jnp.concatenate([v, v], 0) * own


def fold(v):
    return v[:MB] + v[MB:]


def twice(v):
    return jnp.concatenate([v, v], 1)


def pair_index(p, pairs, array):
    return jnp.minimum(lax.axis_index("group") * pairs + p, array.shape[0] - 1)


def load_params(par_ref, sources, places):
    for i, source in enumerate(sources):
        for p, n in enumerate(places):
            par_ref[i, p] = jnp.concatenate([source[pl.ds(2 * n + h, 1)] for h in range(2)], 1)


def rate_rows(rates, p):
    return jnp.concatenate([jnp.broadcast_to(rates[:, n : n + 1], rates.shape) for n in (2 * p, 2 * p + 1)], 0)


def fetch(sems, *moves):
    copies = [pltpu.make_async_copy(src, dst, sems.at[i]) for i, (src, dst) in enumerate(moves)]
    for copy in copies:
        copy.start()
    return copies


ANYWHERE = pl.BlockSpec(memory_space=pl.ANY)


def in_turn(parts):
    while parts:
        parts = [part for part in parts if next(part, parts) is not parts]


def forward_kernel(pairs, head_dim, restart_ref, q_ref, k_ref, v_ref, rate_ref, w1i_in, b1i_ref, w2i_in, b2i_ref, gain_in, bias_in,
                   big_ref, mid_ref, small_ref, n1_ref, pq_ref, uq_ref, n2_ref, out_ref,
                   w1, b1, w2, b2, s_q1, s_x2, s_e2, s_w2, s_b2, s_q, par_ref, w1i_ref, w2i_ref, sems):
    j = pl.program_id(0)
    pair = 2 * head_dim
    inv = 1.0 / head_dim
    own, causal, ones = masks(head_dim)

    @pl.when(j == 0)
    def _():
        places = [pair_index(p, pairs, w1i_in) for p in range(pairs)]
        starts = [(src.at[n], dst.at[p]) for src, dst in ((w1i_in, w1i_ref), (w2i_in, w2i_ref)) for p, n in enumerate(places)]
        copies = fetch(sems, *starts)
        load_params(par_ref, (b2i_ref, gain_in, bias_in), places)
        for copy in copies:
            copy.wait()

    @pl.when(restart_ref[j] > 0)
    def _():
        for p in range(pairs):
            n = pair_index(p, pairs, w1i_in)
            second = w2i_ref[p]
            second_bias = par_ref[0, p] * own
            w1[p] = w1i_ref[p]
            for h in range(2):
                b1[p, h * MB : (h + 1) * MB] = jnp.broadcast_to(b1i_ref[pl.ds(2 * n + h, 1)], (MB, b1i_ref.shape[1]))
                half = second[h * head_dim : (h + 1) * head_dim]
                w2[p, h * head_dim : (h + 1) * head_dim] = half - jnp.sum(half, 0, keepdims=True) * inv
            b2[p] = second_bias - (lane_sum(second_bias) * inv) * own

    loaded = [
        (s_q1[p], s_x2[p], s_e2[p], s_w2[p], s_b2[p], s_q[p], w1[p], w2[p], b1[p], b2[p], rate_rows(rate_ref[...], p))
        for p in range(pairs)
    ]
    tokens = [
        [ref[:, p * pair : (p + 1) * pair] for ref in (q_ref, k_ref, v_ref)]
        + [par_ref[i, p] for i in (1, 2)]
        for p in range(pairs)
    ]
    writes = []

    def write(ref, index, value):
        writes.append((ref, index, value))

    def outputs_before(p):
        q1p, x2p, e2p, w2p, b2p, qp = loaded[p][:6]
        gain, bias = tokens[p][3:]
        p2, lq, _ = gelu_parts(q1p)
        p2b = low(p2)
        yield
        n2 = causal * (dot_nt(p2b, x2p) + 1.0)
        q2 = dot_nt(p2b, w2p)
        yield
        q2 = q2 * own - dot(low(n2), e2p) + b2p
        yield
        sq = lax.rsqrt(lane_sum(q2 * q2) * inv + epsilon)
        uq = q2 * sq
        write(out_ref, (slice(None), slice(p * pair, (p + 1) * pair)), qp + fold(uq) * gain + bias)
        write(pq_ref, (0, p, slice(0, 2 * MB)), p2b)
        write(pq_ref, (0, p, slice(2 * MB, 4 * MB)), low(lq))
        write(uq_ref, (0, p, slice(0, 2 * MB)), uq)
        write(uq_ref, (0, p, slice(2 * MB, 4 * MB)), jnp.broadcast_to(sq, uq.shape))
        write(n2_ref, (0, p), low(n2))

    def inner_step(p):
        w1c, w2c, b1c, b2c, e = loaded[p][6:]
        qc, kc, vc, gain, bias = tokens[p]
        kb, qb = low(spread(kc, own)), low(spread(qc, own))
        w1b, w2b = low(w1c), low(w2c)
        kq = dot(jnp.concatenate([kb, qb], 0), w1b)
        yield
        z1 = kq[: 2 * MB] + b1c
        x2, l1, pdf = gelu_parts(z1)
        x2b = low(x2)
        yield
        c = dot_nt(x2b, w2b)
        n1 = causal * (dot_nt(qb, kb) + 1.0)
        yield
        c = c * own + b2c
        s = lax.rsqrt(lane_sum(c * c) * inv + epsilon)
        u = c * s
        r = u * (gain * gain) + spread((bias - (vc - kc)) * gain, own)
        yield
        mr, m2 = lane_sum(r) * inv, lane_sum(r * u) * inv
        g2 = s * (r - mr * own - u * m2)
        yield
        h = dot(low(g2), w2b)
        e2b = low(e * g2)
        yield
        g1 = h * l1
        e1b = low(twice(e) * g1)
        yield
        u1 = dot_tn(kb, e1b)
        yield
        q1 = kq[2 * MB :] + b1c - dot(low(n1), e1b)
        yield
        write(w1, p, w1c - u1)
        write(b1, p, b1c - dot(ones, e1b))
        write(w2, p, w2c - dot_tn(e2b, x2b))
        write(b2, p, b2c - dot(ones, e2b))
        write(big_ref, (0, p, slice(0, pair)), w1b)
        write(big_ref, (0, p, slice(pair, 2 * pair)), w2b)
        write(big_ref, (0, p, slice(2 * pair, 2 * pair + 2 * MB)), x2b)
        write(big_ref, (0, p, slice(2 * pair + 2 * MB, 2 * pair + 4 * MB)), e1b)
        write(mid_ref, (0, p, slice(0, 2 * MB)), low(g1))
        write(mid_ref, (0, p, slice(2 * MB, 4 * MB)), low(l1))
        write(mid_ref, (0, p, slice(4 * MB, 6 * MB)), low(h * pdf * (2.0 - z1 * z1)))
        for i, value in enumerate((u, s, r, m2, g2)):
            write(small_ref, (0, p, slice(i * 2 * MB, (i + 1) * 2 * MB)), jnp.broadcast_to(value, u.shape))
        write(n1_ref, (0, p), low(n1))
        for ref, value in ((s_q1, q1), (s_x2, x2b), (s_e2, e2b), (s_w2, w2b), (s_b2, b2c), (s_q, qc)):
            write(ref, p, value)

    in_turn([inner_step(p) for p in range(pairs)] + [outputs_before(p) for p in range(pairs)])
    for ref, index, value in writes:
        ref[index] = value


def forward_inner(restarts, q, k, v, rates, w1i, b1i, w2i, b2i, gain, bias):
    _, pair, inner = w1i.shape
    blocks, pairs = q.shape[0] // MB, q.shape[1] // pair
    head_dim = pair // 2
    steps = blocks + 1
    last = blocks - 1
    tok = pl.BlockSpec((MB, pairs * pair), lambda j, r: (jnp.minimum(j, last), 0))
    whole = lambda a: pl.BlockSpec(a.shape, lambda j, r: (0,) * a.ndim)

    def per_step(rows, width, dtype):
        return (
            jax.ShapeDtypeStruct((steps, pairs, rows, width), dtype),
            pl.BlockSpec((1, pairs, rows, width), lambda j, r: (j, 0, 0, 0)),
        )

    outs = [
        per_step(2 * pair + 4 * MB, inner, bf16),
        per_step(6 * MB, inner, bf16),
        per_step(10 * MB, pair, f32),
        per_step(2 * MB, 2 * MB, bf16),
        per_step(4 * MB, inner, bf16),
        per_step(4 * MB, pair, f32),
        per_step(2 * MB, 2 * MB, bf16),
        (
            jax.ShapeDtypeStruct((steps * MB, pairs * pair), f32),
            pl.BlockSpec((MB, pairs * pair), lambda j, r: (j, 0)),
        ),
    ]
    return pl.pallas_call(
        partial(forward_kernel, pairs, head_dim),
        grid_spec=pltpu.PrefetchScalarGridSpec(
            num_scalar_prefetch=1,
            grid=(steps,),
            in_specs=[tok, tok, tok, pl.BlockSpec((MB, 128), lambda j, r: (jnp.minimum(j, last), 0))]
            + [ANYWHERE, whole(b1i), ANYWHERE, whole(b2i), whole(gain), whole(bias)],
            out_specs=[o[1] for o in outs],
            scratch_shapes=[
                pltpu.VMEM((pairs, pair, inner), f32),
                pltpu.VMEM((pairs, 2 * MB, inner), f32),
                pltpu.VMEM((pairs, pair, inner), f32),
                pltpu.VMEM((pairs, 2 * MB, pair), f32),
                pltpu.VMEM((pairs, 2 * MB, inner), f32),
                pltpu.VMEM((pairs, 2 * MB, inner), bf16),
                pltpu.VMEM((pairs, 2 * MB, pair), bf16),
                pltpu.VMEM((pairs, pair, inner), bf16),
                pltpu.VMEM((pairs, 2 * MB, pair), f32),
                pltpu.VMEM((pairs, MB, pair), f32),
                pltpu.VMEM((3, pairs, 1, pair), f32),
                pltpu.VMEM((pairs, pair, inner), f32),
                pltpu.VMEM((pairs, pair, inner), f32),
                pltpu.SemaphoreType.DMA((2 * pairs,)),
            ],
        ),
        out_shape=[o[0] for o in outs],
        compiler_params=pltpu.CompilerParams(vmem_limit_bytes=63 * 1024 * 1024),
        name="inner_forward",
    )(restarts, q, k, v, rates, w1i, b1i, w2i, b2i, gain, bias)


MESH = pl.DeviceIdType.MESH


def greet(peers):
    barrier = pltpu.get_barrier_semaphore()
    for peer in peers:
        pl.semaphore_signal(barrier, inc=1, device_id=peer, device_id_type=MESH)
    pl.semaphore_wait(barrier, len(peers))


class Copies:
    def __init__(self, send_sem, recv_sem):
        self.send_sem, self.recv_sem, self.started = send_sem, recv_sem, []

    def make(self, src, dst, peer):
        i = len(self.started)
        copy = pltpu.make_async_remote_copy(
            src_ref=src, dst_ref=dst, send_sem=self.send_sem.at[i], recv_sem=self.recv_sem.at[i],
            device_id=peer, device_id_type=MESH,
        )
        self.started.append(copy)
        return copy

    def send(self, src, dst, peer):
        copy = self.make(src, dst, peer)
        copy.start()
        return copy


def rows_at(start, size):
    return pl.ds(pl.multiple_of(start, 16), size)


def add_low(a, b):
    return (a.astype(f32) + b.astype(f32)).astype(bf16)


def mates(axis):
    size, here = lax.axis_size(axis), lax.axis_index(axis)
    return [{axis: lax.rem(here + o, size)} for o in range(1, size)]


def feed_sum_steps(ins, outs, got_group, sum_group, got_row, full, copies, whole):
    row, group = lax.axis_index("row"), lax.axis_index("group")
    rows, groups = lax.axis_size("row"), lax.axis_size("group")
    row_mates, group_mates = mates("row"), mates("group")
    count = len(ins)
    part = ins[0].shape[0] // groups
    unit = part // rows
    mine = rows_at(row * unit, unit)
    moves = {}
    for i in range(count):
        moves["X", i] = [
            copies.make(ins[i].at[rows_at(lax.rem(group + o, groups) * part, part)], got_group[i].at[o - 1], group_mates[o - 1])
            for o in range(1, groups)
        ]
        moves["Z", i] = [
            copies.make(sum_group[i].at[rows_at(lax.rem(row + o, rows) * unit, unit)], got_row[i].at[o - 1], row_mates[o - 1])
            for o in range(1, rows)
        ]
        if i < whole:
            here = full[i].at[group, mine]
            moves["ZA", i] = [copies.make(here, here, mate) for mate in row_mates]
            here = full[i].at[group]
            moves["XA", i] = [copies.make(here, here, mate) for mate in group_mates]

    def finish(kind, i):
        for copy in moves[kind, i]:
            copy.wait_recv()
        if kind == "X":
            total = ins[i][rows_at(group * part, part)].astype(f32)
            for o in range(1, groups):
                total = total + got_group[i][o - 1].astype(f32)
            sum_group[i][...] = low(total)
        if kind == "Z":
            total = sum_group[i][mine].astype(f32)
            for o in range(1, rows):
                total = total + got_row[i][o - 1].astype(f32)
            if i < whole:
                full[i][group, mine] = low(total)
            else:
                outs[i][...] = low(total)

    def run(slot):
        _, done, begun = FEED_SLOTS[slot]
        if slot == 0:
            greet(row_mates + group_mates)
        for name in done:
            finish(name[:-1], int(name[-1]))
        for name in begun:
            for copy in moves[name[:-1], int(name[-1])]:
                copy.start()
        if slot == len(FEED_SLOTS) - 1:
            for i in range(whole):
                outs[i][...] = full[i][...]
            for copy in copies.started:
                copy.wait_send()

    return [partial(run, slot) for slot in range(len(FEED_SLOTS))]


def backward_kernel(pairs, head_dim, feeds, restart_ref,
                    qq_ref, kq_ref, doq_ref, eq_ref, bigq_ref, g2q_ref, n1_ref, pqq_ref, uqq_ref, n2_ref,
                    q_ref, k_ref, v_ref, do_ref, e_ref, big_ref, mid_ref, small_ref, pq_ref, uq_ref, gain_in, bias_in, *refs):
    j = pl.program_id(0)
    steps = pl.num_programs(0)
    pair = 2 * head_dim
    inv = 1.0 / head_dim
    own, causal, ones = masks(head_dim)
    feed_in, refs = refs[:feeds], refs[feeds:]
    dq_ref, dk_ref, dv_ref, de_ref, gw1, gb1, gw2, gb2, ggain, gbias = refs[:10]
    feed_out, refs = refs[10 : 10 + feeds], refs[10 + feeds :]
    w1, b1, w2, b2, s_e1, s_e2, s_k, s_x2, s_q1, s_q2, s_q, par_ref = refs[:12]
    if feeds:
        refs, sems = refs[12:-2], refs[-2:]
        buffers = [refs[i * feeds : (i + 1) * feeds] for i in range(3)] + [refs[3 * feeds :]]
        slots = feed_sum_steps(feed_in, feed_out, *buffers, Copies(*sems), FEED_WHOLE)
        for i, run in enumerate(slots):
            pl.when(j == FEED_SLOTS[i][0] * (steps - 1) // 32)(run)

    @pl.when(j == 0)
    def _():
        places = [jnp.minimum(lax.axis_index("group") * pairs + p, gain_in.shape[0] // 2 - 1) for p in range(pairs)]
        load_params(par_ref, (gain_in, bias_in), places)

    @pl.when(j <= 1)
    def _():
        for ref in (w1, b1, w2, b2, gw1, gb1, gw2, gb2, ggain, gbias):
            ref[...] = jnp.zeros_like(ref)

    rows2 = 2 * MB
    piece = lambda ref, p, i: ref[0, p, i * rows2 : (i + 1) * rows2]
    token = lambda ref, p: ref[:, p * pair : (p + 1) * pair]
    first = restart_ref[jnp.minimum(steps - 1 - j, steps - 2)]
    go_on = 1.0 - first
    writes = []

    def write(ref, index, value):
        writes.append((ref, index, value))

    def load_outputs(p):
        return (
            [token(ref, p) for ref in (qq_ref, kq_ref, doq_ref)]
            + [par_ref[0, p]]
            + [bigq_ref[0, p, 0:pair], bigq_ref[0, p, pair : 2 * pair]]
            + [bigq_ref[0, p, 2 * pair : 2 * pair + rows2], bigq_ref[0, p, 2 * pair + rows2 : 2 * pair + 2 * rows2]]
            + [rate_rows(eq_ref[...], p), g2q_ref[0, p], n1_ref[0, p], n2_ref[0, p]]
            + [piece(ref, p, i) for ref in (pqq_ref, uqq_ref) for i in range(2)]
        )

    def load_step(p):
        return (
            [ref[p] for ref in (s_e1, s_e2, s_k, s_x2, s_q1, s_q2, s_q, w1, w2, b1, b2)]
            + [token(ref, p) for ref in (q_ref, k_ref, v_ref, do_ref)]
            + [par_ref[i, p] for i in (0, 1)]
            + [big_ref[0, p, 0:pair], big_ref[0, p, pair : 2 * pair]]
            + [big_ref[0, p, 2 * pair : 2 * pair + rows2], big_ref[0, p, 2 * pair + rows2 : 2 * pair + 2 * rows2]]
            + [piece(mid_ref, p, i).astype(f32) for i in range(3)]
            + [piece(small_ref, p, i) for i in range(5)]
            + [pq_ref[0, p], uq_ref[0, p], rate_rows(e_ref[...], p)]
        )

    def outputs_ahead(p, loaded):
        qc, kc, do, gain, w1b, w2b, x2b, e1b, e, g2, n1b, n2b, p2b, lq, uq, sq = loaded
        qb, kb = low(spread(qc, own)), low(spread(kc, own))
        e2b = low(e * g2)
        w = spread(do * gain, own)
        dq2 = low(sq * (w - (lane_sum(w) * inv) * own - uq * (lane_sum(w * uq) * inv)))
        yield
        dn2 = dot_nt(dq2, e2b)
        dp2 = dot(dq2, w2b)
        yield
        dpx = low(-causal * dn2)
        new_e2 = dot_tn(n2b, dq2)
        dp2 = dp2 + dot(dpx, x2b)
        yield
        dq1 = low(dp2 * lq.astype(f32))
        new_x2 = dot_tn(dpx, p2b)
        yield
        dn1 = dot_nt(dq1, e1b)
        new_q = dot_nt(dq1, w1b)
        yield
        new_e1 = dot_tn(n1b, dq1)
        dqk = low(-causal * dn1)
        yield
        new_k = dot_tn(dqk, qb)
        new_q = do + fold((new_q + dot(dqk, kb)) * own)
        for ref, value in zip((s_e1, s_e2, s_k, s_x2, s_q1, s_q2, s_q), (new_e1, new_e2, new_k, new_x2, dq1, dq2, new_q)):
            write(ref, p, value)

    def step_back(p, loaded):
        e1q, e2q, dkq, x2q, dq1, dq2, dqc, dw1, dw2, db1, db2, qc, kc, vc, do, gain, bias, w1b, w2b, x2b, e1b = loaded[:21]
        g1, l1, hg, u, s, r, m2, g2, p2b, uq, e = loaded[21:]
        cols = (slice(None), slice(p * pair, (p + 1) * pair))
        dw1b, dw2b = low(dw1), low(dw2)
        qb, kb = low(spread(qc, own)), low(spread(kc, own))
        e2b = low(e * g2)
        de1 = dot(kb, dw1b)
        de2 = dot_nt(x2b, dw2b)
        yield
        de1 = -(e1q + de1 + db1)
        de2 = -(e2q + de2 * own + db2)
        dg1 = twice(e) * de1
        dh = low(dg1 * l1)
        yield
        dg2 = dot_nt(dh, w2b)
        dx2 = x2q - dot(e2b, dw2b)
        yield
        dg2 = e * de2 + dg2 * own
        dk = dkq - dot_nt(e1b, dw1b) * own
        ma, mg = lane_sum(dg2 * u) * inv, lane_sum(dg2) * inv
        rate = jnp.broadcast_to(lane_sum(g1 * de1) + lane_sum(g2 * de2), u.shape)
        rates.append(jnp.where(head == 2 * p, rate[:MB], 0.0) + jnp.where(head == 2 * p + 1, rate[MB:], 0.0))
        yield
        dr = s * (dg2 - mg * own - u * ma)
        du = dr * (gain * gain) - s * (dg2 * m2 + r * ma)
        yield
        md, mu = lane_sum(du) * inv, lane_sum(du * u + dg2 * g2) * inv
        dz2 = low(s * (du - md * own - u * mu))
        yield
        dx2 = dx2 + dot(dz2, w2b)
        yield
        dz1 = low(dg1 * hg + dx2 * l1)
        drg = fold(dr) * gain
        write(dq_ref, cols, low(dqc))
        write(dv_ref, cols, low(-drg))
        more_gain = fold(spread_by(do, uq)) + fold(dr * u) * (2.0 * gain) + fold(dr) * (bias - (vc - kc))
        yield
        ndw1 = dw1 + dot_tn(jnp.concatenate([qb, kb], 0), jnp.concatenate([dq1, dz1], 0))
        yield
        dk = dk + dot_nt(dz1, w1b) * own
        write(dk_ref, cols, low(fold(dk) + drg))
        ndw2 = dw2 + dot_tn(jnp.concatenate([dq2, low(g2), dz2], 0), jnp.concatenate([p2b, dh, x2b], 0))
        ndb1 = db1 + dot(ones, dq1) + dot(ones, dz1)
        ndb2 = db2 + dot(ones, dq2) + dot(ones, dz2)
        for ref, value in ((w1, ndw1), (w2, ndw2), (b1, ndb1), (b2, ndb2)):
            write(ref, p, value * go_on)
        more.append((cols, more_gain, do + drg))
        starts.append((p, ndw1, ndw2, ndb1, ndb2))

    more, starts, rates = [], [], []
    head = lax.broadcasted_iota(jnp.int32, (MB, pair), 1)
    ahead_in = [load_outputs(p) for p in range(pairs)]
    step_in = [load_step(p) for p in range(pairs)]
    in_turn([step_back(p, step_in[p]) for p in range(pairs)] + [outputs_ahead(p, ahead_in[p]) for p in range(pairs)])
    for ref, index, value in writes:
        ref[index] = value
    de_ref[...] = sum(rates)
    for cols, more_gain, more_bias in more:
        ggain[cols] += more_gain
        gbias[cols] += more_bias
    for p, *values in starts:
        for ref, value in zip((gw1, gw2, gb1, gb2), values):
            ref[p] += value * first


def spread_by(do, uq):
    return jnp.concatenate([do, do], 0) * uq


def backward_inner(restarts, q, k, v, do, rates, saved, gain, bias, feed_terms, collective_id):
    big, mid, small, n1, pq, uq, n2 = saved
    pairs, pair, inner = big.shape[1], 2 * gain.shape[1], big.shape[3]
    blocks = q.shape[0] // MB
    head_dim = pair // 2
    steps = blocks + 1
    rate = lambda at: pl.BlockSpec((MB, 128), lambda j: (at(j), 0))
    now = lambda j: jnp.minimum(blocks - j, blocks - 1)
    ahead = lambda j: jnp.maximum(blocks - 1 - j, 0)
    tok = lambda at: pl.BlockSpec((MB, pairs * pair), lambda j: (at(j), 0))

    def block(a, at, rows=None, part=0):
        shape = (1, pairs, rows or a.shape[2], a.shape[3])
        return pl.BlockSpec(shape, lambda j: (at(j), 0, part, 0))

    whole = lambda a: pl.BlockSpec(a.shape, lambda j: (0,) * a.ndim)
    later = lambda j: ahead(j) + 1
    at_now = lambda j: now(j) + 1
    operands = [
        (q, tok(ahead)), (k, tok(ahead)), (do, tok(ahead)), (rates, rate(ahead)), (big, block(big, ahead)),
        (small, block(small, ahead, 2 * MB, 4)), (n1, block(n1, ahead)), (pq, block(pq, later)), (uq, block(uq, later)),
        (n2, block(n2, later)),
        (q, tok(now)), (k, tok(now)), (v, tok(now)), (do, tok(now)), (rates, rate(now)), (big, block(big, now)),
        (mid, block(mid, now)), (small, block(small, now)), (pq, block(pq, at_now, 2 * MB)), (uq, block(uq, at_now, 2 * MB)),
        (gain, whole(gain)), (bias, whole(bias)),
    ]
    feeds = len(feed_terms)
    vmem = pl.BlockSpec(memory_space=pltpu.VMEM)
    operands += [(a, vmem) for a in feed_terms]
    width = pairs * pair
    tok_out = (jax.ShapeDtypeStruct((steps * MB, width), bf16), pl.BlockSpec((MB, width), lambda j: (blocks - j, 0)))
    state = [((pairs, pair, inner), f32), ((pairs, 2 * MB, inner), f32), ((pairs, pair, inner), f32), ((pairs, 2 * MB, pair), f32)]
    keep = lambda shape: (jax.ShapeDtypeStruct(shape, f32), pl.BlockSpec(shape, lambda j: (0,) * len(shape)))
    outs = [tok_out] * 3 + [
        (jax.ShapeDtypeStruct((steps * MB, pair), f32), pl.BlockSpec((MB, pair), lambda j: (blocks - j, 0)))
    ] + [keep(shape) for shape, _ in state] + [keep((MB, width))] * 2
    comm = []
    if feeds:
        groups, rows = lax.axis_size("group"), lax.axis_size("row")
        part, wide = feed_terms[0].shape[0] // groups, feed_terms[0].shape[1]
        unit = part // rows
        outs += [
            (jax.ShapeDtypeStruct((groups, part, wide) if i < FEED_WHOLE else (unit, wide), bf16), vmem) for i in range(feeds)
        ]
        comm = [pltpu.VMEM((groups - 1, part, wide), bf16)] * feeds + [pltpu.VMEM((part, wide), bf16)] * feeds
        comm += [pltpu.VMEM((rows - 1, unit, wide), bf16)] * feeds + [pltpu.VMEM((groups, part, wide), bf16)] * FEED_WHOLE
        copies = (feeds + FEED_WHOLE) * (groups + rows - 2)
        comm += [pltpu.SemaphoreType.DMA((copies,))] * 2
    return pl.pallas_call(
        partial(backward_kernel, pairs, head_dim, feeds),
        grid_spec=pltpu.PrefetchScalarGridSpec(
            num_scalar_prefetch=0,
            grid=(steps,),
            in_specs=[pl.BlockSpec(memory_space=pltpu.SMEM)] + [o[1] for o in operands],
            out_specs=[o[1] for o in outs],
            scratch_shapes=[pltpu.VMEM(shape, kind) for shape, kind in state] + [
                pltpu.VMEM((pairs, 2 * MB, inner), f32),
                pltpu.VMEM((pairs, 2 * MB, pair), f32),
                pltpu.VMEM((pairs, 2 * MB, pair), f32),
                pltpu.VMEM((pairs, 2 * MB, inner), f32),
                pltpu.VMEM((pairs, 2 * MB, inner), bf16),
                pltpu.VMEM((pairs, 2 * MB, pair), bf16),
                pltpu.VMEM((pairs, MB, pair), f32),
                pltpu.VMEM((2, pairs, 1, pair), f32),
            ] + comm,
        ),
        out_shape=[o[0] for o in outs],
        compiler_params=pltpu.CompilerParams(
            collective_id=collective_id if feeds else None, has_side_effects=bool(feeds), vmem_limit_bytes=63 * 1024 * 1024
        ),
        name="inner_backward",
    )(restarts.astype(f32), *[o[0] for o in operands])


def norm_parts(v, width):
    centered = v - jnp.sum(v, -1, keepdims=True) * (1.0 / width)
    scale = lax.rsqrt(jnp.sum(centered * centered, -1, keepdims=True) * (1.0 / width) + epsilon)
    return centered * scale, scale


def feed_terms(*items):
    for outs, left, right in items:
        width = left.shape[1]
        for i, out in enumerate(outs):
            both = low(dot_tn(left[...], right[:, i * 256 : (i + 1) * 256]))
            out[0:width] = both[:, :128]
            out[width : 2 * width] = both[:, 128:]


def middle_kernel(span, mixed_in, tok_in, cot_in, wout_in, gate_in, up_in, down_in, gain_ref,
                  block_ref, hid_ref, gmix_ref, gwo_ref, t0, t1, t2, t3, t4, t5, gfeed_ref,
                  tok_ref, cot_ref, wout_ref, gate_ref, up_ref, down_ref, downs, mixed_ref, mixed_got, acts, cots, unit, scales, h_in, gg, gu, ha, pg0, po0, out_core, in_core, out_diag, in_diag, out_y, in_y,
                  branch, branch_row, send_sem, recv_sem, local_sem, sems):
    rows, groups = lax.axis_size("row"), lax.axis_size("group")
    row, group, feat = lax.axis_index("row"), lax.axis_index("group"), lax.axis_index("feat")
    count, width = tok_in.shape
    cols = mixed_ref.shape[1]
    core, y = lax.rem(feat, 2), feat // 2
    core_mate, y_mate = {"feat": feat + 1 - 2 * core}, {"feat": feat + 2 - 4 * y}
    here = row * groups + group
    places = rows * groups
    others = [lax.rem(here + o, places) for o in range(1, places)]
    seq_mates = [{"row": t // groups, "group": lax.rem(t, groups)} for t in others]
    copies = Copies(send_sem, recv_sem)
    send = copies.send
    slot = lambda ref, s: ref.at[s * count : (s + 1) * count]

    loads = fetch(
        sems, (cot_in, cot_ref), (down_in, down_ref), (tok_in, tok_ref), (wout_in, wout_ref), (gate_in, gate_ref), (up_in, up_ref)
    )
    mixed_ref[...] = low(mixed_in[MB:])
    greet([core_mate, y_mate] + seq_mates)
    lanes = pl.ds(pl.multiple_of(group * cols, 128), cols)
    moves = [
        send(mixed_ref.at[rows_at(t * span, span)], mixed_got.at[rows_at(row * span, span), lanes], mate)
        for t, mate in zip(others, seq_mates)
    ]
    own = pltpu.make_async_copy(
        mixed_ref.at[rows_at(here * span, span)], mixed_got.at[rows_at(row * span, span), lanes], local_sem.at[0]
    )
    own.start()
    loads[0].wait()
    cot_core = send(cot_ref, slot(cots, 1), core_mate)
    cot_y = send(cot_ref, slot(cots, 2), y_mate)
    cots[0:count] = cot_ref[...]
    loads[1].wait()
    cot_core.wait_recv()
    downs[0 : 2 * count] = dot(cots[0 : 2 * count], down_ref[...])
    own.wait()
    loads[2].wait()
    loads[3].wait()
    for copy in moves:
        copy.wait_recv()
    hidden = tok_ref[...].astype(f32) + dot(mixed_got[:, :width], wout_ref[:width])
    h_in[...] = hidden
    unit_two, scale_two = norm_parts(hidden, width)
    unit[...] = unit_two
    scales[...] = jnp.broadcast_to(scale_two, scales.shape)
    gain = gain_ref[...].reshape(1, width)
    acts[0:count] = low(unit_two * gain)
    cut = count // 2
    span_of = lambda s, h: slice(s * count + h * cut, s * count + (h + 1) * cut)
    act_y = [send(acts.at[span_of(0, h)], acts.at[span_of(2, h)], y_mate) for h in range(2)]
    act_core = send(slot(acts, 0), slot(acts, 1), core_mate)
    cot_y.wait_recv()
    cot_diag = send(slot(cots, 2), slot(cots, 3), core_mate)
    loads[4].wait()
    loads[5].wait()

    def feed(part):
        gate_pre, up_value = dot(acts[part], gate_ref[...]), dot(acts[part], up_ref[...])
        grad = downs[part]
        sig = jax.nn.sigmoid(gate_pre)
        silu = gate_pre * sig
        ha[part] = low(silu * up_value)
        gg[part] = low(grad * up_value * sig * (1.0 + gate_pre * (1.0 - sig)))
        gu[part] = low(grad * silu)
        return dot_nt(gg[part], gate_ref[...]) + dot_nt(gu[part], up_ref[...])

    def forth(s):
        return dot_nt(ha[s * count : (s + 1) * count], down_ref[...])

    pg0[...] = feed(slice(0, count))
    act_core.wait_recv()
    out_core[0] = low(feed(slice(count, 2 * count)))
    core_sums = [send(out_core.at[0], in_core.at[0], core_mate)]
    cot_diag.wait_recv()
    downs[2 * count : 4 * count] = dot(cots[2 * count : 4 * count], down_ref[...])
    y_sums = []
    for h in range(2):
        rows_h = slice(h * cut, (h + 1) * cut)
        act_y[h].wait_recv()
        act_diag = send(acts.at[span_of(2, h)], acts.at[span_of(3, h)], core_mate)
        ahead = feed(span_of(2, h))
        act_diag.wait_recv()
        out_diag[0, rows_h] = low(feed(span_of(3, h)))
        diag_sum = send(out_diag.at[0, rows_h], in_diag.at[0, rows_h], core_mate)
        diag_sum.wait_recv()
        out_y[0, rows_h] = low(ahead + in_diag[0, rows_h].astype(f32))
        y_sums.append(send(out_y.at[0, rows_h], in_y.at[0, rows_h], y_mate))
    out_diag[1] = low(forth(3))
    diag_sum = send(out_diag.at[1], in_diag.at[1], core_mate)
    out_core[1] = low(forth(1))
    core_sums.append(send(out_core.at[1], in_core.at[1], core_mate))
    ahead = forth(2)
    diag_sum.wait_recv()
    out_y[1] = low(ahead + in_diag[1].astype(f32))
    y_sums.append(send(out_y.at[1], in_y.at[1], y_mate))
    po0[...] = forth(0)
    core_sums[0].wait_recv()
    y_sums[0].wait_recv()
    y_sums[1].wait_recv()
    grad_act = pg0[...] + in_core[0].astype(f32) + in_y[0].astype(f32)
    unit_two = unit[...]
    gfeed_ref[...] = jnp.sum(grad_act * unit_two, 0, keepdims=True)
    w = grad_act * gain
    inv = 1.0 / width
    grad = cot_ref[...].astype(f32) + scales[:, 0:1] * (
        w - jnp.sum(w, -1, keepdims=True) * inv - unit_two * (jnp.sum(w * unit_two, -1, keepdims=True) * inv)
    )
    hid_ref[...] = grad
    branch[...] = low(grad)
    row_mates, group_mates = mates("row"), mates("group")
    block = lambda r: branch_row.at[rows_at((r * groups + group) * span, span)]
    by_row = [
        send(branch.at[rows_at(lax.rem(row + o, rows) * span, span)], block(row), row_mates[o - 1]) for o in range(1, rows)
    ]
    block(row)[...] = branch[rows_at(row * span, span)]
    moves = [send(block(row), block(row), mate) for mate in group_mates]
    feed_terms(((t0, t1), acts, gg), ((t2, t3), acts, gu), ((t4, t5), cots, ha))
    for o in range(1, rows):
        by_row[o - 1].wait_recv()
        from_row = block(lax.rem(row - o + rows, rows))
        moves += [send(from_row, from_row, mate) for mate in group_mates]
    core_sums[1].wait_recv()
    y_sums[2].wait_recv()
    block_ref[...] = low(h_in[...] + po0[...] + in_core[1].astype(f32) + in_y[1].astype(f32))
    for copy in moves:
        copy.wait_recv()
    gmix_ref[...] = dot_nt(branch_row[...], wout_ref[rows_at(group * cols, cols)])
    for h in range(2):
        half = branch_row[:, h * (width // 2) : (h + 1) * (width // 2)]
        gwo_ref[h * cols : (h + 1) * cols] = low(dot_tn(mixed_ref[...], half))
    for copy in copies.started:
        copy.wait_send()


def middle(mixed_row, tokens, cotangent, out_weight, gate_weight, up_weight, down_weight, gain, span, collective_id):
    rows, groups = lax.axis_size("row"), lax.axis_size("group")
    length, cols = mixed_row.shape[0] - MB, mixed_row.shape[1]
    count, width = tokens.shape
    hidden = gate_weight.shape[1]
    copies = (rows * groups - 1) + (rows - 1) + rows * (groups - 1) + 18
    vmem = pl.BlockSpec(memory_space=pltpu.VMEM)
    outs = [
        ((count, width), bf16), ((count, width), f32), ((length, cols), f32), ((2 * cols, width // 2), bf16),
        *[((2 * width, 128), bf16)] * 6, ((1, width), f32),
    ]
    two = pltpu.VMEM((2, count, width), bf16)
    return pl.pallas_call(
        partial(middle_kernel, span),
        in_specs=[vmem] + [ANYWHERE] * 6 + [vmem],
        out_specs=[vmem] * len(outs),
        out_shape=[jax.ShapeDtypeStruct(*o) for o in outs],
        scratch_shapes=[
            pltpu.VMEM((count, width), bf16),
            pltpu.VMEM((count, width), bf16),
            pltpu.VMEM(out_weight.shape, bf16),
            *[pltpu.VMEM((width, hidden), bf16)] * 3,
            pltpu.VMEM((4 * count, hidden), f32),
            pltpu.VMEM((length, cols), bf16),
            pltpu.VMEM((count, groups * cols), bf16),
            pltpu.VMEM((4 * count, width), bf16),
            pltpu.VMEM((4 * count, width), bf16),
            pltpu.VMEM((count, width), f32),
            pltpu.VMEM((count, 128), f32),
            pltpu.VMEM((count, width), f32),
            pltpu.VMEM((4 * count, hidden), bf16),
            pltpu.VMEM((4 * count, hidden), bf16),
            pltpu.VMEM((4 * count, hidden), bf16),
            pltpu.VMEM((count, width), f32),
            pltpu.VMEM((count, width), f32),
            two, two, two, two, two, two,
            pltpu.VMEM((count, width), bf16),
            pltpu.VMEM((length, width), bf16),
            pltpu.SemaphoreType.DMA((copies,)),
            pltpu.SemaphoreType.DMA((copies,)),
            pltpu.SemaphoreType.DMA((1,)),
            pltpu.SemaphoreType.DMA((6,)),
        ],
        compiler_params=pltpu.CompilerParams(
            collective_id=collective_id, has_side_effects=True, vmem_limit_bytes=63 * 1024 * 1024
        ),
        name="middle",
    )(mixed_row, tokens, cotangent, out_weight, gate_weight, up_weight, down_weight, gain)


def own_rows(array, mine):
    total = None
    for g in range(lax.axis_size("group")):
        part = array[g * mine : (g + 1) * mine].astype(f32)
        if part.shape[0]:
            part = jnp.concatenate([part, jnp.zeros((128 - part.shape[0], array.shape[1]), f32)], 0)
            part = jnp.where(lax.axis_index("group") == g, part, 0.0)
            total = part if total is None else total + part
    return total


def head_kernel(span, heads, mine, head_dim, tok_ref, gain_ref, wq_in, wk_in, wv_in, wr_ref, rb_ref,
                q_ref, k_ref, v_ref, act_ref, unit_ref, rate_ref, slope_ref, stat_ref, wown_ref, row_tok, wq_ref, wk_ref, wv_ref, send_sem, recv_sem, sems):
    rows, groups = lax.axis_size("row"), lax.axis_size("group")
    row, group, feat = lax.axis_index("row"), lax.axis_index("group"), lax.axis_index("feat")
    row_mates, group_mates = mates("row"), mates("group")
    width = tok_ref.shape[2]
    cols = q_ref.shape[1]
    copies = Copies(send_sem, recv_sem)
    block = lambda r: row_tok.at[rows_at((r * groups + group) * span, span)]

    lanes = pl.ds(pl.multiple_of(group * cols, 128), cols)
    loads = fetch(sems, *[(src.at[:, lanes], dst) for src, dst in ((wq_in, wq_ref), (wk_in, wk_ref), (wv_in, wv_ref))])
    greet(row_mates + group_mates)
    by_row = [
        copies.send(tok_ref.at[lax.rem(row + o, rows)], block(row), row_mates[o - 1]) for o in range(1, rows)
    ]
    block(row)[...] = tok_ref[row]
    by_group = [copies.send(block(row), block(row), mate) for mate in group_mates]
    for o in range(1, rows):
        by_row[o - 1].wait_recv()
        here = block(lax.rem(row - o + rows, rows))
        by_group += [copies.send(here, here, mate) for mate in group_mates]
    for copy in by_group:
        copy.wait_recv()
    unit, _ = norm_parts(row_tok[...].astype(f32), width)
    unit_ref[...] = unit
    act = low(unit * gain_ref[...].reshape(1, width))
    act_ref[...] = act
    for load, out, weight in zip(loads, (q_ref, k_ref, v_ref), (wq_ref, wk_ref, wv_ref)):
        load.wait()
        out[...] = dot(act, weight[...])
    rate_weight = low(own_rows(wr_ref[...], mine))
    wown_ref[...] = rate_weight
    rate_bias = own_rows(jnp.broadcast_to(rb_ref[...].reshape(1, heads), (8, heads)).T, mine).T[0:1]
    logits = dot_nt(act, rate_weight) + rate_bias
    sigma = jax.nn.sigmoid(logits)
    lane = lax.broadcasted_iota(jnp.int32, logits.shape, 1)
    used = (lane < mine) & (group * mine + lane < heads)
    rate_ref[...] = sigma * (1.0 / head_dim)
    slope_ref[...] = jnp.where(used, sigma * (1.0 - sigma) * (1.0 / head_dim), 0.0)
    stat_ref[0:1] = jnp.sum(logits, 0, keepdims=True)
    top = jnp.max(jnp.max(jnp.where(used, logits, -3e38), 0, keepdims=True), 1, keepdims=True)
    place = row * lax.axis_size("feat") + feat
    stat_ref[1:2] = jnp.where(lane[0:1] == place, top, 0.0)
    for copy in copies.started:
        copy.wait_send()


def head(tokens, gain, weights, rate_weight, rate_bias, heads, mine, head_dim, collective_id):
    rows, groups = lax.axis_size("row"), lax.axis_size("group")
    _, span, width = tokens.shape
    length, cols = rows * groups * span, mine * head_dim
    vmem = pl.BlockSpec(memory_space=pltpu.VMEM)
    copies = (rows - 1) + rows * (groups - 1)
    outs = [((length, cols), f32)] * 3 + [((length, width), bf16), ((length, width), f32)]
    outs += [((length, 128), f32)] * 2 + [((2, 128), f32), ((128, width), bf16)]
    return pl.pallas_call(
        partial(head_kernel, span, heads, mine, head_dim),
        in_specs=[vmem] * 2 + [ANYWHERE] * 3 + [vmem] * 2,
        out_specs=[vmem] * len(outs),
        out_shape=[jax.ShapeDtypeStruct(*o) for o in outs],
        scratch_shapes=[
            pltpu.VMEM((length, width), bf16),
            *[pltpu.VMEM((width, cols), bf16)] * 3,
            pltpu.SemaphoreType.DMA((copies,)),
            pltpu.SemaphoreType.DMA((copies,)),
            pltpu.SemaphoreType.DMA((3,)),
        ],
        compiler_params=pltpu.CompilerParams(
            collective_id=collective_id, has_side_effects=True, vmem_limit_bytes=63 * 1024 * 1024
        ),
        name="head",
    )(tokens, gain, *weights, rate_weight, rate_bias)


TAIL_SLOTS = [
    ([], ["CORE3", "FZ1", "FZ0", "CORE0", "PART0"]),
    (["CORE3"], ["Y3"]),
    (["CORE0"], ["Y0", "CORE2"]),
    (["FZ1"], ["FZ2", "FX1", "CORE4"]),
    (["CORE2"], ["CORE1"]),
    (["CORE4", "FZ0", "Y3"], ["Y4", "Z3"]),
    (["CORE1", "Y0"], ["Y1"]),
    (["FZ2"], ["Z0"]),
    (["PART0"], ["SC0", "FX2"]),
    (["Y4"], ["Y2"]),
    (["SC0", "Z3"], ["ZA3"]),
    (["Y1"], ["SY0"]),
    (["FX1"], ["FX0"]),
    (["Z0"], ["Z1"]),
    (["Y2", "ZA3"], ["ZA0"]),
    (["SY0", "FX2"], ["P3"]),
    (["Z1"], ["ZA1"]),
    (["FX0", "ZA0"], ["Z2", "P0"]),
    (["P3"], ["Q3"]),
    (["ZA1"], ["P1", "Z4"]),
    (["P0"], ["Q0"]),
    (["Z2"], ["ZA2"]),
    (["Z4"], ["ZA4"]),
    (["P1"], ["Q1"]),
    (["ZA2"], ["P2", "SZ0"]),
    (["Q3"], ["C3"]),
    (["ZA4"], ["HOME0", "P4"]),
    (["C3", "Q0"], ["C0"]),
    (["C0", "P2", "Q1"], ["Q2", "C1"]),
    (["SZ0"], ["SX0"]),
    (["C1", "P4"], ["Q4"]),
    (["SX0", "HOME0", "Q4"], ["C4"]),
    (["Q2"], ["C2"]),
    (["C4", "C2"], []),
]
TAIL_GROUP_FIRST = (False, True, True, True, False)


FEED_SLOTS = [
    (0, [], ["X1", "X2"]),
    (7, ["X1"], ["X0", "Z1"]),
    (10, ["X2"], ["X5", "Z2"]),
    (12, ["Z1"], ["ZA1"]),
    (13, ["X0"], ["X3"]),
    (15, ["Z2"], ["Z0"]),
    (16, ["X5"], ["X4"]),
    (18, ["ZA1"], ["ZA2"]),
    (19, ["X3"], ["XA1"]),
    (21, ["Z0"], ["ZA0"]),
    (22, ["X4"], []),
    (24, ["ZA2"], ["XA2", "Z5"]),
    (25, ["XA1"], []),
    (27, ["ZA0"], ["XA0", "Z4"]),
    (29, ["XA2"], []),
    (30, ["Z5"], ["Z3"]),
    (32, ["XA0", "Z4", "Z3"], []),
]
FEED_WHOLE = 3


def tail_kernel(span, shapes, feeds, act_ref, unit_in, gq_ref, gk_ref, gv_ref, de_in, slope_in, wq_in, wk_in, wv_in, wr_ref,
                gwo_ref, gw1, gb1, gw2, gb2, ggain, gbias, gfeed, stat_ref, *refs):
    rows, groups = lax.axis_size("row"), lax.axis_size("group")
    row, group, feat = lax.axis_index("row"), lax.axis_index("group"), lax.axis_index("feat")
    core, y = lax.rem(feat, 2), feat // 2
    core_mate, y_mate = {"feat": feat + 1 - 2 * core}, {"feat": feat + 2 - 4 * y}
    row_mates, group_mates = mates("row"), mates("group")
    count = len(shapes)
    feed_in, refs = refs[:feeds], refs[feeds:]
    outs, (home_out, small_out), refs = refs[:count], refs[count : count + 2], refs[count + 2 :]
    feed_out, refs = refs[:feeds], refs[feeds:]
    own, got_core, sum_core, got_y, sum_y, got_row = (refs[i * count : (i + 1) * count] for i in range(6))
    part, part_got, part_sum, small, small_core, small_got, unit_ref, de_ref, slope_ref, wq_ref, wk_ref, wv_ref, send_sem, recv_sem, sems = refs[6 * count :]
    length, width = act_ref.shape
    cols = gwo_ref.shape[0] // 2
    pairs, pair, inner = gw1.shape
    head_dim = pair // 2
    copies = Copies(send_sem, recv_sem)
    moves = {}

    def start(name, *what):
        moves[name] = [copies.send(*w) for w in what]

    lanes = pl.ds(pl.multiple_of(group * cols, 128), cols)
    loads = fetch(
        sems, (de_in, de_ref), (slope_in, slope_ref),
        *[(src.at[:, lanes], dst) for src, dst in ((wq_in, wq_ref), (wk_in, wk_ref), (wv_in, wv_ref))], (unit_in, unit_ref),
    )
    greet([core_mate, y_mate] + row_mates + group_mates)

    half = [h // 2 for h, _ in shapes]
    quarter = [h // 4 for h, _ in shapes]
    piece = [h // (4 * rows) for h, _ in shapes]
    unit = feed_in[0].shape[0]
    place = (core * 2 + y) * rows + row
    source = list(own[:3]) + [gwo_ref, own[4]]
    grad_refs = (gq_ref, gk_ref, gv_ref)

    def token_gradient():
        for load in loads:
            load.wait()
        logits = low(de_ref[0:length] * slope_ref[...])
        total = dot(logits, wr_ref[...])
        for grad, weight in zip(grad_refs, (wq_ref, wk_ref, wv_ref)):
            total = total + dot_nt(grad[0:length], weight[...])
        for r in range(rows):
            for g in range(groups):
                part[g, r * span : (r + 1) * span] = low(total[(r * groups + g) * span : (r * groups + g + 1) * span])
        start("PART0", *[(part.at[lax.rem(group + o, groups)], part_got.at[o - 1], group_mates[o - 1]) for o in range(1, groups)])
        small[...] = jnp.zeros_like(small)
        small[0 : 2 * pairs] = dot_tn(logits, act_ref[...])[0 : 2 * pairs]
        for p in range(pairs):
            for h in range(2):
                n = 2 * p + h
                small[6 + n // 3 : 7 + n // 3, (n % 3) * inner : (n % 3 + 1) * inner] = gb1[p, h * MB : h * MB + 1]
            small[9:10, p * pair : (p + 1) * pair] = gb2[p, 0:1] + gb2[p, MB : MB + 1]
        small[8:9, 0:cols] = jnp.sum(ggain[...], 0, keepdims=True)
        small[8:9, cols : 2 * cols] = jnp.sum(gbias[...], 0, keepdims=True)
        small[9:10, width - 384 : width - 256] = jnp.sum(logits.astype(f32), 0, keepdims=True)
        small[9:10, width - 256 : width - 128] = stat_ref[0:1]
        small[9:10, width - 128 : width] = stat_ref[1:2]
        small[10:11] = jnp.sum(total * unit_ref[...], 0, keepdims=True)
        small[11:12] = gfeed[...]

    def finish(name):
        for copy in moves[name]:
            copy.wait_recv()
        kind, i = name[:-1], int(name[-1])
        if kind == "CORE":
            sum_core[i][...] = add_low(source[i][rows_at(core * half[i], half[i])], got_core[i][...])
        if kind == "Y":
            sum_y[i][...] = add_low(sum_core[i][rows_at(y * quarter[i], quarter[i])], got_y[i][...])
        if kind == "Z":
            value = sum_y[i][rows_at(row * piece[i], piece[i])].astype(f32)
            for o in range(1, rows):
                value = value + got_row[i][o - 1].astype(f32)
            outs[i][group, rows_at(place * piece[i], piece[i])] = low(value)
        if kind == "PART":
            value = part[group].astype(f32)
            for o in range(1, groups):
                value = value + part_got[o - 1].astype(f32)
            part_sum[...] = low(value)
            home_out[rows_at(row * span, span)] = part_sum[rows_at(row * span, span)]
        if kind == "SC":
            small_core[...] = small[...] + small_got[0]
        if kind == "SY":
            small_got[2 + row] = small_core[...] + small_got[1]
        if kind == "SZ":
            value = small_got[2]
            for r in range(1, rows):
                value = value + small_got[2 + r]
            small_out[group] = value

    def begin(name):
        kind, i = name[:-1], int(name[-1])
        if kind == "PART":
            token_gradient()
        if kind == "HOME":
            here = home_out.at[rows_at(row * span, span)]
            start(name, *[
                (part_sum.at[rows_at(lax.rem(row + o, rows) * span, span)], here, row_mates[o - 1]) for o in range(1, rows)
            ])
        if kind == "SC":
            start(name, (small, small_got.at[0], core_mate))
        if kind == "SY":
            start(name, (small_core, small_got.at[1], y_mate))
        if kind == "SZ":
            here = small_got.at[2 + row]
            start(name, *[(here, here, mate) for mate in row_mates])
        if kind == "SX":
            here = small_out.at[group]
            start(name, *[(here, here, mate) for mate in group_mates])
        if kind == "FZ":
            here = feed_out[i].at[group, rows_at(row * unit, unit)]
            here[...] = feed_in[i][...]
            start(name, *[(here, here, mate) for mate in row_mates])
        if kind == "FX":
            here = feed_out[i].at[group]
            start(name, *[(here, here, mate) for mate in group_mates])
        if kind == "CORE":
            if i < 3:
                own[i][...] = low(dot_tn(act_ref[...], grad_refs[i][0:length]))
            if i == 4:
                for p in range(pairs):
                    own[4][p * pair : (p + 1) * pair] = low(gw1[p])
                    own[4][cols + p * pair : cols + (p + 1) * pair] = low(gw2[p])
            start(name, (source[i].at[rows_at((1 - core) * half[i], half[i])], got_core[i], core_mate))
        if kind == "Y":
            start(name, (sum_core[i].at[rows_at((1 - y) * quarter[i], quarter[i])], got_y[i], y_mate))
        if kind == "Z":
            start(name, *[
                (sum_y[i].at[rows_at(lax.rem(row + o, rows) * piece[i], piece[i])], got_row[i].at[o - 1], row_mates[o - 1])
                for o in range(1, rows)
            ])
        if kind == "ZA":
            here = outs[i].at[group, rows_at(place * piece[i], piece[i])]
            start(name, *[(here, here, mate) for mate in row_mates])
        if kind in ("P", "Q", "C"):
            quarters = rows_at((core * 2 + y) * quarter[i], quarter[i])
            halves = rows_at(core * half[i], half[i])
            by_group = TAIL_GROUP_FIRST[i] == (kind == "P")
            if kind == "C":
                here, to = outs[i].at[:, halves], [core_mate]
            elif by_group:
                here, to = outs[i].at[group, quarters if kind == "P" else halves], group_mates
            else:
                here, to = (outs[i].at[group, quarters] if kind == "P" else outs[i].at[:, quarters]), [y_mate]
            start(name, *[(here, here, mate) for mate in to])

    for done, begun in TAIL_SLOTS:
        for name in done:
            finish(name)
        for name in begun:
            begin(name)
    for copy in copies.started:
        copy.wait_send()


def tail(act_row, unit_row, grads, de, slope, weights, rate_weight, grad_out, states, grad_feed_gain, stat, feed_parts, span, collective_id):
    rows, groups = lax.axis_size("row"), lax.axis_size("group")
    length, width = act_row.shape
    cols = grad_out.shape[0] // 2
    inner = states[0].shape[-1]
    shapes = [(width, cols)] * 3 + [(2 * cols, width // 2), (2 * cols, inner)]
    count, feeds = len(shapes), len(feed_parts)
    unit, wide = feed_parts[0].shape
    copies = count * (2 + 2 * (rows - 1) + (groups - 1) + 2) + (groups - 1) + (rows - 1) + 2 + (rows - 1) + (groups - 1)
    copies += feeds * (rows + groups - 2)
    vmem = pl.BlockSpec(memory_space=pltpu.VMEM)
    operands = [act_row, unit_row, *grads, de, slope, *weights, rate_weight, grad_out, *states, grad_feed_gain, stat, *feed_parts]
    outs = [((groups, h, w), bf16) for h, w in shapes]
    outs += [((rows * span, width), bf16), ((groups, 16, width), f32)]
    outs += [((groups, rows * unit, wide), bf16)] * feeds
    scratch = [pltpu.VMEM((h, w), bf16) for h, w in shapes]
    scratch += [pltpu.VMEM((h // 2, w), bf16) for h, w in shapes] * 2
    scratch += [pltpu.VMEM((h // 4, w), bf16) for h, w in shapes] * 2
    scratch += [pltpu.VMEM((rows - 1, h // (4 * rows), w), bf16) for h, w in shapes]
    scratch += [
        pltpu.VMEM((groups, rows * span, width), bf16),
        pltpu.VMEM((groups - 1, rows * span, width), bf16),
        pltpu.VMEM((rows * span, width), bf16),
        pltpu.VMEM((16, width), f32),
        pltpu.VMEM((16, width), f32),
        pltpu.VMEM((2 + rows, 16, width), f32),
        *[pltpu.VMEM(a.shape, f32) for a in (unit_row, de, slope)],
        *[pltpu.VMEM((width, cols), bf16)] * 3,
        pltpu.SemaphoreType.DMA((copies,)),
        pltpu.SemaphoreType.DMA((copies,)),
        pltpu.SemaphoreType.DMA((6,)),
    ]
    return pl.pallas_call(
        partial(tail_kernel, span, shapes, feeds),
        in_specs=[ANYWHERE if i in (1, 5, 6, 7, 8, 9) else vmem for i in range(len(operands))],
        out_specs=[vmem] * len(outs),
        out_shape=[jax.ShapeDtypeStruct(*o) for o in outs],
        scratch_shapes=scratch,
        compiler_params=pltpu.CompilerParams(
            collective_id=collective_id, has_side_effects=True, vmem_limit_bytes=63 * 1024 * 1024
        ),
        name="tail",
    )(*operands)


def finish_kernel(heads, mine, head_dim, inner, total_logits, small_ref, gain_ref, *refs):
    large_in, refs = refs[:14], refs[14:]
    (rate_ref, rbias_ref, fbias_ref, sbias_ref, gain_out, bias_out, mixer_ref, feed_ref, stat_ref,
     q_out, k_out, v_out, o_out, first_out, second_out, gate_out, up_out, down_out, in_out,
     sq, sk, sv, so, s1, s2, sg, su, sd, si, sems, *large, load_sems) = refs
    f0, f1, f2, f3, f4, f5, q_in, k_in, v_in, o_in, s_in, got_ref, tok_ref, hid_ref = large
    groups, width = q_in.shape[0], q_in.shape[1]
    loads = fetch(load_sems, *zip(large_in, large))
    cols = mine * head_dim
    sent, arrived = [], iter(loads)

    def give(value_ref, out):
        copy = pltpu.make_async_copy(value_ref, out, sems.at[len(sent)])
        copy.start()
        sent.append(copy)

    for out, scratch, left, right in ((gate_out, sg, f0, f1), (up_out, su, f2, f3), (down_out, sd, f4, f5)):
        for i, cut in enumerate((left, right)):
            next(arrived).wait()
            value = cut[...].reshape(2 * width, 128)
            for h in range(2):
                scratch[:, (2 * i + h) * 128 : (2 * i + h + 1) * 128] = value[h * width : (h + 1) * width].astype(f32)
        give(scratch, out)
    for out, scratch, array in ((q_out, sq, q_in), (k_out, sk, k_in), (v_out, sv, v_in)):
        next(arrived).wait()
        for g in range(groups):
            size = min(cols, width - g * cols)
            if size > 0:
                scratch[:, g * cols : g * cols + size] = array[g, :, 0:size].astype(f32)
        give(scratch, out)
    next(arrived).wait()
    for g in range(groups):
        size = min(cols, width - g * cols)
        if size > 0:
            for h in range(2):
                scratch = so.at[g * cols : g * cols + size, h * (width // 2) : (h + 1) * (width // 2)]
                scratch[...] = o_in[g, h * cols : h * cols + size].astype(f32)
    give(so, o_out)
    next(arrived).wait()
    for n in range(heads):
        g, i = n // mine, n % mine
        s1[n] = s_in[g, i * head_dim : (i + 1) * head_dim].astype(f32)
        second = s_in[g, cols + i * head_dim : cols + (i + 1) * head_dim].astype(f32)
        s2[n] = second - jnp.sum(second, 0, keepdims=True) * (1.0 / head_dim)
    give(s1, first_out)
    give(s2, second_out)
    for load in arrived:
        load.wait()
    unit, scale = norm_parts(tok_ref[...].astype(f32), width)
    w = got_ref[...].astype(f32) * gain_ref[...].reshape(1, width)
    inv = 1.0 / width
    si[...] = hid_ref[...] + scale * (
        w - jnp.sum(w, -1, keepdims=True) * inv - unit * (jnp.sum(w * unit, -1, keepdims=True) * inv)
    )
    give(si, in_out)
    total = 0.0
    for n in range(heads):
        g, i = n // mine, n % mine
        rate_ref[n : n + 1] = small_ref[g, i : i + 1]
        rbias_ref[:, n : n + 1] = small_ref[g, 9:10, width - 384 + i : width - 383 + i]
        total = total + small_ref[g, 9:10, width - 256 + i : width - 255 + i]
        fbias_ref[n : n + 1] = small_ref[g, 6 + i // 3 : 7 + i // 3, (i % 3) * inner : (i % 3 + 1) * inner]
        own = slice(i * head_dim, (i + 1) * head_dim)
        second = small_ref[g, 9:10, own]
        sbias_ref[n : n + 1] = second - jnp.sum(second, -1, keepdims=True) * (1.0 / head_dim)
        gain_out[n : n + 1] = small_ref[g, 8:9, own]
        bias_out[n : n + 1] = small_ref[g, 8:9, cols + i * head_dim : cols + (i + 1) * head_dim]
    mixer, feed = small_ref[0, 10:11], small_ref[0, 11:12]
    tops = small_ref[0, 9:10, width - 128 : width]
    peers = lax.axis_size("row") * lax.axis_size("feat")
    for g in range(1, groups):
        mixer, feed = mixer + small_ref[g, 10:11], feed + small_ref[g, 11:12]
        tops = jnp.maximum(tops, small_ref[g, 9:10, width - 128 : width])
    mixer_ref[...], feed_ref[...] = mixer.reshape(width), feed.reshape(width)
    lane = lax.broadcasted_iota(jnp.int32, tops.shape, 1)
    top = jnp.max(jnp.where(lane < peers, tops, -3e38), 1, keepdims=True)
    stat_ref[...] = jnp.where(lane == 0, total * (1.0 / total_logits), top)[:, 0:2].reshape(2)
    for copy in sent:
        copy.wait()


def finish(arrays, got, small, tokens, grad_hidden, gain, feed_sums, heads, mine, head_dim, inner, total_logits):
    count, width = tokens.shape
    hidden = 2 * 2 * 128
    vmem = pl.BlockSpec(memory_space=pltpu.VMEM)
    little = [(heads, width), (1, heads), (heads, inner), (heads, head_dim), (heads, head_dim), (heads, head_dim)]
    little += [(width,), (width,), (2,)]
    large = [(width, width)] * 4 + [(heads, head_dim, inner)] * 2 + [(width, hidden)] * 3 + [(count, width)]
    large_in = [*feed_sums, *arrays, got, tokens, grad_hidden]
    return pl.pallas_call(
        partial(finish_kernel, heads, mine, head_dim, inner, total_logits),
        in_specs=[vmem] * 2 + [ANYWHERE] * len(large_in),
        out_specs=[vmem] * len(little) + [ANYWHERE] * len(large),
        out_shape=[jax.ShapeDtypeStruct(s, f32) for s in little + large],
        scratch_shapes=[
            *[pltpu.VMEM(s, f32) for s in large],
            pltpu.SemaphoreType.DMA((len(large),)),
            *[pltpu.VMEM(a.shape, a.dtype) for a in large_in],
            pltpu.SemaphoreType.DMA((len(large_in),)),
        ],
        compiler_params=pltpu.CompilerParams(vmem_limit_bytes=63 * 1024 * 1024),
        name="finish",
    )(small, gain, *large_in)


SEQ = ("row", "group")


def per_device(
    tokens,
    cotangent,
    doc_starts,
    mixer_gain,
    query_weight,
    key_weight,
    value_weight,
    out_weight,
    rate_weight,
    rate_bias,
    first_init,
    first_bias_init,
    second_init,
    second_bias_init,
    inner_gain,
    inner_bias,
    feed_gain,
    gate_weight,
    up_weight,
    down_weight,
):
    rows, span, width = tokens.shape
    heads, head_dim, inner = first_init.shape
    groups = lax.axis_size("group")
    feats = lax.axis_size("feat")
    row, group = lax.axis_index("row"), lax.axis_index("group")
    count = rows * span
    blocks = span * rows * groups // MB
    pairs = -(-heads // (2 * groups))
    mine = 2 * pairs
    pair = 2 * head_dim
    spare = mine * groups - heads

    def padded(array, axis, size):
        edges = [(0, 0)] * array.ndim
        edges[axis] = (0, spare * size)
        return jnp.pad(array, edges) if spare else array

    weights = [padded(w, 1, head_dim) for w in (query_weight, key_weight, value_weight)]
    flat_tokens = tokens.reshape(count, width)
    queries, keys, values, act_row, unit_row, rates, slope, stat, rate_lanes = head(
        tokens, mixer_gain, weights, rate_weight.T, rate_bias, heads, mine, head_dim, 4
    )
    block_ids = jnp.arange(blocks + 1, dtype=jnp.int32)
    starts = lax.dynamic_index_in_dim(doc_starts, row, 0, False)
    restarts = ((block_ids == 0) | jnp.any(starts[:, None] == block_ids[None], 0)).astype(jnp.int32)
    by_pair = lambda a: a.reshape(heads // 2, pair, inner)
    *saved, mixed = forward_inner(
        restarts, queries, keys, values, rates, by_pair(first_init), first_bias_init, by_pair(second_init),
        second_bias_init, inner_gain, inner_bias,
    )

    block_out, grad_hidden, grad_mixed, grad_out_rows, *feed_terms, grad_feed_gain = middle(
        mixed, flat_tokens, cotangent.reshape(count, width), padded(out_weight, 0, head_dim),
        gate_weight, up_weight, down_weight, feed_gain, span, 1,
    )

    grad_q, grad_k, grad_v, grad_e, g_first, g_first_bias, g_second, g_second_bias, g_gain, g_bias, *feed_sums = (
        backward_inner(restarts, queries, keys, values, grad_mixed, rates, saved, inner_gain, inner_bias, feed_terms, 2)
    )
    reduced = tail(
        act_row, unit_row, (grad_q, grad_k, grad_v), grad_e, slope, weights, rate_lanes, grad_out_rows,
        (g_first, g_first_bias, g_second, g_second_bias, g_gain, g_bias), grad_feed_gain, stat,
        feed_sums[FEED_WHOLE:], span, 3,
    )
    arrays, (got, small), feed_sums = reduced[:5], reduced[5:7], [*feed_sums[:FEED_WHOLE], *reduced[7:]]
    (
        g_rate, g_rate_bias, g_first_bias, g_second_bias, g_gain, g_bias, g_mixer, g_feed, stats,
        g_query, g_key, g_value, g_out, g_first, g_second, g_gate, g_up, g_down, input_grad,
    ) = finish(
        arrays, got, small, flat_tokens, grad_hidden, mixer_gain, feed_sums, heads, mine, head_dim, inner,
        rows * groups * feats * count * heads,
    )
    return (
        block_out.reshape(rows, span, width),
        input_grad.reshape(rows, span, width),
        g_mixer,
        g_query,
        g_key,
        g_value,
        g_out,
        g_rate.T,
        g_rate_bias[0],
        g_first,
        g_first_bias,
        g_second,
        g_second_bias,
        g_gain,
        g_bias,
        g_feed,
        g_gate,
        g_up,
        g_down,
        stats,
    )


def solution(mesh):
    feats = mesh.shape["feat"]

    def run(*arrays):
        rows = arrays[0].shape[0] // feats
        grid = jax.sharding.Mesh(mesh.devices.reshape(rows, -1, feats), ("row", "group", "feat"))
        by_token = P("feat", SEQ, None)
        by_hidden = P(None, "feat")
        return jax.shard_map(
            per_device,
            mesh=grid,
            in_specs=(by_token, by_token, P("feat", None)) + (P(),) * 14 + (by_hidden,) * 3,
            out_specs=(by_token, by_token) + (P(),) * 14 + (by_hidden,) * 3 + (P(),),
            check_vma=False,
        )(*arrays)

    return run
```

```python
from functools import partial

import jax
import jax.numpy as jnp
from jax import lax
from jax.experimental import pallas as pl
from jax.experimental.pallas import tpu as pltpu
from jax.sharding import PartitionSpec as P

MB = 16
epsilon = 1e-05
f32, bf16 = jnp.float32, jnp.bfloat16


def dot(a, b):
    return lax.dot_general(a, b, (((1,), (0,)), ((), ())), preferred_element_type=f32)


def dot_nt(a, b):
    return lax.dot_general(a, b, (((1,), (1,)), ((), ())), preferred_element_type=f32)


def dot_tn(a, b):
    return lax.dot_general(a, b, (((0,), (0,)), ((), ())), preferred_element_type=f32)


def low(v):
    return v.astype(bf16)


def gelu_parts(z):
    a = jnp.abs(z)
    d = 1.0 + 0.23164189 * a
    t = pl.reciprocal(d, approx=True)
    t = t * (2.0 - d * t)
    ex = jnp.exp(-0.5 * (z * z))
    poly = t * (
        0.127414796 + t * (-0.142248368 + t * (0.7107068705 + t * (-0.7265760135 + t * 0.5307027145)))
    )
    h = poly * ex
    cdf = jnp.where(z >= 0, 1.0 - h, h)
    pdf = 0.3989422804014327 * ex
    return z * cdf, cdf + z * pdf, pdf


def lane_sum(v):
    return jnp.sum(v, -1, keepdims=True)


def masks(head_dim):
    pair = 2 * head_dim
    rows, cols = 2 * MB, pair
    r = lax.broadcasted_iota(jnp.int32, (rows, cols), 0)
    c = lax.broadcasted_iota(jnp.int32, (rows, cols), 1)
    own = ((r < MB) == (c < head_dim)).astype(f32)
    r = lax.broadcasted_iota(jnp.int32, (rows, rows), 0)
    c = lax.broadcasted_iota(jnp.int32, (rows, rows), 1)
    same = (r < MB) == (c < MB)
    causal = (same & (c <= r)).astype(f32)
    return own, causal, same.astype(bf16)


def spread(v, own):
    return jnp.concatenate([v, v], 0) * own


def fold(v):
    return v[:MB] + v[MB:]


def twice(v):
    return jnp.concatenate([v, v], 1)


def pair_index(p, pairs, array):
    return jnp.minimum(lax.axis_index("group") * pairs + p, array.shape[0] - 1)


def load_params(par_ref, sources, places):
    for i, source in enumerate(sources):
        for p, n in enumerate(places):
            par_ref[i, p] = jnp.concatenate([source[pl.ds(2 * n + h, 1)] for h in range(2)], 1)


def rate_rows(rates, p):
    return jnp.concatenate([jnp.broadcast_to(rates[:, n : n + 1], rates.shape) for n in (2 * p, 2 * p + 1)], 0)


def fetch(sems, *moves):
    copies = [pltpu.make_async_copy(src, dst, sems.at[i]) for i, (src, dst) in enumerate(moves)]
    for copy in copies:
        copy.start()
    return copies


ANYWHERE = pl.BlockSpec(memory_space=pl.ANY)


def in_turn(parts):
    while parts:
        parts = [part for part in parts if next(part, parts) is not parts]


def forward_kernel(pairs, head_dim, restart_ref, q_all, k_all, v_all, rate_all, w1i_ref, b1i_ref, w2i_ref, b2i_ref, gain_in, bias_in,
                   *refs):
    saved, out_all, refs = refs[:7], refs[7], refs[8:]
    rings, refs, sems = refs[:7], refs[7:-1], refs[-1]
    last = q_all.shape[0] // MB - 1
    slots = rings[0].shape[0]

    def leave(j, i):
        return pltpu.make_async_copy(
            rings[i].at[pl.ds(lax.rem(j, slots), 1)], saved[i].at[pl.ds(j, 1)], sems.at[i, lax.rem(j, slots)]
        )

    def step(j, _):
        @pl.when(j >= slots)
        def _():
            for i in range(7):
                leave(j - slots, i).wait()

        tokens = rows_at(jnp.minimum(j, last) * MB, MB)
        forward_step(
            pairs, head_dim, j, restart_ref, *[ref.at[tokens] for ref in (q_all, k_all, v_all, rate_all)],
            w1i_ref, b1i_ref, w2i_ref, b2i_ref, gain_in, bias_in,
            *[ring.at[pl.ds(lax.rem(j, slots), 1)] for ring in rings], out_all.at[rows_at(j * MB, MB)], *refs,
        )
        for i in range(7):
            leave(j, i).start()

    lax.fori_loop(0, last + 2, step, None)
    for o in range(slots):
        for i in range(7):
            leave(last + 2 - slots + o, i).wait()


def forward_step(pairs, head_dim, j, restart_ref, q_ref, k_ref, v_ref, rate_ref, w1i_ref, b1i_ref, w2i_ref, b2i_ref, gain_in, bias_in,
                 big_ref, mid_ref, small_ref, n1_ref, pq_ref, uq_ref, n2_ref, out_ref,
                 w1, b1, w2, b2, s_q1, s_x2, s_e2, s_w2, s_b2, s_q, par_ref):
    pair = 2 * head_dim
    inv = 1.0 / head_dim
    own, causal, ones = masks(head_dim)

    @pl.when(j == 0)
    def _():
        load_params(par_ref, (b2i_ref, gain_in, bias_in), [pair_index(p, pairs, w1i_ref) for p in range(pairs)])

    @pl.when(restart_ref[j] > 0)
    def _():
        for p in range(pairs):
            n = pair_index(p, pairs, w1i_ref)
            second = w2i_ref[n]
            second_bias = par_ref[0, p] * own
            w1[p] = w1i_ref[n]
            for h in range(2):
                b1[p, h * MB : (h + 1) * MB] = jnp.broadcast_to(b1i_ref[pl.ds(2 * n + h, 1)], (MB, b1i_ref.shape[1]))
                half = second[h * head_dim : (h + 1) * head_dim]
                w2[p, h * head_dim : (h + 1) * head_dim] = half - jnp.sum(half, 0, keepdims=True) * inv
            b2[p] = second_bias - (lane_sum(second_bias) * inv) * own

    loaded = [
        (s_q1[p], s_x2[p], s_e2[p], s_w2[p], s_b2[p], s_q[p], w1[p], w2[p], b1[p], b2[p], rate_rows(rate_ref[...], p))
        for p in range(pairs)
    ]
    tokens = [
        [ref[:, p * pair : (p + 1) * pair] for ref in (q_ref, k_ref, v_ref)]
        + [par_ref[i, p] for i in (1, 2)]
        for p in range(pairs)
    ]
    writes = []

    def write(ref, index, value):
        writes.append((ref, index, value))

    def outputs_before(p):
        q1p, x2p, e2p, w2p, b2p, qp = loaded[p][:6]
        gain, bias = tokens[p][3:]
        p2, lq, _ = gelu_parts(q1p)
        p2b = low(p2)
        yield
        n2 = causal * (dot_nt(p2b, x2p) + 1.0)
        q2 = dot_nt(p2b, w2p)
        yield
        q2 = q2 * own - dot(low(n2), e2p) + b2p
        yield
        sq = lax.rsqrt(lane_sum(q2 * q2) * inv + epsilon)
        uq = q2 * sq
        write(out_ref, (slice(None), slice(p * pair, (p + 1) * pair)), qp + fold(uq) * gain + bias)
        write(pq_ref, (0, p, slice(0, 2 * MB)), p2b)
        write(pq_ref, (0, p, slice(2 * MB, 4 * MB)), low(lq))
        write(uq_ref, (0, p, slice(0, 2 * MB)), uq)
        write(uq_ref, (0, p, slice(2 * MB, 4 * MB)), jnp.broadcast_to(sq, uq.shape))
        write(n2_ref, (0, p), low(n2))

    def inner_step(p):
        w1c, w2c, b1c, b2c, e = loaded[p][6:]
        qc, kc, vc, gain, bias = tokens[p]
        kb, qb = low(spread(kc, own)), low(spread(qc, own))
        w1b, w2b = low(w1c), low(w2c)
        kq = dot(jnp.concatenate([kb, qb], 0), w1b)
        n1 = low(causal * (dot_nt(qb, kb) + 1.0))
        yield
        z1 = kq[: 2 * MB] + b1c
        x2, l1, pdf = gelu_parts(z1)
        x2b = low(x2)
        yield
        c = dot_nt(x2b, w2b)
        yield
        c = c * own + b2c
        s = lax.rsqrt(lane_sum(c * c) * inv + epsilon)
        u = c * s
        r = u * (gain * gain) + spread((bias - (vc - kc)) * gain, own)
        mr, m2 = lane_sum(r) * inv, lane_sum(r * u) * inv
        g2 = s * (r - mr * own - u * m2)
        e2 = e * g2
        e2b = low(e2)
        yield
        h = dot(low(g2), w2b)
        u2 = dot_tn(e2b, x2b)
        yield
        g1 = h * l1
        e1b = low(twice(e) * g1)
        yield
        u1 = dot_tn(kb, e1b)
        below = dot(jnp.concatenate([n1, ones], 0), e1b)
        yield
        q1 = kq[2 * MB :] + b1c - below[: 2 * MB]
        write(w1, p, w1c - u1)
        write(b1, p, b1c - below[2 * MB :])
        write(w2, p, w2c - u2)
        write(b2, p, b2c - jnp.sum(e2, 0, keepdims=True) * own)
        write(big_ref, (0, p, slice(0, pair)), w1b)
        write(big_ref, (0, p, slice(pair, 2 * pair)), w2b)
        write(big_ref, (0, p, slice(2 * pair, 2 * pair + 2 * MB)), x2b)
        write(big_ref, (0, p, slice(2 * pair + 2 * MB, 2 * pair + 4 * MB)), e1b)
        write(mid_ref, (0, p, slice(0, 2 * MB)), low(g1))
        write(mid_ref, (0, p, slice(2 * MB, 4 * MB)), low(l1))
        write(mid_ref, (0, p, slice(4 * MB, 6 * MB)), low(h * pdf * (2.0 - z1 * z1)))
        for i, value in enumerate((u, s, r, m2, g2)):
            write(small_ref, (0, p, slice(i * 2 * MB, (i + 1) * 2 * MB)), jnp.broadcast_to(value, u.shape))
        write(n1_ref, (0, p), n1)
        for ref, value in ((s_q1, q1), (s_x2, x2b), (s_e2, e2b), (s_w2, w2b), (s_b2, b2c), (s_q, qc)):
            write(ref, p, value)

    in_turn([inner_step(p) for p in range(pairs)] + [outputs_before(p) for p in range(pairs)])
    for ref, index, value in writes:
        ref[index] = value


def forward_inner(restarts, q, k, v, rates, w1i, b1i, w2i, b2i, gain, bias):
    _, pair, inner = w1i.shape
    blocks, pairs = q.shape[0] // MB, q.shape[1] // pair
    head_dim = pair // 2
    steps = blocks + 1
    slots = min(8, steps)
    vmem = pl.BlockSpec(memory_space=pltpu.VMEM)
    kinds = [
        (2 * pair + 4 * MB, inner, bf16),
        (6 * MB, inner, bf16),
        (10 * MB, pair, f32),
        (2 * MB, 2 * MB, bf16),
        (4 * MB, inner, bf16),
        (4 * MB, pair, f32),
        (2 * MB, 2 * MB, bf16),
    ]
    return pl.pallas_call(
        partial(forward_kernel, pairs, head_dim),
        in_specs=[pl.BlockSpec(memory_space=pltpu.SMEM)] + [vmem] * 10,
        out_specs=[ANYWHERE] * 7 + [vmem],
        scratch_shapes=[pltpu.VMEM((slots, pairs, h, w), kind) for h, w, kind in kinds] + [
            pltpu.VMEM((pairs, pair, inner), f32),
            pltpu.VMEM((pairs, 2 * MB, inner), f32),
            pltpu.VMEM((pairs, pair, inner), f32),
            pltpu.VMEM((pairs, 2 * MB, pair), f32),
            pltpu.VMEM((pairs, 2 * MB, inner), f32),
            pltpu.VMEM((pairs, 2 * MB, inner), bf16),
            pltpu.VMEM((pairs, 2 * MB, pair), bf16),
            pltpu.VMEM((pairs, pair, inner), bf16),
            pltpu.VMEM((pairs, 2 * MB, pair), f32),
            pltpu.VMEM((pairs, MB, pair), f32),
            pltpu.VMEM((3, pairs, 1, pair), f32),
            pltpu.SemaphoreType.DMA((7, slots)),
        ],
        out_shape=[jax.ShapeDtypeStruct((steps, pairs, h, w), kind) for h, w, kind in kinds]
        + [jax.ShapeDtypeStruct((steps * MB, pairs * pair), f32)],
        compiler_params=pltpu.CompilerParams(vmem_limit_bytes=63 * 1024 * 1024),
        name="inner_forward",
    )(restarts, q, k, v, rates, w1i, b1i, w2i, b2i, gain, bias)


MESH = pl.DeviceIdType.MESH


def greet(peers):
    barrier = pltpu.get_barrier_semaphore()
    for peer in peers:
        pl.semaphore_signal(barrier, inc=1, device_id=peer, device_id_type=MESH)
    pl.semaphore_wait(barrier, len(peers))


class Copies:
    def __init__(self, send_sem, recv_sem):
        self.send_sem, self.recv_sem, self.started = send_sem, recv_sem, []

    def make(self, src, dst, peer):
        i = len(self.started)
        copy = pltpu.make_async_remote_copy(
            src_ref=src, dst_ref=dst, send_sem=self.send_sem.at[i], recv_sem=self.recv_sem.at[i],
            device_id=peer, device_id_type=MESH,
        )
        self.started.append(copy)
        return copy

    def send(self, src, dst, peer):
        copy = self.make(src, dst, peer)
        copy.start()
        return copy


def rows_at(start, size):
    return pl.ds(pl.multiple_of(start, 16), size)


def add_low(a, b):
    return (a.astype(f32) + b.astype(f32)).astype(bf16)


def mates(axis):
    size, here = lax.axis_size(axis), lax.axis_index(axis)
    return [{axis: lax.rem(here + o, size)} for o in range(1, size)]


def feed_sum_steps(ins, outs, got_group, sum_group, got_row, full, copies, whole):
    row, group = lax.axis_index("row"), lax.axis_index("group")
    rows, groups = lax.axis_size("row"), lax.axis_size("group")
    row_mates, group_mates = mates("row"), mates("group")
    count = len(ins)
    part = ins[0].shape[0] // groups
    unit = part // rows
    mine = rows_at(row * unit, unit)
    moves = {}
    for i in range(count):
        moves["X", i] = [
            copies.make(ins[i].at[rows_at(lax.rem(group + o, groups) * part, part)], got_group[i].at[o - 1], group_mates[o - 1])
            for o in range(1, groups)
        ]
        moves["Z", i] = [
            copies.make(sum_group[i].at[rows_at(lax.rem(row + o, rows) * unit, unit)], got_row[i].at[o - 1], row_mates[o - 1])
            for o in range(1, rows)
        ]
        if i < whole:
            here = full[i].at[group, mine]
            moves["ZA", i] = [copies.make(here, here, mate) for mate in row_mates]
            here = full[i].at[group]
            moves["XA", i] = [copies.make(here, here, mate) for mate in group_mates]

    def finish(kind, i):
        for copy in moves[kind, i]:
            copy.wait_recv()
        if kind == "X":
            total = ins[i][rows_at(group * part, part)].astype(f32)
            for o in range(1, groups):
                total = total + got_group[i][o - 1].astype(f32)
            sum_group[i][...] = low(total)
        if kind == "Z":
            total = sum_group[i][mine].astype(f32)
            for o in range(1, rows):
                total = total + got_row[i][o - 1].astype(f32)
            if i < whole:
                full[i][group, mine] = low(total)
            else:
                outs[i][...] = low(total)

    def run(slot):
        _, done, begun = FEED_SLOTS[slot]
        if slot == 0:
            greet(row_mates + group_mates)
        for name in done:
            finish(name[:-1], int(name[-1]))
        for name in begun:
            for copy in moves[name[:-1], int(name[-1])]:
                copy.start()
        if slot == len(FEED_SLOTS) - 1:
            for i in range(whole):
                outs[i][...] = full[i][...]
            for copy in copies.started:
                copy.wait_send()

    return [partial(run, slot) for slot in range(len(FEED_SLOTS))]


def backward_kernel(pairs, head_dim, feeds, restart_ref, q_all, k_all, v_all, do_all, rate_all, gain_in, bias_in, *refs):
    saved, feed_in, refs = refs[:7], refs[7 : 7 + feeds], refs[7 + feeds :]
    tok_out, held, refs = refs[:4], refs[4 : 10 + feeds], refs[10 + feeds :]
    rings, sems, refs = refs[:7], refs[7], refs[8:]
    blocks = q_all.shape[0] // MB
    steps = blocks + 1
    slots = rings[0].shape[0]
    depth = slots - 3

    def arrive(j, i):
        at = jnp.maximum(blocks - 1 - j, 0) + (1 if i >= 4 else 0)
        return pltpu.make_async_copy(saved[i].at[pl.ds(at, 1)], rings[i].at[pl.ds(lax.rem(j, slots), 1)], sems.at[i, lax.rem(j, slots)])

    for j in range(depth):
        for i in range(7):
            arrive(j, i).start()

    def step(j, _):
        @pl.when(j + depth < steps)
        def _():
            for i in range(7):
                arrive(j + depth, i).start()

        for i in range(7):
            arrive(j, i).wait()
        ahead = rows_at(jnp.maximum(blocks - 1 - j, 0) * MB, MB)
        now = rows_at(jnp.minimum(blocks - j, blocks - 1) * MB, MB)
        bigq, _, smallq, n1, pqq, uqq, n2 = (ring.at[pl.ds(lax.rem(j, slots), 1)] for ring in rings)
        big, mid, small, _, pq, uq, _ = (ring.at[pl.ds(lax.rem(j + slots - 1, slots), 1)] for ring in rings)
        backward_step(
            pairs, head_dim, feeds, j, steps, restart_ref,
            *[ref.at[ahead] for ref in (q_all, k_all, do_all, rate_all)], bigq, smallq, n1, pqq, uqq, n2,
            *[ref.at[now] for ref in (q_all, k_all, v_all, do_all, rate_all)], big, mid, small, pq, uq, gain_in, bias_in,
            *feed_in, *[ref.at[rows_at((blocks - j) * MB, MB)] for ref in tok_out], *held, *refs,
        )

    lax.fori_loop(0, steps, step, None)


def backward_step(pairs, head_dim, feeds, j, steps, restart_ref,
                  qq_ref, kq_ref, doq_ref, eq_ref, bigq_ref, smallq_ref, n1_ref, pqq_ref, uqq_ref, n2_ref,
                  q_ref, k_ref, v_ref, do_ref, e_ref, big_ref, mid_ref, small_ref, pq_ref, uq_ref, gain_in, bias_in, *refs):
    pair = 2 * head_dim
    inv = 1.0 / head_dim
    own, causal, ones = masks(head_dim)
    feed_in, refs = refs[:feeds], refs[feeds:]
    dq_ref, dk_ref, dv_ref, de_ref, gw1, gb1, gw2, gb2, ggain, gbias = refs[:10]
    feed_out, refs = refs[10 : 10 + feeds], refs[10 + feeds :]
    w1, b1, w2, b2, s_e1, s_e2, s_k, s_x2, s_q1, s_q2, s_q, par_ref = refs[:12]
    if feeds:
        refs, sems = refs[12:-2], refs[-2:]
        buffers = [refs[i * feeds : (i + 1) * feeds] for i in range(3)] + [refs[3 * feeds :]]
        slots = feed_sum_steps(feed_in, feed_out, *buffers, Copies(*sems), FEED_WHOLE)
        for i, run in enumerate(slots):
            pl.when(j == FEED_SLOTS[i][0] * (steps - 1) // 32)(run)

    @pl.when(j == 0)
    def _():
        places = [jnp.minimum(lax.axis_index("group") * pairs + p, gain_in.shape[0] // 2 - 1) for p in range(pairs)]
        load_params(par_ref, (gain_in, bias_in), places)

    @pl.when(j <= 1)
    def _():
        for ref in (w1, b1, w2, b2, gw1, gb1, gw2, gb2, ggain, gbias):
            ref[...] = jnp.zeros_like(ref)

    rows2 = 2 * MB
    piece = lambda ref, p, i: ref[0, p, i * rows2 : (i + 1) * rows2]
    token = lambda ref, p: ref[:, p * pair : (p + 1) * pair]
    first = restart_ref[jnp.minimum(steps - 1 - j, steps - 2)]
    go_on = 1.0 - first
    writes = []

    def write(ref, index, value):
        writes.append((ref, index, value))

    def load_outputs(p):
        return (
            [token(ref, p) for ref in (qq_ref, kq_ref, doq_ref)]
            + [par_ref[0, p]]
            + [bigq_ref[0, p, 0:pair], bigq_ref[0, p, pair : 2 * pair]]
            + [bigq_ref[0, p, 2 * pair : 2 * pair + rows2], bigq_ref[0, p, 2 * pair + rows2 : 2 * pair + 2 * rows2]]
            + [rate_rows(eq_ref[...], p), piece(smallq_ref, p, 4), n1_ref[0, p], n2_ref[0, p]]
            + [piece(ref, p, i) for ref in (pqq_ref, uqq_ref) for i in range(2)]
        )

    def load_step(p):
        return (
            [ref[p] for ref in (s_e1, s_e2, s_k, s_x2, s_q1, s_q2, s_q, w1, w2, b1, b2)]
            + [token(ref, p) for ref in (q_ref, k_ref, v_ref, do_ref)]
            + [par_ref[i, p] for i in (0, 1)]
            + [big_ref[0, p, 0:pair], big_ref[0, p, pair : 2 * pair]]
            + [big_ref[0, p, 2 * pair : 2 * pair + rows2], big_ref[0, p, 2 * pair + rows2 : 2 * pair + 2 * rows2]]
            + [piece(mid_ref, p, i).astype(f32) for i in range(3)]
            + [piece(small_ref, p, i) for i in range(5)]
            + [piece(pq_ref, p, 0), piece(uq_ref, p, 0), rate_rows(e_ref[...], p)]
        )

    def outputs_ahead(p, loaded):
        qc, kc, do, gain, w1b, w2b, x2b, e1b, e, g2, n1b, n2b, p2b, lq, uq, sq = loaded
        qb, kb = low(spread(qc, own)), low(spread(kc, own))
        e2b = low(e * g2)
        w = spread(do * gain, own)
        dq2 = low(sq * (w - (lane_sum(w) * inv) * own - uq * (lane_sum(w * uq) * inv)))
        yield
        dn2 = dot_nt(dq2, e2b)
        dp2 = dot(dq2, w2b)
        yield
        dpx = low(-causal * dn2)
        new_e2 = dot_tn(n2b, dq2)
        dp2 = dp2 + dot(dpx, x2b)
        yield
        dq1 = low(dp2 * lq.astype(f32))
        new_x2 = dot_tn(dpx, p2b)
        yield
        dn1 = dot_nt(dq1, e1b)
        new_q = dot_nt(dq1, w1b)
        yield
        new_e1 = dot_tn(n1b, dq1)
        dqk = low(-causal * dn1)
        yield
        new_k = dot_tn(dqk, qb)
        new_q = do + fold((new_q + dot(dqk, kb)) * own)
        for ref, value in zip((s_e1, s_e2, s_k, s_x2, s_q1, s_q2, s_q), (new_e1, new_e2, new_k, new_x2, dq1, dq2, new_q)):
            write(ref, p, value)

    def step_back(p, loaded):
        e1q, e2q, dkq, x2q, dq1, dq2, dqc, dw1, dw2, db1, db2, qc, kc, vc, do, gain, bias, w1b, w2b, x2b, e1b = loaded[:21]
        g1, l1, hg, u, s, r, m2, g2, p2b, uq, e = loaded[21:]
        cols = (slice(None), slice(p * pair, (p + 1) * pair))
        dw1b, dw2b = low(dw1), low(dw2)
        qb, kb = low(spread(qc, own)), low(spread(kc, own))
        e2b = low(e * g2)
        de1 = dot(kb, dw1b)
        de2 = dot_nt(x2b, dw2b)
        yield
        de1 = -(e1q + de1 + db1)
        de2 = -(e2q + de2 * own + db2)
        dg1 = twice(e) * de1
        dh = low(dg1 * l1)
        yield
        dg2 = dot_nt(dh, w2b)
        dx2 = x2q - dot(e2b, dw2b)
        yield
        dg2 = e * de2 + dg2 * own
        dk = dkq - dot_nt(e1b, dw1b) * own
        ma, mg = lane_sum(dg2 * u) * inv, lane_sum(dg2) * inv
        rate = jnp.broadcast_to(lane_sum(g1 * de1) + lane_sum(g2 * de2), u.shape)
        rates.append(jnp.where(head == 2 * p, rate[:MB], 0.0) + jnp.where(head == 2 * p + 1, rate[MB:], 0.0))
        yield
        dr = s * (dg2 - mg * own - u * ma)
        du = dr * (gain * gain) - s * (dg2 * m2 + r * ma)
        yield
        md, mu = lane_sum(du) * inv, lane_sum(du * u + dg2 * g2) * inv
        dz2 = low(s * (du - md * own - u * mu))
        yield
        dx2 = dx2 + dot(dz2, w2b)
        yield
        dz1 = low(dg1 * hg + dx2 * l1)
        drg = fold(dr) * gain
        write(dq_ref, cols, low(dqc))
        write(dv_ref, cols, low(-drg))
        more_gain = fold(spread_by(do, uq)) + fold(dr * u) * (2.0 * gain) + fold(dr) * (bias - (vc - kc))
        yield
        ndw1 = dw1 + dot_tn(jnp.concatenate([qb, kb], 0), jnp.concatenate([dq1, dz1], 0))
        yield
        dk = dk + dot_nt(dz1, w1b) * own
        write(dk_ref, cols, low(fold(dk) + drg))
        ndw2 = dw2 + dot_tn(jnp.concatenate([dq2, low(g2), dz2], 0), jnp.concatenate([p2b, dh, x2b], 0))
        ndb1 = db1 + dot(ones, dq1) + dot(ones, dz1)
        ndb2 = db2 + dot(ones, dq2) + dot(ones, dz2)
        for ref, value in ((w1, ndw1), (w2, ndw2), (b1, ndb1), (b2, ndb2)):
            write(ref, p, value * go_on)
        more.append((cols, more_gain, do + drg))
        starts.append((p, ndw1, ndw2, ndb1, ndb2))

    more, starts, rates = [], [], []
    head = lax.broadcasted_iota(jnp.int32, (MB, pair), 1)
    ahead_in = [load_outputs(p) for p in range(pairs)]
    step_in = [load_step(p) for p in range(pairs)]
    in_turn([step_back(p, step_in[p]) for p in range(pairs)] + [outputs_ahead(p, ahead_in[p]) for p in range(pairs)])
    for ref, index, value in writes:
        ref[index] = value
    de_ref[...] = sum(rates)
    for cols, more_gain, more_bias in more:
        ggain[cols] += more_gain
        gbias[cols] += more_bias
    for p, *values in starts:
        for ref, value in zip((gw1, gw2, gb1, gb2), values):
            ref[p] += value * first


def spread_by(do, uq):
    return jnp.concatenate([do, do], 0) * uq


def backward_inner(restarts, q, k, v, do, rates, saved, gain, bias, feed_terms, collective_id):
    big, mid, small, n1, pq, uq, n2 = saved
    pairs, pair, inner = big.shape[1], 2 * gain.shape[1], big.shape[3]
    blocks = q.shape[0] // MB
    head_dim = pair // 2
    steps = blocks + 1
    slots = min(8, steps)
    vmem = pl.BlockSpec(memory_space=pltpu.VMEM)
    feeds = len(feed_terms)
    width = pairs * pair
    tok_out = (jax.ShapeDtypeStruct((steps * MB, width), bf16), vmem)
    state = [((pairs, pair, inner), f32), ((pairs, 2 * MB, inner), f32), ((pairs, pair, inner), f32), ((pairs, 2 * MB, pair), f32)]
    keep = lambda shape: (jax.ShapeDtypeStruct(shape, f32), vmem)
    outs = [tok_out] * 3 + [
        (jax.ShapeDtypeStruct((steps * MB, pair), f32), vmem)
    ] + [keep(shape) for shape, _ in state] + [keep((MB, width))] * 2
    comm = []
    if feeds:
        groups, rows = lax.axis_size("group"), lax.axis_size("row")
        part, wide = feed_terms[0].shape[0] // groups, feed_terms[0].shape[1]
        unit = part // rows
        outs += [
            (jax.ShapeDtypeStruct((groups, part, wide) if i < FEED_WHOLE else (unit, wide), bf16), vmem) for i in range(feeds)
        ]
        comm = [pltpu.VMEM((groups - 1, part, wide), bf16)] * feeds + [pltpu.VMEM((part, wide), bf16)] * feeds
        comm += [pltpu.VMEM((rows - 1, unit, wide), bf16)] * feeds + [pltpu.VMEM((groups, part, wide), bf16)] * FEED_WHOLE
        copies = (feeds + FEED_WHOLE) * (groups + rows - 2)
        comm += [pltpu.SemaphoreType.DMA((copies,))] * 2
    return pl.pallas_call(
        partial(backward_kernel, pairs, head_dim, feeds),
        in_specs=[pl.BlockSpec(memory_space=pltpu.SMEM)] + [vmem] * 7 + [ANYWHERE] * 7 + [vmem] * feeds,
        out_specs=[o[1] for o in outs],
        scratch_shapes=[pltpu.VMEM((slots,) + a.shape[1:], a.dtype) for a in saved] + [
            pltpu.SemaphoreType.DMA((7, slots)),
        ] + [pltpu.VMEM(shape, kind) for shape, kind in state] + [
                pltpu.VMEM((pairs, 2 * MB, inner), f32),
                pltpu.VMEM((pairs, 2 * MB, pair), f32),
                pltpu.VMEM((pairs, 2 * MB, pair), f32),
                pltpu.VMEM((pairs, 2 * MB, inner), f32),
                pltpu.VMEM((pairs, 2 * MB, inner), bf16),
                pltpu.VMEM((pairs, 2 * MB, pair), bf16),
                pltpu.VMEM((pairs, MB, pair), f32),
                pltpu.VMEM((2, pairs, 1, pair), f32),
            ] + comm,
        out_shape=[o[0] for o in outs],
        compiler_params=pltpu.CompilerParams(
            collective_id=collective_id if feeds else None, has_side_effects=bool(feeds), vmem_limit_bytes=63 * 1024 * 1024
        ),
        name="inner_backward",
    )(restarts.astype(f32), q, k, v, do, rates, gain, bias, *saved, *feed_terms)


def norm_parts(v, width):
    centered = v - jnp.sum(v, -1, keepdims=True) * (1.0 / width)
    scale = lax.rsqrt(jnp.sum(centered * centered, -1, keepdims=True) * (1.0 / width) + epsilon)
    return centered * scale, scale


def feed_terms(*items):
    for outs, left, right in items:
        width = left.shape[1]
        for i, out in enumerate(outs):
            both = low(dot_tn(left[...], right[:, i * 256 : (i + 1) * 256]))
            out[0:width] = both[:, :128]
            out[width : 2 * width] = both[:, 128:]


def middle_kernel(span, mixed_in, tok_in, cot_in, wout_in, gate_in, up_in, down_in, gain_ref,
                  block_ref, hid_ref, gmix_ref, gwo_ref, t0, t1, t2, t3, t4, t5, gfeed_ref,
                  tok_ref, cot_ref, wout_ref, gate_ref, up_ref, down_ref, downs, mixed_ref, mixed_got, acts, cots, unit, scales, h_in, gg, gu, ha, pg0, po0, out_core, in_core, out_diag, in_diag, out_y, in_y,
                  branch, branch_row, send_sem, recv_sem, local_sem, sems):
    rows, groups = lax.axis_size("row"), lax.axis_size("group")
    row, group, feat = lax.axis_index("row"), lax.axis_index("group"), lax.axis_index("feat")
    count, width = tok_in.shape
    cols = mixed_ref.shape[1]
    core, y = lax.rem(feat, 2), feat // 2
    core_mate, y_mate = {"feat": feat + 1 - 2 * core}, {"feat": feat + 2 - 4 * y}
    here = row * groups + group
    places = rows * groups
    others = [lax.rem(here + o, places) for o in range(1, places)]
    seq_mates = [{"row": t // groups, "group": lax.rem(t, groups)} for t in others]
    copies = Copies(send_sem, recv_sem)
    send = copies.send
    slot = lambda ref, s: ref.at[s * count : (s + 1) * count]

    loads = fetch(
        sems, (cot_in, cot_ref), (down_in, down_ref), (tok_in, tok_ref), (wout_in, wout_ref), (gate_in, gate_ref), (up_in, up_ref)
    )
    mixed_ref[...] = low(mixed_in[MB:])
    greet([core_mate, y_mate] + seq_mates)
    lanes = pl.ds(pl.multiple_of(group * cols, 128), cols)
    moves = [
        send(mixed_ref.at[rows_at(t * span, span)], mixed_got.at[rows_at(row * span, span), lanes], mate)
        for t, mate in zip(others, seq_mates)
    ]
    own = pltpu.make_async_copy(
        mixed_ref.at[rows_at(here * span, span)], mixed_got.at[rows_at(row * span, span), lanes], local_sem.at[0]
    )
    own.start()
    loads[0].wait()
    cot_core = send(cot_ref, slot(cots, 1), core_mate)
    cot_y = send(cot_ref, slot(cots, 2), y_mate)
    cots[0:count] = cot_ref[...]
    loads[1].wait()
    cot_core.wait_recv()
    downs[0 : 2 * count] = dot(cots[0 : 2 * count], down_ref[...])
    own.wait()
    loads[2].wait()
    loads[3].wait()
    for copy in moves:
        copy.wait_recv()
    hidden = tok_ref[...].astype(f32) + dot(mixed_got[:, :width], wout_ref[:width])
    h_in[...] = hidden
    unit_two, scale_two = norm_parts(hidden, width)
    unit[...] = unit_two
    scales[...] = jnp.broadcast_to(scale_two, scales.shape)
    gain = gain_ref[...].reshape(1, width)
    acts[0:count] = low(unit_two * gain)
    cut = count // 2
    span_of = lambda s, h: slice(s * count + h * cut, s * count + (h + 1) * cut)
    act_y = [send(acts.at[span_of(0, h)], acts.at[span_of(2, h)], y_mate) for h in range(2)]
    act_core = send(slot(acts, 0), slot(acts, 1), core_mate)
    cot_y.wait_recv()
    cot_diag = send(slot(cots, 2), slot(cots, 3), core_mate)
    loads[4].wait()
    loads[5].wait()

    def feed(part):
        gate_pre, up_value = dot(acts[part], gate_ref[...]), dot(acts[part], up_ref[...])
        grad = downs[part]
        sig = jax.nn.sigmoid(gate_pre)
        silu = gate_pre * sig
        ha[part] = low(silu * up_value)
        gg[part] = low(grad * up_value * sig * (1.0 + gate_pre * (1.0 - sig)))
        gu[part] = low(grad * silu)
        return dot_nt(gg[part], gate_ref[...]) + dot_nt(gu[part], up_ref[...])

    def forth(s):
        return dot_nt(ha[s * count : (s + 1) * count], down_ref[...])

    pg0[...] = feed(slice(0, count))
    act_core.wait_recv()
    out_core[0] = low(feed(slice(count, 2 * count)))
    core_sums = [send(out_core.at[0], in_core.at[0], core_mate)]
    cot_diag.wait_recv()
    downs[2 * count : 4 * count] = dot(cots[2 * count : 4 * count], down_ref[...])
    y_sums = []
    for h in range(2):
        rows_h = slice(h * cut, (h + 1) * cut)
        act_y[h].wait_recv()
        act_diag = send(acts.at[span_of(2, h)], acts.at[span_of(3, h)], core_mate)
        ahead = feed(span_of(2, h))
        act_diag.wait_recv()
        out_diag[0, rows_h] = low(feed(span_of(3, h)))
        diag_sum = send(out_diag.at[0, rows_h], in_diag.at[0, rows_h], core_mate)
        diag_sum.wait_recv()
        out_y[0, rows_h] = low(ahead + in_diag[0, rows_h].astype(f32))
        y_sums.append(send(out_y.at[0, rows_h], in_y.at[0, rows_h], y_mate))
    out_diag[1] = low(forth(3))
    diag_sum = send(out_diag.at[1], in_diag.at[1], core_mate)
    out_core[1] = low(forth(1))
    core_sums.append(send(out_core.at[1], in_core.at[1], core_mate))
    ahead = forth(2)
    diag_sum.wait_recv()
    out_y[1] = low(ahead + in_diag[1].astype(f32))
    y_sums.append(send(out_y.at[1], in_y.at[1], y_mate))
    po0[...] = forth(0)
    core_sums[0].wait_recv()
    y_sums[0].wait_recv()
    y_sums[1].wait_recv()
    grad_act = pg0[...] + in_core[0].astype(f32) + in_y[0].astype(f32)
    unit_two = unit[...]
    gfeed_ref[...] = jnp.sum(grad_act * unit_two, 0, keepdims=True)
    w = grad_act * gain
    inv = 1.0 / width
    grad = cot_ref[...].astype(f32) + scales[:, 0:1] * (
        w - jnp.sum(w, -1, keepdims=True) * inv - unit_two * (jnp.sum(w * unit_two, -1, keepdims=True) * inv)
    )
    hid_ref[...] = grad
    branch[...] = low(grad)
    row_mates, group_mates = mates("row"), mates("group")
    block = lambda r: branch_row.at[rows_at((r * groups + group) * span, span)]
    by_row = [
        send(branch.at[rows_at(lax.rem(row + o, rows) * span, span)], block(row), row_mates[o - 1]) for o in range(1, rows)
    ]
    block(row)[...] = branch[rows_at(row * span, span)]
    moves = [send(block(row), block(row), mate) for mate in group_mates]
    feed_terms(((t0, t1), acts, gg), ((t2, t3), acts, gu), ((t4, t5), cots, ha))
    for o in range(1, rows):
        by_row[o - 1].wait_recv()
        from_row = block(lax.rem(row - o + rows, rows))
        moves += [send(from_row, from_row, mate) for mate in group_mates]
    core_sums[1].wait_recv()
    y_sums[2].wait_recv()
    block_ref[...] = low(h_in[...] + po0[...] + in_core[1].astype(f32) + in_y[1].astype(f32))
    for copy in moves:
        copy.wait_recv()
    gmix_ref[...] = dot_nt(branch_row[...], wout_ref[rows_at(group * cols, cols)])
    for h in range(2):
        half = branch_row[:, h * (width // 2) : (h + 1) * (width // 2)]
        gwo_ref[h * cols : (h + 1) * cols] = low(dot_tn(mixed_ref[...], half))
    for copy in copies.started:
        copy.wait_send()


def middle(mixed_row, tokens, cotangent, out_weight, gate_weight, up_weight, down_weight, gain, span, collective_id):
    rows, groups = lax.axis_size("row"), lax.axis_size("group")
    length, cols = mixed_row.shape[0] - MB, mixed_row.shape[1]
    count, width = tokens.shape
    hidden = gate_weight.shape[1]
    copies = (rows * groups - 1) + (rows - 1) + rows * (groups - 1) + 18
    vmem = pl.BlockSpec(memory_space=pltpu.VMEM)
    outs = [
        ((count, width), bf16), ((count, width), f32), ((length, cols), f32), ((2 * cols, width // 2), bf16),
        *[((2 * width, 128), bf16)] * 6, ((1, width), f32),
    ]
    two = pltpu.VMEM((2, count, width), bf16)
    return pl.pallas_call(
        partial(middle_kernel, span),
        in_specs=[vmem] + [ANYWHERE] * 6 + [vmem],
        out_specs=[vmem] * len(outs),
        out_shape=[jax.ShapeDtypeStruct(*o) for o in outs],
        scratch_shapes=[
            pltpu.VMEM((count, width), bf16),
            pltpu.VMEM((count, width), bf16),
            pltpu.VMEM(out_weight.shape, bf16),
            *[pltpu.VMEM((width, hidden), bf16)] * 3,
            pltpu.VMEM((4 * count, hidden), f32),
            pltpu.VMEM((length, cols), bf16),
            pltpu.VMEM((count, groups * cols), bf16),
            pltpu.VMEM((4 * count, width), bf16),
            pltpu.VMEM((4 * count, width), bf16),
            pltpu.VMEM((count, width), f32),
            pltpu.VMEM((count, 128), f32),
            pltpu.VMEM((count, width), f32),
            pltpu.VMEM((4 * count, hidden), bf16),
            pltpu.VMEM((4 * count, hidden), bf16),
            pltpu.VMEM((4 * count, hidden), bf16),
            pltpu.VMEM((count, width), f32),
            pltpu.VMEM((count, width), f32),
            two, two, two, two, two, two,
            pltpu.VMEM((count, width), bf16),
            pltpu.VMEM((length, width), bf16),
            pltpu.SemaphoreType.DMA((copies,)),
            pltpu.SemaphoreType.DMA((copies,)),
            pltpu.SemaphoreType.DMA((1,)),
            pltpu.SemaphoreType.DMA((6,)),
        ],
        compiler_params=pltpu.CompilerParams(
            collective_id=collective_id, has_side_effects=True, vmem_limit_bytes=63 * 1024 * 1024
        ),
        name="middle",
    )(mixed_row, tokens, cotangent, out_weight, gate_weight, up_weight, down_weight, gain)


def own_rows(array, mine):
    total = None
    for g in range(lax.axis_size("group")):
        part = array[g * mine : (g + 1) * mine].astype(f32)
        if part.shape[0]:
            part = jnp.concatenate([part, jnp.zeros((128 - part.shape[0], array.shape[1]), f32)], 0)
            part = jnp.where(lax.axis_index("group") == g, part, 0.0)
            total = part if total is None else total + part
    return total


def head_kernel(span, heads, mine, head_dim, tok_ref, gain_ref, wq_in, wk_in, wv_in, wr_ref, rb_ref,
                q_ref, k_ref, v_ref, act_ref, unit_ref, rate_ref, slope_ref, stat_ref, wown_ref, row_tok, wq_ref, wk_ref, wv_ref, send_sem, recv_sem, sems):
    rows, groups = lax.axis_size("row"), lax.axis_size("group")
    row, group, feat = lax.axis_index("row"), lax.axis_index("group"), lax.axis_index("feat")
    row_mates, group_mates = mates("row"), mates("group")
    width = tok_ref.shape[2]
    cols = q_ref.shape[1]
    copies = Copies(send_sem, recv_sem)
    block = lambda r: row_tok.at[rows_at((r * groups + group) * span, span)]

    lanes = pl.ds(pl.multiple_of(group * cols, 128), cols)
    loads = fetch(sems, *[(src.at[:, lanes], dst) for src, dst in ((wq_in, wq_ref), (wk_in, wk_ref), (wv_in, wv_ref))])
    greet(row_mates + group_mates)
    by_row = [
        copies.send(tok_ref.at[lax.rem(row + o, rows)], block(row), row_mates[o - 1]) for o in range(1, rows)
    ]
    block(row)[...] = tok_ref[row]
    by_group = {row_offset: [] for row_offset in range(rows)}
    by_group[0] = [copies.send(block(row), block(row), mate) for mate in group_mates]
    gain = gain_ref[...].reshape(1, width)
    for load in loads:
        load.wait()

    def work_on(place):
        here = rows_at(place * span, span)
        unit, _ = norm_parts(row_tok[here].astype(f32), width)
        unit_ref[here] = unit
        act = low(unit * gain)
        act_ref[here] = act
        for out, weight in ((q_ref, wq_ref), (k_ref, wk_ref), (v_ref, wv_ref)):
            out[here] = dot(act, weight[...])

    work_on(row * groups + group)
    for o in range(1, rows):
        r = lax.rem(row - o + rows, rows)
        by_row[o - 1].wait_recv()
        by_group[o] = [copies.send(block(r), block(r), mate) for mate in group_mates]
        if o > 1:
            work_on(lax.rem(row - o + 1 + rows, rows) * groups + group)
    work_on(lax.rem(row - rows + 1 + rows, rows) * groups + group)
    for o in range(rows):
        r = lax.rem(row - o + rows, rows)
        for copy in by_group[o]:
            copy.wait_recv()
        lax.fori_loop(1, groups, lambda g, _: work_on(r * groups + lax.rem(group + g, groups)), None)
    rate_weight = low(own_rows(wr_ref[...], mine))
    wown_ref[...] = rate_weight
    rate_bias = own_rows(jnp.broadcast_to(rb_ref[...].reshape(1, heads), (8, heads)).T, mine).T[0:1]
    logits = dot_nt(act_ref[...], rate_weight) + rate_bias
    sigma = jax.nn.sigmoid(logits)
    lane = lax.broadcasted_iota(jnp.int32, logits.shape, 1)
    used = (lane < mine) & (group * mine + lane < heads)
    rate_ref[...] = sigma * (1.0 / head_dim)
    slope_ref[...] = jnp.where(used, sigma * (1.0 - sigma) * (1.0 / head_dim), 0.0)
    stat_ref[0:1] = jnp.sum(logits, 0, keepdims=True)
    top = jnp.max(jnp.max(jnp.where(used, logits, -3e38), 0, keepdims=True), 1, keepdims=True)
    place = row * lax.axis_size("feat") + feat
    stat_ref[1:2] = jnp.where(lane[0:1] == place, top, 0.0)
    for copy in copies.started:
        copy.wait_send()


def head(tokens, gain, weights, rate_weight, rate_bias, heads, mine, head_dim, collective_id):
    rows, groups = lax.axis_size("row"), lax.axis_size("group")
    _, span, width = tokens.shape
    length, cols = rows * groups * span, mine * head_dim
    vmem = pl.BlockSpec(memory_space=pltpu.VMEM)
    copies = (rows - 1) + rows * (groups - 1)
    outs = [((length, cols), f32)] * 3 + [((length, width), bf16), ((length, width), f32)]
    outs += [((length, 128), f32)] * 2 + [((2, 128), f32), ((128, width), bf16)]
    return pl.pallas_call(
        partial(head_kernel, span, heads, mine, head_dim),
        in_specs=[vmem] * 2 + [ANYWHERE] * 3 + [vmem] * 2,
        out_specs=[vmem] * len(outs),
        out_shape=[jax.ShapeDtypeStruct(*o) for o in outs],
        scratch_shapes=[
            pltpu.VMEM((length, width), bf16),
            *[pltpu.VMEM((width, cols), bf16)] * 3,
            pltpu.SemaphoreType.DMA((copies,)),
            pltpu.SemaphoreType.DMA((copies,)),
            pltpu.SemaphoreType.DMA((3,)),
        ],
        compiler_params=pltpu.CompilerParams(
            collective_id=collective_id, has_side_effects=True, vmem_limit_bytes=63 * 1024 * 1024
        ),
        name="head",
    )(tokens, gain, *weights, rate_weight, rate_bias)


TAIL_SLOTS = [
    ([], ["FZ1", "CORE3", "FZ2", "FZ0", "PART0"]),
    (["CORE3"], ["Y3", "CORE0", "CORE2"]),
    (["FZ1"], ["FX1", "FZ3", "CORE4"]),
    (["CORE0"], ["Y0", "CORE1"]),
    (["CORE2"], ["Y2"]),
    (["CORE4", "Y3"], ["Y4"]),
    (["CORE1", "FZ2"], ["Z3", "FX2"]),
    (["Y0"], ["Y1"]),
    (["FZ0"], ["Z0"]),
    (["PART0"], ["SC0", "FX0"]),
    (["Y2", "SC0"], ["SY0"]),
    (["Y4", "FZ3"], ["Z2"]),
    (["FX1"], ["FX3"]),
    (["Z3"], ["ZA3"]),
    (["Y1", "SY0", "FX2", "Z0"], ["ZA0"]),
    (["FX0", "Z2"], ["Z4"]),
    (["ZA3"], ["Z1", "PY3", "PX3"]),
    (["FX3", "ZA0"], ["PY0", "PX0", "ZA2"]),
    (["Z4"], ["ZA4"]),
    (["PY3"], ["QX3"]),
    (["PX3"], ["QY3"]),
    (["Z1"], ["ZA1"]),
    (["PY0"], ["QX0"]),
    (["PX0"], ["QY0"]),
    (["QY3", "QX3"], ["C3"]),
    (["ZA2"], ["PY2", "PX2", "SZ0"]),
    (["C3", "QX0", "QY0"], ["C0"]),
    (["ZA4"], ["PX4", "PY4", "HOME0"]),
    (["C0", "ZA1"], ["PX1", "PY1"]),
    (["PY2", "PX2"], ["QX2", "QY2"]),
    (["PY4", "PX4"], ["QX4", "QY4"]),
    (["SZ0", "PY1", "PX1"], ["QY1", "QX1"]),
    (["QY2", "QX2"], ["SX0", "C2"]),
    (["QY4", "QX4"], ["C4"]),
    (["C2", "QY1", "QX1"], ["C1"]),
    (["C4", "SX0", "HOME0", "C1"], []),
]


FEED_SLOTS = [
    (0, [], ["X1", "X0"]),
    (6, ["X1"], ["Z1", "X3"]),
    (9, ["X0"], ["Z0", "X2"]),
    (12, ["Z1"], ["ZA1"]),
    (12, ["X3"], ["X4"]),
    (15, ["Z0"], ["ZA0"]),
    (15, ["X2"], ["X5"]),
    (17, ["ZA1"], ["Z3"]),
    (18, ["X4"], ["XA1"]),
    (20, ["ZA0"], ["Z4"]),
    (21, ["X5"], ["XA0"]),
    (23, ["Z3"], ["Z2"]),
    (24, ["XA1"], []),
    (26, ["Z4"], ["Z5"]),
    (27, ["XA0"], []),
    (29, ["Z2"], []),
    (32, ["Z5"], []),
]
FEED_WHOLE = 2


def tail_kernel(span, shapes, feeds, act_ref, unit_in, gq_ref, gk_ref, gv_ref, de_in, slope_in, wq_in, wk_in, wv_in, wr_ref,
                gwo_ref, gw1, gb1, gw2, gb2, ggain, gbias, gfeed, stat_ref, *refs):
    rows, groups = lax.axis_size("row"), lax.axis_size("group")
    row, group, feat = lax.axis_index("row"), lax.axis_index("group"), lax.axis_index("feat")
    core, y = lax.rem(feat, 2), feat // 2
    core_mate, y_mate = {"feat": feat + 1 - 2 * core}, {"feat": feat + 2 - 4 * y}
    row_mates, group_mates = mates("row"), mates("group")
    count = len(shapes)
    feed_in, refs = refs[:feeds], refs[feeds:]
    outs, (home_out, small_out), refs = refs[:count], refs[count : count + 2], refs[count + 2 :]
    feed_out, refs = refs[:feeds], refs[feeds:]
    own, got_core, sum_core, got_y, sum_y, got_row = (refs[i * count : (i + 1) * count] for i in range(6))
    part, part_got, part_sum, small, small_core, small_got, unit_ref, de_ref, slope_ref, wq_ref, wk_ref, wv_ref, send_sem, recv_sem, sems = refs[6 * count :]
    length, width = act_ref.shape
    cols = gwo_ref.shape[0] // 2
    pairs, pair, inner = gw1.shape
    head_dim = pair // 2
    copies = Copies(send_sem, recv_sem)
    moves = {}

    def start(name, *what):
        moves[name] = [copies.send(*w) for w in what]

    lanes = pl.ds(pl.multiple_of(group * cols, 128), cols)
    loads = fetch(
        sems, (de_in, de_ref), (slope_in, slope_ref),
        *[(src.at[:, lanes], dst) for src, dst in ((wq_in, wq_ref), (wk_in, wk_ref), (wv_in, wv_ref))], (unit_in, unit_ref),
    )
    greet([core_mate, y_mate] + row_mates + group_mates)

    half = [h // 2 for h, _ in shapes]
    quarter = [h // 4 for h, _ in shapes]
    piece = [h // (4 * rows) for h, _ in shapes]
    unit = feed_in[0].shape[0]
    place = (core * 2 + y) * rows + row
    source = list(own[:3]) + [gwo_ref, own[4]]
    grad_refs = (gq_ref, gk_ref, gv_ref)

    def token_gradient():
        for load in loads:
            load.wait()
        logits = low(de_ref[0:length] * slope_ref[...])
        total = dot(logits, wr_ref[...])
        for grad, weight in zip(grad_refs, (wq_ref, wk_ref, wv_ref)):
            total = total + dot_nt(grad[0:length], weight[...])
        for r in range(rows):
            for g in range(groups):
                part[g, r * span : (r + 1) * span] = low(total[(r * groups + g) * span : (r * groups + g + 1) * span])
        start("PART0", *[(part.at[lax.rem(group + o, groups)], part_got.at[o - 1], group_mates[o - 1]) for o in range(1, groups)])
        small[...] = jnp.zeros_like(small)
        small[0 : 2 * pairs] = dot_tn(logits, act_ref[...])[0 : 2 * pairs]
        for p in range(pairs):
            for h in range(2):
                n = 2 * p + h
                small[6 + n // 3 : 7 + n // 3, (n % 3) * inner : (n % 3 + 1) * inner] = gb1[p, h * MB : h * MB + 1]
            small[9:10, p * pair : (p + 1) * pair] = gb2[p, 0:1] + gb2[p, MB : MB + 1]
        small[8:9, 0:cols] = jnp.sum(ggain[...], 0, keepdims=True)
        small[8:9, cols : 2 * cols] = jnp.sum(gbias[...], 0, keepdims=True)
        small[9:10, width - 384 : width - 256] = jnp.sum(logits.astype(f32), 0, keepdims=True)
        small[9:10, width - 256 : width - 128] = stat_ref[0:1]
        small[9:10, width - 128 : width] = stat_ref[1:2]
        small[10:11] = jnp.sum(total * unit_ref[...], 0, keepdims=True)
        small[11:12] = gfeed[...]

    def finish(name):
        for copy in moves[name]:
            copy.wait_recv()
        kind, i = name[:-1], int(name[-1])
        if kind == "CORE":
            sum_core[i][...] = add_low(source[i][rows_at(core * half[i], half[i])], got_core[i][...])
        if kind == "Y":
            sum_y[i][...] = add_low(sum_core[i][rows_at(y * quarter[i], quarter[i])], got_y[i][...])
        if kind == "Z":
            value = sum_y[i][rows_at(row * piece[i], piece[i])].astype(f32)
            for o in range(1, rows):
                value = value + got_row[i][o - 1].astype(f32)
            outs[i][group, rows_at(place * piece[i], piece[i])] = low(value)
        if kind == "PART":
            value = part[group].astype(f32)
            for o in range(1, groups):
                value = value + part_got[o - 1].astype(f32)
            part_sum[...] = low(value)
            home_out[rows_at(row * span, span)] = part_sum[rows_at(row * span, span)]
        if kind == "SC":
            small_core[...] = small[...] + small_got[0]
        if kind == "SY":
            small_got[2 + row] = small_core[...] + small_got[1]
        if kind == "SZ":
            value = small_got[2]
            for r in range(1, rows):
                value = value + small_got[2 + r]
            small_out[group] = value

    def begin(name):
        kind, i = name[:-1], int(name[-1])
        if kind == "PART":
            token_gradient()
        if kind == "HOME":
            here = home_out.at[rows_at(row * span, span)]
            start(name, *[
                (part_sum.at[rows_at(lax.rem(row + o, rows) * span, span)], here, row_mates[o - 1]) for o in range(1, rows)
            ])
        if kind == "SC":
            start(name, (small, small_got.at[0], core_mate))
        if kind == "SY":
            start(name, (small_core, small_got.at[1], y_mate))
        if kind == "SZ":
            here = small_got.at[2 + row]
            start(name, *[(here, here, mate) for mate in row_mates])
        if kind == "SX":
            here = small_out.at[group]
            start(name, *[(here, here, mate) for mate in group_mates])
        if kind == "FZ":
            here = feed_out[i].at[group, rows_at(row * unit, unit)]
            here[...] = feed_in[i][...]
            start(name, *[(here, here, mate) for mate in row_mates])
        if kind == "FX":
            here = feed_out[i].at[group]
            start(name, *[(here, here, mate) for mate in group_mates])
        if kind == "CORE":
            if i < 3:
                own[i][...] = low(dot_tn(act_ref[...], grad_refs[i][0:length]))
            if i == 4:
                for p in range(pairs):
                    own[4][p * pair : (p + 1) * pair] = low(gw1[p])
                    own[4][cols + p * pair : cols + (p + 1) * pair] = low(gw2[p])
            start(name, (source[i].at[rows_at((1 - core) * half[i], half[i])], got_core[i], core_mate))
        if kind == "Y":
            start(name, (sum_core[i].at[rows_at((1 - y) * quarter[i], quarter[i])], got_y[i], y_mate))
        if kind == "Z":
            start(name, *[
                (sum_y[i].at[rows_at(lax.rem(row + o, rows) * piece[i], piece[i])], got_row[i].at[o - 1], row_mates[o - 1])
                for o in range(1, rows)
            ])
        if kind == "ZA":
            here = outs[i].at[group, rows_at(place * piece[i], piece[i])]
            start(name, *[(here, here, mate) for mate in row_mates])
        step = quarter[i] // 2
        quarter_of = lambda at_y, first, size: rows_at((core * 2 + at_y) * quarter[i] + first, size)
        if kind in ("PX", "PY"):
            here = outs[i].at[group, quarter_of(y, 0, quarter[i])]
            start(name, *[(here, here, mate) for mate in (group_mates if kind == "PX" else [y_mate])])
        if kind == "QX":
            here = outs[i].at[group, quarter_of(1 - y, step, step)]
            start(name, *[(here, here, mate) for mate in group_mates])
        if kind == "QY":
            others = [outs[i].at[lax.rem(group + o, groups), quarter_of(y, 0, step)] for o in range(1, groups)]
            start(name, *[(here, here, y_mate) for here in others])
        if kind == "C":
            here = outs[i].at[:, rows_at(core * half[i], half[i])]
            start(name, (here, here, core_mate))

    for done, begun in TAIL_SLOTS:
        for name in done:
            finish(name)
        for name in begun:
            begin(name)
    for copy in copies.started:
        copy.wait_send()


def tail(act_row, unit_row, grads, de, slope, weights, rate_weight, grad_out, states, grad_feed_gain, stat, feed_parts, span, collective_id):
    rows, groups = lax.axis_size("row"), lax.axis_size("group")
    length, width = act_row.shape
    cols = grad_out.shape[0] // 2
    inner = states[0].shape[-1]
    shapes = [(width, cols)] * 3 + [(2 * cols, width // 2), (2 * cols, inner)]
    count, feeds = len(shapes), len(feed_parts)
    unit, wide = feed_parts[0].shape
    copies = count * (2 + 2 * (rows - 1) + 3 * (groups - 1) + 2) + (groups - 1) + (rows - 1) + 2 + (rows - 1) + (groups - 1)
    copies += feeds * (rows + groups - 2)
    vmem = pl.BlockSpec(memory_space=pltpu.VMEM)
    operands = [act_row, unit_row, *grads, de, slope, *weights, rate_weight, grad_out, *states, grad_feed_gain, stat, *feed_parts]
    outs = [((groups, h, w), bf16) for h, w in shapes]
    outs += [((rows * span, width), bf16), ((groups, 16, width), f32)]
    outs += [((groups, rows * unit, wide), bf16)] * feeds
    scratch = [pltpu.VMEM((h, w), bf16) for h, w in shapes]
    scratch += [pltpu.VMEM((h // 2, w), bf16) for h, w in shapes] * 2
    scratch += [pltpu.VMEM((h // 4, w), bf16) for h, w in shapes] * 2
    scratch += [pltpu.VMEM((rows - 1, h // (4 * rows), w), bf16) for h, w in shapes]
    scratch += [
        pltpu.VMEM((groups, rows * span, width), bf16),
        pltpu.VMEM((groups - 1, rows * span, width), bf16),
        pltpu.VMEM((rows * span, width), bf16),
        pltpu.VMEM((16, width), f32),
        pltpu.VMEM((16, width), f32),
        pltpu.VMEM((2 + rows, 16, width), f32),
        *[pltpu.VMEM(a.shape, f32) for a in (unit_row, de, slope)],
        *[pltpu.VMEM((width, cols), bf16)] * 3,
        pltpu.SemaphoreType.DMA((copies,)),
        pltpu.SemaphoreType.DMA((copies,)),
        pltpu.SemaphoreType.DMA((6,)),
    ]
    return pl.pallas_call(
        partial(tail_kernel, span, shapes, feeds),
        in_specs=[ANYWHERE if i in (1, 5, 6, 7, 8, 9) else vmem for i in range(len(operands))],
        out_specs=[vmem] * len(outs),
        out_shape=[jax.ShapeDtypeStruct(*o) for o in outs],
        scratch_shapes=scratch,
        compiler_params=pltpu.CompilerParams(
            collective_id=collective_id, has_side_effects=True, vmem_limit_bytes=63 * 1024 * 1024
        ),
        name="tail",
    )(*operands)


def finish_kernel(heads, mine, head_dim, inner, total_logits, small_ref, gain_ref, *refs):
    large_in, refs = refs[:14], refs[14:]
    (rate_ref, rbias_ref, fbias_ref, sbias_ref, gain_out, bias_out, mixer_ref, feed_ref, stat_ref,
     q_out, k_out, v_out, o_out, first_out, second_out, gate_out, up_out, down_out, in_out,
     sq, sk, sv, so, s1, s2, sg, su, sd, si, sems, *large, load_sems) = refs
    f0, f1, f2, f3, f4, f5, q_in, k_in, v_in, o_in, s_in, got_ref, tok_ref, hid_ref = large
    groups, width = q_in.shape[0], q_in.shape[1]
    loads = fetch(load_sems, *zip(large_in, large))
    cols = mine * head_dim
    sent, arrived = [], iter(loads)

    def give(value_ref, out):
        copy = pltpu.make_async_copy(value_ref, out, sems.at[len(sent)])
        copy.start()
        sent.append(copy)

    for out, scratch, left, right in ((gate_out, sg, f0, f1), (up_out, su, f2, f3), (down_out, sd, f4, f5)):
        for i, cut in enumerate((left, right)):
            next(arrived).wait()
            value = cut[...].reshape(2 * width, 128)
            for h in range(2):
                scratch[:, (2 * i + h) * 128 : (2 * i + h + 1) * 128] = value[h * width : (h + 1) * width].astype(f32)
        give(scratch, out)
    for out, scratch, array in ((q_out, sq, q_in), (k_out, sk, k_in), (v_out, sv, v_in)):
        next(arrived).wait()
        for g in range(groups):
            size = min(cols, width - g * cols)
            if size > 0:
                scratch[:, g * cols : g * cols + size] = array[g, :, 0:size].astype(f32)
        give(scratch, out)
    next(arrived).wait()
    for g in range(groups):
        size = min(cols, width - g * cols)
        if size > 0:
            for h in range(2):
                scratch = so.at[g * cols : g * cols + size, h * (width // 2) : (h + 1) * (width // 2)]
                scratch[...] = o_in[g, h * cols : h * cols + size].astype(f32)
    give(so, o_out)
    next(arrived).wait()
    for n in range(heads):
        g, i = n // mine, n % mine
        s1[n] = s_in[g, i * head_dim : (i + 1) * head_dim].astype(f32)
        second = s_in[g, cols + i * head_dim : cols + (i + 1) * head_dim].astype(f32)
        s2[n] = second - jnp.sum(second, 0, keepdims=True) * (1.0 / head_dim)
    give(s1, first_out)
    give(s2, second_out)
    for load in arrived:
        load.wait()
    unit, scale = norm_parts(tok_ref[...].astype(f32), width)
    w = got_ref[...].astype(f32) * gain_ref[...].reshape(1, width)
    inv = 1.0 / width
    si[...] = hid_ref[...] + scale * (
        w - jnp.sum(w, -1, keepdims=True) * inv - unit * (jnp.sum(w * unit, -1, keepdims=True) * inv)
    )
    give(si, in_out)
    total = 0.0
    for n in range(heads):
        g, i = n // mine, n % mine
        rate_ref[n : n + 1] = small_ref[g, i : i + 1]
        rbias_ref[:, n : n + 1] = small_ref[g, 9:10, width - 384 + i : width - 383 + i]
        total = total + small_ref[g, 9:10, width - 256 + i : width - 255 + i]
        fbias_ref[n : n + 1] = small_ref[g, 6 + i // 3 : 7 + i // 3, (i % 3) * inner : (i % 3 + 1) * inner]
        own = slice(i * head_dim, (i + 1) * head_dim)
        second = small_ref[g, 9:10, own]
        sbias_ref[n : n + 1] = second - jnp.sum(second, -1, keepdims=True) * (1.0 / head_dim)
        gain_out[n : n + 1] = small_ref[g, 8:9, own]
        bias_out[n : n + 1] = small_ref[g, 8:9, cols + i * head_dim : cols + (i + 1) * head_dim]
    mixer, feed = small_ref[0, 10:11], small_ref[0, 11:12]
    tops = small_ref[0, 9:10, width - 128 : width]
    peers = lax.axis_size("row") * lax.axis_size("feat")
    for g in range(1, groups):
        mixer, feed = mixer + small_ref[g, 10:11], feed + small_ref[g, 11:12]
        tops = jnp.maximum(tops, small_ref[g, 9:10, width - 128 : width])
    mixer_ref[...], feed_ref[...] = mixer.reshape(width), feed.reshape(width)
    lane = lax.broadcasted_iota(jnp.int32, tops.shape, 1)
    top = jnp.max(jnp.where(lane < peers, tops, -3e38), 1, keepdims=True)
    stat_ref[...] = jnp.where(lane == 0, total * (1.0 / total_logits), top)[:, 0:2].reshape(2)
    for copy in sent:
        copy.wait()


def finish(arrays, got, small, tokens, grad_hidden, gain, feed_sums, heads, mine, head_dim, inner, total_logits):
    count, width = tokens.shape
    hidden = 2 * 2 * 128
    vmem = pl.BlockSpec(memory_space=pltpu.VMEM)
    little = [(heads, width), (1, heads), (heads, inner), (heads, head_dim), (heads, head_dim), (heads, head_dim)]
    little += [(width,), (width,), (2,)]
    large = [(width, width)] * 4 + [(heads, head_dim, inner)] * 2 + [(width, hidden)] * 3 + [(count, width)]
    large_in = [*feed_sums, *arrays, got, tokens, grad_hidden]
    return pl.pallas_call(
        partial(finish_kernel, heads, mine, head_dim, inner, total_logits),
        in_specs=[vmem] * 2 + [ANYWHERE] * len(large_in),
        out_specs=[vmem] * len(little) + [ANYWHERE] * len(large),
        out_shape=[jax.ShapeDtypeStruct(s, f32) for s in little + large],
        scratch_shapes=[
            *[pltpu.VMEM(s, f32) for s in large],
            pltpu.SemaphoreType.DMA((len(large),)),
            *[pltpu.VMEM(a.shape, a.dtype) for a in large_in],
            pltpu.SemaphoreType.DMA((len(large_in),)),
        ],
        compiler_params=pltpu.CompilerParams(vmem_limit_bytes=63 * 1024 * 1024),
        name="finish",
    )(small, gain, *large_in)


SEQ = ("row", "group")


def per_device(
    tokens,
    cotangent,
    doc_starts,
    mixer_gain,
    query_weight,
    key_weight,
    value_weight,
    out_weight,
    rate_weight,
    rate_bias,
    first_init,
    first_bias_init,
    second_init,
    second_bias_init,
    inner_gain,
    inner_bias,
    feed_gain,
    gate_weight,
    up_weight,
    down_weight,
):
    rows, span, width = tokens.shape
    heads, head_dim, inner = first_init.shape
    groups = lax.axis_size("group")
    feats = lax.axis_size("feat")
    row, group = lax.axis_index("row"), lax.axis_index("group")
    count = rows * span
    blocks = span * rows * groups // MB
    pairs = -(-heads // (2 * groups))
    mine = 2 * pairs
    pair = 2 * head_dim
    spare = mine * groups - heads

    def padded(array, axis, size):
        edges = [(0, 0)] * array.ndim
        edges[axis] = (0, spare * size)
        return jnp.pad(array, edges) if spare else array

    weights = [padded(w, 1, head_dim) for w in (query_weight, key_weight, value_weight)]
    flat_tokens = tokens.reshape(count, width)
    queries, keys, values, act_row, unit_row, rates, slope, stat, rate_lanes = head(
        tokens, mixer_gain, weights, rate_weight.T, rate_bias, heads, mine, head_dim, 4
    )
    block_ids = jnp.arange(blocks + 1, dtype=jnp.int32)
    starts = lax.dynamic_index_in_dim(doc_starts, row, 0, False)
    restarts = ((block_ids == 0) | jnp.any(starts[:, None] == block_ids[None], 0)).astype(jnp.int32)
    by_pair = lambda a: a.reshape(heads // 2, pair, inner)
    *saved, mixed = forward_inner(
        restarts, queries, keys, values, rates, by_pair(first_init), first_bias_init, by_pair(second_init),
        second_bias_init, inner_gain, inner_bias,
    )

    block_out, grad_hidden, grad_mixed, grad_out_rows, *feed_terms, grad_feed_gain = middle(
        mixed, flat_tokens, cotangent.reshape(count, width), padded(out_weight, 0, head_dim),
        gate_weight, up_weight, down_weight, feed_gain, span, 1,
    )

    grad_q, grad_k, grad_v, grad_e, g_first, g_first_bias, g_second, g_second_bias, g_gain, g_bias, *feed_sums = (
        backward_inner(restarts, queries, keys, values, grad_mixed, rates, saved, inner_gain, inner_bias, feed_terms, 2)
    )
    reduced = tail(
        act_row, unit_row, (grad_q, grad_k, grad_v), grad_e, slope, weights, rate_lanes, grad_out_rows,
        (g_first, g_first_bias, g_second, g_second_bias, g_gain, g_bias), grad_feed_gain, stat,
        feed_sums[FEED_WHOLE:], span, 3,
    )
    arrays, (got, small), feed_sums = reduced[:5], reduced[5:7], [*feed_sums[:FEED_WHOLE], *reduced[7:]]
    (
        g_rate, g_rate_bias, g_first_bias, g_second_bias, g_gain, g_bias, g_mixer, g_feed, stats,
        g_query, g_key, g_value, g_out, g_first, g_second, g_gate, g_up, g_down, input_grad,
    ) = finish(
        arrays, got, small, flat_tokens, grad_hidden, mixer_gain, feed_sums, heads, mine, head_dim, inner,
        rows * groups * feats * count * heads,
    )
    return (
        block_out.reshape(rows, span, width),
        input_grad.reshape(rows, span, width),
        g_mixer,
        g_query,
        g_key,
        g_value,
        g_out,
        g_rate.T,
        g_rate_bias[0],
        g_first,
        g_first_bias,
        g_second,
        g_second_bias,
        g_gain,
        g_bias,
        g_feed,
        g_gate,
        g_up,
        g_down,
        stats,
    )


def solution(mesh):
    feats = mesh.shape["feat"]

    def run(*arrays):
        rows = arrays[0].shape[0] // feats
        grid = jax.sharding.Mesh(mesh.devices.reshape(rows, -1, feats), ("row", "group", "feat"))
        by_token = P("feat", SEQ, None)
        by_hidden = P(None, "feat")
        return jax.shard_map(
            per_device,
            mesh=grid,
            in_specs=(by_token, by_token, P("feat", None)) + (P(),) * 14 + (by_hidden,) * 3,
            out_specs=(by_token, by_token) + (P(),) * 14 + (by_hidden,) * 3 + (P(),),
            check_vma=False,
        )(*arrays)

    return run
```

```python
from functools import partial

import jax
import jax.numpy as jnp
from jax import lax
from jax.experimental import pallas as pl
from jax.experimental.pallas import tpu as pltpu
from jax.sharding import PartitionSpec as P

MB = 16
epsilon = 1e-05
f32, bf16 = jnp.float32, jnp.bfloat16


def dot(a, b):
    return lax.dot_general(a, b, (((1,), (0,)), ((), ())), preferred_element_type=f32)


def dot_nt(a, b):
    return lax.dot_general(a, b, (((1,), (1,)), ((), ())), preferred_element_type=f32)


def dot_tn(a, b):
    return lax.dot_general(a, b, (((0,), (0,)), ((), ())), preferred_element_type=f32)


def low(v):
    return v.astype(bf16)


def gelu_parts(z):
    a = jnp.abs(z)
    d = 1.0 + 0.23164189 * a
    t = pl.reciprocal(d, approx=True)
    t = t * (2.0 - d * t)
    ex = jnp.exp(-0.5 * (z * z))
    poly = t * (
        0.127414796 + t * (-0.142248368 + t * (0.7107068705 + t * (-0.7265760135 + t * 0.5307027145)))
    )
    h = poly * ex
    cdf = jnp.where(z >= 0, 1.0 - h, h)
    pdf = 0.3989422804014327 * ex
    return z * cdf, cdf + z * pdf, pdf


def lane_sum(v):
    return jnp.sum(v, -1, keepdims=True)


def masks(head_dim):
    pair = 2 * head_dim
    rows, cols = 2 * MB, pair
    r = lax.broadcasted_iota(jnp.int32, (rows, cols), 0)
    c = lax.broadcasted_iota(jnp.int32, (rows, cols), 1)
    own = ((r < MB) == (c < head_dim)).astype(f32)
    r = lax.broadcasted_iota(jnp.int32, (rows, rows), 0)
    c = lax.broadcasted_iota(jnp.int32, (rows, rows), 1)
    same = (r < MB) == (c < MB)
    causal = (same & (c <= r)).astype(f32)
    return own, causal, same.astype(bf16)


def spread(v, own):
    return jnp.concatenate([v, v], 0) * own


def fold(v):
    return v[:MB] + v[MB:]


def twice(v):
    return jnp.concatenate([v, v], 1)


def pair_index(p, pairs, array):
    return jnp.minimum(lax.axis_index("group") * pairs + p, array.shape[0] - 1)


def load_params(par_ref, sources, places):
    for i, source in enumerate(sources):
        for p, n in enumerate(places):
            par_ref[i, p] = jnp.concatenate([source[pl.ds(2 * n + h, 1)] for h in range(2)], 1)


def rate_rows(rates, p):
    return jnp.concatenate([jnp.broadcast_to(rates[:, n : n + 1], rates.shape) for n in (2 * p, 2 * p + 1)], 0)


def fetch(sems, *moves):
    copies = [pltpu.make_async_copy(src, dst, sems.at[i]) for i, (src, dst) in enumerate(moves)]
    for copy in copies:
        copy.start()
    return copies


ANYWHERE = pl.BlockSpec(memory_space=pl.ANY)


def in_turn(parts):
    while parts:
        parts = [part for part in parts if next(part, parts) is not parts]


def forward_kernel(pairs, head_dim, restart_ref, q_in, k_in, v_in, rate_in, w1i_ref, b1i_ref, w2i_ref, b2i_ref, gain_in, bias_in,
                   *refs):
    saved, out_all, refs = refs[:7], refs[7], refs[8:]
    rings, refs, sems = refs[:7], refs[7:-1], refs[-1]
    (q_all, k_all, v_all, rate_all, first_sems, rest_sems), refs = refs[:6], refs[6:]
    last = q_in.shape[0] // MB - 1
    arrays = list(zip((q_in, k_in, v_in, rate_in), (q_all, k_all, v_all, rate_all)))
    lead, length = 4 * MB, q_in.shape[0]
    first, rest = (
        fetch(fetch_sems, *[(src.at[pl.ds(at, size)], dst.at[pl.ds(at, size)]) for src, dst in arrays])
        for fetch_sems, at, size in ((first_sems, 0, lead), (rest_sems, lead, length - lead))
    )
    for copy in first:
        copy.wait()
    slots = rings[0].shape[0]

    def leave(j, i):
        return pltpu.make_async_copy(
            rings[i].at[pl.ds(lax.rem(j, slots), 1)], saved[i].at[pl.ds(j, 1)], sems.at[i, lax.rem(j, slots)]
        )

    def step(j, _):
        @pl.when(j >= slots)
        def _():
            for i in range(7):
                leave(j - slots, i).wait()

        @pl.when(j == 3)
        def _():
            for copy in rest:
                copy.wait()

        tokens = rows_at(jnp.minimum(j, last) * MB, MB)
        forward_step(
            pairs, head_dim, j, restart_ref, *[ref.at[tokens] for ref in (q_all, k_all, v_all, rate_all)],
            w1i_ref, b1i_ref, w2i_ref, b2i_ref, gain_in, bias_in,
            *[ring.at[pl.ds(lax.rem(j, slots), 1)] for ring in rings], out_all.at[rows_at(j * MB, MB)], *refs,
        )
        for i in range(7):
            leave(j, i).start()

    lax.fori_loop(0, last + 2, step, None)
    for o in range(slots):
        for i in range(7):
            leave(last + 2 - slots + o, i).wait()


def forward_step(pairs, head_dim, j, restart_ref, q_ref, k_ref, v_ref, rate_ref, w1i_ref, b1i_ref, w2i_ref, b2i_ref, gain_in, bias_in,
                 big_ref, mid_ref, small_ref, n1_ref, pq_ref, uq_ref, n2_ref, out_ref,
                 w1, b1, w2, b2, s_q1, s_x2, s_e2, s_w2, s_b2, s_q, par_ref):
    pair = 2 * head_dim
    inv = 1.0 / head_dim
    own, causal, ones = masks(head_dim)

    @pl.when(j == 0)
    def _():
        load_params(par_ref, (b2i_ref, gain_in, bias_in), [pair_index(p, pairs, w1i_ref) for p in range(pairs)])

    @pl.when(restart_ref[j] > 0)
    def _():
        for p in range(pairs):
            n = pair_index(p, pairs, w1i_ref)
            second = w2i_ref[n]
            second_bias = par_ref[0, p] * own
            w1[p] = w1i_ref[n]
            for h in range(2):
                b1[p, h * MB : (h + 1) * MB] = jnp.broadcast_to(b1i_ref[pl.ds(2 * n + h, 1)], (MB, b1i_ref.shape[1]))
                half = second[h * head_dim : (h + 1) * head_dim]
                w2[p, h * head_dim : (h + 1) * head_dim] = half - jnp.sum(half, 0, keepdims=True) * inv
            b2[p] = second_bias - (lane_sum(second_bias) * inv) * own

    loaded = [
        (s_q1[p], s_x2[p], s_e2[p], s_w2[p], s_b2[p], s_q[p], w1[p], w2[p], b1[p], b2[p], rate_rows(rate_ref[...], p))
        for p in range(pairs)
    ]
    tokens = [
        [ref[:, p * pair : (p + 1) * pair] for ref in (q_ref, k_ref, v_ref)]
        + [par_ref[i, p] for i in (1, 2)]
        for p in range(pairs)
    ]
    writes = []

    def write(ref, index, value):
        writes.append((ref, index, value))

    def outputs_before(p):
        q1p, x2p, e2p, w2p, b2p, qp = loaded[p][:6]
        gain, bias = tokens[p][3:]
        p2, lq, _ = gelu_parts(q1p)
        p2b = low(p2)
        yield
        n2 = causal * (dot_nt(p2b, x2p) + 1.0)
        q2 = dot_nt(p2b, w2p)
        yield
        q2 = q2 * own - dot(low(n2), e2p) + b2p
        yield
        sq = lax.rsqrt(lane_sum(q2 * q2) * inv + epsilon)
        uq = q2 * sq
        write(out_ref, (slice(None), slice(p * pair, (p + 1) * pair)), qp + fold(uq) * gain + bias)
        write(pq_ref, (0, p, slice(0, 2 * MB)), p2b)
        write(pq_ref, (0, p, slice(2 * MB, 4 * MB)), low(lq))
        write(uq_ref, (0, p, slice(0, 2 * MB)), uq)
        write(uq_ref, (0, p, slice(2 * MB, 4 * MB)), jnp.broadcast_to(sq, uq.shape))
        write(n2_ref, (0, p), low(n2))

    def inner_step(p):
        w1c, w2c, b1c, b2c, e = loaded[p][6:]
        qc, kc, vc, gain, bias = tokens[p]
        kb, qb = low(spread(kc, own)), low(spread(qc, own))
        w1b, w2b = low(w1c), low(w2c)
        kq = dot(jnp.concatenate([kb, qb], 0), w1b)
        n1 = low(causal * (dot_nt(qb, kb) + 1.0))
        yield
        z1 = kq[: 2 * MB] + b1c
        x2, l1, pdf = gelu_parts(z1)
        x2b = low(x2)
        yield
        c = dot_nt(x2b, w2b)
        yield
        c = c * own + b2c
        s = lax.rsqrt(lane_sum(c * c) * inv + epsilon)
        u = c * s
        r = u * (gain * gain) + spread((bias - (vc - kc)) * gain, own)
        mr, m2 = lane_sum(r) * inv, lane_sum(r * u) * inv
        g2 = s * (r - mr * own - u * m2)
        e2 = e * g2
        e2b = low(e2)
        yield
        h = dot(low(g2), w2b)
        u2 = dot_tn(e2b, x2b)
        yield
        g1 = h * l1
        e1b = low(twice(e) * g1)
        yield
        u1 = dot_tn(kb, e1b)
        below = dot(jnp.concatenate([n1, ones], 0), e1b)
        yield
        q1 = kq[2 * MB :] + b1c - below[: 2 * MB]
        write(w1, p, w1c - u1)
        write(b1, p, b1c - below[2 * MB :])
        write(w2, p, w2c - u2)
        write(b2, p, b2c - jnp.sum(e2, 0, keepdims=True) * own)
        write(big_ref, (0, p, slice(0, pair)), w1b)
        write(big_ref, (0, p, slice(pair, 2 * pair)), w2b)
        write(big_ref, (0, p, slice(2 * pair, 2 * pair + 2 * MB)), x2b)
        write(big_ref, (0, p, slice(2 * pair + 2 * MB, 2 * pair + 4 * MB)), e1b)
        write(mid_ref, (0, p, slice(0, 2 * MB)), low(g1))
        write(mid_ref, (0, p, slice(2 * MB, 4 * MB)), low(l1))
        write(mid_ref, (0, p, slice(4 * MB, 6 * MB)), low(h * pdf * (2.0 - z1 * z1)))
        for i, value in enumerate((u, s, r, m2, g2)):
            write(small_ref, (0, p, slice(i * 2 * MB, (i + 1) * 2 * MB)), jnp.broadcast_to(value, u.shape))
        write(n1_ref, (0, p), n1)
        for ref, value in ((s_q1, q1), (s_x2, x2b), (s_e2, e2b), (s_w2, w2b), (s_b2, b2c), (s_q, qc)):
            write(ref, p, value)

    in_turn([inner_step(p) for p in range(pairs)] + [outputs_before(p) for p in range(pairs)])
    for ref, index, value in writes:
        ref[index] = value


def forward_inner(restarts, q, k, v, rates, w1i, b1i, w2i, b2i, gain, bias):
    _, pair, inner = w1i.shape
    blocks, pairs = q.shape[0] // MB, q.shape[1] // pair
    head_dim = pair // 2
    steps = blocks + 1
    slots = min(8, steps)
    vmem = pl.BlockSpec(memory_space=pltpu.VMEM)
    kinds = [
        (2 * pair + 4 * MB, inner, bf16),
        (6 * MB, inner, bf16),
        (10 * MB, pair, f32),
        (2 * MB, 2 * MB, bf16),
        (4 * MB, inner, bf16),
        (4 * MB, pair, f32),
        (2 * MB, 2 * MB, bf16),
    ]
    return pl.pallas_call(
        partial(forward_kernel, pairs, head_dim),
        in_specs=[pl.BlockSpec(memory_space=pltpu.SMEM)] + [ANYWHERE] * 4 + [vmem] * 6,
        out_specs=[ANYWHERE] * 7 + [vmem],
        scratch_shapes=[pltpu.VMEM((slots, pairs, h, w), kind) for h, w, kind in kinds] + [
            *[pltpu.VMEM(a.shape, f32) for a in (q, k, v, rates)],
            pltpu.SemaphoreType.DMA((4,)),
            pltpu.SemaphoreType.DMA((4,)),
            pltpu.VMEM((pairs, pair, inner), f32),
            pltpu.VMEM((pairs, 2 * MB, inner), f32),
            pltpu.VMEM((pairs, pair, inner), f32),
            pltpu.VMEM((pairs, 2 * MB, pair), f32),
            pltpu.VMEM((pairs, 2 * MB, inner), f32),
            pltpu.VMEM((pairs, 2 * MB, inner), bf16),
            pltpu.VMEM((pairs, 2 * MB, pair), bf16),
            pltpu.VMEM((pairs, pair, inner), bf16),
            pltpu.VMEM((pairs, 2 * MB, pair), f32),
            pltpu.VMEM((pairs, MB, pair), f32),
            pltpu.VMEM((3, pairs, 1, pair), f32),
            pltpu.SemaphoreType.DMA((7, slots)),
        ],
        out_shape=[jax.ShapeDtypeStruct((steps, pairs, h, w), kind) for h, w, kind in kinds]
        + [jax.ShapeDtypeStruct((steps * MB, pairs * pair), f32)],
        compiler_params=pltpu.CompilerParams(vmem_limit_bytes=63 * 1024 * 1024),
        name="inner_forward",
    )(restarts, q, k, v, rates, w1i, b1i, w2i, b2i, gain, bias)


MESH = pl.DeviceIdType.MESH


def greet(peers):
    barrier = pltpu.get_barrier_semaphore()
    for peer in peers:
        pl.semaphore_signal(barrier, inc=1, device_id=peer, device_id_type=MESH)
    pl.semaphore_wait(barrier, len(peers))


class Copies:
    def __init__(self, send_sem, recv_sem):
        self.send_sem, self.recv_sem, self.started = send_sem, recv_sem, []

    def make(self, src, dst, peer):
        i = len(self.started)
        copy = pltpu.make_async_remote_copy(
            src_ref=src, dst_ref=dst, send_sem=self.send_sem.at[i], recv_sem=self.recv_sem.at[i],
            device_id=peer, device_id_type=MESH,
        )
        self.started.append(copy)
        return copy

    def send(self, src, dst, peer):
        copy = self.make(src, dst, peer)
        copy.start()
        return copy


def rows_at(start, size):
    return pl.ds(pl.multiple_of(start, 16), size)


def add_low(a, b):
    return (a.astype(f32) + b.astype(f32)).astype(bf16)


def mates(axis):
    size, here = lax.axis_size(axis), lax.axis_index(axis)
    return [{axis: lax.rem(here + o, size)} for o in range(1, size)]


def feed_sum_steps(ins, outs, got_group, sum_group, got_row, full, copies, whole):
    row, group = lax.axis_index("row"), lax.axis_index("group")
    rows, groups = lax.axis_size("row"), lax.axis_size("group")
    row_mates, group_mates = mates("row"), mates("group")
    count = len(ins)
    part = ins[0].shape[0] // groups
    unit = part // rows
    mine = rows_at(row * unit, unit)
    moves = {}
    for i in range(count):
        moves["X", i] = [
            copies.make(ins[i].at[rows_at(lax.rem(group + o, groups) * part, part)], got_group[i].at[o - 1], group_mates[o - 1])
            for o in range(1, groups)
        ]
        moves["Z", i] = [
            copies.make(sum_group[i].at[rows_at(lax.rem(row + o, rows) * unit, unit)], got_row[i].at[o - 1], row_mates[o - 1])
            for o in range(1, rows)
        ]
        if i < whole:
            here = full[i].at[group, mine]
            moves["ZA", i] = [copies.make(here, here, mate) for mate in row_mates]
            here = full[i].at[group]
            moves["XA", i] = [copies.make(here, here, mate) for mate in group_mates]

    def finish(kind, i):
        for copy in moves[kind, i]:
            copy.wait_recv()
        if kind == "X":
            total = ins[i][rows_at(group * part, part)].astype(f32)
            for o in range(1, groups):
                total = total + got_group[i][o - 1].astype(f32)
            sum_group[i][...] = low(total)
        if kind == "Z":
            total = sum_group[i][mine].astype(f32)
            for o in range(1, rows):
                total = total + got_row[i][o - 1].astype(f32)
            if i < whole:
                full[i][group, mine] = low(total)
            else:
                outs[i][...] = low(total)

    def run(slot):
        _, done, begun = FEED_SLOTS[slot]
        if slot == 0:
            greet(row_mates + group_mates)
        for name in done:
            finish(name[:-1], int(name[-1]))
        for name in begun:
            for copy in moves[name[:-1], int(name[-1])]:
                copy.start()
        if slot == len(FEED_SLOTS) - 1:
            for i in range(whole):
                outs[i][...] = full[i][...]
            for copy in copies.started:
                copy.wait_send()

    return [partial(run, slot) for slot in range(len(FEED_SLOTS))]


def backward_kernel(pairs, head_dim, feeds, restart_ref, q_all, k_all, v_all, do_all, rate_all, gain_in, bias_in, *refs):
    saved, feed_in, refs = refs[:7], refs[7 : 7 + feeds], refs[7 + feeds :]
    tok_out, held, refs = refs[:4], refs[4 : 10 + feeds], refs[10 + feeds :]
    rings, sems, refs = refs[:7], refs[7], refs[8:]
    blocks = q_all.shape[0] // MB
    steps = blocks + 1
    slots = rings[0].shape[0]
    depth = slots - 3

    def arrive(j, i):
        at = jnp.maximum(blocks - 1 - j, 0) + (1 if i >= 4 else 0)
        return pltpu.make_async_copy(saved[i].at[pl.ds(at, 1)], rings[i].at[pl.ds(lax.rem(j, slots), 1)], sems.at[i, lax.rem(j, slots)])

    for j in range(depth):
        for i in range(7):
            arrive(j, i).start()

    def step(j, _):
        @pl.when(j + depth < steps)
        def _():
            for i in range(7):
                arrive(j + depth, i).start()

        for i in range(7):
            arrive(j, i).wait()
        ahead = rows_at(jnp.maximum(blocks - 1 - j, 0) * MB, MB)
        now = rows_at(jnp.minimum(blocks - j, blocks - 1) * MB, MB)
        bigq, _, smallq, n1, pqq, uqq, n2 = (ring.at[pl.ds(lax.rem(j, slots), 1)] for ring in rings)
        big, mid, small, _, pq, uq, _ = (ring.at[pl.ds(lax.rem(j + slots - 1, slots), 1)] for ring in rings)
        backward_step(
            pairs, head_dim, feeds, j, steps, restart_ref,
            *[ref.at[ahead] for ref in (q_all, k_all, do_all, rate_all)], bigq, smallq, n1, pqq, uqq, n2,
            *[ref.at[now] for ref in (q_all, k_all, v_all, do_all, rate_all)], big, mid, small, pq, uq, gain_in, bias_in,
            *feed_in, *[ref.at[rows_at((blocks - j) * MB, MB)] for ref in tok_out], *held, *refs,
        )

    lax.fori_loop(0, steps, step, None)


def backward_step(pairs, head_dim, feeds, j, steps, restart_ref,
                  qq_ref, kq_ref, doq_ref, eq_ref, bigq_ref, smallq_ref, n1_ref, pqq_ref, uqq_ref, n2_ref,
                  q_ref, k_ref, v_ref, do_ref, e_ref, big_ref, mid_ref, small_ref, pq_ref, uq_ref, gain_in, bias_in, *refs):
    pair = 2 * head_dim
    inv = 1.0 / head_dim
    own, causal, ones = masks(head_dim)
    feed_in, refs = refs[:feeds], refs[feeds:]
    dq_ref, dk_ref, dv_ref, de_ref, gw1, gb1, gw2, gb2, ggain, gbias = refs[:10]
    feed_out, refs = refs[10 : 10 + feeds], refs[10 + feeds :]
    w1, b1, w2, b2, s_e1, s_e2, s_k, s_x2, s_q1, s_q2, s_q, par_ref = refs[:12]
    if feeds:
        refs, sems = refs[12:-2], refs[-2:]
        buffers = [refs[i * feeds : (i + 1) * feeds] for i in range(3)] + [refs[3 * feeds :]]
        slots = feed_sum_steps(feed_in, feed_out, *buffers, Copies(*sems), FEED_WHOLE)
        for i, run in enumerate(slots):
            pl.when(j == FEED_SLOTS[i][0] * (steps - 1) // 32)(run)

    @pl.when(j == 0)
    def _():
        places = [jnp.minimum(lax.axis_index("group") * pairs + p, gain_in.shape[0] // 2 - 1) for p in range(pairs)]
        load_params(par_ref, (gain_in, bias_in), places)

    @pl.when(j <= 1)
    def _():
        for ref in (w1, b1, w2, b2, gw1, gb1, gw2, gb2, ggain, gbias):
            ref[...] = jnp.zeros_like(ref)

    rows2 = 2 * MB
    piece = lambda ref, p, i: ref[0, p, i * rows2 : (i + 1) * rows2]
    token = lambda ref, p: ref[:, p * pair : (p + 1) * pair]
    first = restart_ref[jnp.minimum(steps - 1 - j, steps - 2)]
    go_on = 1.0 - first
    writes = []

    def write(ref, index, value):
        writes.append((ref, index, value))

    def load_outputs(p):
        return (
            [token(ref, p) for ref in (qq_ref, kq_ref, doq_ref)]
            + [par_ref[0, p]]
            + [bigq_ref[0, p, 0:pair], bigq_ref[0, p, pair : 2 * pair]]
            + [bigq_ref[0, p, 2 * pair : 2 * pair + rows2], bigq_ref[0, p, 2 * pair + rows2 : 2 * pair + 2 * rows2]]
            + [rate_rows(eq_ref[...], p), piece(smallq_ref, p, 4), n1_ref[0, p], n2_ref[0, p]]
            + [piece(ref, p, i) for ref in (pqq_ref, uqq_ref) for i in range(2)]
        )

    def load_step(p):
        return (
            [ref[p] for ref in (s_e1, s_e2, s_k, s_x2, s_q1, s_q2, s_q, w1, w2, b1, b2)]
            + [token(ref, p) for ref in (q_ref, k_ref, v_ref, do_ref)]
            + [par_ref[i, p] for i in (0, 1)]
            + [big_ref[0, p, 0:pair], big_ref[0, p, pair : 2 * pair]]
            + [big_ref[0, p, 2 * pair : 2 * pair + rows2], big_ref[0, p, 2 * pair + rows2 : 2 * pair + 2 * rows2]]
            + [piece(mid_ref, p, i).astype(f32) for i in range(3)]
            + [piece(small_ref, p, i) for i in range(5)]
            + [piece(pq_ref, p, 0), piece(uq_ref, p, 0), rate_rows(e_ref[...], p)]
        )

    def outputs_ahead(p, loaded):
        qc, kc, do, gain, w1b, w2b, x2b, e1b, e, g2, n1b, n2b, p2b, lq, uq, sq = loaded
        qb, kb = low(spread(qc, own)), low(spread(kc, own))
        e2b = low(e * g2)
        w = spread(do * gain, own)
        dq2 = low(sq * (w - (lane_sum(w) * inv) * own - uq * (lane_sum(w * uq) * inv)))
        yield
        dn2 = dot_nt(dq2, e2b)
        dp2 = dot(dq2, w2b)
        yield
        dpx = low(-causal * dn2)
        new_e2 = dot_tn(n2b, dq2)
        dp2 = dp2 + dot(dpx, x2b)
        yield
        dq1 = low(dp2 * lq.astype(f32))
        new_x2 = dot_tn(dpx, p2b)
        yield
        dn1 = dot_nt(dq1, e1b)
        new_q = dot_nt(dq1, w1b)
        yield
        new_e1 = dot_tn(n1b, dq1)
        dqk = low(-causal * dn1)
        yield
        new_k = dot_tn(dqk, qb)
        new_q = do + fold((new_q + dot(dqk, kb)) * own)
        for ref, value in zip((s_e1, s_e2, s_k, s_x2, s_q1, s_q2, s_q), (new_e1, new_e2, new_k, new_x2, dq1, dq2, new_q)):
            write(ref, p, value)

    def step_back(p, loaded):
        e1q, e2q, dkq, x2q, dq1, dq2, dqc, dw1, dw2, db1, db2, qc, kc, vc, do, gain, bias, w1b, w2b, x2b, e1b = loaded[:21]
        g1, l1, hg, u, s, r, m2, g2, p2b, uq, e = loaded[21:]
        cols = (slice(None), slice(p * pair, (p + 1) * pair))
        dw1b, dw2b = low(dw1), low(dw2)
        qb, kb = low(spread(qc, own)), low(spread(kc, own))
        e2b = low(e * g2)
        de1 = dot(kb, dw1b)
        de2 = dot_nt(x2b, dw2b)
        yield
        de1 = -(e1q + de1 + db1)
        de2 = -(e2q + de2 * own + db2)
        dg1 = twice(e) * de1
        dh = low(dg1 * l1)
        yield
        dg2 = dot_nt(dh, w2b)
        dx2 = x2q - dot(e2b, dw2b)
        yield
        dg2 = e * de2 + dg2 * own
        dk = dkq - dot_nt(e1b, dw1b) * own
        ma, mg = lane_sum(dg2 * u) * inv, lane_sum(dg2) * inv
        rate = jnp.broadcast_to(lane_sum(g1 * de1) + lane_sum(g2 * de2), u.shape)
        rates.append(jnp.where(head == 2 * p, rate[:MB], 0.0) + jnp.where(head == 2 * p + 1, rate[MB:], 0.0))
        yield
        dr = s * (dg2 - mg * own - u * ma)
        du = dr * (gain * gain) - s * (dg2 * m2 + r * ma)
        yield
        md, mu = lane_sum(du) * inv, lane_sum(du * u + dg2 * g2) * inv
        dz2 = low(s * (du - md * own - u * mu))
        yield
        dx2 = dx2 + dot(dz2, w2b)
        yield
        dz1 = low(dg1 * hg + dx2 * l1)
        drg = fold(dr) * gain
        write(dq_ref, cols, low(dqc))
        write(dv_ref, cols, low(-drg))
        more_gain = fold(spread_by(do, uq)) + fold(dr * u) * (2.0 * gain) + fold(dr) * (bias - (vc - kc))
        yield
        ndw1 = dw1 + dot_tn(jnp.concatenate([qb, kb], 0), jnp.concatenate([dq1, dz1], 0))
        yield
        dk = dk + dot_nt(dz1, w1b) * own
        write(dk_ref, cols, low(fold(dk) + drg))
        ndw2 = dw2 + dot_tn(jnp.concatenate([dq2, low(g2), dz2], 0), jnp.concatenate([p2b, dh, x2b], 0))
        ndb1 = db1 + dot(ones, dq1) + dot(ones, dz1)
        ndb2 = db2 + dot(ones, dq2) + dot(ones, dz2)
        for ref, value in ((w1, ndw1), (w2, ndw2), (b1, ndb1), (b2, ndb2)):
            write(ref, p, value * go_on)
        more.append((cols, more_gain, do + drg))
        starts.append((p, ndw1, ndw2, ndb1, ndb2))

    more, starts, rates = [], [], []
    head = lax.broadcasted_iota(jnp.int32, (MB, pair), 1)
    ahead_in = [load_outputs(p) for p in range(pairs)]
    step_in = [load_step(p) for p in range(pairs)]
    in_turn([step_back(p, step_in[p]) for p in range(pairs)] + [outputs_ahead(p, ahead_in[p]) for p in range(pairs)])
    for ref, index, value in writes:
        ref[index] = value
    de_ref[...] = sum(rates)
    for cols, more_gain, more_bias in more:
        ggain[cols] += more_gain
        gbias[cols] += more_bias
    for p, *values in starts:
        for ref, value in zip((gw1, gw2, gb1, gb2), values):
            ref[p] += value * first


def spread_by(do, uq):
    return jnp.concatenate([do, do], 0) * uq


def backward_inner(restarts, q, k, v, do, rates, saved, gain, bias, feed_terms, collective_id):
    big, mid, small, n1, pq, uq, n2 = saved
    pairs, pair, inner = big.shape[1], 2 * gain.shape[1], big.shape[3]
    blocks = q.shape[0] // MB
    head_dim = pair // 2
    steps = blocks + 1
    slots = min(8, steps)
    vmem = pl.BlockSpec(memory_space=pltpu.VMEM)
    feeds = len(feed_terms)
    width = pairs * pair
    tok_out = (jax.ShapeDtypeStruct((steps * MB, width), bf16), vmem)
    state = [((pairs, pair, inner), f32), ((pairs, 2 * MB, inner), f32), ((pairs, pair, inner), f32), ((pairs, 2 * MB, pair), f32)]
    keep = lambda shape: (jax.ShapeDtypeStruct(shape, f32), vmem)
    outs = [tok_out] * 3 + [
        (jax.ShapeDtypeStruct((steps * MB, pair), f32), vmem)
    ] + [keep(shape) for shape, _ in state] + [keep((MB, width))] * 2
    comm = []
    if feeds:
        groups, rows = lax.axis_size("group"), lax.axis_size("row")
        part, wide = feed_terms[0].shape[0] // groups, feed_terms[0].shape[1]
        unit = part // rows
        outs += [
            (jax.ShapeDtypeStruct((groups, part, wide) if i < FEED_WHOLE else (unit, wide), bf16), vmem) for i in range(feeds)
        ]
        comm = [pltpu.VMEM((groups - 1, part, wide), bf16)] * feeds + [pltpu.VMEM((part, wide), bf16)] * feeds
        comm += [pltpu.VMEM((rows - 1, unit, wide), bf16)] * feeds + [pltpu.VMEM((groups, part, wide), bf16)] * FEED_WHOLE
        copies = (feeds + FEED_WHOLE) * (groups + rows - 2)
        comm += [pltpu.SemaphoreType.DMA((copies,))] * 2
    return pl.pallas_call(
        partial(backward_kernel, pairs, head_dim, feeds),
        in_specs=[pl.BlockSpec(memory_space=pltpu.SMEM)] + [vmem] * 7 + [ANYWHERE] * 7 + [vmem] * feeds,
        out_specs=[o[1] for o in outs],
        scratch_shapes=[pltpu.VMEM((slots,) + a.shape[1:], a.dtype) for a in saved] + [
            pltpu.SemaphoreType.DMA((7, slots)),
        ] + [pltpu.VMEM(shape, kind) for shape, kind in state] + [
                pltpu.VMEM((pairs, 2 * MB, inner), f32),
                pltpu.VMEM((pairs, 2 * MB, pair), f32),
                pltpu.VMEM((pairs, 2 * MB, pair), f32),
                pltpu.VMEM((pairs, 2 * MB, inner), f32),
                pltpu.VMEM((pairs, 2 * MB, inner), bf16),
                pltpu.VMEM((pairs, 2 * MB, pair), bf16),
                pltpu.VMEM((pairs, MB, pair), f32),
                pltpu.VMEM((2, pairs, 1, pair), f32),
            ] + comm,
        out_shape=[o[0] for o in outs],
        compiler_params=pltpu.CompilerParams(
            collective_id=collective_id if feeds else None, has_side_effects=bool(feeds), vmem_limit_bytes=63 * 1024 * 1024
        ),
        name="inner_backward",
    )(restarts.astype(f32), q, k, v, do, rates, gain, bias, *saved, *feed_terms)


def norm_parts(v, width):
    centered = v - jnp.sum(v, -1, keepdims=True) * (1.0 / width)
    scale = lax.rsqrt(jnp.sum(centered * centered, -1, keepdims=True) * (1.0 / width) + epsilon)
    return centered * scale, scale


def feed_terms(*items):
    for outs, left, right in items:
        width = left.shape[1]
        for i, out in enumerate(outs):
            both = low(dot_tn(left[...], right[:, i * 256 : (i + 1) * 256]))
            out[0:width] = both[:, :128]
            out[width : 2 * width] = both[:, 128:]


def middle_kernel(span, mixed_in, tok_in, cot_in, wout_in, gate_in, up_in, down_in, gain_ref,
                  block_ref, hid_ref, gmix_ref, gwo_ref, t0, t1, t2, t3, t4, t5, gfeed_ref,
                  tok_ref, cot_ref, wout_ref, gate_ref, up_ref, down_ref, downs, mixed_ref, mixed_got, acts, cots, unit, scales, h_in, gg, gu, ha, pg0, po0, out_core, in_core, out_diag, in_diag, out_y, in_y,
                  branch, branch_row, send_sem, recv_sem, local_sem, sems):
    rows, groups = lax.axis_size("row"), lax.axis_size("group")
    row, group, feat = lax.axis_index("row"), lax.axis_index("group"), lax.axis_index("feat")
    count, width = tok_in.shape
    cols = mixed_ref.shape[1]
    core, y = lax.rem(feat, 2), feat // 2
    core_mate, y_mate = {"feat": feat + 1 - 2 * core}, {"feat": feat + 2 - 4 * y}
    here = row * groups + group
    places = rows * groups
    others = [lax.rem(here + o, places) for o in range(1, places)]
    seq_mates = [{"row": t // groups, "group": lax.rem(t, groups)} for t in others]
    copies = Copies(send_sem, recv_sem)
    send = copies.send
    slot = lambda ref, s: ref.at[s * count : (s + 1) * count]

    loads = fetch(
        sems, (cot_in, cot_ref), (down_in, down_ref), (tok_in, tok_ref), (wout_in, wout_ref), (gate_in, gate_ref), (up_in, up_ref)
    )
    mixed_ref[...] = low(mixed_in[MB:])
    greet([core_mate, y_mate] + seq_mates)
    lanes = pl.ds(pl.multiple_of(group * cols, 128), cols)
    moves = [
        send(mixed_ref.at[rows_at(t * span, span)], mixed_got.at[rows_at(row * span, span), lanes], mate)
        for t, mate in zip(others, seq_mates)
    ]
    own = pltpu.make_async_copy(
        mixed_ref.at[rows_at(here * span, span)], mixed_got.at[rows_at(row * span, span), lanes], local_sem.at[0]
    )
    own.start()
    loads[0].wait()
    cot_core = send(cot_ref, slot(cots, 1), core_mate)
    cot_y = send(cot_ref, slot(cots, 2), y_mate)
    cots[0:count] = cot_ref[...]
    loads[1].wait()
    cot_core.wait_recv()
    downs[0 : 2 * count] = dot(cots[0 : 2 * count], down_ref[...])
    own.wait()
    loads[2].wait()
    loads[3].wait()
    for copy in moves:
        copy.wait_recv()
    hidden = tok_ref[...].astype(f32) + dot(mixed_got[:, :width], wout_ref[:width])
    h_in[...] = hidden
    unit_two, scale_two = norm_parts(hidden, width)
    unit[...] = unit_two
    scales[...] = jnp.broadcast_to(scale_two, scales.shape)
    gain = gain_ref[...].reshape(1, width)
    acts[0:count] = low(unit_two * gain)
    cut = count // 2
    span_of = lambda s, h: slice(s * count + h * cut, s * count + (h + 1) * cut)
    act_y = [send(acts.at[span_of(0, h)], acts.at[span_of(2, h)], y_mate) for h in range(2)]
    act_core = send(slot(acts, 0), slot(acts, 1), core_mate)
    cot_y.wait_recv()
    cot_diag = send(slot(cots, 2), slot(cots, 3), core_mate)
    loads[4].wait()
    loads[5].wait()

    def feed(part):
        gate_pre, up_value = dot(acts[part], gate_ref[...]), dot(acts[part], up_ref[...])
        grad = downs[part]
        sig = jax.nn.sigmoid(gate_pre)
        silu = gate_pre * sig
        ha[part] = low(silu * up_value)
        gg[part] = low(grad * up_value * sig * (1.0 + gate_pre * (1.0 - sig)))
        gu[part] = low(grad * silu)
        return dot_nt(gg[part], gate_ref[...]) + dot_nt(gu[part], up_ref[...])

    def forth(s):
        return dot_nt(ha[s * count : (s + 1) * count], down_ref[...])

    pg0[...] = feed(slice(0, count))
    act_core.wait_recv()
    out_core[0] = low(feed(slice(count, 2 * count)))
    core_sums = [send(out_core.at[0], in_core.at[0], core_mate)]
    cot_diag.wait_recv()
    downs[2 * count : 4 * count] = dot(cots[2 * count : 4 * count], down_ref[...])
    y_sums = []
    for h in range(2):
        rows_h = slice(h * cut, (h + 1) * cut)
        act_y[h].wait_recv()
        act_diag = send(acts.at[span_of(2, h)], acts.at[span_of(3, h)], core_mate)
        ahead = feed(span_of(2, h))
        act_diag.wait_recv()
        out_diag[0, rows_h] = low(feed(span_of(3, h)))
        diag_sum = send(out_diag.at[0, rows_h], in_diag.at[0, rows_h], core_mate)
        diag_sum.wait_recv()
        out_y[0, rows_h] = low(ahead + in_diag[0, rows_h].astype(f32))
        y_sums.append(send(out_y.at[0, rows_h], in_y.at[0, rows_h], y_mate))
    out_diag[1] = low(forth(3))
    diag_sum = send(out_diag.at[1], in_diag.at[1], core_mate)
    out_core[1] = low(forth(1))
    core_sums.append(send(out_core.at[1], in_core.at[1], core_mate))
    ahead = forth(2)
    diag_sum.wait_recv()
    out_y[1] = low(ahead + in_diag[1].astype(f32))
    y_sums.append(send(out_y.at[1], in_y.at[1], y_mate))
    po0[...] = forth(0)
    core_sums[0].wait_recv()
    y_sums[0].wait_recv()
    y_sums[1].wait_recv()
    grad_act = pg0[...] + in_core[0].astype(f32) + in_y[0].astype(f32)
    unit_two = unit[...]
    gfeed_ref[...] = jnp.sum(grad_act * unit_two, 0, keepdims=True)
    w = grad_act * gain
    inv = 1.0 / width
    grad = cot_ref[...].astype(f32) + scales[:, 0:1] * (
        w - jnp.sum(w, -1, keepdims=True) * inv - unit_two * (jnp.sum(w * unit_two, -1, keepdims=True) * inv)
    )
    hid_ref[...] = grad
    branch[...] = low(grad)
    row_mates, group_mates = mates("row"), mates("group")
    block = lambda r: branch_row.at[rows_at((r * groups + group) * span, span)]
    by_row = [
        send(branch.at[rows_at(lax.rem(row + o, rows) * span, span)], block(row), row_mates[o - 1]) for o in range(1, rows)
    ]
    block(row)[...] = branch[rows_at(row * span, span)]
    moves = [send(block(row), block(row), mate) for mate in group_mates]
    feed_terms(((t0, t1), acts, gg), ((t2, t3), acts, gu), ((t4, t5), cots, ha))
    for o in range(1, rows):
        by_row[o - 1].wait_recv()
        from_row = block(lax.rem(row - o + rows, rows))
        moves += [send(from_row, from_row, mate) for mate in group_mates]
    core_sums[1].wait_recv()
    y_sums[2].wait_recv()
    block_ref[...] = low(h_in[...] + po0[...] + in_core[1].astype(f32) + in_y[1].astype(f32))
    for copy in moves:
        copy.wait_recv()
    gmix_ref[...] = dot_nt(branch_row[...], wout_ref[rows_at(group * cols, cols)])
    for h in range(2):
        half = branch_row[:, h * (width // 2) : (h + 1) * (width // 2)]
        gwo_ref[h * cols : (h + 1) * cols] = low(dot_tn(mixed_ref[...], half))
    for copy in copies.started:
        copy.wait_send()


def middle(mixed_row, tokens, cotangent, out_weight, gate_weight, up_weight, down_weight, gain, span, collective_id):
    rows, groups = lax.axis_size("row"), lax.axis_size("group")
    length, cols = mixed_row.shape[0] - MB, mixed_row.shape[1]
    count, width = tokens.shape
    hidden = gate_weight.shape[1]
    copies = (rows * groups - 1) + (rows - 1) + rows * (groups - 1) + 18
    vmem = pl.BlockSpec(memory_space=pltpu.VMEM)
    outs = [
        ((count, width), bf16), ((count, width), f32), ((length, cols), f32), ((2 * cols, width // 2), bf16),
        *[((2 * width, 128), bf16)] * 6, ((1, width), f32),
    ]
    two = pltpu.VMEM((2, count, width), bf16)
    return pl.pallas_call(
        partial(middle_kernel, span),
        in_specs=[vmem] + [ANYWHERE] * 6 + [vmem],
        out_specs=[vmem] * len(outs),
        out_shape=[jax.ShapeDtypeStruct(*o) for o in outs],
        scratch_shapes=[
            pltpu.VMEM((count, width), bf16),
            pltpu.VMEM((count, width), bf16),
            pltpu.VMEM(out_weight.shape, bf16),
            *[pltpu.VMEM((width, hidden), bf16)] * 3,
            pltpu.VMEM((4 * count, hidden), f32),
            pltpu.VMEM((length, cols), bf16),
            pltpu.VMEM((count, groups * cols), bf16),
            pltpu.VMEM((4 * count, width), bf16),
            pltpu.VMEM((4 * count, width), bf16),
            pltpu.VMEM((count, width), f32),
            pltpu.VMEM((count, 128), f32),
            pltpu.VMEM((count, width), f32),
            pltpu.VMEM((4 * count, hidden), bf16),
            pltpu.VMEM((4 * count, hidden), bf16),
            pltpu.VMEM((4 * count, hidden), bf16),
            pltpu.VMEM((count, width), f32),
            pltpu.VMEM((count, width), f32),
            two, two, two, two, two, two,
            pltpu.VMEM((count, width), bf16),
            pltpu.VMEM((length, width), bf16),
            pltpu.SemaphoreType.DMA((copies,)),
            pltpu.SemaphoreType.DMA((copies,)),
            pltpu.SemaphoreType.DMA((1,)),
            pltpu.SemaphoreType.DMA((6,)),
        ],
        compiler_params=pltpu.CompilerParams(
            collective_id=collective_id, has_side_effects=True, vmem_limit_bytes=63 * 1024 * 1024
        ),
        name="middle",
    )(mixed_row, tokens, cotangent, out_weight, gate_weight, up_weight, down_weight, gain)


def own_rows(array, mine):
    total = None
    for g in range(lax.axis_size("group")):
        part = array[g * mine : (g + 1) * mine].astype(f32)
        if part.shape[0]:
            part = jnp.concatenate([part, jnp.zeros((128 - part.shape[0], array.shape[1]), f32)], 0)
            part = jnp.where(lax.axis_index("group") == g, part, 0.0)
            total = part if total is None else total + part
    return total


def head_kernel(span, heads, mine, head_dim, tok_ref, gain_ref, wq_in, wk_in, wv_in, wr_ref, rb_ref,
                q_out, k_out, v_out, act_out, unit_out, rate_ref, slope_ref, stat_ref, wown_ref,
                q_ref, k_ref, v_ref, act_ref, unit_ref, out_sems, row_tok, wq_ref, wk_ref, wv_ref, send_sem, recv_sem, sems):
    rows, groups = lax.axis_size("row"), lax.axis_size("group")
    row, group, feat = lax.axis_index("row"), lax.axis_index("group"), lax.axis_index("feat")
    row_mates, group_mates = mates("row"), mates("group")
    width = tok_ref.shape[2]
    cols = q_out.shape[1]
    copies = Copies(send_sem, recv_sem)
    block = lambda r: row_tok.at[rows_at((r * groups + group) * span, span)]

    lanes = pl.ds(pl.multiple_of(group * cols, 128), cols)
    loads = fetch(sems, *[(src.at[:, lanes], dst) for src, dst in ((wq_in, wq_ref), (wk_in, wk_ref), (wv_in, wv_ref))])
    greet(row_mates + group_mates)
    by_row = [
        copies.send(tok_ref.at[lax.rem(row + o, rows)], block(row), row_mates[o - 1]) for o in range(1, rows)
    ]
    block(row)[...] = tok_ref[row]
    by_group = {row_offset: [] for row_offset in range(rows)}
    by_group[0] = [copies.send(block(row), block(row), mate) for mate in group_mates]
    gain = gain_ref[...].reshape(1, width)
    for load in loads:
        load.wait()

    results = list(zip((q_ref, k_ref, v_ref, act_ref, unit_ref), (q_out, k_out, v_out, act_out, unit_out)))

    def work_on(place):
        here = rows_at(place * span, span)
        unit, _ = norm_parts(row_tok[here].astype(f32), width)
        unit_ref[here] = unit
        act = low(unit * gain)
        act_ref[here] = act
        for out, weight in ((q_ref, wq_ref), (k_ref, wk_ref), (v_ref, wv_ref)):
            out[here] = dot(act, weight[...])
        for i, (held, out) in enumerate(results):
            pltpu.make_async_copy(held.at[here], out.at[here], out_sems.at[i]).start()

    work_on(row * groups + group)
    for o in range(1, rows):
        r = lax.rem(row - o + rows, rows)
        by_row[o - 1].wait_recv()
        by_group[o] = [copies.send(block(r), block(r), mate) for mate in group_mates]
        if o > 1:
            work_on(lax.rem(row - o + 1 + rows, rows) * groups + group)
    work_on(lax.rem(row - rows + 1 + rows, rows) * groups + group)
    for o in range(rows):
        r = lax.rem(row - o + rows, rows)
        for copy in by_group[o]:
            copy.wait_recv()
        lax.fori_loop(1, groups, lambda g, _: work_on(r * groups + lax.rem(group + g, groups)), None)
    rate_weight = low(own_rows(wr_ref[...], mine))
    wown_ref[...] = rate_weight
    rate_bias = own_rows(jnp.broadcast_to(rb_ref[...].reshape(1, heads), (8, heads)).T, mine).T[0:1]
    logits = dot_nt(act_ref[...], rate_weight) + rate_bias
    sigma = jax.nn.sigmoid(logits)
    lane = lax.broadcasted_iota(jnp.int32, logits.shape, 1)
    used = (lane < mine) & (group * mine + lane < heads)
    rate_ref[...] = sigma * (1.0 / head_dim)
    slope_ref[...] = jnp.where(used, sigma * (1.0 - sigma) * (1.0 / head_dim), 0.0)
    stat_ref[0:1] = jnp.sum(logits, 0, keepdims=True)
    top = jnp.max(jnp.max(jnp.where(used, logits, -3e38), 0, keepdims=True), 1, keepdims=True)
    place = row * lax.axis_size("feat") + feat
    stat_ref[1:2] = jnp.where(lane[0:1] == place, top, 0.0)
    for copy in copies.started:
        copy.wait_send()
    for i, (held, out) in enumerate(results):
        pltpu.make_async_copy(held, out, out_sems.at[i]).wait()


def head(tokens, gain, weights, rate_weight, rate_bias, heads, mine, head_dim, collective_id):
    rows, groups = lax.axis_size("row"), lax.axis_size("group")
    _, span, width = tokens.shape
    length, cols = rows * groups * span, mine * head_dim
    vmem = pl.BlockSpec(memory_space=pltpu.VMEM)
    copies = (rows - 1) + rows * (groups - 1)
    outs = [((length, cols), f32)] * 3 + [((length, width), bf16), ((length, width), f32)]
    outs += [((length, 128), f32)] * 2 + [((2, 128), f32), ((128, width), bf16)]
    return pl.pallas_call(
        partial(head_kernel, span, heads, mine, head_dim),
        in_specs=[vmem] * 2 + [ANYWHERE] * 3 + [vmem] * 2,
        out_specs=[ANYWHERE] * 5 + [vmem] * (len(outs) - 5),
        out_shape=[jax.ShapeDtypeStruct(*o) for o in outs],
        scratch_shapes=[
            *[pltpu.VMEM(*o) for o in outs[:5]],
            pltpu.SemaphoreType.DMA((5,)),
            pltpu.VMEM((length, width), bf16),
            *[pltpu.VMEM((width, cols), bf16)] * 3,
            pltpu.SemaphoreType.DMA((copies,)),
            pltpu.SemaphoreType.DMA((copies,)),
            pltpu.SemaphoreType.DMA((3,)),
        ],
        compiler_params=pltpu.CompilerParams(
            collective_id=collective_id, has_side_effects=True, vmem_limit_bytes=63 * 1024 * 1024
        ),
        name="head",
    )(tokens, gain, *weights, rate_weight, rate_bias)


TAIL_SLOTS = [
    ([], ["FZ1", "CORE3", "FZ2", "FZ0", "PART0"]),
    (["CORE3"], ["Y3", "CORE0", "CORE2"]),
    (["FZ1"], ["FX1", "FZ3", "CORE4"]),
    (["CORE0"], ["Y0", "CORE1"]),
    (["CORE2"], ["Y2"]),
    (["CORE4", "Y3"], ["Y4"]),
    (["CORE1", "FZ2"], ["Z3", "FX2"]),
    (["Y0"], ["Y1"]),
    (["FZ0"], ["Z0"]),
    (["PART0"], ["SC0", "FX0"]),
    (["Y2", "SC0"], ["SY0"]),
    (["Y4", "FZ3"], ["Z2"]),
    (["FX1"], ["FX3"]),
    (["Z3"], ["ZA3"]),
    (["Y1", "SY0", "FX2", "Z0"], ["ZA0"]),
    (["FX0", "Z2"], ["Z4"]),
    (["ZA3"], ["Z1", "PY3", "PX3"]),
    (["FX3", "ZA0"], ["PY0", "PX0", "ZA2"]),
    (["Z4"], ["ZA4"]),
    (["PY3"], ["QX3"]),
    (["PX3"], ["QY3"]),
    (["Z1"], ["ZA1"]),
    (["PY0"], ["QX0"]),
    (["PX0"], ["QY0"]),
    (["QY3", "QX3"], ["C3"]),
    (["ZA2"], ["PY2", "PX2", "SZ0"]),
    (["C3", "QX0", "QY0"], ["C0"]),
    (["ZA4"], ["PX4", "PY4", "HOME0"]),
    (["C0", "ZA1"], ["PX1", "PY1"]),
    (["PY2", "PX2"], ["QX2", "QY2"]),
    (["PY4", "PX4"], ["QX4", "QY4"]),
    (["SZ0", "PY1", "PX1"], ["QY1", "QX1"]),
    (["QY2", "QX2"], ["SX0", "C2"]),
    (["QY4", "QX4"], ["C4"]),
    (["C2", "QY1", "QX1"], ["C1"]),
    (["C4", "SX0", "HOME0", "C1"], []),
]


FEED_SLOTS = [
    (0, [], ["X1", "X0"]),
    (6, ["X1"], ["Z1", "X3"]),
    (9, ["X0"], ["Z0", "X2"]),
    (12, ["Z1"], ["ZA1"]),
    (12, ["X3"], ["X4"]),
    (15, ["Z0"], ["ZA0"]),
    (15, ["X2"], ["X5"]),
    (17, ["ZA1"], ["Z3"]),
    (18, ["X4"], ["XA1"]),
    (20, ["ZA0"], ["Z4"]),
    (21, ["X5"], ["XA0"]),
    (23, ["Z3"], ["Z2"]),
    (24, ["XA1"], []),
    (26, ["Z4"], ["Z5"]),
    (27, ["XA0"], []),
    (29, ["Z2"], []),
    (32, ["Z5"], []),
]
FEED_WHOLE = 2


def tail_kernel(span, shapes, feeds, act_ref, unit_in, gq_ref, gk_ref, gv_ref, de_in, slope_in, wq_in, wk_in, wv_in, wr_ref,
                gwo_ref, gw1, gb1, gw2, gb2, ggain, gbias, gfeed, stat_ref, *refs):
    rows, groups = lax.axis_size("row"), lax.axis_size("group")
    row, group, feat = lax.axis_index("row"), lax.axis_index("group"), lax.axis_index("feat")
    core, y = lax.rem(feat, 2), feat // 2
    core_mate, y_mate = {"feat": feat + 1 - 2 * core}, {"feat": feat + 2 - 4 * y}
    row_mates, group_mates = mates("row"), mates("group")
    count = len(shapes)
    feed_in, refs = refs[:feeds], refs[feeds:]
    outs, (home_out, small_out), refs = refs[:count], refs[count : count + 2], refs[count + 2 :]
    feed_out, refs = refs[:feeds], refs[feeds:]
    own, got_core, sum_core, got_y, sum_y, got_row = (refs[i * count : (i + 1) * count] for i in range(6))
    part, part_got, part_sum, small, small_core, small_got, unit_ref, de_ref, slope_ref, wq_ref, wk_ref, wv_ref, send_sem, recv_sem, sems = refs[6 * count :]
    length, width = act_ref.shape
    cols = gwo_ref.shape[0] // 2
    pairs, pair, inner = gw1.shape
    head_dim = pair // 2
    copies = Copies(send_sem, recv_sem)
    moves = {}

    def start(name, *what):
        moves[name] = [copies.send(*w) for w in what]

    lanes = pl.ds(pl.multiple_of(group * cols, 128), cols)
    loads = fetch(
        sems, (de_in, de_ref), (slope_in, slope_ref),
        *[(src.at[:, lanes], dst) for src, dst in ((wq_in, wq_ref), (wk_in, wk_ref), (wv_in, wv_ref))], (unit_in, unit_ref),
    )
    greet([core_mate, y_mate] + row_mates + group_mates)

    half = [h // 2 for h, _ in shapes]
    quarter = [h // 4 for h, _ in shapes]
    piece = [h // (4 * rows) for h, _ in shapes]
    unit = feed_in[0].shape[0]
    place = (core * 2 + y) * rows + row
    source = list(own[:3]) + [gwo_ref, own[4]]
    grad_refs = (gq_ref, gk_ref, gv_ref)

    def token_gradient():
        for load in loads:
            load.wait()
        logits = low(de_ref[0:length] * slope_ref[...])
        total = dot(logits, wr_ref[...])
        for grad, weight in zip(grad_refs, (wq_ref, wk_ref, wv_ref)):
            total = total + dot_nt(grad[0:length], weight[...])
        for r in range(rows):
            for g in range(groups):
                part[g, r * span : (r + 1) * span] = low(total[(r * groups + g) * span : (r * groups + g + 1) * span])
        start("PART0", *[(part.at[lax.rem(group + o, groups)], part_got.at[o - 1], group_mates[o - 1]) for o in range(1, groups)])
        small[...] = jnp.zeros_like(small)
        small[0 : 2 * pairs] = dot_tn(logits, act_ref[...])[0 : 2 * pairs]
        for p in range(pairs):
            for h in range(2):
                n = 2 * p + h
                small[6 + n // 3 : 7 + n // 3, (n % 3) * inner : (n % 3 + 1) * inner] = gb1[p, h * MB : h * MB + 1]
            small[9:10, p * pair : (p + 1) * pair] = gb2[p, 0:1] + gb2[p, MB : MB + 1]
        small[8:9, 0:cols] = jnp.sum(ggain[...], 0, keepdims=True)
        small[8:9, cols : 2 * cols] = jnp.sum(gbias[...], 0, keepdims=True)
        small[9:10, width - 384 : width - 256] = jnp.sum(logits.astype(f32), 0, keepdims=True)
        small[9:10, width - 256 : width - 128] = stat_ref[0:1]
        small[9:10, width - 128 : width] = stat_ref[1:2]
        small[10:11] = jnp.sum(total * unit_ref[...], 0, keepdims=True)
        small[11:12] = gfeed[...]

    def finish(name):
        for copy in moves[name]:
            copy.wait_recv()
        kind, i = name[:-1], int(name[-1])
        if kind == "CORE":
            sum_core[i][...] = add_low(source[i][rows_at(core * half[i], half[i])], got_core[i][...])
        if kind == "Y":
            sum_y[i][...] = add_low(sum_core[i][rows_at(y * quarter[i], quarter[i])], got_y[i][...])
        if kind == "Z":
            value = sum_y[i][rows_at(row * piece[i], piece[i])].astype(f32)
            for o in range(1, rows):
                value = value + got_row[i][o - 1].astype(f32)
            outs[i][group, rows_at(place * piece[i], piece[i])] = low(value)
        if kind == "PART":
            value = part[group].astype(f32)
            for o in range(1, groups):
                value = value + part_got[o - 1].astype(f32)
            part_sum[...] = low(value)
            home_out[rows_at(row * span, span)] = part_sum[rows_at(row * span, span)]
        if kind == "SC":
            small_core[...] = small[...] + small_got[0]
        if kind == "SY":
            small_got[2 + row] = small_core[...] + small_got[1]
        if kind == "SZ":
            value = small_got[2]
            for r in range(1, rows):
                value = value + small_got[2 + r]
            small_out[group] = value

    def begin(name):
        kind, i = name[:-1], int(name[-1])
        if kind == "PART":
            token_gradient()
        if kind == "HOME":
            here = home_out.at[rows_at(row * span, span)]
            start(name, *[
                (part_sum.at[rows_at(lax.rem(row + o, rows) * span, span)], here, row_mates[o - 1]) for o in range(1, rows)
            ])
        if kind == "SC":
            start(name, (small, small_got.at[0], core_mate))
        if kind == "SY":
            start(name, (small_core, small_got.at[1], y_mate))
        if kind == "SZ":
            here = small_got.at[2 + row]
            start(name, *[(here, here, mate) for mate in row_mates])
        if kind == "SX":
            here = small_out.at[group]
            start(name, *[(here, here, mate) for mate in group_mates])
        if kind == "FZ":
            here = feed_out[i].at[group, rows_at(row * unit, unit)]
            here[...] = feed_in[i][...]
            start(name, *[(here, here, mate) for mate in row_mates])
        if kind == "FX":
            here = feed_out[i].at[group]
            start(name, *[(here, here, mate) for mate in group_mates])
        if kind == "CORE":
            if i < 3:
                own[i][...] = low(dot_tn(act_ref[...], grad_refs[i][0:length]))
            if i == 4:
                for p in range(pairs):
                    own[4][p * pair : (p + 1) * pair] = low(gw1[p])
                    own[4][cols + p * pair : cols + (p + 1) * pair] = low(gw2[p])
            start(name, (source[i].at[rows_at((1 - core) * half[i], half[i])], got_core[i], core_mate))
        if kind == "Y":
            start(name, (sum_core[i].at[rows_at((1 - y) * quarter[i], quarter[i])], got_y[i], y_mate))
        if kind == "Z":
            start(name, *[
                (sum_y[i].at[rows_at(lax.rem(row + o, rows) * piece[i], piece[i])], got_row[i].at[o - 1], row_mates[o - 1])
                for o in range(1, rows)
            ])
        if kind == "ZA":
            here = outs[i].at[group, rows_at(place * piece[i], piece[i])]
            start(name, *[(here, here, mate) for mate in row_mates])
        step = quarter[i] // 2
        quarter_of = lambda at_y, first, size: rows_at((core * 2 + at_y) * quarter[i] + first, size)
        if kind in ("PX", "PY"):
            here = outs[i].at[group, quarter_of(y, 0, quarter[i])]
            start(name, *[(here, here, mate) for mate in (group_mates if kind == "PX" else [y_mate])])
        if kind == "QX":
            here = outs[i].at[group, quarter_of(1 - y, step, step)]
            start(name, *[(here, here, mate) for mate in group_mates])
        if kind == "QY":
            others = [outs[i].at[lax.rem(group + o, groups), quarter_of(y, 0, step)] for o in range(1, groups)]
            start(name, *[(here, here, y_mate) for here in others])
        if kind == "C":
            here = outs[i].at[:, rows_at(core * half[i], half[i])]
            start(name, (here, here, core_mate))

    for done, begun in TAIL_SLOTS:
        for name in done:
            finish(name)
        for name in begun:
            begin(name)
    for copy in copies.started:
        copy.wait_send()


def tail(act_row, unit_row, grads, de, slope, weights, rate_weight, grad_out, states, grad_feed_gain, stat, feed_parts, span, collective_id):
    rows, groups = lax.axis_size("row"), lax.axis_size("group")
    length, width = act_row.shape
    cols = grad_out.shape[0] // 2
    inner = states[0].shape[-1]
    shapes = [(width, cols)] * 3 + [(2 * cols, width // 2), (2 * cols, inner)]
    count, feeds = len(shapes), len(feed_parts)
    unit, wide = feed_parts[0].shape
    copies = count * (2 + 2 * (rows - 1) + 3 * (groups - 1) + 2) + (groups - 1) + (rows - 1) + 2 + (rows - 1) + (groups - 1)
    copies += feeds * (rows + groups - 2)
    vmem = pl.BlockSpec(memory_space=pltpu.VMEM)
    operands = [act_row, unit_row, *grads, de, slope, *weights, rate_weight, grad_out, *states, grad_feed_gain, stat, *feed_parts]
    outs = [((groups, h, w), bf16) for h, w in shapes]
    outs += [((rows * span, width), bf16), ((groups, 16, width), f32)]
    outs += [((groups, rows * unit, wide), bf16)] * feeds
    scratch = [pltpu.VMEM((h, w), bf16) for h, w in shapes]
    scratch += [pltpu.VMEM((h // 2, w), bf16) for h, w in shapes] * 2
    scratch += [pltpu.VMEM((h // 4, w), bf16) for h, w in shapes] * 2
    scratch += [pltpu.VMEM((rows - 1, h // (4 * rows), w), bf16) for h, w in shapes]
    scratch += [
        pltpu.VMEM((groups, rows * span, width), bf16),
        pltpu.VMEM((groups - 1, rows * span, width), bf16),
        pltpu.VMEM((rows * span, width), bf16),
        pltpu.VMEM((16, width), f32),
        pltpu.VMEM((16, width), f32),
        pltpu.VMEM((2 + rows, 16, width), f32),
        *[pltpu.VMEM(a.shape, f32) for a in (unit_row, de, slope)],
        *[pltpu.VMEM((width, cols), bf16)] * 3,
        pltpu.SemaphoreType.DMA((copies,)),
        pltpu.SemaphoreType.DMA((copies,)),
        pltpu.SemaphoreType.DMA((6,)),
    ]
    return pl.pallas_call(
        partial(tail_kernel, span, shapes, feeds),
        in_specs=[ANYWHERE if i in (1, 5, 6, 7, 8, 9) else vmem for i in range(len(operands))],
        out_specs=[vmem] * len(outs),
        out_shape=[jax.ShapeDtypeStruct(*o) for o in outs],
        scratch_shapes=scratch,
        compiler_params=pltpu.CompilerParams(
            collective_id=collective_id, has_side_effects=True, vmem_limit_bytes=63 * 1024 * 1024
        ),
        name="tail",
    )(*operands)


def finish_kernel(heads, mine, head_dim, inner, total_logits, small_ref, gain_ref, *refs):
    large_in, refs = refs[:14], refs[14:]
    (rate_ref, rbias_ref, fbias_ref, sbias_ref, gain_out, bias_out, mixer_ref, feed_ref, stat_ref,
     q_out, k_out, v_out, o_out, first_out, second_out, gate_out, up_out, down_out, in_out,
     sq, sk, sv, so, s1, s2, sg, su, sd, si, sems, *large, load_sems) = refs
    f0, f1, f2, f3, f4, f5, q_in, k_in, v_in, o_in, s_in, got_ref, tok_ref, hid_ref = large
    groups, width = q_in.shape[0], q_in.shape[1]
    loads = fetch(load_sems, *zip(large_in, large))
    cols = mine * head_dim
    sent, arrived = [], iter(loads)

    def give(value_ref, out):
        copy = pltpu.make_async_copy(value_ref, out, sems.at[len(sent)])
        copy.start()
        sent.append(copy)

    for out, scratch, left, right in ((gate_out, sg, f0, f1), (up_out, su, f2, f3), (down_out, sd, f4, f5)):
        for i, cut in enumerate((left, right)):
            next(arrived).wait()
            value = cut[...].reshape(2 * width, 128)
            for h in range(2):
                scratch[:, (2 * i + h) * 128 : (2 * i + h + 1) * 128] = value[h * width : (h + 1) * width].astype(f32)
        give(scratch, out)
    for out, scratch, array in ((q_out, sq, q_in), (k_out, sk, k_in), (v_out, sv, v_in)):
        next(arrived).wait()
        for g in range(groups):
            size = min(cols, width - g * cols)
            if size > 0:
                scratch[:, g * cols : g * cols + size] = array[g, :, 0:size].astype(f32)
        give(scratch, out)
    next(arrived).wait()
    for g in range(groups):
        size = min(cols, width - g * cols)
        if size > 0:
            for h in range(2):
                scratch = so.at[g * cols : g * cols + size, h * (width // 2) : (h + 1) * (width // 2)]
                scratch[...] = o_in[g, h * cols : h * cols + size].astype(f32)
    give(so, o_out)
    next(arrived).wait()
    for n in range(heads):
        g, i = n // mine, n % mine
        s1[n] = s_in[g, i * head_dim : (i + 1) * head_dim].astype(f32)
        second = s_in[g, cols + i * head_dim : cols + (i + 1) * head_dim].astype(f32)
        s2[n] = second - jnp.sum(second, 0, keepdims=True) * (1.0 / head_dim)
    give(s1, first_out)
    give(s2, second_out)
    for load in arrived:
        load.wait()
    unit, scale = norm_parts(tok_ref[...].astype(f32), width)
    w = got_ref[...].astype(f32) * gain_ref[...].reshape(1, width)
    inv = 1.0 / width
    si[...] = hid_ref[...] + scale * (
        w - jnp.sum(w, -1, keepdims=True) * inv - unit * (jnp.sum(w * unit, -1, keepdims=True) * inv)
    )
    give(si, in_out)
    total = 0.0
    for n in range(heads):
        g, i = n // mine, n % mine
        rate_ref[n : n + 1] = small_ref[g, i : i + 1]
        rbias_ref[:, n : n + 1] = small_ref[g, 9:10, width - 384 + i : width - 383 + i]
        total = total + small_ref[g, 9:10, width - 256 + i : width - 255 + i]
        fbias_ref[n : n + 1] = small_ref[g, 6 + i // 3 : 7 + i // 3, (i % 3) * inner : (i % 3 + 1) * inner]
        own = slice(i * head_dim, (i + 1) * head_dim)
        second = small_ref[g, 9:10, own]
        sbias_ref[n : n + 1] = second - jnp.sum(second, -1, keepdims=True) * (1.0 / head_dim)
        gain_out[n : n + 1] = small_ref[g, 8:9, own]
        bias_out[n : n + 1] = small_ref[g, 8:9, cols + i * head_dim : cols + (i + 1) * head_dim]
    mixer, feed = small_ref[0, 10:11], small_ref[0, 11:12]
    tops = small_ref[0, 9:10, width - 128 : width]
    peers = lax.axis_size("row") * lax.axis_size("feat")
    for g in range(1, groups):
        mixer, feed = mixer + small_ref[g, 10:11], feed + small_ref[g, 11:12]
        tops = jnp.maximum(tops, small_ref[g, 9:10, width - 128 : width])
    mixer_ref[...], feed_ref[...] = mixer.reshape(width), feed.reshape(width)
    lane = lax.broadcasted_iota(jnp.int32, tops.shape, 1)
    top = jnp.max(jnp.where(lane < peers, tops, -3e38), 1, keepdims=True)
    stat_ref[...] = jnp.where(lane == 0, total * (1.0 / total_logits), top)[:, 0:2].reshape(2)
    for copy in sent:
        copy.wait()


def finish(arrays, got, small, tokens, grad_hidden, gain, feed_sums, heads, mine, head_dim, inner, total_logits):
    count, width = tokens.shape
    hidden = 2 * 2 * 128
    vmem = pl.BlockSpec(memory_space=pltpu.VMEM)
    little = [(heads, width), (1, heads), (heads, inner), (heads, head_dim), (heads, head_dim), (heads, head_dim)]
    little += [(width,), (width,), (2,)]
    large = [(width, width)] * 4 + [(heads, head_dim, inner)] * 2 + [(width, hidden)] * 3 + [(count, width)]
    large_in = [*feed_sums, *arrays, got, tokens, grad_hidden]
    return pl.pallas_call(
        partial(finish_kernel, heads, mine, head_dim, inner, total_logits),
        in_specs=[vmem] * 2 + [ANYWHERE] * len(large_in),
        out_specs=[vmem] * len(little) + [ANYWHERE] * len(large),
        out_shape=[jax.ShapeDtypeStruct(s, f32) for s in little + large],
        scratch_shapes=[
            *[pltpu.VMEM(s, f32) for s in large],
            pltpu.SemaphoreType.DMA((len(large),)),
            *[pltpu.VMEM(a.shape, a.dtype) for a in large_in],
            pltpu.SemaphoreType.DMA((len(large_in),)),
        ],
        compiler_params=pltpu.CompilerParams(vmem_limit_bytes=63 * 1024 * 1024),
        name="finish",
    )(small, gain, *large_in)


SEQ = ("row", "group")


def per_device(
    tokens,
    cotangent,
    doc_starts,
    mixer_gain,
    query_weight,
    key_weight,
    value_weight,
    out_weight,
    rate_weight,
    rate_bias,
    first_init,
    first_bias_init,
    second_init,
    second_bias_init,
    inner_gain,
    inner_bias,
    feed_gain,
    gate_weight,
    up_weight,
    down_weight,
):
    rows, span, width = tokens.shape
    heads, head_dim, inner = first_init.shape
    groups = lax.axis_size("group")
    feats = lax.axis_size("feat")
    row, group = lax.axis_index("row"), lax.axis_index("group")
    count = rows * span
    blocks = span * rows * groups // MB
    pairs = -(-heads // (2 * groups))
    mine = 2 * pairs
    pair = 2 * head_dim
    spare = mine * groups - heads

    def padded(array, axis, size):
        edges = [(0, 0)] * array.ndim
        edges[axis] = (0, spare * size)
        return jnp.pad(array, edges) if spare else array

    weights = [padded(w, 1, head_dim) for w in (query_weight, key_weight, value_weight)]
    flat_tokens = tokens.reshape(count, width)
    queries, keys, values, act_row, unit_row, rates, slope, stat, rate_lanes = head(
        tokens, mixer_gain, weights, rate_weight.T, rate_bias, heads, mine, head_dim, 4
    )
    block_ids = jnp.arange(blocks + 1, dtype=jnp.int32)
    starts = lax.dynamic_index_in_dim(doc_starts, row, 0, False)
    restarts = ((block_ids == 0) | jnp.any(starts[:, None] == block_ids[None], 0)).astype(jnp.int32)
    by_pair = lambda a: a.reshape(heads // 2, pair, inner)
    *saved, mixed = forward_inner(
        restarts, queries, keys, values, rates, by_pair(first_init), first_bias_init, by_pair(second_init),
        second_bias_init, inner_gain, inner_bias,
    )

    block_out, grad_hidden, grad_mixed, grad_out_rows, *feed_terms, grad_feed_gain = middle(
        mixed, flat_tokens, cotangent.reshape(count, width), padded(out_weight, 0, head_dim),
        gate_weight, up_weight, down_weight, feed_gain, span, 1,
    )

    grad_q, grad_k, grad_v, grad_e, g_first, g_first_bias, g_second, g_second_bias, g_gain, g_bias, *feed_sums = (
        backward_inner(restarts, queries, keys, values, grad_mixed, rates, saved, inner_gain, inner_bias, feed_terms, 2)
    )
    reduced = tail(
        act_row, unit_row, (grad_q, grad_k, grad_v), grad_e, slope, weights, rate_lanes, grad_out_rows,
        (g_first, g_first_bias, g_second, g_second_bias, g_gain, g_bias), grad_feed_gain, stat,
        feed_sums[FEED_WHOLE:], span, 3,
    )
    arrays, (got, small), feed_sums = reduced[:5], reduced[5:7], [*feed_sums[:FEED_WHOLE], *reduced[7:]]
    (
        g_rate, g_rate_bias, g_first_bias, g_second_bias, g_gain, g_bias, g_mixer, g_feed, stats,
        g_query, g_key, g_value, g_out, g_first, g_second, g_gate, g_up, g_down, input_grad,
    ) = finish(
        arrays, got, small, flat_tokens, grad_hidden, mixer_gain, feed_sums, heads, mine, head_dim, inner,
        rows * groups * feats * count * heads,
    )
    return (
        block_out.reshape(rows, span, width),
        input_grad.reshape(rows, span, width),
        g_mixer,
        g_query,
        g_key,
        g_value,
        g_out,
        g_rate.T,
        g_rate_bias[0],
        g_first,
        g_first_bias,
        g_second,
        g_second_bias,
        g_gain,
        g_bias,
        g_feed,
        g_gate,
        g_up,
        g_down,
        stats,
    )


def solution(mesh):
    feats = mesh.shape["feat"]

    def run(*arrays):
        rows = arrays[0].shape[0] // feats
        grid = jax.sharding.Mesh(mesh.devices.reshape(rows, -1, feats), ("row", "group", "feat"))
        by_token = P("feat", SEQ, None)
        by_hidden = P(None, "feat")
        return jax.shard_map(
            per_device,
            mesh=grid,
            in_specs=(by_token, by_token, P("feat", None)) + (P(),) * 14 + (by_hidden,) * 3,
            out_specs=(by_token, by_token) + (P(),) * 14 + (by_hidden,) * 3 + (P(),),
            check_vma=False,
        )(*arrays)

    return run
```

```python
from functools import partial

import jax
import jax.numpy as jnp
from jax import lax
from jax.experimental import pallas as pl
from jax.experimental.pallas import tpu as pltpu
from jax.sharding import PartitionSpec as P

MB = 16
epsilon = 1e-05
f32, bf16 = jnp.float32, jnp.bfloat16


def dot(a, b):
    return lax.dot_general(a, b, (((1,), (0,)), ((), ())), preferred_element_type=f32)


def dot_nt(a, b):
    return lax.dot_general(a, b, (((1,), (1,)), ((), ())), preferred_element_type=f32)


def dot_tn(a, b):
    return lax.dot_general(a, b, (((0,), (0,)), ((), ())), preferred_element_type=f32)


def low(v):
    return v.astype(bf16)


def gelu_parts(z):
    a = jnp.abs(z)
    d = 1.0 + 0.23164189 * a
    t = pl.reciprocal(d, approx=True)
    t = t * (2.0 - d * t)
    ex = jnp.exp(-0.5 * (z * z))
    poly = t * (
        0.127414796 + t * (-0.142248368 + t * (0.7107068705 + t * (-0.7265760135 + t * 0.5307027145)))
    )
    h = poly * ex
    cdf = jnp.where(z >= 0, 1.0 - h, h)
    pdf = 0.3989422804014327 * ex
    return z * cdf, cdf + z * pdf, pdf


def lane_sum(v):
    return jnp.sum(v, -1, keepdims=True)


def masks(head_dim):
    pair = 2 * head_dim
    rows, cols = 2 * MB, pair
    r = lax.broadcasted_iota(jnp.int32, (rows, cols), 0)
    c = lax.broadcasted_iota(jnp.int32, (rows, cols), 1)
    own = ((r < MB) == (c < head_dim)).astype(f32)
    r = lax.broadcasted_iota(jnp.int32, (rows, rows), 0)
    c = lax.broadcasted_iota(jnp.int32, (rows, rows), 1)
    same = (r < MB) == (c < MB)
    causal = (same & (c <= r)).astype(f32)
    return own, causal, same.astype(bf16)


def spread(v, own):
    return jnp.concatenate([v, v], 0) * own


def fold(v):
    return v[:MB] + v[MB:]


def twice(v):
    return jnp.concatenate([v, v], 1)


def pair_index(p, pairs, array):
    return jnp.minimum(lax.axis_index("group") * pairs + p, array.shape[0] - 1)


def load_params(par_ref, sources, places):
    for i, source in enumerate(sources):
        for p, n in enumerate(places):
            par_ref[i, p] = jnp.concatenate([source[pl.ds(2 * n + h, 1)] for h in range(2)], 1)


def rate_rows(rates, p):
    return jnp.concatenate([jnp.broadcast_to(rates[:, n : n + 1], rates.shape) for n in (2 * p, 2 * p + 1)], 0)


def fetch(sems, *moves):
    copies = [pltpu.make_async_copy(src, dst, sems.at[i]) for i, (src, dst) in enumerate(moves)]
    for copy in copies:
        copy.start()
    return copies


ANYWHERE = pl.BlockSpec(memory_space=pl.ANY)


def in_turn(parts):
    while parts:
        parts = [part for part in parts if next(part, parts) is not parts]


def forward_kernel(pairs, head_dim, restart_ref, q_in, k_in, v_in, rate_in, w1i_ref, b1i_ref, w2i_ref, b2i_ref, gain_in, bias_in,
                   *refs):
    saved, out_all, refs = refs[:7], refs[7], refs[8:]
    rings, refs, sems = refs[:7], refs[7:-1], refs[-1]
    (q_all, k_all, v_all, rate_all, first_sems, rest_sems), refs = refs[:6], refs[6:]
    last = q_in.shape[0] // MB - 1
    arrays = list(zip((q_in, k_in, v_in, rate_in), (q_all, k_all, v_all, rate_all)))
    lead, length = 4 * MB, q_in.shape[0]
    first, rest = (
        fetch(fetch_sems, *[(src.at[pl.ds(at, size)], dst.at[pl.ds(at, size)]) for src, dst in arrays])
        for fetch_sems, at, size in ((first_sems, 0, lead), (rest_sems, lead, length - lead))
    )
    for copy in first:
        copy.wait()
    slots = rings[0].shape[0]

    def leave(j, i):
        return pltpu.make_async_copy(
            rings[i].at[pl.ds(lax.rem(j, slots), 1)], saved[i].at[pl.ds(j, 1)], sems.at[i, lax.rem(j, slots)]
        )

    def step(j, _):
        @pl.when(j >= slots)
        def _():
            for i in range(7):
                leave(j - slots, i).wait()

        @pl.when(j == 3)
        def _():
            for copy in rest:
                copy.wait()

        tokens = rows_at(jnp.minimum(j, last) * MB, MB)
        forward_step(
            pairs, head_dim, j, restart_ref, *[ref.at[tokens] for ref in (q_all, k_all, v_all, rate_all)],
            w1i_ref, b1i_ref, w2i_ref, b2i_ref, gain_in, bias_in,
            *[ring.at[pl.ds(lax.rem(j, slots), 1)] for ring in rings], out_all.at[rows_at(j * MB, MB)], *refs,
        )
        for i in range(7):
            leave(j, i).start()

    lax.fori_loop(0, last + 2, step, None)
    for o in range(slots):
        for i in range(7):
            leave(last + 2 - slots + o, i).wait()


def forward_step(pairs, head_dim, j, restart_ref, q_ref, k_ref, v_ref, rate_ref, w1i_ref, b1i_ref, w2i_ref, b2i_ref, gain_in, bias_in,
                 big_ref, mid_ref, small_ref, n1_ref, pq_ref, uq_ref, n2_ref, out_ref,
                 w1, b1, w2, b2, s_q1, s_x2, s_e2, s_w2, s_b2, s_q, par_ref):
    pair = 2 * head_dim
    inv = 1.0 / head_dim
    own, causal, ones = masks(head_dim)

    @pl.when(j == 0)
    def _():
        load_params(par_ref, (b2i_ref, gain_in, bias_in), [pair_index(p, pairs, w1i_ref) for p in range(pairs)])

    @pl.when(restart_ref[j] > 0)
    def _():
        for p in range(pairs):
            n = pair_index(p, pairs, w1i_ref)
            second = w2i_ref[n]
            second_bias = par_ref[0, p] * own
            w1[p] = w1i_ref[n]
            for h in range(2):
                b1[p, h * MB : (h + 1) * MB] = jnp.broadcast_to(b1i_ref[pl.ds(2 * n + h, 1)], (MB, b1i_ref.shape[1]))
                half = second[h * head_dim : (h + 1) * head_dim]
                w2[p, h * head_dim : (h + 1) * head_dim] = half - jnp.sum(half, 0, keepdims=True) * inv
            b2[p] = second_bias - (lane_sum(second_bias) * inv) * own

    loaded = [
        (s_q1[p], s_x2[p], s_e2[p], s_w2[p], s_b2[p], s_q[p], w1[p], w2[p], b1[p], b2[p], rate_rows(rate_ref[...], p))
        for p in range(pairs)
    ]
    tokens = [
        [ref[:, p * pair : (p + 1) * pair] for ref in (q_ref, k_ref, v_ref)]
        + [par_ref[i, p] for i in (1, 2)]
        for p in range(pairs)
    ]
    writes = []

    def write(ref, index, value):
        writes.append((ref, index, value))

    def outputs_before(p):
        q1p, x2p, e2p, w2p, b2p, qp = loaded[p][:6]
        gain, bias = tokens[p][3:]
        p2, lq, _ = gelu_parts(q1p)
        p2b = low(p2)
        yield
        n2 = causal * (dot_nt(p2b, x2p) + 1.0)
        q2 = dot_nt(p2b, w2p)
        yield
        q2 = q2 * own - dot(low(n2), e2p) + b2p
        yield
        sq = lax.rsqrt(lane_sum(q2 * q2) * inv + epsilon)
        uq = q2 * sq
        write(out_ref, (slice(None), slice(p * pair, (p + 1) * pair)), qp + fold(uq) * gain + bias)
        write(pq_ref, (0, p, slice(0, 2 * MB)), p2b)
        write(pq_ref, (0, p, slice(2 * MB, 4 * MB)), low(lq))
        write(uq_ref, (0, p, slice(0, 2 * MB)), uq)
        write(uq_ref, (0, p, slice(2 * MB, 4 * MB)), jnp.broadcast_to(sq, uq.shape))
        write(n2_ref, (0, p), low(n2))

    def inner_step(p):
        w1c, w2c, b1c, b2c, e = loaded[p][6:]
        qc, kc, vc, gain, bias = tokens[p]
        kb, qb = low(spread(kc, own)), low(spread(qc, own))
        w1b, w2b = low(w1c), low(w2c)
        kq = dot(jnp.concatenate([kb, qb], 0), w1b)
        n1 = low(causal * (dot_nt(qb, kb) + 1.0))
        yield
        z1 = kq[: 2 * MB] + b1c
        x2, l1, pdf = gelu_parts(z1)
        x2b = low(x2)
        yield
        c = dot_nt(x2b, w2b)
        yield
        c = c * own + b2c
        s = lax.rsqrt(lane_sum(c * c) * inv + epsilon)
        u = c * s
        r = u * (gain * gain) + spread((bias - (vc - kc)) * gain, own)
        mr, m2 = lane_sum(r) * inv, lane_sum(r * u) * inv
        g2 = s * (r - mr * own - u * m2)
        e2 = e * g2
        e2b = low(e2)
        yield
        h = dot(low(g2), w2b)
        u2 = dot_tn(e2b, x2b)
        yield
        g1 = h * l1
        e1b = low(twice(e) * g1)
        yield
        u1 = dot_tn(kb, e1b)
        below = dot(jnp.concatenate([n1, ones], 0), e1b)
        yield
        q1 = kq[2 * MB :] + b1c - below[: 2 * MB]
        write(w1, p, w1c - u1)
        write(b1, p, b1c - below[2 * MB :])
        write(w2, p, w2c - u2)
        write(b2, p, b2c - jnp.sum(e2, 0, keepdims=True) * own)
        write(big_ref, (0, p, slice(0, pair)), w1b)
        write(big_ref, (0, p, slice(pair, 2 * pair)), w2b)
        write(big_ref, (0, p, slice(2 * pair, 2 * pair + 2 * MB)), x2b)
        write(big_ref, (0, p, slice(2 * pair + 2 * MB, 2 * pair + 4 * MB)), e1b)
        write(mid_ref, (0, p, slice(0, 2 * MB)), low(g1))
        write(mid_ref, (0, p, slice(2 * MB, 4 * MB)), low(l1))
        write(mid_ref, (0, p, slice(4 * MB, 6 * MB)), low(h * pdf * (2.0 - z1 * z1)))
        for i, value in enumerate((u, s, r, m2, g2)):
            write(small_ref, (0, p, slice(i * 2 * MB, (i + 1) * 2 * MB)), jnp.broadcast_to(value, u.shape))
        write(n1_ref, (0, p), n1)
        for ref, value in ((s_q1, q1), (s_x2, x2b), (s_e2, e2b), (s_w2, w2b), (s_b2, b2c), (s_q, qc)):
            write(ref, p, value)

    in_turn([inner_step(p) for p in range(pairs)] + [outputs_before(p) for p in range(pairs)])
    for ref, index, value in writes:
        ref[index] = value


def forward_inner(restarts, q, k, v, rates, w1i, b1i, w2i, b2i, gain, bias):
    _, pair, inner = w1i.shape
    blocks, pairs = q.shape[0] // MB, q.shape[1] // pair
    head_dim = pair // 2
    steps = blocks + 1
    slots = min(8, steps)
    vmem = pl.BlockSpec(memory_space=pltpu.VMEM)
    kinds = [
        (2 * pair + 4 * MB, inner, bf16),
        (6 * MB, inner, bf16),
        (10 * MB, pair, f32),
        (2 * MB, 2 * MB, bf16),
        (4 * MB, inner, bf16),
        (4 * MB, pair, f32),
        (2 * MB, 2 * MB, bf16),
    ]
    return pl.pallas_call(
        partial(forward_kernel, pairs, head_dim),
        in_specs=[pl.BlockSpec(memory_space=pltpu.SMEM)] + [ANYWHERE] * 4 + [vmem] * 6,
        out_specs=[ANYWHERE] * 7 + [vmem],
        scratch_shapes=[pltpu.VMEM((slots, pairs, h, w), kind) for h, w, kind in kinds] + [
            *[pltpu.VMEM(a.shape, f32) for a in (q, k, v, rates)],
            pltpu.SemaphoreType.DMA((4,)),
            pltpu.SemaphoreType.DMA((4,)),
            pltpu.VMEM((pairs, pair, inner), f32),
            pltpu.VMEM((pairs, 2 * MB, inner), f32),
            pltpu.VMEM((pairs, pair, inner), f32),
            pltpu.VMEM((pairs, 2 * MB, pair), f32),
            pltpu.VMEM((pairs, 2 * MB, inner), f32),
            pltpu.VMEM((pairs, 2 * MB, inner), bf16),
            pltpu.VMEM((pairs, 2 * MB, pair), bf16),
            pltpu.VMEM((pairs, pair, inner), bf16),
            pltpu.VMEM((pairs, 2 * MB, pair), f32),
            pltpu.VMEM((pairs, MB, pair), f32),
            pltpu.VMEM((3, pairs, 1, pair), f32),
            pltpu.SemaphoreType.DMA((7, slots)),
        ],
        out_shape=[jax.ShapeDtypeStruct((steps, pairs, h, w), kind) for h, w, kind in kinds]
        + [jax.ShapeDtypeStruct((steps * MB, pairs * pair), f32)],
        compiler_params=pltpu.CompilerParams(vmem_limit_bytes=63 * 1024 * 1024),
        name="inner_forward",
    )(restarts, q, k, v, rates, w1i, b1i, w2i, b2i, gain, bias)


MESH = pl.DeviceIdType.MESH


def greet(peers):
    barrier = pltpu.get_barrier_semaphore()
    for peer in peers:
        pl.semaphore_signal(barrier, inc=1, device_id=peer, device_id_type=MESH)
    pl.semaphore_wait(barrier, len(peers))


class Copies:
    def __init__(self, send_sem, recv_sem):
        self.send_sem, self.recv_sem, self.started = send_sem, recv_sem, []

    def make(self, src, dst, peer):
        i = len(self.started)
        copy = pltpu.make_async_remote_copy(
            src_ref=src, dst_ref=dst, send_sem=self.send_sem.at[i], recv_sem=self.recv_sem.at[i],
            device_id=peer, device_id_type=MESH,
        )
        self.started.append(copy)
        return copy

    def send(self, src, dst, peer):
        copy = self.make(src, dst, peer)
        copy.start()
        return copy


def rows_at(start, size):
    return pl.ds(pl.multiple_of(start, 16), size)


def add_low(a, b):
    return (a.astype(f32) + b.astype(f32)).astype(bf16)


def mates(axis):
    size, here = lax.axis_size(axis), lax.axis_index(axis)
    return [{axis: lax.rem(here + o, size)} for o in range(1, size)]


def feed_sum_steps(ins, outs, got_group, sum_group, got_row, full, copies, whole):
    row, group = lax.axis_index("row"), lax.axis_index("group")
    rows, groups = lax.axis_size("row"), lax.axis_size("group")
    row_mates, group_mates = mates("row"), mates("group")
    count = len(ins)
    part = ins[0].shape[0] // groups
    unit = part // rows
    mine = rows_at(row * unit, unit)
    moves = {}
    for i in range(count):
        moves["X", i] = [
            copies.make(ins[i].at[rows_at(lax.rem(group + o, groups) * part, part)], got_group[i].at[o - 1], group_mates[o - 1])
            for o in range(1, groups)
        ]
        moves["Z", i] = [
            copies.make(sum_group[i].at[rows_at(lax.rem(row + o, rows) * unit, unit)], got_row[i].at[o - 1], row_mates[o - 1])
            for o in range(1, rows)
        ]
        if i < whole:
            here = full[i].at[group, mine]
            moves["ZA", i] = [copies.make(here, here, mate) for mate in row_mates]
            here = full[i].at[group]
            moves["XA", i] = [copies.make(here, here, mate) for mate in group_mates]

    def finish(kind, i):
        for copy in moves[kind, i]:
            copy.wait_recv()
        if kind == "X":
            total = ins[i][rows_at(group * part, part)].astype(f32)
            for o in range(1, groups):
                total = total + got_group[i][o - 1].astype(f32)
            sum_group[i][...] = low(total)
        if kind == "Z":
            total = sum_group[i][mine].astype(f32)
            for o in range(1, rows):
                total = total + got_row[i][o - 1].astype(f32)
            if i < whole:
                full[i][group, mine] = low(total)
            else:
                outs[i][...] = low(total)

    def run(slot):
        _, done, begun = FEED_SLOTS[slot]
        if slot == 0:
            greet(row_mates + group_mates)
        for name in done:
            finish(name[:-1], int(name[-1]))
        for name in begun:
            for copy in moves[name[:-1], int(name[-1])]:
                copy.start()
        if slot == len(FEED_SLOTS) - 1:
            for i in range(whole):
                outs[i][...] = full[i][...]
            for copy in copies.started:
                copy.wait_send()

    return [partial(run, slot) for slot in range(len(FEED_SLOTS))]


def backward_kernel(pairs, head_dim, feeds, restart_ref, q_all, k_all, v_all, do_all, rate_all, gain_in, bias_in, *refs):
    saved, feed_in, refs = refs[:7], refs[7 : 7 + feeds], refs[7 + feeds :]
    tok_out, held, refs = refs[:4], refs[4 : 10 + feeds], refs[10 + feeds :]
    rings, sems, refs = refs[:7], refs[7], refs[8:]
    blocks = q_all.shape[0] // MB
    steps = blocks + 1
    slots = rings[0].shape[0]
    depth = slots - 3

    def arrive(j, i):
        at = jnp.maximum(blocks - 1 - j, 0) + (1 if i >= 4 else 0)
        return pltpu.make_async_copy(saved[i].at[pl.ds(at, 1)], rings[i].at[pl.ds(lax.rem(j, slots), 1)], sems.at[i, lax.rem(j, slots)])

    for j in range(depth):
        for i in range(7):
            arrive(j, i).start()

    def step(j, _):
        @pl.when(j + depth < steps)
        def _():
            for i in range(7):
                arrive(j + depth, i).start()

        for i in range(7):
            arrive(j, i).wait()
        ahead = rows_at(jnp.maximum(blocks - 1 - j, 0) * MB, MB)
        now = rows_at(jnp.minimum(blocks - j, blocks - 1) * MB, MB)
        bigq, _, smallq, n1, pqq, uqq, n2 = (ring.at[pl.ds(lax.rem(j, slots), 1)] for ring in rings)
        big, mid, small, _, pq, uq, _ = (ring.at[pl.ds(lax.rem(j + slots - 1, slots), 1)] for ring in rings)
        backward_step(
            pairs, head_dim, feeds, j, steps, restart_ref,
            *[ref.at[ahead] for ref in (q_all, k_all, do_all, rate_all)], bigq, smallq, n1, pqq, uqq, n2,
            *[ref.at[now] for ref in (q_all, k_all, v_all, do_all, rate_all)], big, mid, small, pq, uq, gain_in, bias_in,
            *feed_in, *[ref.at[rows_at((blocks - j) * MB, MB)] for ref in tok_out], *held, *refs,
        )

    lax.fori_loop(0, steps, step, None)


def backward_step(pairs, head_dim, feeds, j, steps, restart_ref,
                  qq_ref, kq_ref, doq_ref, eq_ref, bigq_ref, smallq_ref, n1_ref, pqq_ref, uqq_ref, n2_ref,
                  q_ref, k_ref, v_ref, do_ref, e_ref, big_ref, mid_ref, small_ref, pq_ref, uq_ref, gain_in, bias_in, *refs):
    pair = 2 * head_dim
    inv = 1.0 / head_dim
    own, causal, ones = masks(head_dim)
    feed_in, refs = refs[:feeds], refs[feeds:]
    dq_ref, dk_ref, dv_ref, de_ref, gw1, gb1, gw2, gb2, ggain, gbias = refs[:10]
    feed_out, refs = refs[10 : 10 + feeds], refs[10 + feeds :]
    w1, b1, w2, b2, s_e1, s_e2, s_k, s_x2, s_q1, s_q2, s_q, par_ref = refs[:12]
    if feeds:
        refs, sems = refs[12:-2], refs[-2:]
        buffers = [refs[i * feeds : (i + 1) * feeds] for i in range(3)] + [refs[3 * feeds :]]
        slots = feed_sum_steps(feed_in, feed_out, *buffers, Copies(*sems), FEED_WHOLE)
        for i, run in enumerate(slots):
            pl.when(j == FEED_SLOTS[i][0] * (steps - 1) // 32)(run)

    @pl.when(j == 0)
    def _():
        places = [jnp.minimum(lax.axis_index("group") * pairs + p, gain_in.shape[0] // 2 - 1) for p in range(pairs)]
        load_params(par_ref, (gain_in, bias_in), places)

    @pl.when(j <= 1)
    def _():
        for ref in (w1, b1, w2, b2, gw1, gb1, gw2, gb2, ggain, gbias):
            ref[...] = jnp.zeros_like(ref)

    rows2 = 2 * MB
    piece = lambda ref, p, i: ref[0, p, i * rows2 : (i + 1) * rows2]
    token = lambda ref, p: ref[:, p * pair : (p + 1) * pair]
    first = restart_ref[jnp.minimum(steps - 1 - j, steps - 2)]
    go_on = 1.0 - first
    writes = []

    def write(ref, index, value):
        writes.append((ref, index, value))

    def load_outputs(p):
        return (
            [token(ref, p) for ref in (qq_ref, kq_ref, doq_ref)]
            + [par_ref[0, p]]
            + [bigq_ref[0, p, 0:pair], bigq_ref[0, p, pair : 2 * pair]]
            + [bigq_ref[0, p, 2 * pair : 2 * pair + rows2], bigq_ref[0, p, 2 * pair + rows2 : 2 * pair + 2 * rows2]]
            + [rate_rows(eq_ref[...], p), piece(smallq_ref, p, 4), n1_ref[0, p], n2_ref[0, p]]
            + [piece(ref, p, i) for ref in (pqq_ref, uqq_ref) for i in range(2)]
        )

    def load_step(p):
        return (
            [ref[p] for ref in (s_e1, s_e2, s_k, s_x2, s_q1, s_q2, s_q, w1, w2, b1, b2)]
            + [token(ref, p) for ref in (q_ref, k_ref, v_ref, do_ref)]
            + [par_ref[i, p] for i in (0, 1)]
            + [big_ref[0, p, 0:pair], big_ref[0, p, pair : 2 * pair]]
            + [big_ref[0, p, 2 * pair : 2 * pair + rows2], big_ref[0, p, 2 * pair + rows2 : 2 * pair + 2 * rows2]]
            + [piece(mid_ref, p, i).astype(f32) for i in range(3)]
            + [piece(small_ref, p, i) for i in range(5)]
            + [piece(pq_ref, p, 0), piece(uq_ref, p, 0), rate_rows(e_ref[...], p)]
        )

    def outputs_ahead(p, loaded):
        qc, kc, do, gain, w1b, w2b, x2b, e1b, e, g2, n1b, n2b, p2b, lq, uq, sq = loaded
        qb, kb = low(spread(qc, own)), low(spread(kc, own))
        e2b = low(e * g2)
        w = spread(do * gain, own)
        dq2 = low(sq * (w - (lane_sum(w) * inv) * own - uq * (lane_sum(w * uq) * inv)))
        yield
        dn2 = dot_nt(dq2, e2b)
        dp2 = dot(dq2, w2b)
        yield
        dpx = low(-causal * dn2)
        new_e2 = dot_tn(n2b, dq2)
        dp2 = dp2 + dot(dpx, x2b)
        yield
        dq1 = low(dp2 * lq.astype(f32))
        new_x2 = dot_tn(dpx, p2b)
        yield
        dn1 = dot_nt(dq1, e1b)
        new_q = dot_nt(dq1, w1b)
        yield
        new_e1 = dot_tn(n1b, dq1)
        dqk = low(-causal * dn1)
        yield
        new_k = dot_tn(dqk, qb)
        new_q = do + fold((new_q + dot(dqk, kb)) * own)
        for ref, value in zip((s_e1, s_e2, s_k, s_x2, s_q1, s_q2, s_q), (new_e1, new_e2, new_k, new_x2, dq1, dq2, new_q)):
            write(ref, p, value)

    def step_back(p, loaded):
        e1q, e2q, dkq, x2q, dq1, dq2, dqc, dw1, dw2, db1, db2, qc, kc, vc, do, gain, bias, w1b, w2b, x2b, e1b = loaded[:21]
        g1, l1, hg, u, s, r, m2, g2, p2b, uq, e = loaded[21:]
        cols = (slice(None), slice(p * pair, (p + 1) * pair))
        dw1b, dw2b = low(dw1), low(dw2)
        qb, kb = low(spread(qc, own)), low(spread(kc, own))
        e2b = low(e * g2)
        de1 = dot(kb, dw1b)
        de2 = dot_nt(x2b, dw2b)
        yield
        de1 = -(e1q + de1 + db1)
        de2 = -(e2q + de2 * own + db2)
        dg1 = twice(e) * de1
        dh = low(dg1 * l1)
        yield
        dg2 = dot_nt(dh, w2b)
        dx2 = x2q - dot(e2b, dw2b)
        yield
        dg2 = e * de2 + dg2 * own
        dk = dkq - dot_nt(e1b, dw1b) * own
        ma, mg = lane_sum(dg2 * u) * inv, lane_sum(dg2) * inv
        rate = jnp.broadcast_to(lane_sum(g1 * de1) + lane_sum(g2 * de2), u.shape)
        rates.append(jnp.where(head == 2 * p, rate[:MB], 0.0) + jnp.where(head == 2 * p + 1, rate[MB:], 0.0))
        yield
        dr = s * (dg2 - mg * own - u * ma)
        du = dr * (gain * gain) - s * (dg2 * m2 + r * ma)
        yield
        md, mu = lane_sum(du) * inv, lane_sum(du * u + dg2 * g2) * inv
        dz2 = low(s * (du - md * own - u * mu))
        yield
        dx2 = dx2 + dot(dz2, w2b)
        yield
        dz1 = low(dg1 * hg + dx2 * l1)
        drg = fold(dr) * gain
        write(dq_ref, cols, low(dqc))
        write(dv_ref, cols, low(-drg))
        more_gain = fold(spread_by(do, uq)) + fold(dr * u) * (2.0 * gain) + fold(dr) * (bias - (vc - kc))
        yield
        ndw1 = dw1 + dot_tn(jnp.concatenate([qb, kb], 0), jnp.concatenate([dq1, dz1], 0))
        yield
        dk = dk + dot_nt(dz1, w1b) * own
        write(dk_ref, cols, low(fold(dk) + drg))
        ndw2 = dw2 + dot_tn(jnp.concatenate([dq2, low(g2), dz2], 0), jnp.concatenate([p2b, dh, x2b], 0))
        ndb1 = db1 + dot(ones, dq1) + dot(ones, dz1)
        ndb2 = db2 + dot(ones, dq2) + dot(ones, dz2)
        for ref, value in ((w1, ndw1), (w2, ndw2), (b1, ndb1), (b2, ndb2)):
            write(ref, p, value * go_on)
        more.append((cols, more_gain, do + drg))
        starts.append((p, ndw1, ndw2, ndb1, ndb2))

    more, starts, rates = [], [], []
    head = lax.broadcasted_iota(jnp.int32, (MB, pair), 1)
    ahead_in = [load_outputs(p) for p in range(pairs)]
    step_in = [load_step(p) for p in range(pairs)]
    in_turn([step_back(p, step_in[p]) for p in range(pairs)] + [outputs_ahead(p, ahead_in[p]) for p in range(pairs)])
    for ref, index, value in writes:
        ref[index] = value
    de_ref[...] = sum(rates)
    for cols, more_gain, more_bias in more:
        ggain[cols] += more_gain
        gbias[cols] += more_bias
    for p, *values in starts:
        for ref, value in zip((gw1, gw2, gb1, gb2), values):
            ref[p] += value * first


def spread_by(do, uq):
    return jnp.concatenate([do, do], 0) * uq


def backward_inner(restarts, q, k, v, do, rates, saved, gain, bias, feed_terms, collective_id):
    big, mid, small, n1, pq, uq, n2 = saved
    pairs, pair, inner = big.shape[1], 2 * gain.shape[1], big.shape[3]
    blocks = q.shape[0] // MB
    head_dim = pair // 2
    steps = blocks + 1
    slots = min(8, steps)
    vmem = pl.BlockSpec(memory_space=pltpu.VMEM)
    feeds = len(feed_terms)
    width = pairs * pair
    tok_out = (jax.ShapeDtypeStruct((steps * MB, width), bf16), vmem)
    state = [((pairs, pair, inner), f32), ((pairs, 2 * MB, inner), f32), ((pairs, pair, inner), f32), ((pairs, 2 * MB, pair), f32)]
    keep = lambda shape: (jax.ShapeDtypeStruct(shape, f32), vmem)
    outs = [tok_out] * 3 + [
        (jax.ShapeDtypeStruct((steps * MB, pair), f32), vmem)
    ] + [keep(shape) for shape, _ in state] + [keep((MB, width))] * 2
    comm = []
    if feeds:
        groups, rows = lax.axis_size("group"), lax.axis_size("row")
        part, wide = feed_terms[0].shape[0] // groups, feed_terms[0].shape[1]
        unit = part // rows
        outs += [
            (jax.ShapeDtypeStruct((groups, part, wide) if i < FEED_WHOLE else (unit, wide), bf16), vmem) for i in range(feeds)
        ]
        comm = [pltpu.VMEM((groups - 1, part, wide), bf16)] * feeds + [pltpu.VMEM((part, wide), bf16)] * feeds
        comm += [pltpu.VMEM((rows - 1, unit, wide), bf16)] * feeds + [pltpu.VMEM((groups, part, wide), bf16)] * FEED_WHOLE
        copies = (feeds + FEED_WHOLE) * (groups + rows - 2)
        comm += [pltpu.SemaphoreType.DMA((copies,))] * 2
    return pl.pallas_call(
        partial(backward_kernel, pairs, head_dim, feeds),
        in_specs=[pl.BlockSpec(memory_space=pltpu.SMEM)] + [vmem] * 7 + [ANYWHERE] * 7 + [vmem] * feeds,
        out_specs=[o[1] for o in outs],
        scratch_shapes=[pltpu.VMEM((slots,) + a.shape[1:], a.dtype) for a in saved] + [
            pltpu.SemaphoreType.DMA((7, slots)),
        ] + [pltpu.VMEM(shape, kind) for shape, kind in state] + [
                pltpu.VMEM((pairs, 2 * MB, inner), f32),
                pltpu.VMEM((pairs, 2 * MB, pair), f32),
                pltpu.VMEM((pairs, 2 * MB, pair), f32),
                pltpu.VMEM((pairs, 2 * MB, inner), f32),
                pltpu.VMEM((pairs, 2 * MB, inner), bf16),
                pltpu.VMEM((pairs, 2 * MB, pair), bf16),
                pltpu.VMEM((pairs, MB, pair), f32),
                pltpu.VMEM((2, pairs, 1, pair), f32),
            ] + comm,
        out_shape=[o[0] for o in outs],
        compiler_params=pltpu.CompilerParams(
            collective_id=collective_id if feeds else None, has_side_effects=bool(feeds), vmem_limit_bytes=63 * 1024 * 1024
        ),
        name="inner_backward",
    )(restarts.astype(f32), q, k, v, do, rates, gain, bias, *saved, *feed_terms)


def norm_parts(v, width):
    centered = v - jnp.sum(v, -1, keepdims=True) * (1.0 / width)
    scale = lax.rsqrt(jnp.sum(centered * centered, -1, keepdims=True) * (1.0 / width) + epsilon)
    return centered * scale, scale


def feed_terms(*items):
    for outs, left, right in items:
        width = left.shape[1]
        for i, out in enumerate(outs):
            both = low(dot_tn(left[...], right[:, i * 256 : (i + 1) * 256]))
            out[0:width] = both[:, :128]
            out[width : 2 * width] = both[:, 128:]


def middle_kernel(span, mixed_in, tok_in, cot_in, wout_in, gate_in, up_in, down_in, gain_ref,
                  block_ref, hid_ref, gmix_ref, gwo_ref, t0, t1, t2, t3, t4, t5, gfeed_ref,
                  tok_ref, cot_ref, wout_ref, gate_ref, up_ref, down_ref, downs, mixed_ref, mixed_got, acts, cots, unit, scales, h_in, gg, gu, ha, pg0, po0, out_core, in_core, out_diag, in_diag, out_y, in_y,
                  branch, branch_row, send_sem, recv_sem, local_sem, sems):
    rows, groups = lax.axis_size("row"), lax.axis_size("group")
    row, group, feat = lax.axis_index("row"), lax.axis_index("group"), lax.axis_index("feat")
    count, width = tok_in.shape
    cols = mixed_ref.shape[1]
    core, y = lax.rem(feat, 2), feat // 2
    core_mate, y_mate = {"feat": feat + 1 - 2 * core}, {"feat": feat + 2 - 4 * y}
    here = row * groups + group
    places = rows * groups
    others = [lax.rem(here + o, places) for o in range(1, places)]
    seq_mates = [{"row": t // groups, "group": lax.rem(t, groups)} for t in others]
    copies = Copies(send_sem, recv_sem)
    send = copies.send
    slot = lambda ref, s: ref.at[s * count : (s + 1) * count]

    loads = fetch(
        sems, (cot_in, cot_ref), (down_in, down_ref), (tok_in, tok_ref), (wout_in, wout_ref), (gate_in, gate_ref), (up_in, up_ref)
    )
    mixed_ref[...] = low(mixed_in[MB:])
    greet([core_mate, y_mate] + seq_mates)
    lanes = pl.ds(pl.multiple_of(group * cols, 128), cols)
    moves = [
        send(mixed_ref.at[rows_at(t * span, span)], mixed_got.at[rows_at(row * span, span), lanes], mate)
        for t, mate in zip(others, seq_mates)
    ]
    own = pltpu.make_async_copy(
        mixed_ref.at[rows_at(here * span, span)], mixed_got.at[rows_at(row * span, span), lanes], local_sem.at[0]
    )
    own.start()
    loads[0].wait()
    cot_core = send(cot_ref, slot(cots, 1), core_mate)
    cot_y = send(cot_ref, slot(cots, 2), y_mate)
    cots[0:count] = cot_ref[...]
    loads[1].wait()
    cot_core.wait_recv()
    downs[0 : 2 * count] = dot(cots[0 : 2 * count], down_ref[...])
    own.wait()
    loads[2].wait()
    loads[3].wait()
    for copy in moves:
        copy.wait_recv()
    hidden = tok_ref[...].astype(f32) + dot(mixed_got[:, :width], wout_ref[:width])
    h_in[...] = hidden
    unit_two, scale_two = norm_parts(hidden, width)
    unit[...] = unit_two
    scales[...] = jnp.broadcast_to(scale_two, scales.shape)
    gain = gain_ref[...].reshape(1, width)
    acts[0:count] = low(unit_two * gain)
    cut = count // 2
    span_of = lambda s, h: slice(s * count + h * cut, s * count + (h + 1) * cut)
    act_y = [send(acts.at[span_of(0, h)], acts.at[span_of(2, h)], y_mate) for h in range(2)]
    act_core = send(slot(acts, 0), slot(acts, 1), core_mate)
    cot_y.wait_recv()
    cot_diag = send(slot(cots, 2), slot(cots, 3), core_mate)
    loads[4].wait()
    loads[5].wait()

    def feed(part):
        gate_pre, up_value = dot(acts[part], gate_ref[...]), dot(acts[part], up_ref[...])
        grad = downs[part]
        sig = jax.nn.sigmoid(gate_pre)
        silu = gate_pre * sig
        ha[part] = low(silu * up_value)
        gg[part] = low(grad * up_value * sig * (1.0 + gate_pre * (1.0 - sig)))
        gu[part] = low(grad * silu)
        return dot_nt(gg[part], gate_ref[...]) + dot_nt(gu[part], up_ref[...])

    def forth(s):
        return dot_nt(ha[s * count : (s + 1) * count], down_ref[...])

    pg0[...] = feed(slice(0, count))
    act_core.wait_recv()
    out_core[0] = low(feed(slice(count, 2 * count)))
    core_sums = [send(out_core.at[0], in_core.at[0], core_mate)]
    cot_diag.wait_recv()
    downs[2 * count : 4 * count] = dot(cots[2 * count : 4 * count], down_ref[...])
    y_sums = []
    for h in range(2):
        rows_h = slice(h * cut, (h + 1) * cut)
        act_y[h].wait_recv()
        act_diag = send(acts.at[span_of(2, h)], acts.at[span_of(3, h)], core_mate)
        ahead = feed(span_of(2, h))
        act_diag.wait_recv()
        out_diag[0, rows_h] = low(feed(span_of(3, h)))
        diag_sum = send(out_diag.at[0, rows_h], in_diag.at[0, rows_h], core_mate)
        diag_sum.wait_recv()
        out_y[0, rows_h] = low(ahead + in_diag[0, rows_h].astype(f32))
        y_sums.append(send(out_y.at[0, rows_h], in_y.at[0, rows_h], y_mate))
    out_diag[1] = low(forth(3))
    diag_sum = send(out_diag.at[1], in_diag.at[1], core_mate)
    out_core[1] = low(forth(1))
    core_sums.append(send(out_core.at[1], in_core.at[1], core_mate))
    ahead = forth(2)
    diag_sum.wait_recv()
    out_y[1] = low(ahead + in_diag[1].astype(f32))
    y_sums.append(send(out_y.at[1], in_y.at[1], y_mate))
    po0[...] = forth(0)
    core_sums[0].wait_recv()
    y_sums[0].wait_recv()
    y_sums[1].wait_recv()
    grad_act = pg0[...] + in_core[0].astype(f32) + in_y[0].astype(f32)
    unit_two = unit[...]
    gfeed_ref[...] = jnp.sum(grad_act * unit_two, 0, keepdims=True)
    w = grad_act * gain
    inv = 1.0 / width
    grad = cot_ref[...].astype(f32) + scales[:, 0:1] * (
        w - jnp.sum(w, -1, keepdims=True) * inv - unit_two * (jnp.sum(w * unit_two, -1, keepdims=True) * inv)
    )
    hid_ref[...] = grad
    branch[...] = low(grad)
    row_mates, group_mates = mates("row"), mates("group")
    block = lambda r: branch_row.at[rows_at((r * groups + group) * span, span)]
    by_row = [
        send(branch.at[rows_at(lax.rem(row + o, rows) * span, span)], block(row), row_mates[o - 1]) for o in range(1, rows)
    ]
    block(row)[...] = branch[rows_at(row * span, span)]
    moves = [send(block(row), block(row), mate) for mate in group_mates]
    feed_terms(((t0, t1), acts, gg), ((t2, t3), acts, gu), ((t4, t5), cots, ha))
    for o in range(1, rows):
        by_row[o - 1].wait_recv()
        from_row = block(lax.rem(row - o + rows, rows))
        moves += [send(from_row, from_row, mate) for mate in group_mates]
    core_sums[1].wait_recv()
    y_sums[2].wait_recv()
    block_ref[...] = low(h_in[...] + po0[...] + in_core[1].astype(f32) + in_y[1].astype(f32))
    for copy in moves:
        copy.wait_recv()
    gmix_ref[...] = dot_nt(branch_row[...], wout_ref[rows_at(group * cols, cols)])
    for h in range(2):
        half = branch_row[:, h * (width // 2) : (h + 1) * (width // 2)]
        gwo_ref[h * cols : (h + 1) * cols] = low(dot_tn(mixed_ref[...], half))
    for copy in copies.started:
        copy.wait_send()


def middle(mixed_row, tokens, cotangent, out_weight, gate_weight, up_weight, down_weight, gain, span, collective_id):
    rows, groups = lax.axis_size("row"), lax.axis_size("group")
    length, cols = mixed_row.shape[0] - MB, mixed_row.shape[1]
    count, width = tokens.shape
    hidden = gate_weight.shape[1]
    copies = (rows * groups - 1) + (rows - 1) + rows * (groups - 1) + 18
    vmem = pl.BlockSpec(memory_space=pltpu.VMEM)
    outs = [
        ((count, width), bf16), ((count, width), f32), ((length, cols), f32), ((2 * cols, width // 2), bf16),
        *[((2 * width, 128), bf16)] * 6, ((1, width), f32),
    ]
    two = pltpu.VMEM((2, count, width), bf16)
    return pl.pallas_call(
        partial(middle_kernel, span),
        in_specs=[vmem] + [ANYWHERE] * 6 + [vmem],
        out_specs=[vmem] * len(outs),
        out_shape=[jax.ShapeDtypeStruct(*o) for o in outs],
        scratch_shapes=[
            pltpu.VMEM((count, width), bf16),
            pltpu.VMEM((count, width), bf16),
            pltpu.VMEM(out_weight.shape, bf16),
            *[pltpu.VMEM((width, hidden), bf16)] * 3,
            pltpu.VMEM((4 * count, hidden), f32),
            pltpu.VMEM((length, cols), bf16),
            pltpu.VMEM((count, groups * cols), bf16),
            pltpu.VMEM((4 * count, width), bf16),
            pltpu.VMEM((4 * count, width), bf16),
            pltpu.VMEM((count, width), f32),
            pltpu.VMEM((count, 128), f32),
            pltpu.VMEM((count, width), f32),
            pltpu.VMEM((4 * count, hidden), bf16),
            pltpu.VMEM((4 * count, hidden), bf16),
            pltpu.VMEM((4 * count, hidden), bf16),
            pltpu.VMEM((count, width), f32),
            pltpu.VMEM((count, width), f32),
            two, two, two, two, two, two,
            pltpu.VMEM((count, width), bf16),
            pltpu.VMEM((length, width), bf16),
            pltpu.SemaphoreType.DMA((copies,)),
            pltpu.SemaphoreType.DMA((copies,)),
            pltpu.SemaphoreType.DMA((1,)),
            pltpu.SemaphoreType.DMA((6,)),
        ],
        compiler_params=pltpu.CompilerParams(
            collective_id=collective_id, has_side_effects=True, vmem_limit_bytes=63 * 1024 * 1024
        ),
        name="middle",
    )(mixed_row, tokens, cotangent, out_weight, gate_weight, up_weight, down_weight, gain)


def own_rows(array, mine):
    total = None
    for g in range(lax.axis_size("group")):
        part = array[g * mine : (g + 1) * mine].astype(f32)
        if part.shape[0]:
            part = jnp.concatenate([part, jnp.zeros((128 - part.shape[0], array.shape[1]), f32)], 0)
            part = jnp.where(lax.axis_index("group") == g, part, 0.0)
            total = part if total is None else total + part
    return total


def head_kernel(span, heads, mine, head_dim, tok_ref, gain_ref, wq_in, wk_in, wv_in, wr_ref, rb_ref,
                q_out, k_out, v_out, act_out, unit_out, rate_ref, slope_ref, stat_ref, wown_ref,
                q_ref, k_ref, v_ref, act_ref, unit_ref, out_sems, row_tok, wq_ref, wk_ref, wv_ref, send_sem, recv_sem, sems):
    rows, groups = lax.axis_size("row"), lax.axis_size("group")
    row, group, feat = lax.axis_index("row"), lax.axis_index("group"), lax.axis_index("feat")
    row_mates, group_mates = mates("row"), mates("group")
    width = tok_ref.shape[2]
    cols = q_out.shape[1]
    copies = Copies(send_sem, recv_sem)
    block = lambda r: row_tok.at[rows_at((r * groups + group) * span, span)]

    lanes = pl.ds(pl.multiple_of(group * cols, 128), cols)
    loads = fetch(sems, *[(src.at[:, lanes], dst) for src, dst in ((wq_in, wq_ref), (wk_in, wk_ref), (wv_in, wv_ref))])
    greet(row_mates + group_mates)
    by_row = [
        copies.send(tok_ref.at[lax.rem(row + o, rows)], block(row), row_mates[o - 1]) for o in range(1, rows)
    ]
    block(row)[...] = tok_ref[row]
    by_group = {row_offset: [] for row_offset in range(rows)}
    by_group[0] = [copies.send(block(row), block(row), mate) for mate in group_mates]
    gain = gain_ref[...].reshape(1, width)
    for load in loads:
        load.wait()

    results = list(zip((q_ref, k_ref, v_ref, act_ref, unit_ref), (q_out, k_out, v_out, act_out, unit_out)))

    def work_on(place):
        here = rows_at(place * span, span)
        unit, _ = norm_parts(row_tok[here].astype(f32), width)
        unit_ref[here] = unit
        act = low(unit * gain)
        act_ref[here] = act
        for out, weight in ((q_ref, wq_ref), (k_ref, wk_ref), (v_ref, wv_ref)):
            out[here] = dot(act, weight[...])
        for i, (held, out) in enumerate(results):
            pltpu.make_async_copy(held.at[here], out.at[here], out_sems.at[i]).start()

    work_on(row * groups + group)
    for o in range(1, rows):
        r = lax.rem(row - o + rows, rows)
        by_row[o - 1].wait_recv()
        by_group[o] = [copies.send(block(r), block(r), mate) for mate in group_mates]
        if o > 1:
            work_on(lax.rem(row - o + 1 + rows, rows) * groups + group)
    work_on(lax.rem(row - rows + 1 + rows, rows) * groups + group)
    for o in range(rows):
        r = lax.rem(row - o + rows, rows)
        for copy in by_group[o]:
            copy.wait_recv()
        lax.fori_loop(1, groups, lambda g, _: work_on(r * groups + lax.rem(group + g, groups)), None)
    rate_weight = low(own_rows(wr_ref[...], mine))
    wown_ref[...] = rate_weight
    rate_bias = own_rows(jnp.broadcast_to(rb_ref[...].reshape(1, heads), (8, heads)).T, mine).T[0:1]
    logits = dot_nt(act_ref[...], rate_weight) + rate_bias
    sigma = jax.nn.sigmoid(logits)
    lane = lax.broadcasted_iota(jnp.int32, logits.shape, 1)
    used = (lane < mine) & (group * mine + lane < heads)
    rate_ref[...] = sigma * (1.0 / head_dim)
    slope_ref[...] = jnp.where(used, sigma * (1.0 - sigma) * (1.0 / head_dim), 0.0)
    stat_ref[0:1] = jnp.sum(logits, 0, keepdims=True)
    top = jnp.max(jnp.max(jnp.where(used, logits, -3e38), 0, keepdims=True), 1, keepdims=True)
    place = row * lax.axis_size("feat") + feat
    stat_ref[1:2] = jnp.where(lane[0:1] == place, top, 0.0)
    for copy in copies.started:
        copy.wait_send()
    for i, (held, out) in enumerate(results):
        pltpu.make_async_copy(held, out, out_sems.at[i]).wait()


def head(tokens, gain, weights, rate_weight, rate_bias, heads, mine, head_dim, collective_id):
    rows, groups = lax.axis_size("row"), lax.axis_size("group")
    _, span, width = tokens.shape
    length, cols = rows * groups * span, mine * head_dim
    vmem = pl.BlockSpec(memory_space=pltpu.VMEM)
    copies = (rows - 1) + rows * (groups - 1)
    outs = [((length, cols), f32)] * 3 + [((length, width), bf16), ((length, width), f32)]
    outs += [((length, 128), f32)] * 2 + [((2, 128), f32), ((128, width), bf16)]
    return pl.pallas_call(
        partial(head_kernel, span, heads, mine, head_dim),
        in_specs=[vmem] * 2 + [ANYWHERE] * 3 + [vmem] * 2,
        out_specs=[ANYWHERE] * 5 + [vmem] * (len(outs) - 5),
        out_shape=[jax.ShapeDtypeStruct(*o) for o in outs],
        scratch_shapes=[
            *[pltpu.VMEM(*o) for o in outs[:5]],
            pltpu.SemaphoreType.DMA((5,)),
            pltpu.VMEM((length, width), bf16),
            *[pltpu.VMEM((width, cols), bf16)] * 3,
            pltpu.SemaphoreType.DMA((copies,)),
            pltpu.SemaphoreType.DMA((copies,)),
            pltpu.SemaphoreType.DMA((3,)),
        ],
        compiler_params=pltpu.CompilerParams(
            collective_id=collective_id, has_side_effects=True, vmem_limit_bytes=63 * 1024 * 1024
        ),
        name="head",
    )(tokens, gain, *weights, rate_weight, rate_bias)


TAIL_SLOTS = [
    ([], ["FZ1", "CORE3", "FZ2", "FZ0", "PART0"]),
    (["CORE3"], ["Y3", "CORE0", "CORE2"]),
    (["FZ1"], ["FX1", "FZ3", "CORE4"]),
    (["CORE0"], ["Y0", "CORE1"]),
    (["CORE2"], ["Y2"]),
    (["CORE4", "Y3"], ["Y4"]),
    (["CORE1", "FZ2"], ["Z3", "FX2"]),
    (["Y0"], ["Y1"]),
    (["FZ0"], ["Z0"]),
    (["PART0"], ["SC0", "FX0"]),
    (["Y2", "SC0"], ["SY0"]),
    (["Y4", "FZ3"], ["Z2"]),
    (["FX1"], ["FX3"]),
    (["Z3"], ["ZA3"]),
    (["Y1", "SY0", "FX2", "Z0"], ["ZA0"]),
    (["FX0", "Z2"], ["Z4"]),
    (["ZA3"], ["Z1", "PY3", "PX3"]),
    (["FX3", "ZA0"], ["PY0", "PX0", "ZA2"]),
    (["Z4"], ["ZA4"]),
    (["PY3"], ["QX3"]),
    (["PX3"], ["QY3"]),
    (["Z1"], ["ZA1"]),
    (["PY0"], ["QX0"]),
    (["PX0"], ["QY0"]),
    (["QY3", "QX3"], ["C3"]),
    (["ZA2"], ["PY2", "PX2", "SZ0"]),
    (["C3", "QX0", "QY0"], ["C0"]),
    (["ZA4"], ["PX4", "PY4", "HOME0"]),
    (["C0", "ZA1"], ["PX1", "PY1"]),
    (["PY2", "PX2"], ["QX2", "QY2"]),
    (["PY4", "PX4"], ["QX4", "QY4"]),
    (["SZ0", "PY1", "PX1"], ["QY1", "QX1"]),
    (["QY2", "QX2"], ["SX0", "C2"]),
    (["QY4", "QX4"], ["C4"]),
    (["C2", "QY1", "QX1"], ["C1"]),
    (["C4", "SX0", "HOME0", "C1"], []),
]


FEED_SLOTS = [
    (0, [], ["X1", "X0"]),
    (6, ["X1"], ["Z1", "X3"]),
    (9, ["X0"], ["Z0", "X2"]),
    (12, ["Z1"], ["ZA1"]),
    (12, ["X3"], ["X4"]),
    (15, ["Z0"], ["ZA0"]),
    (15, ["X2"], ["X5"]),
    (17, ["ZA1"], ["Z3"]),
    (18, ["X4"], ["XA1"]),
    (20, ["ZA0"], ["Z4"]),
    (21, ["X5"], ["XA0"]),
    (23, ["Z3"], ["Z2"]),
    (24, ["XA1"], []),
    (26, ["Z4"], ["Z5"]),
    (27, ["XA0"], []),
    (29, ["Z2"], []),
    (32, ["Z5"], []),
]
FEED_WHOLE = 2


def tail_kernel(span, shapes, feeds, act_ref, unit_in, gq_ref, gk_ref, gv_ref, de_in, slope_in, wq_in, wk_in, wv_in, wr_ref,
                gwo_ref, gw1, gb1, gw2, gb2, ggain, gbias, gfeed, stat_ref, *refs):
    rows, groups = lax.axis_size("row"), lax.axis_size("group")
    row, group, feat = lax.axis_index("row"), lax.axis_index("group"), lax.axis_index("feat")
    core, y = lax.rem(feat, 2), feat // 2
    core_mate, y_mate = {"feat": feat + 1 - 2 * core}, {"feat": feat + 2 - 4 * y}
    row_mates, group_mates = mates("row"), mates("group")
    count = len(shapes)
    feed_in, refs = refs[:feeds], refs[feeds:]
    outs, (home_out, small_out), refs = refs[:count], refs[count : count + 2], refs[count + 2 :]
    feed_out, refs = refs[:feeds], refs[feeds:]
    own, got_core, sum_core, got_y, sum_y, got_row = (refs[i * count : (i + 1) * count] for i in range(6))
    part, part_got, part_sum, small, small_core, small_got, unit_ref, de_ref, slope_ref, wq_ref, wk_ref, wv_ref, send_sem, recv_sem, sems = refs[6 * count :]
    length, width = act_ref.shape
    cols = gwo_ref.shape[0] // 2
    pairs, pair, inner = gw1.shape
    head_dim = pair // 2
    copies = Copies(send_sem, recv_sem)
    moves = {}

    def start(name, *what):
        moves[name] = [copies.send(*w) for w in what]

    lanes = pl.ds(pl.multiple_of(group * cols, 128), cols)
    loads = fetch(
        sems, (de_in, de_ref), (slope_in, slope_ref),
        *[(src.at[:, lanes], dst) for src, dst in ((wq_in, wq_ref), (wk_in, wk_ref), (wv_in, wv_ref))], (unit_in, unit_ref),
    )
    greet([core_mate, y_mate] + row_mates + group_mates)

    half = [h // 2 for h, _ in shapes]
    quarter = [h // 4 for h, _ in shapes]
    piece = [h // (4 * rows) for h, _ in shapes]
    unit = feed_in[0].shape[0]
    place = (core * 2 + y) * rows + row
    source = list(own[:3]) + [gwo_ref, own[4]]
    grad_refs = (gq_ref, gk_ref, gv_ref)

    def token_gradient():
        for load in loads:
            load.wait()
        logits = low(de_ref[0:length] * slope_ref[...])
        total = dot(logits, wr_ref[...])
        for grad, weight in zip(grad_refs, (wq_ref, wk_ref, wv_ref)):
            total = total + dot_nt(grad[0:length], weight[...])
        for r in range(rows):
            for g in range(groups):
                part[g, r * span : (r + 1) * span] = low(total[(r * groups + g) * span : (r * groups + g + 1) * span])
        start("PART0", *[(part.at[lax.rem(group + o, groups)], part_got.at[o - 1], group_mates[o - 1]) for o in range(1, groups)])
        small[...] = jnp.zeros_like(small)
        small[0 : 2 * pairs] = dot_tn(logits, act_ref[...])[0 : 2 * pairs]
        for p in range(pairs):
            for h in range(2):
                n = 2 * p + h
                small[6 + n // 3 : 7 + n // 3, (n % 3) * inner : (n % 3 + 1) * inner] = gb1[p, h * MB : h * MB + 1]
            small[9:10, p * pair : (p + 1) * pair] = gb2[p, 0:1] + gb2[p, MB : MB + 1]
        small[8:9, 0:cols] = jnp.sum(ggain[...], 0, keepdims=True)
        small[8:9, cols : 2 * cols] = jnp.sum(gbias[...], 0, keepdims=True)
        small[9:10, width - 384 : width - 256] = jnp.sum(logits.astype(f32), 0, keepdims=True)
        small[9:10, width - 256 : width - 128] = stat_ref[0:1]
        small[9:10, width - 128 : width] = stat_ref[1:2]
        small[10:11] = jnp.sum(total * unit_ref[...], 0, keepdims=True)
        small[11:12] = gfeed[...]

    def finish(name):
        for copy in moves[name]:
            copy.wait_recv()
        kind, i = name[:-1], int(name[-1])
        if kind == "CORE":
            sum_core[i][...] = add_low(source[i][rows_at(core * half[i], half[i])], got_core[i][...])
        if kind == "Y":
            sum_y[i][...] = add_low(sum_core[i][rows_at(y * quarter[i], quarter[i])], got_y[i][...])
        if kind == "Z":
            value = sum_y[i][rows_at(row * piece[i], piece[i])].astype(f32)
            for o in range(1, rows):
                value = value + got_row[i][o - 1].astype(f32)
            outs[i][group, rows_at(place * piece[i], piece[i])] = low(value)
        if kind == "PART":
            value = part[group].astype(f32)
            for o in range(1, groups):
                value = value + part_got[o - 1].astype(f32)
            part_sum[...] = low(value)
            home_out[rows_at(row * span, span)] = part_sum[rows_at(row * span, span)]
        if kind == "SC":
            small_core[...] = small[...] + small_got[0]
        if kind == "SY":
            small_got[2 + row] = small_core[...] + small_got[1]
        if kind == "SZ":
            value = small_got[2]
            for r in range(1, rows):
                value = value + small_got[2 + r]
            small_out[group] = value

    def begin(name):
        kind, i = name[:-1], int(name[-1])
        if kind == "PART":
            token_gradient()
        if kind == "HOME":
            here = home_out.at[rows_at(row * span, span)]
            start(name, *[
                (part_sum.at[rows_at(lax.rem(row + o, rows) * span, span)], here, row_mates[o - 1]) for o in range(1, rows)
            ])
        if kind == "SC":
            start(name, (small, small_got.at[0], core_mate))
        if kind == "SY":
            start(name, (small_core, small_got.at[1], y_mate))
        if kind == "SZ":
            here = small_got.at[2 + row]
            start(name, *[(here, here, mate) for mate in row_mates])
        if kind == "SX":
            here = small_out.at[group]
            start(name, *[(here, here, mate) for mate in group_mates])
        if kind == "FZ":
            here = feed_out[i].at[group, rows_at(row * unit, unit)]
            here[...] = feed_in[i][...]
            start(name, *[(here, here, mate) for mate in row_mates])
        if kind == "FX":
            here = feed_out[i].at[group]
            start(name, *[(here, here, mate) for mate in group_mates])
        if kind == "CORE":
            if i < 3:
                own[i][...] = low(dot_tn(act_ref[...], grad_refs[i][0:length]))
            if i == 4:
                for p in range(pairs):
                    own[4][p * pair : (p + 1) * pair] = low(gw1[p])
                    own[4][cols + p * pair : cols + (p + 1) * pair] = low(gw2[p])
            start(name, (source[i].at[rows_at((1 - core) * half[i], half[i])], got_core[i], core_mate))
        if kind == "Y":
            start(name, (sum_core[i].at[rows_at((1 - y) * quarter[i], quarter[i])], got_y[i], y_mate))
        if kind == "Z":
            start(name, *[
                (sum_y[i].at[rows_at(lax.rem(row + o, rows) * piece[i], piece[i])], got_row[i].at[o - 1], row_mates[o - 1])
                for o in range(1, rows)
            ])
        if kind == "ZA":
            here = outs[i].at[group, rows_at(place * piece[i], piece[i])]
            start(name, *[(here, here, mate) for mate in row_mates])
        step = quarter[i] // 2
        quarter_of = lambda at_y, first, size: rows_at((core * 2 + at_y) * quarter[i] + first, size)
        if kind in ("PX", "PY"):
            here = outs[i].at[group, quarter_of(y, 0, quarter[i])]
            start(name, *[(here, here, mate) for mate in (group_mates if kind == "PX" else [y_mate])])
        if kind == "QX":
            here = outs[i].at[group, quarter_of(1 - y, step, step)]
            start(name, *[(here, here, mate) for mate in group_mates])
        if kind == "QY":
            others = [outs[i].at[lax.rem(group + o, groups), quarter_of(y, 0, step)] for o in range(1, groups)]
            start(name, *[(here, here, y_mate) for here in others])
        if kind == "C":
            here = outs[i].at[:, rows_at(core * half[i], half[i])]
            start(name, (here, here, core_mate))

    for done, begun in TAIL_SLOTS:
        for name in done:
            finish(name)
        for name in begun:
            begin(name)
    for copy in copies.started:
        copy.wait_send()


def tail(act_row, unit_row, grads, de, slope, weights, rate_weight, grad_out, states, grad_feed_gain, stat, feed_parts, span, collective_id):
    rows, groups = lax.axis_size("row"), lax.axis_size("group")
    length, width = act_row.shape
    cols = grad_out.shape[0] // 2
    inner = states[0].shape[-1]
    shapes = [(width, cols)] * 3 + [(2 * cols, width // 2), (2 * cols, inner)]
    count, feeds = len(shapes), len(feed_parts)
    unit, wide = feed_parts[0].shape
    copies = count * (2 + 2 * (rows - 1) + 3 * (groups - 1) + 2) + (groups - 1) + (rows - 1) + 2 + (rows - 1) + (groups - 1)
    copies += feeds * (rows + groups - 2)
    vmem = pl.BlockSpec(memory_space=pltpu.VMEM)
    operands = [act_row, unit_row, *grads, de, slope, *weights, rate_weight, grad_out, *states, grad_feed_gain, stat, *feed_parts]
    outs = [((groups, h, w), bf16) for h, w in shapes]
    outs += [((rows * span, width), bf16), ((groups, 16, width), f32)]
    outs += [((groups, rows * unit, wide), bf16)] * feeds
    scratch = [pltpu.VMEM((h, w), bf16) for h, w in shapes]
    scratch += [pltpu.VMEM((h // 2, w), bf16) for h, w in shapes] * 2
    scratch += [pltpu.VMEM((h // 4, w), bf16) for h, w in shapes] * 2
    scratch += [pltpu.VMEM((rows - 1, h // (4 * rows), w), bf16) for h, w in shapes]
    scratch += [
        pltpu.VMEM((groups, rows * span, width), bf16),
        pltpu.VMEM((groups - 1, rows * span, width), bf16),
        pltpu.VMEM((rows * span, width), bf16),
        pltpu.VMEM((16, width), f32),
        pltpu.VMEM((16, width), f32),
        pltpu.VMEM((2 + rows, 16, width), f32),
        *[pltpu.VMEM(a.shape, f32) for a in (unit_row, de, slope)],
        *[pltpu.VMEM((width, cols), bf16)] * 3,
        pltpu.SemaphoreType.DMA((copies,)),
        pltpu.SemaphoreType.DMA((copies,)),
        pltpu.SemaphoreType.DMA((6,)),
    ]
    return pl.pallas_call(
        partial(tail_kernel, span, shapes, feeds),
        in_specs=[ANYWHERE if i in (1, 5, 6, 7, 8, 9) else vmem for i in range(len(operands))],
        out_specs=[vmem] * len(outs),
        out_shape=[jax.ShapeDtypeStruct(*o) for o in outs],
        scratch_shapes=scratch,
        compiler_params=pltpu.CompilerParams(
            collective_id=collective_id, has_side_effects=True, vmem_limit_bytes=63 * 1024 * 1024
        ),
        name="tail",
    )(*operands)


def finish_kernel(heads, mine, head_dim, inner, total_logits, small_ref, gain_ref, *refs):
    large_in, refs = refs[:14], refs[14:]
    (rate_ref, rbias_ref, fbias_ref, sbias_ref, gain_out, bias_out, mixer_ref, feed_ref, stat_ref,
     q_out, k_out, v_out, o_out, first_out, second_out, gate_out, up_out, down_out, in_out,
     sq, sk, sv, so, s1, s2, sg, su, sd, si, sems, *large, load_sems) = refs
    f0, f1, f2, f3, f4, f5, q_in, k_in, v_in, o_in, s_in, got_ref, tok_ref, hid_ref = large
    groups, width = q_in.shape[0], q_in.shape[1]
    loads = [pltpu.make_async_copy(src, dst, load_sems.at[i]) for i, (src, dst) in enumerate(zip(large_in, large))]
    for load in loads[:6]:
        load.start()
    cols = mine * head_dim
    sent = []

    def arrivals():
        for n, load in enumerate(loads):
            load.wait()
            if n == 1:
                for later in loads[6:]:
                    later.start()
            yield

    arrived = arrivals()

    def give(value_ref, out):
        copy = pltpu.make_async_copy(value_ref, out, sems.at[len(sent)])
        copy.start()
        sent.append(copy)

    for out, scratch, left, right in ((gate_out, sg, f0, f1), (up_out, su, f2, f3), (down_out, sd, f4, f5)):
        for i, cut in enumerate((left, right)):
            next(arrived)
            value = cut[...].reshape(2 * width, 128)
            for h in range(2):
                scratch[:, (2 * i + h) * 128 : (2 * i + h + 1) * 128] = value[h * width : (h + 1) * width].astype(f32)
        give(scratch, out)
    for out, scratch, array in ((q_out, sq, q_in), (k_out, sk, k_in), (v_out, sv, v_in)):
        next(arrived)
        for g in range(groups):
            size = min(cols, width - g * cols)
            if size > 0:
                scratch[:, g * cols : g * cols + size] = array[g, :, 0:size].astype(f32)
        give(scratch, out)
    next(arrived)
    for g in range(groups):
        size = min(cols, width - g * cols)
        if size > 0:
            for h in range(2):
                scratch = so.at[g * cols : g * cols + size, h * (width // 2) : (h + 1) * (width // 2)]
                scratch[...] = o_in[g, h * cols : h * cols + size].astype(f32)
    give(so, o_out)
    next(arrived)
    for n in range(heads):
        g, i = n // mine, n % mine
        s1[n] = s_in[g, i * head_dim : (i + 1) * head_dim].astype(f32)
        second = s_in[g, cols + i * head_dim : cols + (i + 1) * head_dim].astype(f32)
        s2[n] = second - jnp.sum(second, 0, keepdims=True) * (1.0 / head_dim)
    give(s1, first_out)
    give(s2, second_out)
    for _ in arrived:
        pass
    unit, scale = norm_parts(tok_ref[...].astype(f32), width)
    w = got_ref[...].astype(f32) * gain_ref[...].reshape(1, width)
    inv = 1.0 / width
    si[...] = hid_ref[...] + scale * (
        w - jnp.sum(w, -1, keepdims=True) * inv - unit * (jnp.sum(w * unit, -1, keepdims=True) * inv)
    )
    give(si, in_out)
    total = 0.0
    for n in range(heads):
        g, i = n // mine, n % mine
        rate_ref[n : n + 1] = small_ref[g, i : i + 1]
        rbias_ref[:, n : n + 1] = small_ref[g, 9:10, width - 384 + i : width - 383 + i]
        total = total + small_ref[g, 9:10, width - 256 + i : width - 255 + i]
        fbias_ref[n : n + 1] = small_ref[g, 6 + i // 3 : 7 + i // 3, (i % 3) * inner : (i % 3 + 1) * inner]
        own = slice(i * head_dim, (i + 1) * head_dim)
        second = small_ref[g, 9:10, own]
        sbias_ref[n : n + 1] = second - jnp.sum(second, -1, keepdims=True) * (1.0 / head_dim)
        gain_out[n : n + 1] = small_ref[g, 8:9, own]
        bias_out[n : n + 1] = small_ref[g, 8:9, cols + i * head_dim : cols + (i + 1) * head_dim]
    mixer, feed = small_ref[0, 10:11], small_ref[0, 11:12]
    tops = small_ref[0, 9:10, width - 128 : width]
    peers = lax.axis_size("row") * lax.axis_size("feat")
    for g in range(1, groups):
        mixer, feed = mixer + small_ref[g, 10:11], feed + small_ref[g, 11:12]
        tops = jnp.maximum(tops, small_ref[g, 9:10, width - 128 : width])
    mixer_ref[...], feed_ref[...] = mixer.reshape(width), feed.reshape(width)
    lane = lax.broadcasted_iota(jnp.int32, tops.shape, 1)
    top = jnp.max(jnp.where(lane < peers, tops, -3e38), 1, keepdims=True)
    stat_ref[...] = jnp.where(lane == 0, total * (1.0 / total_logits), top)[:, 0:2].reshape(2)
    for copy in sent:
        copy.wait()


def finish(arrays, got, small, tokens, grad_hidden, gain, feed_sums, heads, mine, head_dim, inner, total_logits):
    count, width = tokens.shape
    hidden = 2 * 2 * 128
    vmem = pl.BlockSpec(memory_space=pltpu.VMEM)
    little = [(heads, width), (1, heads), (heads, inner), (heads, head_dim), (heads, head_dim), (heads, head_dim)]
    little += [(width,), (width,), (2,)]
    large = [(width, width)] * 4 + [(heads, head_dim, inner)] * 2 + [(width, hidden)] * 3 + [(count, width)]
    large_in = [*feed_sums, *arrays, got, tokens, grad_hidden]
    return pl.pallas_call(
        partial(finish_kernel, heads, mine, head_dim, inner, total_logits),
        in_specs=[vmem] * 2 + [ANYWHERE] * len(large_in),
        out_specs=[vmem] * len(little) + [ANYWHERE] * len(large),
        out_shape=[jax.ShapeDtypeStruct(s, f32) for s in little + large],
        scratch_shapes=[
            *[pltpu.VMEM(s, f32) for s in large],
            pltpu.SemaphoreType.DMA((len(large),)),
            *[pltpu.VMEM(a.shape, a.dtype) for a in large_in],
            pltpu.SemaphoreType.DMA((len(large_in),)),
        ],
        compiler_params=pltpu.CompilerParams(vmem_limit_bytes=63 * 1024 * 1024),
        name="finish",
    )(small, gain, *large_in)


SEQ = ("row", "group")


def per_device(
    tokens,
    cotangent,
    doc_starts,
    mixer_gain,
    query_weight,
    key_weight,
    value_weight,
    out_weight,
    rate_weight,
    rate_bias,
    first_init,
    first_bias_init,
    second_init,
    second_bias_init,
    inner_gain,
    inner_bias,
    feed_gain,
    gate_weight,
    up_weight,
    down_weight,
):
    rows, span, width = tokens.shape
    heads, head_dim, inner = first_init.shape
    groups = lax.axis_size("group")
    feats = lax.axis_size("feat")
    row, group = lax.axis_index("row"), lax.axis_index("group")
    count = rows * span
    blocks = span * rows * groups // MB
    pairs = -(-heads // (2 * groups))
    mine = 2 * pairs
    pair = 2 * head_dim
    spare = mine * groups - heads

    def padded(array, axis, size):
        edges = [(0, 0)] * array.ndim
        edges[axis] = (0, spare * size)
        return jnp.pad(array, edges) if spare else array

    weights = [padded(w, 1, head_dim) for w in (query_weight, key_weight, value_weight)]
    flat_tokens = tokens.reshape(count, width)
    queries, keys, values, act_row, unit_row, rates, slope, stat, rate_lanes = head(
        tokens, mixer_gain, weights, rate_weight.T, rate_bias, heads, mine, head_dim, 4
    )
    block_ids = jnp.arange(blocks + 1, dtype=jnp.int32)
    starts = lax.dynamic_index_in_dim(doc_starts, row, 0, False)
    restarts = ((block_ids == 0) | jnp.any(starts[:, None] == block_ids[None], 0)).astype(jnp.int32)
    by_pair = lambda a: a.reshape(heads // 2, pair, inner)
    *saved, mixed = forward_inner(
        restarts, queries, keys, values, rates, by_pair(first_init), first_bias_init, by_pair(second_init),
        second_bias_init, inner_gain, inner_bias,
    )

    block_out, grad_hidden, grad_mixed, grad_out_rows, *feed_terms, grad_feed_gain = middle(
        mixed, flat_tokens, cotangent.reshape(count, width), padded(out_weight, 0, head_dim),
        gate_weight, up_weight, down_weight, feed_gain, span, 1,
    )

    grad_q, grad_k, grad_v, grad_e, g_first, g_first_bias, g_second, g_second_bias, g_gain, g_bias, *feed_sums = (
        backward_inner(restarts, queries, keys, values, grad_mixed, rates, saved, inner_gain, inner_bias, feed_terms, 2)
    )
    reduced = tail(
        act_row, unit_row, (grad_q, grad_k, grad_v), grad_e, slope, weights, rate_lanes, grad_out_rows,
        (g_first, g_first_bias, g_second, g_second_bias, g_gain, g_bias), grad_feed_gain, stat,
        feed_sums[FEED_WHOLE:], span, 3,
    )
    arrays, (got, small), feed_sums = reduced[:5], reduced[5:7], [*feed_sums[:FEED_WHOLE], *reduced[7:]]
    (
        g_rate, g_rate_bias, g_first_bias, g_second_bias, g_gain, g_bias, g_mixer, g_feed, stats,
        g_query, g_key, g_value, g_out, g_first, g_second, g_gate, g_up, g_down, input_grad,
    ) = finish(
        arrays, got, small, flat_tokens, grad_hidden, mixer_gain, feed_sums, heads, mine, head_dim, inner,
        rows * groups * feats * count * heads,
    )
    return (
        block_out.reshape(rows, span, width),
        input_grad.reshape(rows, span, width),
        g_mixer,
        g_query,
        g_key,
        g_value,
        g_out,
        g_rate.T,
        g_rate_bias[0],
        g_first,
        g_first_bias,
        g_second,
        g_second_bias,
        g_gain,
        g_bias,
        g_feed,
        g_gate,
        g_up,
        g_down,
        stats,
    )


def solution(mesh):
    feats = mesh.shape["feat"]

    def run(*arrays):
        rows = arrays[0].shape[0] // feats
        grid = jax.sharding.Mesh(mesh.devices.reshape(rows, -1, feats), ("row", "group", "feat"))
        by_token = P("feat", SEQ, None)
        by_hidden = P(None, "feat")
        return jax.shard_map(
            per_device,
            mesh=grid,
            in_specs=(by_token, by_token, P("feat", None)) + (P(),) * 14 + (by_hidden,) * 3,
            out_specs=(by_token, by_token) + (P(),) * 14 + (by_hidden,) * 3 + (P(),),
            check_vma=False,
        )(*arrays)

    return run
```
